32 devices in a mesh: slot: 2 (over core), ctx: 4 (over y, x), uly: 4 (over z).
Axes of the slice: x: 2, y: 2, z: 4, core: 2. Of those that a mesh axis runs over, the one named last changes fastest.
Arguments:
- tokens: bfloat16 [2, 2048, 2048], P('slot', ('ctx', 'uly')), may hold values from -6 to 6
- segment_ids: int32 [2, 2048], P('slot', ('ctx', 'uly')), may hold values from 0 to 1, as said below
- qkv_weight: bfloat16 [3, 2048, 2048], P(None, ('slot', 'ctx'), 'uly'), may hold values from -0.125 to 0.125
- out_weight: bfloat16 [2048, 2048], P('uly', ('slot', 'ctx')), may hold values from -0.125 to 0.125
- gate_up: bfloat16 [2, 2048, 8192], P(None, ('slot', 'ctx'), 'uly'), may hold values from -0.125 to 0.125
- down_weight: bfloat16 [8192, 2048], P('uly', ('slot', 'ctx')), may hold values from -0.0625 to 0.0625
- qk_gain: float32 [2, 2048], P(None, 'uly'), may hold values from 0.1 to 1.9
- post_gain: float32 [2, 2048], replicated, may hold values from 0.1 to 1.9
- cotangent: bfloat16 [2, 2048, 2048], P('slot', ('ctx', 'uly')), may hold values from -6 to 6
Outputs:
- block_out: bfloat16 [2, 2048, 2048], P('slot', ('ctx', 'uly'))
- input_grad: bfloat16 [2, 2048, 2048], P('slot', ('ctx', 'uly'))
- qkv_grad: float32 [3, 2048, 2048], P(None, ('slot', 'ctx'), 'uly')
- out_grad: float32 [2048, 2048], P('uly', ('slot', 'ctx'))
- gate_up_grad: float32 [2, 2048, 8192], P(None, ('slot', 'ctx'), 'uly')
- down_grad: float32 [8192, 2048], P('uly', ('slot', 'ctx'))
- gain_grad: float32 [4, 2048], P(None, ('slot', 'ctx'))
The draws below stay inside these ranges and needn't reach their ends.
Inputs may be any that keep to these rules, and one draw needn't show every extreme that they name: `segment_ids`: in each slot the ids never fall: all 0 (one sequence), or 0 up to a boundary of the slot's own and 1 from there on (two sequences), the boundary lying between 512 and 1536. One slot, drawn from the seed, holds one sequence; every other slot holds two.
All inputs are finite; a program needn't handle non-finite values.
Results may differ from the reference program's by a relative error of at most 0.025.
Values may be sent and summed in bfloat16 or wider, within the bound.
A program may use at most 192 MiB of HBM per device.

```python
import jax
import jax.numpy as jnp
from jax import lax

D = 2048
HEADS = 16
HEAD_DIM = 128
FF = 8192
SLOTS = 2
SLOT_LEN = 2048


def draw_segment_ids(key, part):
    key = jax.random.fold_in(key, 7)
    single = jax.random.randint(jax.random.fold_in(key, 1), (), 0, SLOTS)
    bounds = jax.random.randint(jax.random.fold_in(key, 2), (SLOTS,), SLOT_LEN // 4, 3 * SLOT_LEN // 4 + 1)
    bounds = jnp.where(jnp.arange(SLOTS) == single, SLOT_LEN, bounds).astype(jnp.int32)
    places = jnp.arange(SLOT_LEN, dtype=jnp.int32)
    return (places[None, :] >= bounds[:, None]).astype(jnp.int32)


def levels(stream_key, shape, shards, smallest, high):
    gain = 1.0
    for dim, shards_of in shards:
        heights = jax.random.uniform(jax.random.fold_in(jax.random.fold_in(stream_key, 6), dim), (shards_of,), jnp.float32, smallest / len(shards), high / len(shards))
        gain = gain * jnp.repeat(jnp.exp(heights), shape[dim] // shards_of).reshape((-1,) + (1,) * (len(shape) - 1 - dim))
    return gain


def centred(key, dims, deviation, most, split=(), kind=jnp.bfloat16):
    loudness = levels(key, dims, split, -0.22, 0.18) if split else 1.0
    values = jax.random.normal(key, dims, jnp.float32) * deviation * loudness
    return jnp.minimum(jnp.maximum(values, -most), most).astype(kind)


def setup_inputs(seed: int = 0) -> dict:
    seeds = jax.random.split(jax.random.key(seed), 10)
    return {
        "tokens": centred(seeds[0], (SLOTS, SLOT_LEN, D), 1.0, 6.0, ((0, 2), (1, 16))),
        "segment_ids": draw_segment_ids(jax.random.fold_in(seeds[9], 71), 0),
        "qkv_weight": centred(seeds[2], (3, D, D), D ** -0.5, 0.125, ((1, 8), (2, 4))),
        "out_weight": centred(seeds[3], (D, D), D ** -0.5, 0.125, ((0, 4), (1, 8))),
        "gate_up": centred(seeds[4], (2, D, FF), D ** -0.5, 0.125, ((1, 8), (2, 4))),
        "down_weight": centred(seeds[5], (FF, D), FF ** -0.5, 0.0625, ((0, 4), (1, 8))),
        "qk_gain": jnp.clip(1.0 + 0.18 * jax.random.normal(seeds[6], (2, D), jnp.float32), 0.1, 1.9),
        "post_gain": jnp.clip(1.0 + 0.18 * jax.random.normal(seeds[7], (2, D), jnp.float32), 0.1, 1.9),
        "cotangent": centred(seeds[8], (SLOTS, SLOT_LEN, D), 1.0, 6.0, ((0, 2), (1, 16))),
    }


@jax.custom_vjp
def low(v):
    return lax.optimization_barrier(v.astype(jnp.bfloat16)).astype(jnp.float32)

@jax.custom_vjp
def low_back(v):
    return v

def low_keep(v):
    return (low(v), None)

def low_pass(kept, grad):
    return (grad,)

def back_keep(v):
    return (v, None)

def back_low(kept, grad):
    return (low(grad),)
low.defvjp(low_keep, low_pass)
low_back.defvjp(back_keep, back_low)
epsilon = 1e-06
rope_base = 500000.0
floor_value = -1e+30

def rotate(values, positions, direction):
    half = values.shape[-1] // 2
    freqs = rope_base ** (-(jnp.arange(half, dtype=jnp.float32) * 2.0 / values.shape[-1]))
    angles = positions.astype(jnp.float32)[:, None] * freqs[None, :]
    cosine = jnp.cos(angles)[:, None, :]
    sine = jnp.sin(angles)[:, None, :]
    first = values[..., :half]
    second = values[..., half:]
    return jnp.concatenate([first * cosine - direction * second * sine, second * cosine + direction * first * sine], axis=-1)

def rms_norm(values):
    return values * lax.rsqrt(lax.optimization_barrier(jnp.mean(values * values, axis=-1, keepdims=True)) + epsilon)

def slot_forward(x_slot, seg_slot, qkv_w, out_w, gate_w, down_w, qk_g, post_g):
    highest = lax.Precision.HIGHEST
    length = x_slot.shape[0]
    scale = HEAD_DIM ** (-0.5)
    projected = low_back(jnp.einsum('td,cde->cte', x_slot, qkv_w, precision=highest))
    query_norm = rms_norm(projected[0]) * qk_g[0]
    key_norm = rms_norm(projected[1]) * qk_g[1]
    positions = jnp.arange(length, dtype=jnp.int32)
    query_low = low(rotate(query_norm.reshape(length, HEADS, HEAD_DIM), positions, 1.0))
    key_low = low(rotate(key_norm.reshape(length, HEADS, HEAD_DIM), positions, 1.0))
    value_low = low(projected[2].reshape(length, HEADS, HEAD_DIM))
    block_rows = min(512, length)
    count = length // block_rows

    @jax.checkpoint
    def attend(query_block, query_pos, query_seg):
        scores = jnp.einsum('qhd,khd->hqk', query_block, key_low, precision=highest) * scale
        scores = low_back(scores)
        mask = (positions[None, :] <= query_pos[:, None]) & (seg_slot[None, :] == query_seg[:, None])
        scores = jnp.where(mask[None], scores, floor_value)
        probs = jax.nn.softmax(scores, axis=-1)
        return jnp.einsum('hqk,khd->qhd', low(probs), value_low, precision=highest)
    attended = lax.map(lambda item: attend(item[0], item[1], item[2]), (query_low.reshape(count, block_rows, HEADS, HEAD_DIM), positions.reshape(count, block_rows), seg_slot.reshape(count, block_rows)))
    attn_low = low(low_back(attended.reshape(length, D)))
    branch = low_back(jnp.dot(attn_low, out_w, precision=highest))
    resid = x_slot + rms_norm(branch) * post_g[0]
    resid_low = low(resid)
    gate_lin = low_back(jnp.einsum('td,cdf->ctf', resid_low, gate_w, precision=highest))
    hidden = low(jax.nn.silu(gate_lin[0]) * gate_lin[1])
    mlp_out = low_back(jnp.dot(hidden, down_w, precision=highest))
    return resid + rms_norm(mlp_out) * post_g[1]

def reference(tokens, segment_ids, qkv_weight, out_weight, gate_up, down_weight, qk_gain, post_gain, cotangent):

    def forward(x_all, qkv_w, out_w, gate_w, down_w, qk_g, post_g):
        return lax.map(lambda item: slot_forward(item[0], item[1], qkv_w, out_w, gate_w, down_w, qk_g, post_g), (x_all, segment_ids))
    output, pullback = jax.vjp(forward, tokens.astype(jnp.float32), qkv_weight.astype(jnp.float32), out_weight.astype(jnp.float32), gate_up.astype(jnp.float32), down_weight.astype(jnp.float32), qk_gain.astype(jnp.float32), post_gain.astype(jnp.float32))
    grads = pullback(cotangent.astype(jnp.float32))
    gain_grad = jnp.concatenate([grads[5], grads[6]], axis=0)
    return (output.astype(jnp.bfloat16), grads[0].astype(jnp.bfloat16), grads[1], grads[2], grads[3], grads[4], gain_grad)
```

```python
import functools

import jax
import jax.numpy as jnp
import numpy as np
from jax import lax
from jax.experimental import pallas as pl
from jax.experimental.pallas import tpu as pltpu
from jax.sharding import PartitionSpec as P

HEAD_DIM = 128
HALF = HEAD_DIM // 2
EPS = 1e-06
ROPE_BASE = 500000.0
FLOOR = -1e30
LOG2E = 1.4426950408889634
SCALE2 = HEAD_DIM ** (-0.5) * LOG2E
MESH_ID = pl.DeviceIdType.MESH
BF16 = jnp.bfloat16
F32 = jnp.float32
VMEM_LIMIT = 60 * 1024 * 1024
CHUNKS = 4

VM = pl.BlockSpec(memory_space=pltpu.VMEM)
HB = pl.BlockSpec(memory_space=pl.ANY)


def shape(dims, dtype):
    return jax.ShapeDtypeStruct(dims, dtype)


def where_am_i():
    return lax.axis_index("slot"), lax.axis_index("ctx"), lax.axis_index("uly")


def rows_of(index, rows):
    return pl.ds(pl.multiple_of(index * rows, rows), rows)


def greet(peers):
    barrier = pltpu.get_barrier_semaphore()
    total = 0
    for condition, peer in peers:
        if condition is None:
            pl.semaphore_signal(barrier, inc=1, device_id=peer, device_id_type=MESH_ID)
            total = total + 1
        else:

            @pl.when(condition)
            def _():
                pl.semaphore_signal(barrier, inc=1, device_id=peer, device_id_type=MESH_ID)

            total = total + condition.astype(jnp.int32)
    pl.semaphore_wait(barrier, total)


def line_peers(n):
    s, c, u = where_am_i()
    return [(u > 0, (s, c, u - 1)), (u < n - 1, (s, c, u + 1))]


def plane_peers():
    s, c, u = where_am_i()
    return [(None, (s, c ^ 1, u)), (None, (s, c ^ 2, u))]


def remote(src, dst, send, recv, peer):
    return pltpu.make_async_remote_copy(
        src_ref=src,
        dst_ref=dst,
        send_sem=send,
        recv_sem=recv,
        device_id=peer,
        device_id_type=MESH_ID,
    )


def line_sems(n, chunks=None):
    dims = (n - 1,) if chunks is None else (n - 1, chunks)
    return [pltpu.SemaphoreType.DMA(dims)] * 4


class LineGather:
    def __init__(self, n, rows, buf, sems):
        self.n, self.rows, self.buf, self.sems = n, rows, buf, sems

    def copy(self, right, slot, shard):
        s, c, u = where_am_i()
        send_r, recv_r, send_l, recv_l = self.sems
        view = self.buf.at[rows_of(shard, self.rows)]
        if right:
            return remote(view, view, send_r.at[slot], recv_r.at[slot], (s, c, u + 1))
        return remote(view, view, send_l.at[slot], recv_l.at[slot], (s, c, u - 1))

    def send(self, slot):
        u, n = lax.axis_index("uly"), self.n

        @pl.when((u < n - 1) & (u - slot >= 0))
        def _():
            self.copy(True, slot, u - slot).start()

        @pl.when((u > 0) & (u + slot <= n - 1))
        def _():
            self.copy(False, slot, u + slot).start()

    def wait(self, slot):
        u, n = lax.axis_index("uly"), self.n

        @pl.when(u - 1 - slot >= 0)
        def _():
            self.copy(True, slot, u - 1 - slot).wait_recv()

        @pl.when(u + 1 + slot <= n - 1)
        def _():
            self.copy(False, slot, u + 1 + slot).wait_recv()

        if slot + 1 < n - 1:
            self.send(slot + 1)

    def finish(self):
        u, n = lax.axis_index("uly"), self.n
        for slot in range(n - 1):

            @pl.when((u < n - 1) & (u - slot >= 0))
            def _():
                self.copy(True, slot, u - slot).wait_send()

            @pl.when((u > 0) & (u + slot <= n - 1))
            def _():
                self.copy(False, slot, u + slot).wait_send()

    def run(self):
        self.send(0)
        for slot in range(self.n - 1):
            self.wait(slot)
        self.finish()


class LineReduce:
    def __init__(self, n, rows, part, from_l, from_r, sems):
        self.n, self.rows, self.sems = n, rows, sems
        self.part, self.from_l, self.from_r = part, from_l, from_r
        self.chunks = part.shape[0]

    def copy(self, right, slot, chunk, block):
        s, c, u = where_am_i()
        send_r, recv_r, send_l, recv_l = self.sems
        where = rows_of(block, self.rows)
        src = self.part.at[chunk, where]
        if right:
            return remote(
                src,
                self.from_l.at[chunk, where],
                send_r.at[slot, chunk],
                recv_r.at[slot, chunk],
                (s, c, u + 1),
            )
        return remote(
            src,
            self.from_r.at[chunk, where],
            send_l.at[slot, chunk],
            recv_l.at[slot, chunk],
            (s, c, u - 1),
        )

    def add(self, chunk, block, source):
        where = rows_of(block, self.rows)
        self.part[chunk, where, :] = (
            self.part[chunk, where, :].astype(F32) + source[chunk, where, :].astype(F32)
        ).astype(BF16)

    def step(self, slot, chunk):
        u, n = lax.axis_index("uly"), self.n
        block_r = n - 1 - slot + u
        block_l = slot - (n - 1) + u

        @pl.when(u <= slot)
        def _():
            if slot > 0:

                @pl.when(u > 0)
                def _():
                    self.copy(True, slot - 1, chunk, block_r).wait_recv()
                    self.add(chunk, block_r, self.from_l)

            self.copy(True, slot, chunk, block_r).start()

        @pl.when(u >= n - 1 - slot)
        def _():
            if slot > 0:

                @pl.when(u < n - 1)
                def _():
                    self.copy(False, slot - 1, chunk, block_l).wait_recv()
                    self.add(chunk, block_l, self.from_r)

            self.copy(False, slot, chunk, block_l).start()

    def last(self, out):
        u, n = lax.axis_index("uly"), self.n
        where = rows_of(u, self.rows)
        width = self.part.shape[2]
        for chunk in range(self.chunks):
            cols = slice(chunk * width, (chunk + 1) * width)
            out[:, cols] = self.part[chunk, where, :].astype(F32)

            @pl.when(u > 0)
            def _():
                self.copy(True, n - 2, chunk, u).wait_recv()
                out[:, cols] += self.from_l[chunk, where, :].astype(F32)

            @pl.when(u < n - 1)
            def _():
                self.copy(False, n - 2, chunk, u).wait_recv()
                out[:, cols] += self.from_r[chunk, where, :].astype(F32)

    def finish(self):
        u, n = lax.axis_index("uly"), self.n
        for slot in range(n - 1):
            for chunk in range(self.chunks):

                @pl.when(u <= slot)
                def _():
                    self.copy(True, slot, chunk, n - 1 - slot + u).wait_send()

                @pl.when(u >= n - 1 - slot)
                def _():
                    self.copy(False, slot, chunk, slot - (n - 1) + u).wait_send()

    def run(self, compute, out):
        for slot in range(self.n - 1):
            for chunk in range(self.chunks):
                if slot == 0:
                    compute(chunk)
                self.step(slot, chunk)
        self.last(out)
        self.finish()


def dot(a, b, dims):
    return lax.dot_general(a, b, ((dims[:1], dims[1:]), ((), ())), preferred_element_type=F32)


NN, NT, TN = (1, 0), (1, 1), (0, 0)


def tiles(total, size):
    size = min(total, size)
    return total // size, size


def inverse_rms(values):
    return lax.rsqrt(jnp.mean(values * values, axis=-1, keepdims=True) + EPS)


def norm_back(values, inverse, grad_scaled, width):
    return inverse * grad_scaled - values * inverse**3 * (
        jnp.sum(values * grad_scaled, axis=-1, keepdims=True) / width
    )


def rope_factors(table):
    lane = lax.broadcasted_iota(jnp.int32, table.shape, 1)
    turned = pltpu.roll(table, HALF, 1)
    cosine = jnp.where(lane < HALF, table, turned)
    sine = jnp.where(lane < HALF, -turned, table)
    return cosine, sine


def exchange_rows(n, mine, msg, send, recv):
    s, c, u = where_am_i()
    msg[pl.ds(u, 1)] = mine[None]
    copies = []
    for step in range(1, n):
        peer = lax.rem(u + step, n)
        copy = remote(msg.at[u], msg.at[u], send.at[step - 1], recv.at[step - 1], (s, c, peer))
        copy.start()
        copies.append(copy)
    for step in range(1, n):
        source = lax.rem(u + n - step, n)
        remote(
            msg.at[source], msg.at[source], send.at[step - 1], recv.at[step - 1], (s, c, source)
        ).wait_recv()
    total = msg[0]
    for j in range(1, n):
        total = total + msg[j]
    for copy in copies:
        copy.wait_send()
    return total


def to_rows(col0, col1):
    span = col0.shape[0]
    lane = lax.broadcasted_iota(jnp.int32, (span, 128), 1)
    both = jnp.where(lane == 0, col0, jnp.where(lane == 1, col1, 0.0))
    return jnp.transpose(both)[:8]


def to_columns(rows8):
    return jnp.transpose(jnp.concatenate([rows8] * 16, axis=0))


def all_uly_peers(n):
    s, c, u = where_am_i()
    return [(None, (s, c, lax.rem(u + k, n))) for k in range(1, n)]


def proj_kernel(
    n,
    x_ref,
    w_ref,
    tab_ref,
    gain_ref,
    seg_ref,
    xg_out,
    wq_out,
    proj_ref,
    q_ref,
    kv_ref,
    inv_ref,
    zero_ref,
    xg,
    wq,
    tab,
    msg,
    local_sem,
    w_send,
    w_recv,
    m_send,
    m_recv,
    *line,
):
    s, c, u = where_am_i()
    rows, width = x_ref.shape
    span = n * rows
    kb = w_ref.shape[1]
    sib, xn, yn = (1 - s, c, u), (s, c ^ 1, u), (s, c ^ 2, u)
    tab_copy = pltpu.make_async_copy(tab_ref.at[rows_of(c, span)], tab, local_sem.at[0])
    tab_copy.start()
    own_block = s * 4 + c
    own_copy = pltpu.make_async_copy(w_ref, wq.at[:, rows_of(own_block, kb)], local_sem.at[1])
    own_copy.start()
    xg[rows_of(u, rows), :] = x_ref[...]
    greet(all_uly_peers(n) + plane_peers() + [(None, sib)])

    def block(b):
        return wq.at[:, rows_of(b, kb)]

    def half(b, part):
        return wq.at[:, pl.ds(pl.multiple_of(b * kb + part * (kb // 2), kb // 2), kb // 2)]

    def sent(k, src, dst, peer):
        return remote(src, dst, w_send.at[k], w_recv.at[k], peer)

    bx, by, bd = s * 4 + (c ^ 1), s * 4 + (c ^ 2), s * 4 + (c ^ 3)
    gather = LineGather(n, rows, xg, line)
    gather.send(0)
    copies = [
        sent(0, w_ref, block(own_block), xn),
        sent(1, w_ref, block(own_block), yn),
        sent(2, w_ref, block(own_block), sib),
    ]
    for copy in copies:
        copy.start()
    gather.wait(0)
    sent(0, block(bx), block(bx), xn).wait_recv()
    more = [sent(3, half(bx, 0), half(bx, 0), yn), sent(4, block(bx), block(bx), sib)]
    for copy in more:
        copy.start()
    copies += more
    sent(1, block(by), block(by), yn).wait_recv()
    more = [sent(5, half(by, 1), half(by, 1), xn), sent(6, block(by), block(by), sib)]
    for copy in more:
        copy.start()
    copies += more
    if n > 2:
        gather.wait(1)
    sent(3, half(bd, 0), half(bd, 0), yn).wait_recv()
    more = [sent(7, half(bd, 0), half(bd, 0), sib)]
    more[0].start()
    copies += more
    sent(5, half(bd, 1), half(bd, 1), xn).wait_recv()
    more = [sent(8, half(bd, 1), half(bd, 1), sib)]
    more[0].start()
    copies += more
    for slot in range(2 if n > 2 else 1, n - 1):
        gather.wait(slot)
    far = (1 - s) * 4
    sent(2, block(far + c), block(far + c), sib).wait_recv()
    sent(4, block(far + (c ^ 1)), block(far + (c ^ 1)), sib).wait_recv()
    sent(6, block(far + (c ^ 2)), block(far + (c ^ 2)), sib).wait_recv()
    sent(7, half(far + (c ^ 3), 0), half(far + (c ^ 3), 0), sib).wait_recv()
    sent(8, half(far + (c ^ 3), 1), half(far + (c ^ 3), 1), sib).wait_recv()
    own_copy.wait()
    tab_copy.wait()
    keep = [
        pltpu.make_async_copy(xg, xg_out, local_sem.at[2]),
        pltpu.make_async_copy(wq, wq_out, local_sem.at[3]),
    ]
    for copy in keep:
        copy.start()

    count, size = tiles(span, 512)

    def project(i, carry):
        where = pl.ds(pl.multiple_of(i * size, size), size)
        xs = xg[where, :]
        proj_ref[0, where, :] = dot(xs, wq[0], NN)
        proj_ref[1, where, :] = dot(xs, wq[1], NN)
        kv_ref[1, where, :] = dot(xs, wq[2], NN).astype(BF16)
        return carry

    lax.fori_loop(0, count, project, 0)
    squares = [jnp.sum(proj_ref[i] * proj_ref[i], axis=-1, keepdims=True) for i in range(2)]
    mine = to_rows(*squares)
    zeros = jnp.sum((1 - seg_ref[...]).astype(F32))
    row = lax.broadcasted_iota(jnp.int32, mine.shape, 0)
    mine = jnp.where(row == 2, zeros, mine)
    total = exchange_rows(n, mine, msg, m_send, m_recv)
    zero_ref[...] = jnp.broadcast_to(total[2:3, :128], (8, 128))
    inv = lax.rsqrt(to_columns(total) / width + EPS)
    inv_ref[...] = inv
    cosine, sine = rope_factors(tab[...])
    heads = proj_ref.shape[2] // HEAD_DIM
    for i in range(2):
        inverse = inv_ref[:, i : i + 1]
        for h in range(heads):
            cols = slice(h * HEAD_DIM, (h + 1) * HEAD_DIM)
            v = proj_ref[i, :, cols] * inverse * gain_ref[i : i + 1, cols]
            v = (v * cosine + pltpu.roll(v, HALF, 1) * sine).astype(BF16)
            if i == 0:
                q_ref[:, cols] = v
            else:
                kv_ref[0, :, cols] = v
    for copy in copies:
        copy.wait_send()
    gather.finish()
    for copy in keep:
        copy.wait()


def project(n, x, w, table, gain, seg):
    rows, width = x.shape
    span, cols = n * rows, w.shape[2]
    return pl.pallas_call(
        functools.partial(proj_kernel, n),
        out_shape=(
            shape((span, width), BF16),
            shape((3, width, cols), BF16),
            shape((2, span, cols), F32),
            shape((span, cols), BF16),
            shape((2, span, cols), BF16),
            shape((span, 128), F32),
            shape((8, 128), F32),
        ),
        in_specs=[VM, HB, HB, VM, VM],
        out_specs=(HB, HB, VM, VM, VM, VM, VM),
        scratch_shapes=[
            pltpu.VMEM((span, width), BF16),
            pltpu.VMEM((3, width, cols), BF16),
            pltpu.VMEM((span, 128), F32),
            pltpu.VMEM((n, 8, span), F32),
            pltpu.SemaphoreType.DMA((4,)),
            pltpu.SemaphoreType.DMA((9,)),
            pltpu.SemaphoreType.DMA((9,)),
            pltpu.SemaphoreType.DMA((n - 1,)),
            pltpu.SemaphoreType.DMA((n - 1,)),
        ]
        + line_sems(n),
        compiler_params=pltpu.CompilerParams(
            collective_id=1, has_side_effects=True, vmem_limit_bytes=VMEM_LIMIT
        ),
        cost_estimate=pl.CostEstimate(
            flops=40 * 10**9, bytes_accessed=10**7, transcendentals=0
        ),
        name="project",
    )(x, w, table, gain, seg)


def score_mask(scores, key_first, query_first, starts, diagonal):
    key_pos = key_first + lax.broadcasted_iota(jnp.int32, scores.shape, 0)
    keep = key_pos >= starts
    if diagonal:
        query_pos = query_first + lax.broadcasted_iota(jnp.int32, scores.shape, 1)
        keep = keep & (key_pos <= query_pos)
    return jnp.where(keep, scores, FLOOR)


def segment_starts(first, size, bound):
    pos = first + lax.broadcasted_iota(jnp.int32, (1, size), 1)
    return jnp.where(pos >= bound, bound, 0)


def attend_kernel(
    q_ref,
    kv_ref,
    zero_ref,
    kvall_out,
    attn_ref,
    attn32_ref,
    lse_ref,
    bound_ref,
    kvall,
    peaks,
    sums,
    acct,
    zmsg,
    send,
    recv,
    z_send,
    z_recv,
    keep_sem,
):
    s, c, u = where_am_i()
    span, cols = q_ref.shape
    heads = cols // HEAD_DIM
    xn, yn, dn = (s, c ^ 1, u), (s, c ^ 2, u), (s, c ^ 3, u)
    kvall[pl.ds(c, 1)] = kv_ref[...][None]
    zmsg[pl.ds(c, 1)] = zero_ref[...][None]
    greet(plane_peers() + [(None, dn)])

    def sent(k, view, peer):
        return remote(view, view, send.at[k], recv.at[k], peer)

    bx, by, bd = c ^ 1, c ^ 2, c ^ 3
    zs = [
        remote(zmsg.at[c], zmsg.at[c], z_send.at[k], z_recv.at[k], peer)
        for k, peer in enumerate((xn, yn, dn))
    ]
    for copy in zs:
        copy.start()
    copies = [sent(0, kvall.at[c], xn), sent(1, kvall.at[c], yn)]
    for copy in copies:
        copy.start()
    for k, (b, peer) in enumerate(((bx, xn), (by, yn), (bd, dn))):
        remote(zmsg.at[b], zmsg.at[b], z_send.at[k], z_recv.at[k], peer).wait_recv()
    ahead = jnp.zeros((8, 128), F32)
    for j in range(4):
        ahead = ahead + jnp.where(j <= c, zmsg[j], 0.0)
    bounds = ahead.astype(jnp.int32)
    bound_ref[...] = bounds
    bound = bounds[:1, :1]

    peaks[...] = jnp.full_like(peaks, FLOOR)
    sums[...] = jnp.zeros_like(sums)
    acct[...] = jnp.zeros_like(acct)
    nq, tq = tiles(span, 512)
    nk, tk = tiles(span, 512)

    def update(number, diagonal):
        def over_queries(i, carry):
            first_q = c * span + i * tq
            starts = segment_starts(first_q, tq, bound)
            where_q = pl.ds(pl.multiple_of(i * tq, tq), tq)

            def over_keys(j, carry):
                first_k = number * span + j * tk
                where_k = pl.ds(pl.multiple_of(j * tk, tk), tk)
                for h in range(heads):
                    lanes = slice(h * HEAD_DIM, (h + 1) * HEAD_DIM)
                    scores = dot(kvall[number, 0, where_k, lanes], q_ref[where_q, lanes], NT)
                    scores = score_mask(scores * SCALE2, first_k, first_q, starts, diagonal)
                    old = peaks[h, :1, where_q]
                    new = jnp.maximum(old, jnp.max(scores, axis=0, keepdims=True))
                    factor = jnp.exp2(old - new)
                    weights = jnp.exp2(scores - new)
                    peaks[h, :1, where_q] = new
                    sums[h, :1, where_q] = sums[h, :1, where_q] * factor + jnp.sum(
                        weights, axis=0, keepdims=True
                    )
                    acct[h, :, where_q] = acct[h, :, where_q] * factor + dot(
                        kvall[number, 1, where_k, lanes], weights.astype(BF16), TN
                    )
                return carry

            return lax.fori_loop(0, nk, over_keys, carry)

        lax.fori_loop(0, nq, over_queries, 0)

    update(c, True)
    half = span // 2
    sent(0, kvall.at[bx], xn).wait_recv()
    more = [sent(2, kvall.at[bx, :, pl.ds(0, half)], yn)]
    more[0].start()
    copies += more
    sent(1, kvall.at[by], yn).wait_recv()
    more = [sent(3, kvall.at[by, :, pl.ds(half, half)], xn)]
    more[0].start()
    copies += more
    for b in (bx, by):

        @pl.when(b < c)
        def _():
            update(b, False)

    sent(2, kvall.at[bd, :, pl.ds(0, half)], yn).wait_recv()
    sent(3, kvall.at[bd, :, pl.ds(half, half)], xn).wait_recv()
    keep = pltpu.make_async_copy(kvall, kvall_out, keep_sem)
    keep.start()

    @pl.when(bd < c)
    def _():
        update(bd, False)

    for h in range(heads):
        lanes = slice(h * HEAD_DIM, (h + 1) * HEAD_DIM)
        total = sums[h, :1, :]
        attention = jnp.transpose(acct[h] / total)
        attn32_ref[:, lanes] = attention
        attn_ref[:, lanes] = attention.astype(BF16)
        lse_ref[h, :1, :] = peaks[h, :1, :] + jnp.log2(total)
    for copy in copies + zs:
        copy.wait_send()
    keep.wait()


def attend(q, kv, zero):
    span, cols = q.shape
    heads = cols // HEAD_DIM
    return pl.pallas_call(
        attend_kernel,
        out_shape=(
            shape((4, 2, span, cols), BF16),
            shape((span, cols), BF16),
            shape((span, cols), F32),
            shape((heads, 8, span), F32),
            shape((8, 128), jnp.int32),
        ),
        in_specs=[VM] * 3,
        out_specs=(HB, VM, VM, VM, VM),
        scratch_shapes=[
            pltpu.VMEM((4, 2, span, cols), BF16),
            pltpu.VMEM((heads, 8, span), F32),
            pltpu.VMEM((heads, 8, span), F32),
            pltpu.VMEM((heads, HEAD_DIM, span), F32),
            pltpu.VMEM((4, 8, 128), F32),
            pltpu.SemaphoreType.DMA((4,)),
            pltpu.SemaphoreType.DMA((4,)),
            pltpu.SemaphoreType.DMA((3,)),
            pltpu.SemaphoreType.DMA((3,)),
            pltpu.SemaphoreType.DMA,
        ],
        compiler_params=pltpu.CompilerParams(
            collective_id=2, has_side_effects=True, vmem_limit_bytes=VMEM_LIMIT
        ),
        cost_estimate=pl.CostEstimate(
            flops=40 * 10**9, bytes_accessed=10**7, transcendentals=0
        ),
        name="attend",
    )(q, kv, zero)


def attend_back_kernel(
    q_ref,
    kvall_ref,
    do_ref,
    attn32_ref,
    lse_ref,
    bound_ref,
    dq_ref,
    dkv_ref,
    part,
    got,
    acc,
    delta,
    send,
    recv,
):
    s, c, u = where_am_i()
    span, cols = q_ref.shape
    heads = cols // HEAD_DIM
    xn, yn = (s, c ^ 1, u), (s, c ^ 2, u)
    bx, by, bd = c ^ 1, c ^ 2, c ^ 3
    greet(plane_peers())
    bound = bound_ref[:1, :1]
    nq, tq = tiles(span, 512)
    nk, tk = tiles(span, 512)
    scale = HEAD_DIM ** (-0.5)
    dq_ref[...] = jnp.zeros_like(dq_ref)
    for h in range(heads):
        lanes = slice(h * HEAD_DIM, (h + 1) * HEAD_DIM)
        both = jnp.transpose(do_ref[:, lanes].astype(F32) * attn32_ref[:, lanes])
        delta[h, :1, :] = jnp.sum(both, axis=0, keepdims=True)

    def update(number, diagonal):
        acc[...] = jnp.zeros_like(acc)

        def over_queries(i, carry):
            first_q = c * span + i * tq
            starts = segment_starts(first_q, tq, bound)
            where_q = pl.ds(pl.multiple_of(i * tq, tq), tq)

            def over_keys(j, carry):
                first_k = number * span + j * tk
                where_k = pl.ds(pl.multiple_of(j * tk, tk), tk)
                for h in range(heads):
                    lanes = slice(h * HEAD_DIM, (h + 1) * HEAD_DIM)
                    keys = kvall_ref[number, 0, where_k, lanes]
                    values = kvall_ref[number, 1, where_k, lanes]
                    query, d_out = q_ref[where_q, lanes], do_ref[where_q, lanes]
                    scores = dot(keys, query, NT) * SCALE2
                    scores = score_mask(scores, first_k, first_q, starts, diagonal)
                    probs = jnp.exp2(scores - lse_ref[h, :1, where_q])
                    acc[1, where_k, lanes] += dot(probs.astype(BF16), d_out, NN)
                    d_probs = dot(values, d_out, NT)
                    d_scores = (probs * (d_probs - delta[h, :1, where_q])).astype(BF16)
                    acc[0, where_k, lanes] += dot(d_scores, query, NN) * scale
                    dq_ref[where_q, lanes] += dot(d_scores, keys, TN) * scale
                return carry

            return lax.fori_loop(0, nk, over_keys, carry)

        lax.fori_loop(0, nq, over_queries, 0)

    def work(number):
        @pl.when(number < c)
        def _():
            update(number, False)
            part[pl.ds(number, 1)] = acc[...].astype(BF16)[None]

        @pl.when(number > c)
        def _():
            part[pl.ds(number, 1)] = jnp.zeros_like(part[pl.ds(number, 1)])

    half = span // 2
    lo, hi = pl.ds(0, half), pl.ds(half, half)

    def sent(k, src, dst, peer):
        return remote(src, dst, send.at[k], recv.at[k], peer)

    work(bd)
    copies = [
        sent(0, part.at[bd, :, lo], got.at[0, :, lo], xn),
        sent(1, part.at[bd, :, hi], got.at[0, :, hi], yn),
    ]
    for copy in copies:
        copy.start()
    work(bx)
    sent(1, part.at[bx, :, hi], got.at[0, :, hi], yn).wait_recv()
    part[bx, :, half:, :] = (
        part[bx, :, half:, :].astype(F32) + got[0, :, half:, :].astype(F32)
    ).astype(BF16)
    more = [sent(2, part.at[bx], got.at[1], xn)]
    more[0].start()
    copies += more
    work(by)
    sent(0, part.at[by, :, lo], got.at[0, :, lo], xn).wait_recv()
    part[by, :, :half, :] = (
        part[by, :, :half, :].astype(F32) + got[0, :, :half, :].astype(F32)
    ).astype(BF16)
    more = [sent(3, part.at[by], got.at[2], yn)]
    more[0].start()
    copies += more
    update(c, True)
    sent(2, part.at[bx], got.at[1], xn).wait_recv()
    sent(3, part.at[by], got.at[2], yn).wait_recv()
    dkv_ref[...] = acc[...] + got[1].astype(F32) + got[2].astype(F32)
    for copy in copies:
        copy.wait_send()


def attend_back(q, kvall, d_out, attn32, lse, bound):
    span, cols = q.shape
    heads = cols // HEAD_DIM
    return pl.pallas_call(
        attend_back_kernel,
        out_shape=(shape((span, cols), F32), shape((2, span, cols), F32)),
        in_specs=[VM] * 6,
        out_specs=(VM, VM),
        scratch_shapes=[
            pltpu.VMEM((4, 2, span, cols), BF16),
            pltpu.VMEM((3, 2, span, cols), BF16),
            pltpu.VMEM((2, span, cols), F32),
            pltpu.VMEM((heads, 8, span), F32),
            pltpu.SemaphoreType.DMA((4,)),
            pltpu.SemaphoreType.DMA((4,)),
        ],
        compiler_params=pltpu.CompilerParams(
            collective_id=3, has_side_effects=True, vmem_limit_bytes=VMEM_LIMIT
        ),
        cost_estimate=pl.CostEstimate(
            flops=50 * 10**9, bytes_accessed=10**7, transcendentals=0
        ),
        name="attend_back",
    )(q, kvall, d_out, attn32, lse, bound)


def load_blocks(src, dst, sem, axis):
    blocks = src.shape[0]
    size = dst.shape[axis] // blocks
    copies = []
    for b in range(blocks):
        where = [slice(None)] * len(dst.shape)
        where[axis] = pl.ds(b * size, size)
        copies.append(pltpu.make_async_copy(src.at[b], dst.at[tuple(where)], sem.at[b]))
    for copy in copies:
        copy.start()
    return copies


def wait_all(copies):
    for copy in copies:
        copy.wait()


def mlp_in_kernel(
    n,
    attn_ref,
    wo_ref,
    x_ref,
    gain_ref,
    wg_ref,
    branch_ref,
    resid_ref,
    group_out,
    gate_ref,
    up_ref,
    hidden_ref,
    wo,
    wg,
    group,
    part,
    from_l,
    from_r,
    sem_o,
    sem_g,
    keep_sem,
    *sems,
):
    s, c, u = where_am_i()
    rows, width = x_ref.shape
    load_o = load_blocks(wo_ref, wo, sem_o, 1)
    load_g = load_blocks(wg_ref, wg, sem_g, 1)
    greet(line_peers(n))
    wait_all(load_o)
    chunk_cols = width // part.shape[0]
    span = n * rows
    count, size = tiles(span, 512)

    def compute(chunk):
        def tile(i, carry):
            where = pl.ds(pl.multiple_of(i * size, size), size)
            part[chunk, where, :] = dot(
                attn_ref[where, :], wo[:, chunk * chunk_cols : (chunk + 1) * chunk_cols], NN
            ).astype(BF16)
            return carry

        lax.fori_loop(0, count, tile, 0)

    LineReduce(n, rows, part, from_l, from_r, sems[:4]).run(compute, branch_ref)
    branch = branch_ref[...]
    resid = x_ref[...].astype(F32) + branch * inverse_rms(branch) * gain_ref[0:1, :]
    resid_ref[...] = resid
    group[rows_of(u, rows), :] = resid.astype(BF16)
    LineGather(n, rows, group, sems[4:]).run()
    keep = pltpu.make_async_copy(group, group_out, keep_sem)
    keep.start()
    wait_all(load_g)
    ntile, tsize = tiles(gate_ref.shape[1], 512)

    def body(i, carry):
        lanes = pl.ds(pl.multiple_of(i * tsize, tsize), tsize)

        def tile(j, carry):
            where = pl.ds(pl.multiple_of(j * size, size), size)
            gate = dot(group[where, :], wg[0, :, lanes], NN)
            up = dot(group[where, :], wg[1, :, lanes], NN)
            gate_ref[where, lanes] = gate.astype(BF16)
            up_ref[where, lanes] = up.astype(BF16)
            hidden_ref[where, lanes] = (gate * jax.nn.sigmoid(gate) * up).astype(BF16)
            return carry

        return lax.fori_loop(0, count, tile, carry)

    lax.fori_loop(0, ntile, body, 0)
    keep.wait()


def reduce_scratch(n, rows, width):
    dims = (CHUNKS, n * rows, width // CHUNKS)
    return [pltpu.VMEM(dims, BF16)] * 3


def mlp_in(n, attn, wo, x, gain, wg):
    rows, width = x.shape
    span, cols = attn.shape
    ff = wg.shape[3]
    return pl.pallas_call(
        functools.partial(mlp_in_kernel, n),
        out_shape=(
            shape((rows, width), F32),
            shape((rows, width), F32),
            shape((span, width), BF16),
            shape((span, ff), BF16),
            shape((span, ff), BF16),
            shape((span, ff), BF16),
        ),
        in_specs=[VM, HB, VM, VM, HB],
        out_specs=(VM, VM, HB, VM, VM, VM),
        scratch_shapes=[
            pltpu.VMEM((cols, width), BF16),
            pltpu.VMEM((2, width, ff), BF16),
            pltpu.VMEM((span, width), BF16),
        ]
        + reduce_scratch(n, rows, width)
        + [
            pltpu.SemaphoreType.DMA((8,)),
            pltpu.SemaphoreType.DMA((8,)),
            pltpu.SemaphoreType.DMA,
        ]
        + line_sems(n, CHUNKS)
        + line_sems(n),
        compiler_params=pltpu.CompilerParams(
            collective_id=4, has_side_effects=True, vmem_limit_bytes=VMEM_LIMIT
        ),
        cost_estimate=pl.CostEstimate(
            flops=80 * 10**9, bytes_accessed=10**7, transcendentals=0
        ),
        name="mlp_in",
    )(attn, wo, x, gain, wg)


def mlp_out_kernel(
    n,
    hidden_ref,
    wd_ref,
    resid_ref,
    gain_ref,
    cot_ref,
    gate_ref,
    up_ref,
    out_ref,
    group_out,
    dgu_ref,
    dgain_ref,
    wd,
    mlp,
    group,
    part,
    from_l,
    from_r,
    sem_d,
    keep_sem,
    *sems,
):
    s, c, u = where_am_i()
    rows, width = resid_ref.shape
    load_d = load_blocks(wd_ref, wd, sem_d, 1)
    greet(line_peers(n))
    wait_all(load_d)
    chunk_cols = width // part.shape[0]
    span = n * rows
    count, size = tiles(span, 512)

    def compute(chunk):
        def tile(i, carry):
            where = pl.ds(pl.multiple_of(i * size, size), size)
            part[chunk, where, :] = dot(
                hidden_ref[where, :], wd[:, chunk * chunk_cols : (chunk + 1) * chunk_cols], NN
            ).astype(BF16)
            return carry

        lax.fori_loop(0, count, tile, 0)

    LineReduce(n, rows, part, from_l, from_r, sems[:4]).run(compute, mlp)
    values = mlp[...]
    inverse = inverse_rms(values)
    grad = cot_ref[...].astype(F32)
    d_mlp = norm_back(values, inverse, grad * gain_ref[1:2, :], width)
    group[rows_of(u, rows), :] = d_mlp.astype(BF16)
    gather = LineGather(n, rows, group, sems[4:])
    gather.send(0)
    scaled = values * inverse
    out_ref[...] = (resid_ref[...] + scaled * gain_ref[1:2, :]).astype(BF16)
    dgain_ref[...] = jnp.sum(grad * scaled, axis=0, keepdims=True)
    for slot in range(n - 1):
        gather.wait(slot)
    gather.finish()
    keep = pltpu.make_async_copy(group, group_out, keep_sem)
    keep.start()
    ntile, tsize = tiles(gate_ref.shape[1], 512)

    def body(i, carry):
        lanes = pl.ds(pl.multiple_of(i * tsize, tsize), tsize)

        def tile(j, carry):
            where = pl.ds(pl.multiple_of(j * size, size), size)
            d_hidden = dot(group[where, :], wd[lanes, :], NT)
            gate = gate_ref[where, lanes].astype(F32)
            up = up_ref[where, lanes].astype(F32)
            sig = jax.nn.sigmoid(gate)
            slope = sig * (1.0 + gate * (1.0 - sig))
            dgu_ref[0, where, lanes] = (d_hidden * up * slope).astype(BF16)
            dgu_ref[1, where, lanes] = (d_hidden * (gate * sig)).astype(BF16)
            return carry

        return lax.fori_loop(0, count, tile, carry)

    lax.fori_loop(0, ntile, body, 0)
    keep.wait()


def mlp_out(n, hidden, wd, resid, gain, cot, gate, up):
    rows, width = resid.shape
    span, ff = hidden.shape
    return pl.pallas_call(
        functools.partial(mlp_out_kernel, n),
        out_shape=(
            shape((rows, width), BF16),
            shape((span, width), BF16),
            shape((2, span, ff), BF16),
            shape((1, width), F32),
        ),
        in_specs=[VM, HB, VM, VM, VM, VM, VM],
        out_specs=(VM, HB, VM, VM),
        scratch_shapes=[
            pltpu.VMEM((ff, width), BF16),
            pltpu.VMEM((rows, width), F32),
            pltpu.VMEM((span, width), BF16),
        ]
        + reduce_scratch(n, rows, width)
        + [pltpu.SemaphoreType.DMA((8,)), pltpu.SemaphoreType.DMA]
        + line_sems(n, CHUNKS)
        + line_sems(n),
        compiler_params=pltpu.CompilerParams(
            collective_id=5, has_side_effects=True, vmem_limit_bytes=VMEM_LIMIT
        ),
        cost_estimate=pl.CostEstimate(
            flops=80 * 10**9, bytes_accessed=10**7, transcendentals=0
        ),
        name="mlp_out",
    )(hidden, wd, resid, gain, cot, gate, up)


def mlp_back_kernel(
    n,
    dgu_ref,
    wg_ref,
    cot_ref,
    branch_ref,
    gain_ref,
    wo_ref,
    dresid_ref,
    group_out,
    dattn_ref,
    dgain_ref,
    wo,
    wg,
    group,
    part,
    from_l,
    from_r,
    sem_o,
    sem_g,
    keep_sem,
    *sems,
):
    s, c, u = where_am_i()
    rows, width = cot_ref.shape
    load_g = load_blocks(wg_ref, wg, sem_g, 1)
    load_o = load_blocks(wo_ref, wo, sem_o, 1)
    greet(line_peers(n))
    wait_all(load_g)
    chunk_cols = width // part.shape[0]
    span = n * rows
    count, size = tiles(span, 512)

    def compute(chunk):
        cols = slice(chunk * chunk_cols, (chunk + 1) * chunk_cols)

        def tile(i, carry):
            where = pl.ds(pl.multiple_of(i * size, size), size)
            part[chunk, where, :] = (
                dot(dgu_ref[0, where, :], wg[0, cols, :], NT)
                + dot(dgu_ref[1, where, :], wg[1, cols, :], NT)
            ).astype(BF16)
            return carry

        lax.fori_loop(0, count, tile, 0)

    LineReduce(n, rows, part, from_l, from_r, sems[:4]).run(compute, dresid_ref)
    d_resid = dresid_ref[...] + cot_ref[...].astype(F32)
    dresid_ref[...] = d_resid
    branch = branch_ref[...]
    inverse = inverse_rms(branch)
    d_branch = norm_back(branch, inverse, d_resid * gain_ref[0:1, :], width)
    group[rows_of(u, rows), :] = d_branch.astype(BF16)
    gather = LineGather(n, rows, group, sems[4:])
    gather.send(0)
    dgain_ref[...] = jnp.sum(d_resid * branch * inverse, axis=0, keepdims=True)
    wait_all(load_o)
    for slot in range(n - 1):
        gather.wait(slot)
    gather.finish()
    keep = pltpu.make_async_copy(group, group_out, keep_sem)
    keep.start()

    def tile(j, carry):
        where = pl.ds(pl.multiple_of(j * size, size), size)
        dattn_ref[where, :] = dot(group[where, :], wo[...], NT).astype(BF16)
        return carry

    lax.fori_loop(0, count, tile, 0)
    keep.wait()


def mlp_back(n, dgu, wg, cot, branch, gain, wo):
    rows, width = branch.shape
    span, ff = dgu.shape[1:]
    cols = wo.shape[1]
    return pl.pallas_call(
        functools.partial(mlp_back_kernel, n),
        out_shape=(
            shape((rows, width), F32),
            shape((span, width), BF16),
            shape((span, cols), BF16),
            shape((1, width), F32),
        ),
        in_specs=[VM, HB, VM, VM, VM, HB],
        out_specs=(VM, HB, VM, VM),
        scratch_shapes=[
            pltpu.VMEM((cols, width), BF16),
            pltpu.VMEM((2, width, ff), BF16),
            pltpu.VMEM((span, width), BF16),
        ]
        + reduce_scratch(n, rows, width)
        + [
            pltpu.SemaphoreType.DMA((8,)),
            pltpu.SemaphoreType.DMA((8,)),
            pltpu.SemaphoreType.DMA,
        ]
        + line_sems(n, CHUNKS)
        + line_sems(n),
        compiler_params=pltpu.CompilerParams(
            collective_id=6, has_side_effects=True, vmem_limit_bytes=VMEM_LIMIT
        ),
        cost_estimate=pl.CostEstimate(
            flops=80 * 10**9, bytes_accessed=10**7, transcendentals=0
        ),
        name="mlp_back",
    )(dgu, wg, cot, branch, gain, wo)


def proj_back_kernel(
    n,
    dq_ref,
    dkv_ref,
    proj_ref,
    inv_ref,
    gain_ref,
    tab_ref,
    wq_ref,
    dresid_ref,
    out_ref,
    dproj_ref,
    dgain_ref,
    wq,
    tab,
    scaled_ref,
    total_ref,
    msg,
    part,
    from_l,
    from_r,
    local_sem,
    m_send,
    m_recv,
    *sems,
):
    s, c, u = where_am_i()
    rows, width = dresid_ref.shape
    span = n * rows
    load = [
        pltpu.make_async_copy(tab_ref.at[rows_of(c, span)], tab, local_sem.at[0]),
        pltpu.make_async_copy(wq_ref, wq, local_sem.at[1]),
    ]
    for copy in load:
        copy.start()
    greet(all_uly_peers(n))
    load[0].wait()
    cosine, sine = rope_factors(tab[...])
    heads = dq_ref.shape[1] // HEAD_DIM
    dots = []
    for i in range(2):
        inverse = inv_ref[:, i : i + 1]
        row_dot = jnp.zeros((span, 1), F32)
        for h in range(heads):
            cols = slice(h * HEAD_DIM, (h + 1) * HEAD_DIM)
            v = dq_ref[:, cols] if i == 0 else dkv_ref[0, :, cols]
            v = v * cosine - pltpu.roll(v, HALF, 1) * sine
            values = proj_ref[i, :, cols]
            dgain_ref[i : i + 1, cols] = jnp.sum(v * values * inverse, axis=0, keepdims=True)
            v = v * gain_ref[i : i + 1, cols]
            scaled_ref[i, :, cols] = v
            row_dot = row_dot + jnp.sum(values * v, axis=-1, keepdims=True)
        dots.append(row_dot)
    total = exchange_rows(n, to_rows(*dots), msg, m_send, m_recv)
    means = to_columns(total) / width
    total_ref[...] = means
    for i in range(2):
        inverse = inv_ref[:, i : i + 1]
        factor = inverse**3 * total_ref[:, i : i + 1]
        dproj_ref[i] = (inverse * scaled_ref[i] - proj_ref[i] * factor).astype(BF16)
    dproj_ref[2] = dkv_ref[1].astype(BF16)
    load[1].wait()
    chunk_cols = width // part.shape[0]
    count, size = tiles(span, 512)

    def compute(chunk):
        cols = slice(chunk * chunk_cols, (chunk + 1) * chunk_cols)

        def tile(i, carry):
            where = pl.ds(pl.multiple_of(i * size, size), size)
            part[chunk, where, :] = (
                dot(dproj_ref[0, where, :], wq[0, cols, :], NT)
                + dot(dproj_ref[1, where, :], wq[1, cols, :], NT)
                + dot(dproj_ref[2, where, :], wq[2, cols, :], NT)
            ).astype(BF16)
            return carry

        lax.fori_loop(0, count, tile, 0)

    LineReduce(n, rows, part, from_l, from_r, sems[:4]).run(compute, total_wide := sems[4])
    out_ref[...] = (dresid_ref[...] + total_wide[...]).astype(BF16)


def proj_back(n, dq, dkv, proj, inv, gain, table, wq, dresid):
    rows, width = dresid.shape
    span, cols = dq.shape
    return pl.pallas_call(
        functools.partial(proj_back_kernel, n),
        out_shape=(
            shape((rows, width), BF16),
            shape((3, span, cols), BF16),
            shape((2, cols), F32),
        ),
        in_specs=[VM, VM, VM, VM, VM, HB, HB, VM],
        out_specs=(VM, VM, VM),
        scratch_shapes=[
            pltpu.VMEM((3, width, cols), BF16),
            pltpu.VMEM((span, 128), F32),
            pltpu.VMEM((2, span, cols), F32),
            pltpu.VMEM((span, 128), F32),
            pltpu.VMEM((n, 8, span), F32),
        ]
        + reduce_scratch(n, rows, width)
        + [
            pltpu.SemaphoreType.DMA((2,)),
            pltpu.SemaphoreType.DMA((n - 1,)),
            pltpu.SemaphoreType.DMA((n - 1,)),
        ]
        + line_sems(n, CHUNKS)
        + [pltpu.VMEM((rows, width), F32)],
        compiler_params=pltpu.CompilerParams(
            collective_id=7, has_side_effects=True, vmem_limit_bytes=VMEM_LIMIT
        ),
        cost_estimate=pl.CostEstimate(
            flops=50 * 10**9, bytes_accessed=10**7, transcendentals=0
        ),
        name="proj_back",
    )(dq, dkv, proj, inv, gain, table, wq, dresid)


def rope_table(length):
    freqs = np.power(
        np.float32(ROPE_BASE), -(np.arange(HALF, dtype=np.float32) * 2.0 / HEAD_DIM)
    ).astype(np.float32)
    angles = (np.arange(length, dtype=np.float32)[:, None] * freqs[None, :]).astype(np.float64)
    return np.concatenate([np.cos(angles), np.sin(angles)], axis=1).astype(np.float32)


def on_device(
    n,
    table,
    tokens,
    segment_ids,
    qkv_weight,
    out_weight,
    gate_up,
    down_weight,
    qk_gain,
    post_gain,
    cotangent,
):
    x = tokens[0]
    width = x.shape[1]
    cot = cotangent[0]
    spread = ("slot", "ctx")
    wo = lax.all_gather(out_weight, spread, axis=0)
    wg = lax.all_gather(gate_up, spread, axis=0)
    wd = lax.all_gather(down_weight, spread, axis=0)
    table = jnp.asarray(table)
    group_x, wq, proj, q, kv, inv, zero = project(n, x, qkv_weight, table, qk_gain, segment_ids)
    kvall, attn, attn32, lse, bound = attend(q, kv, zero)
    branch, resid, group_resid, gate, up, hidden = mlp_in(n, attn, wo, x, post_gain, wg)
    block_out, group_dmlp, dgu, gain_mlp = mlp_out(n, hidden, wd, resid, post_gain, cot, gate, up)
    down_grad = dot(hidden, group_dmlp, TN).astype(BF16)
    d_resid, group_dbranch, d_attn, gain_attn = mlp_back(n, dgu, wg, cot, branch, post_gain, wo)
    gate_grad = jnp.einsum(
        "td,ctf->cdf", group_resid, dgu, preferred_element_type=F32
    ).astype(BF16)
    out_grad = dot(attn, group_dbranch, TN).astype(BF16)
    dq, dkv = attend_back(q, kvall, d_attn, attn32, lse, bound)
    input_grad, d_proj, gain_cols = proj_back(n, dq, dkv, proj, inv, qk_gain, table, wq, d_resid)
    qkv_grad = jnp.einsum(
        "td,cte->cde", group_x, d_proj, preferred_element_type=F32
    ).astype(BF16)
    local_cols = q.shape[1]
    gain_block = lax.dynamic_update_slice(
        jnp.zeros((2, width), F32), gain_cols, (0, lax.axis_index("uly") * local_cols)
    )
    gain_terms = jnp.concatenate([gain_block, gain_attn, gain_mlp], axis=0)
    gain_totals = lax.psum(gain_terms, "uly")

    def scatter(value, dim):
        return lax.psum_scatter(value, spread, scatter_dimension=dim, tiled=True).astype(F32)

    return (
        block_out[None],
        input_grad[None],
        scatter(qkv_grad, 1),
        scatter(out_grad, 1),
        scatter(gate_grad, 1),
        scatter(down_grad, 1),
        scatter(gain_totals, 1),
    )


def solution(mesh):
    n = mesh.shape["uly"]
    in_specs = (
        P("slot", ("ctx", "uly"), None),
        P("slot", ("ctx", "uly")),
        P(None, ("slot", "ctx"), "uly"),
        P("uly", ("slot", "ctx")),
        P(None, ("slot", "ctx"), "uly"),
        P("uly", ("slot", "ctx")),
        P(None, "uly"),
        P(),
        P("slot", ("ctx", "uly"), None),
    )
    out_specs = (
        P("slot", ("ctx", "uly"), None),
        P("slot", ("ctx", "uly"), None),
        P(None, ("slot", "ctx"), "uly"),
        P("uly", ("slot", "ctx")),
        P(None, ("slot", "ctx"), "uly"),
        P("uly", ("slot", "ctx")),
        P(None, ("slot", "ctx")),
    )

    def whole(tokens, *rest):
        table = rope_table(tokens.shape[1])
        return jax.shard_map(
            functools.partial(on_device, n, table),
            mesh=mesh,
            in_specs=in_specs,
            out_specs=out_specs,
            check_vma=False,
        )(tokens, *rest)

    return whole
```

```python
import functools

import jax
import jax.numpy as jnp
import numpy as np
from jax import lax
from jax.experimental import pallas as pl
from jax.experimental.pallas import tpu as pltpu
from jax.sharding import PartitionSpec as P

HEAD_DIM = 128
HALF = HEAD_DIM // 2
EPS = 1e-06
ROPE_BASE = 500000.0
FLOOR = -1e30
LOG2E = 1.4426950408889634
SCALE2 = HEAD_DIM ** (-0.5) * LOG2E
MESH_ID = pl.DeviceIdType.MESH
BF16 = jnp.bfloat16
F32 = jnp.float32
VMEM_LIMIT = 62 * 1024 * 1024
CHUNKS = 4

VM = pl.BlockSpec(memory_space=pltpu.VMEM)
HB = pl.BlockSpec(memory_space=pl.ANY)


def shape(dims, dtype):
    return jax.ShapeDtypeStruct(dims, dtype)


def where_am_i():
    return lax.axis_index("slot"), lax.axis_index("ctx"), lax.axis_index("uly")


def rows_of(index, rows):
    return pl.ds(pl.multiple_of(index * rows, rows), rows)


def greet(peers):
    barrier = pltpu.get_barrier_semaphore()
    total = 0
    for condition, peer in peers:
        if condition is None:
            pl.semaphore_signal(barrier, inc=1, device_id=peer, device_id_type=MESH_ID)
            total = total + 1
        else:

            @pl.when(condition)
            def _():
                pl.semaphore_signal(barrier, inc=1, device_id=peer, device_id_type=MESH_ID)

            total = total + condition.astype(jnp.int32)
    pl.semaphore_wait(barrier, total)


def line_peers(n):
    s, c, u = where_am_i()
    return [(u > 0, (s, c, u - 1)), (u < n - 1, (s, c, u + 1))]


def plane_peers():
    s, c, u = where_am_i()
    return [(None, (s, c ^ 1, u)), (None, (s, c ^ 2, u))]


def remote(src, dst, send, recv, peer):
    return pltpu.make_async_remote_copy(
        src_ref=src,
        dst_ref=dst,
        send_sem=send,
        recv_sem=recv,
        device_id=peer,
        device_id_type=MESH_ID,
    )


def line_sems(n, chunks=None):
    dims = (n - 1,) if chunks is None else (n - 1, chunks)
    return [pltpu.SemaphoreType.DMA(dims)] * 4


class LineGather:
    def __init__(self, n, rows, buf, sems):
        self.n, self.rows, self.buf, self.sems = n, rows, buf, sems

    def copy(self, right, slot, shard):
        s, c, u = where_am_i()
        send_r, recv_r, send_l, recv_l = self.sems
        view = self.buf.at[rows_of(shard, self.rows)]
        if right:
            return remote(view, view, send_r.at[slot], recv_r.at[slot], (s, c, u + 1))
        return remote(view, view, send_l.at[slot], recv_l.at[slot], (s, c, u - 1))

    def send(self, slot):
        u, n = lax.axis_index("uly"), self.n

        @pl.when((u < n - 1) & (u - slot >= 0))
        def _():
            self.copy(True, slot, u - slot).start()

        @pl.when((u > 0) & (u + slot <= n - 1))
        def _():
            self.copy(False, slot, u + slot).start()

    def wait(self, slot):
        u, n = lax.axis_index("uly"), self.n

        @pl.when(u - 1 - slot >= 0)
        def _():
            self.copy(True, slot, u - 1 - slot).wait_recv()

        @pl.when(u + 1 + slot <= n - 1)
        def _():
            self.copy(False, slot, u + 1 + slot).wait_recv()

        if slot + 1 < n - 1:
            self.send(slot + 1)

    def finish(self):
        u, n = lax.axis_index("uly"), self.n
        for slot in range(n - 1):

            @pl.when((u < n - 1) & (u - slot >= 0))
            def _():
                self.copy(True, slot, u - slot).wait_send()

            @pl.when((u > 0) & (u + slot <= n - 1))
            def _():
                self.copy(False, slot, u + slot).wait_send()

    def run(self, hook=None):
        for slot in range(self.n - 1):
            self.wait(slot)
            if hook is not None:
                hook(slot)
        self.finish()


class LineReduce:
    def __init__(self, n, rows, part, got, sems):
        self.n, self.rows, self.sems = n, rows, sems
        self.part, self.got = part, got
        self.chunks = part.shape[0]

    def copy(self, right, slot, chunk, block):
        s, c, u = where_am_i()
        send_r, recv_r, send_l, recv_l = self.sems
        where = rows_of(block, self.rows)
        src = self.part.at[chunk, where]
        if right:
            return remote(
                src,
                self.got.at[chunk, rows_of(block + 1, self.rows)],
                send_r.at[slot, chunk],
                recv_r.at[slot, chunk],
                (s, c, u + 1),
            )
        return remote(
            src,
            self.got.at[chunk, where],
            send_l.at[slot, chunk],
            recv_l.at[slot, chunk],
            (s, c, u - 1),
        )

    def add(self, chunk, block, place):
        where = rows_of(block, self.rows)
        self.part[chunk, where, :] = (
            self.part[chunk, where, :].astype(F32)
            + self.got[chunk, rows_of(place, self.rows), :].astype(F32)
        ).astype(BF16)

    def step(self, slot, chunk):
        u, n = lax.axis_index("uly"), self.n
        block_r = n - 1 - slot + u
        block_l = slot - (n - 1) + u

        @pl.when(u <= slot)
        def _():
            if slot > 0:

                @pl.when(u > 0)
                def _():
                    self.copy(True, slot - 1, chunk, block_r).wait_recv()
                    self.add(chunk, block_r, block_r + 1)

            self.copy(True, slot, chunk, block_r).start()

        @pl.when(u >= n - 1 - slot)
        def _():
            if slot > 0:

                @pl.when(u < n - 1)
                def _():
                    self.copy(False, slot - 1, chunk, block_l).wait_recv()
                    self.add(chunk, block_l, block_l)

            self.copy(False, slot, chunk, block_l).start()

    def last(self, out):
        u, n = lax.axis_index("uly"), self.n
        where = rows_of(u, self.rows)
        width = self.part.shape[2]
        for chunk in range(self.chunks):
            cols = slice(chunk * width, (chunk + 1) * width)
            out[:, cols] = self.part[chunk, where, :].astype(F32)

            @pl.when(u > 0)
            def _():
                self.copy(True, n - 2, chunk, u).wait_recv()
                out[:, cols] += self.got[chunk, rows_of(u + 1, self.rows), :].astype(F32)

            @pl.when(u < n - 1)
            def _():
                self.copy(False, n - 2, chunk, u).wait_recv()
                out[:, cols] += self.got[chunk, where, :].astype(F32)

    def finish(self):
        u, n = lax.axis_index("uly"), self.n
        for slot in range(n - 1):
            for chunk in range(self.chunks):

                @pl.when(u <= slot)
                def _():
                    self.copy(True, slot, chunk, n - 1 - slot + u).wait_send()

                @pl.when(u >= n - 1 - slot)
                def _():
                    self.copy(False, slot, chunk, slot - (n - 1) + u).wait_send()

    def run(self, compute, out, hook=None):
        for slot in range(self.n - 1):
            for chunk in range(self.chunks):
                if slot == 0:
                    compute(chunk)
                self.step(slot, chunk)
            if hook is not None:
                hook(slot)
        self.last(out)
        self.finish()


class PlaneGather:
    SEMS = 9

    def __init__(self, src, block, half_rows, send, recv, local):
        self.s, self.c, self.u = where_am_i()
        self.src, self.block, self.half_rows = src, block, half_rows
        self.send_sem, self.recv_sem = send, recv
        s, c, u = self.s, self.c, self.u
        self.xn, self.yn, self.sib = (s, c ^ 1, u), (s, c ^ 2, u), (1 - s, c, u)
        self.started = []
        self.own = pltpu.make_async_copy(src, block(s * 4 + c), local)

    def half(self, b, part):
        rows = self.half_rows
        view = self.block(b)
        where = [slice(None)] * len(view.shape)
        where[-2] = pl.ds(part * rows, rows)
        return view.at[tuple(where)]

    def copy(self, k, view, peer, src=None):
        return remote(
            view if src is None else src, view, self.send_sem.at[k], self.recv_sem.at[k], peer
        )

    def go(self, *copies):
        for copy in copies:
            copy.start()
            self.started.append(copy)

    def start(self):
        own = self.block(self.s * 4 + self.c)
        self.go(
            self.copy(0, own, self.xn, self.src),
            self.copy(1, own, self.yn, self.src),
            self.copy(2, own, self.sib, self.src),
        )
        self.own.start()

    def middle(self):
        bx, by = self.s * 4 + (self.c ^ 1), self.s * 4 + (self.c ^ 2)
        self.copy(0, self.block(bx), self.xn).wait_recv()
        self.go(
            self.copy(3, self.half(bx, 0), self.yn), self.copy(4, self.block(bx), self.sib)
        )
        self.copy(1, self.block(by), self.yn).wait_recv()
        self.go(
            self.copy(5, self.half(by, 1), self.xn), self.copy(6, self.block(by), self.sib)
        )

    def corner(self):
        bd = self.s * 4 + (self.c ^ 3)
        self.copy(3, self.half(bd, 0), self.yn).wait_recv()
        self.go(self.copy(7, self.half(bd, 0), self.sib))
        self.copy(5, self.half(bd, 1), self.xn).wait_recv()
        self.go(self.copy(8, self.half(bd, 1), self.sib))

    def arrive(self):
        far, c = (1 - self.s) * 4, self.c
        self.copy(2, self.block(far + c), self.sib).wait_recv()
        self.copy(4, self.block(far + (c ^ 1)), self.sib).wait_recv()
        self.copy(6, self.block(far + (c ^ 2)), self.sib).wait_recv()
        self.copy(7, self.half(far + (c ^ 3), 0), self.sib).wait_recv()
        self.copy(8, self.half(far + (c ^ 3), 1), self.sib).wait_recv()
        self.own.wait()

    def finish(self):
        for copy in self.started:
            copy.wait_send()


class PlaneReduce:
    SEMS = 6

    def __init__(self, ring, got, outs, place, send, recv, local):
        self.s, self.c, self.u = where_am_i()
        s, c, u = self.s, self.c, self.u
        self.xn, self.yn = (s, c ^ 1, u), (s, c ^ 2, u)
        self.ring, self.got, self.outs, self.place = ring, got, outs, place
        self.send_sem, self.recv_sem, self.local = send, recv, local
        self.slots, self.rows = ring.shape[0], ring.shape[2]
        self.open = {}

    def halves(self):
        h = self.rows // 2
        return pl.ds(0, h), pl.ds(h, h)

    def copy(self, piece, k, src, dst, peer):
        return remote(src, dst, self.send_sem.at[piece, k], self.recv_sem.at[piece, k], peer)

    def slot(self, piece):
        if piece >= self.slots:
            self.close(piece - self.slots)
        return self.ring.at[piece % self.slots]

    def close(self, piece):
        if piece in self.open:
            remotes, own = self.open.pop(piece)
            for copy in remotes:
                copy.wait_send()
            own.wait()

    def first(self, piece):
        c = self.c
        lo, hi = self.halves()
        blocks = self.ring.at[piece % self.slots]
        own_out, out_x, out_y = self.outs
        bx, by, bd = c ^ 1, c ^ 2, c ^ 3
        copies = [
            self.copy(piece, 0, blocks.at[bd, lo], self.got.at[piece, lo], self.xn),
            self.copy(piece, 1, blocks.at[bd, hi], self.got.at[piece, hi], self.yn),
            self.copy(piece, 2, blocks.at[bx, lo], self.place(out_x, piece, 0), self.xn),
            self.copy(piece, 3, blocks.at[by, hi], self.place(out_y, piece, 1), self.yn),
        ]
        for copy in copies:
            copy.start()
        own = pltpu.make_async_copy(
            blocks.at[c], self.place(own_out, piece, None), self.local.at[piece]
        )
        own.start()
        self.open[piece] = (copies, own)

    def second(self, piece):
        c, h = self.c, self.rows // 2
        lo, hi = self.halves()
        slot = piece % self.slots
        blocks = self.ring.at[slot]
        own_out, out_x, out_y = self.outs
        bx, by, bd = c ^ 1, c ^ 2, c ^ 3
        self.copy(piece, 0, blocks.at[bd, lo], self.got.at[piece, lo], self.xn).wait_recv()
        self.ring[slot, by, :h, :] = (
            self.ring[slot, by, :h, :].astype(F32) + self.got[piece, :h, :].astype(F32)
        ).astype(BF16)
        first = self.copy(piece, 4, blocks.at[by, lo], self.place(out_y, piece, 0), self.yn)
        first.start()
        self.copy(piece, 1, blocks.at[bd, hi], self.got.at[piece, hi], self.yn).wait_recv()
        self.ring[slot, bx, h:, :] = (
            self.ring[slot, bx, h:, :].astype(F32) + self.got[piece, h:, :].astype(F32)
        ).astype(BF16)
        second = self.copy(piece, 5, blocks.at[bx, hi], self.place(out_x, piece, 1), self.xn)
        second.start()
        self.open[piece][0].extend([first, second])

    def finish(self, pieces):
        own_out, out_x, out_y = self.outs
        slot = self.ring.at[0]
        lo, hi = self.halves()
        for piece in range(pieces):
            self.close(piece)
            for k, out, half, peer in (
                (2, out_x, 0, self.xn),
                (3, out_y, 1, self.yn),
                (4, out_y, 0, self.yn),
                (5, out_x, 1, self.xn),
            ):
                where = self.place(out, piece, half)
                self.copy(piece, k, where, where, peer).wait_recv()


class Pieces:
    def __init__(self, work):
        self.work, self.done, self.behind = work, 0, []

    def step(self, count=1):
        for _ in range(count):
            if self.done < len(self.work):
                plane, piece, compute = self.work[self.done]
                compute(plane.slot(piece), piece)
                plane.first(piece)
                self.behind.append((plane, piece))
                self.done += 1
                if len(self.behind) > 2:
                    self.catch_up()

    def catch_up(self):
        plane, piece = self.behind.pop(0)
        plane.second(piece)

    def finish(self):
        self.step(len(self.work))
        while self.behind:
            self.catch_up()


def wide_piece(own, other, lanes):
    def compute(out, piece):
        take = lanes(piece)
        cols = out.shape[2]

        def pair(i, carry):
            where = pl.ds(pl.multiple_of(i * 2 * cols, 2 * cols), 2 * cols)
            total = dot(own[0][:, take], own[1][:, where], TN) + dot(
                other[0][:, take], other[1][:, where], TN
            )
            total = total.astype(BF16)
            out[pl.ds(2 * i, 1)] = total[:, :cols][None]
            out[pl.ds(2 * i + 1, 1)] = total[:, cols:][None]
            return carry

        lax.fori_loop(0, 2, pair, 0)

    return compute


def tall_piece(own, other, right):
    def compute(out, piece):
        rows, cols = out.shape[1:]

        def pair(i, carry):
            where = pl.ds(pl.multiple_of(i * 2 * rows, 2 * rows), 2 * rows)
            total = dot(own[0][:, where], right(own[1], piece), TN) + dot(
                other[0][:, where], right(other[1], piece), TN
            )
            out[pl.ds(2 * i, 2)] = total.astype(BF16).reshape(2, rows, cols)
            return carry

        lax.fori_loop(0, 2, pair, 0)

    return compute


def half_columns(ref, s):
    half = ref.shape[1] // 2
    return ref.at[:, pl.ds(pl.multiple_of(s * half, half), half)]


class Sibling:
    def __init__(self, send, recv):
        s, c, u = where_am_i()
        self.peer, self.send, self.recv = (1 - s, c, u), send, recv
        self.copies = []

    def start(self, src, dst):
        k = len(self.copies)
        copy = remote(src, dst, self.send.at[k], self.recv.at[k], self.peer)
        copy.start()
        self.copies.append(copy)

    def wait(self, k):
        self.copies[k].wait_recv()

    def finish(self):
        for copy in self.copies:
            copy.wait_send()


def dot(a, b, dims):
    return lax.dot_general(a, b, ((dims[:1], dims[1:]), ((), ())), preferred_element_type=F32)


NN, NT, TN = (1, 0), (1, 1), (0, 0)


def tiles(total, size):
    size = min(total, size)
    return total // size, size


def inverse_rms(values):
    return lax.rsqrt(jnp.mean(values * values, axis=-1, keepdims=True) + EPS)


def norm_back(values, inverse, grad_scaled, width):
    return inverse * grad_scaled - values * inverse**3 * (
        jnp.sum(values * grad_scaled, axis=-1, keepdims=True) / width
    )


def rope_factors(table):
    lane = lax.broadcasted_iota(jnp.int32, table.shape, 1)
    turned = pltpu.roll(table, HALF, 1)
    cosine = jnp.where(lane < HALF, table, turned)
    sine = jnp.where(lane < HALF, -turned, table)
    return cosine, sine


def exchange_rows(n, mine, msg, send, recv):
    s, c, u = where_am_i()
    msg[pl.ds(u, 1)] = mine[None]
    copies = []
    for step in range(1, n):
        peer = lax.rem(u + step, n)
        copy = remote(msg.at[u], msg.at[u], send.at[step - 1], recv.at[step - 1], (s, c, peer))
        copy.start()
        copies.append(copy)
    for step in range(1, n):
        source = lax.rem(u + n - step, n)
        remote(
            msg.at[source], msg.at[source], send.at[step - 1], recv.at[step - 1], (s, c, source)
        ).wait_recv()
    total = msg[0]
    for j in range(1, n):
        total = total + msg[j]
    for copy in copies:
        copy.wait_send()
    return total


def to_rows(col0, col1):
    span = col0.shape[0]
    lane = lax.broadcasted_iota(jnp.int32, (span, 128), 1)
    both = jnp.where(lane == 0, col0, jnp.where(lane == 1, col1, 0.0))
    return jnp.transpose(both)[:8]


def to_columns(rows8):
    return jnp.transpose(jnp.concatenate([rows8] * 16, axis=0))


def all_uly_peers(n):
    s, c, u = where_am_i()
    return [(None, (s, c, lax.rem(u + k, n))) for k in range(1, n)]


def proj_kernel(
    n,
    x_ref,
    w_ref,
    tab_ref,
    gain_ref,
    seg_ref,
    wo_ref,
    gu_ref,
    xg_out,
    wq_out,
    wo_out,
    wga_out,
    proj_ref,
    q_ref,
    kv_ref,
    inv_ref,
    zero_ref,
    xg,
    wq,
    tab,
    msg,
    local_sem,
    w_send,
    w_recv,
    m_send,
    m_recv,
    *line,
):
    s, c, u = where_am_i()
    rows, width = x_ref.shape
    span = n * rows
    kb = w_ref.shape[1]
    sib = (1 - s, c, u)
    tab_copy = pltpu.make_async_copy(tab_ref.at[rows_of(c, span)], tab, local_sem.at[0])
    tab_copy.start()
    xg[rows_of(u, rows), :] = x_ref[...]
    greet(all_uly_peers(n) + plane_peers() + [(None, sib)])

    def plane(k, src, block, half_rows):
        return PlaneGather(
            src, block, half_rows, w_send.at[k], w_recv.at[k], local_sem.at[3 + k]
        )

    half = kb // 2
    gather = LineGather(n, rows, xg, line)
    first = plane(0, w_ref, lambda b: wq.at[:, rows_of(b, kb)], half)
    second = plane(1, wo_ref, lambda b: wo_out.at[b], wo_ref.shape[0] // 2)
    third = plane(2, gu_ref.at[0, pl.ds(0, half)], lambda b: wga_out.at[b], half // 2)
    gather.send(0)
    first.start()
    gather.wait(0)
    first.middle()
    second.start()
    if n > 2:
        gather.wait(1)
    first.corner()
    second.middle()
    third.start()
    for slot in range(2 if n > 2 else 1, n - 1):
        gather.wait(slot)
    first.arrive()
    tab_copy.wait()
    keep = [
        pltpu.make_async_copy(xg, xg_out, local_sem.at[1]),
        pltpu.make_async_copy(wq, wq_out, local_sem.at[2]),
    ]
    for copy in keep:
        copy.start()

    count, size = tiles(span, 512)

    def project(i, carry):
        where = pl.ds(pl.multiple_of(i * size, size), size)
        xs = xg[where, :]
        proj_ref[0, where, :] = dot(xs, wq[0], NN)
        proj_ref[1, where, :] = dot(xs, wq[1], NN)
        kv_ref[1, where, :] = dot(xs, wq[2], NN).astype(BF16)
        return carry

    lax.fori_loop(0, count, project, 0)
    squares = [jnp.sum(proj_ref[i] * proj_ref[i], axis=-1, keepdims=True) for i in range(2)]
    mine = to_rows(*squares)
    zeros = jnp.sum((1 - seg_ref[...]).astype(F32))
    row = lax.broadcasted_iota(jnp.int32, mine.shape, 0)
    mine = jnp.where(row == 2, zeros, mine)
    second.corner()
    third.middle()
    total = exchange_rows(n, mine, msg, m_send, m_recv)
    zero_ref[...] = jnp.broadcast_to(total[2:3, :128], (8, 128))
    inv = lax.rsqrt(to_columns(total) / width + EPS)
    inv_ref[...] = inv
    cosine, sine = rope_factors(tab[...])
    heads = proj_ref.shape[2] // HEAD_DIM
    for i in range(2):
        inverse = inv_ref[:, i : i + 1]
        for h in range(heads):
            cols = slice(h * HEAD_DIM, (h + 1) * HEAD_DIM)
            v = proj_ref[i, :, cols] * inverse * gain_ref[i : i + 1, cols]
            v = (v * cosine + pltpu.roll(v, HALF, 1) * sine).astype(BF16)
            if i == 0:
                q_ref[:, cols] = v
            else:
                kv_ref[0, :, cols] = v
    second.arrive()
    third.corner()
    third.arrive()
    for work in (first, second, third, gather):
        work.finish()
    for copy in keep:
        copy.wait()


def project(n, x, w, table, gain, seg, wo, gu):
    rows, width = x.shape
    span, cols = n * rows, w.shape[2]
    return pl.pallas_call(
        functools.partial(proj_kernel, n),
        out_shape=(
            shape((span, width), BF16),
            shape((3, width, cols), BF16),
            shape((8,) + wo.shape, BF16),
            shape((8, gu.shape[1] // 2, gu.shape[2]), BF16),
            shape((2, span, cols), F32),
            shape((span, cols), BF16),
            shape((2, span, cols), BF16),
            shape((span, 128), F32),
            shape((8, 128), F32),
        ),
        in_specs=[VM, HB, HB, VM, VM, HB, HB],
        out_specs=(HB, HB, HB, HB, VM, VM, VM, VM, VM),
        scratch_shapes=[
            pltpu.VMEM((span, width), BF16),
            pltpu.VMEM((3, width, cols), BF16),
            pltpu.VMEM((span, 128), F32),
            pltpu.VMEM((n, 8, span), F32),
            pltpu.SemaphoreType.DMA((6,)),
            pltpu.SemaphoreType.DMA((3, 9)),
            pltpu.SemaphoreType.DMA((3, 9)),
            pltpu.SemaphoreType.DMA((n - 1,)),
            pltpu.SemaphoreType.DMA((n - 1,)),
        ]
        + line_sems(n),
        compiler_params=pltpu.CompilerParams(
            collective_id=1, has_side_effects=True, vmem_limit_bytes=VMEM_LIMIT
        ),
        name="project",
    )(x, w, table, gain, seg, wo, gu)


def score_mask(scores, key_first, query_first, starts, diagonal):
    key_pos = key_first + lax.broadcasted_iota(jnp.int32, scores.shape, 0)
    keep = key_pos >= starts
    if diagonal:
        query_pos = query_first + lax.broadcasted_iota(jnp.int32, scores.shape, 1)
        keep = keep & (key_pos <= query_pos)
    return jnp.where(keep, scores, FLOOR)


def segment_starts(first, size, bound):
    pos = first + lax.broadcasted_iota(jnp.int32, (1, size), 1)
    return jnp.where(pos >= bound, bound, 0)


def attend_kernel(
    q_ref,
    kv_ref,
    zero_ref,
    kvall_out,
    attn_ref,
    attn32_ref,
    lse_ref,
    bound_ref,
    kvall,
    peaks,
    sums,
    acct,
    zmsg,
    send,
    recv,
    z_send,
    z_recv,
    keep_sem,
):
    s, c, u = where_am_i()
    span, cols = q_ref.shape
    heads = cols // HEAD_DIM
    xn, yn, dn = (s, c ^ 1, u), (s, c ^ 2, u), (s, c ^ 3, u)
    kvall[pl.ds(c, 1)] = kv_ref[...][None]
    zmsg[pl.ds(c, 1)] = zero_ref[...][None]
    greet(plane_peers() + [(None, dn)])

    def sent(k, view, peer):
        return remote(view, view, send.at[k], recv.at[k], peer)

    bx, by, bd = c ^ 1, c ^ 2, c ^ 3
    zs = [
        remote(zmsg.at[c], zmsg.at[c], z_send.at[k], z_recv.at[k], peer)
        for k, peer in enumerate((xn, yn, dn))
    ]
    for copy in zs:
        copy.start()
    copies = [sent(0, kvall.at[c], xn), sent(1, kvall.at[c], yn)]
    for copy in copies:
        copy.start()
    for k, (b, peer) in enumerate(((bx, xn), (by, yn), (bd, dn))):
        remote(zmsg.at[b], zmsg.at[b], z_send.at[k], z_recv.at[k], peer).wait_recv()
    ahead = jnp.zeros((8, 128), F32)
    for j in range(4):
        ahead = ahead + jnp.where(j <= c, zmsg[j], 0.0)
    bounds = ahead.astype(jnp.int32)
    bound_ref[...] = bounds
    bound = bounds[:1, :1]

    peaks[...] = jnp.full_like(peaks, FLOOR)
    sums[...] = jnp.zeros_like(sums)
    acct[...] = jnp.zeros_like(acct)
    nq, tq = tiles(span, 512)
    nk, tk = tiles(span, 512)

    def update(number, diagonal):
        def over_queries(i, carry):
            first_q = c * span + i * tq
            starts = segment_starts(first_q, tq, bound)
            where_q = pl.ds(pl.multiple_of(i * tq, tq), tq)

            def over_keys(j, carry):
                first_k = number * span + j * tk
                where_k = pl.ds(pl.multiple_of(j * tk, tk), tk)
                for h in range(heads):
                    lanes = slice(h * HEAD_DIM, (h + 1) * HEAD_DIM)
                    scores = dot(kvall[number, 0, where_k, lanes], q_ref[where_q, lanes], NT)
                    scores = score_mask(scores * SCALE2, first_k, first_q, starts, diagonal)
                    old = peaks[h, :1, where_q]
                    new = jnp.maximum(old, jnp.max(scores, axis=0, keepdims=True))
                    factor = jnp.exp2(old - new)
                    weights = jnp.exp2(scores - new)
                    peaks[h, :1, where_q] = new
                    sums[h, :1, where_q] = sums[h, :1, where_q] * factor + jnp.sum(
                        weights, axis=0, keepdims=True
                    )
                    acct[h, :, where_q] = acct[h, :, where_q] * factor + dot(
                        kvall[number, 1, where_k, lanes], weights.astype(BF16), TN
                    )
                return carry

            return lax.fori_loop(0, nk, over_keys, carry)

        lax.fori_loop(0, nq, over_queries, 0)

    update(c, True)
    half = span // 2
    sent(0, kvall.at[bx], xn).wait_recv()
    more = [sent(2, kvall.at[bx, :, pl.ds(0, half)], yn)]
    more[0].start()
    copies += more
    sent(1, kvall.at[by], yn).wait_recv()
    more = [sent(3, kvall.at[by, :, pl.ds(half, half)], xn)]
    more[0].start()
    copies += more
    for b in (bx, by):

        @pl.when(b < c)
        def _():
            update(b, False)

    sent(2, kvall.at[bd, :, pl.ds(0, half)], yn).wait_recv()
    sent(3, kvall.at[bd, :, pl.ds(half, half)], xn).wait_recv()
    keep = pltpu.make_async_copy(kvall, kvall_out, keep_sem)
    keep.start()

    @pl.when(bd < c)
    def _():
        update(bd, False)

    for h in range(heads):
        lanes = slice(h * HEAD_DIM, (h + 1) * HEAD_DIM)
        total = sums[h, :1, :]
        attention = jnp.transpose(acct[h] / total)
        attn32_ref[:, lanes] = attention
        attn_ref[:, lanes] = attention.astype(BF16)
        lse_ref[h, :1, :] = peaks[h, :1, :] + jnp.log2(total)
    for copy in copies + zs:
        copy.wait_send()
    keep.wait()


def attend(q, kv, zero):
    span, cols = q.shape
    heads = cols // HEAD_DIM
    return pl.pallas_call(
        attend_kernel,
        out_shape=(
            shape((4, 2, span, cols), BF16),
            shape((span, cols), BF16),
            shape((span, cols), F32),
            shape((heads, 8, span), F32),
            shape((8, 128), jnp.int32),
        ),
        in_specs=[VM] * 3,
        out_specs=(HB, VM, VM, VM, VM),
        scratch_shapes=[
            pltpu.VMEM((4, 2, span, cols), BF16),
            pltpu.VMEM((heads, 8, span), F32),
            pltpu.VMEM((heads, 8, span), F32),
            pltpu.VMEM((heads, HEAD_DIM, span), F32),
            pltpu.VMEM((4, 8, 128), F32),
            pltpu.SemaphoreType.DMA((4,)),
            pltpu.SemaphoreType.DMA((4,)),
            pltpu.SemaphoreType.DMA((3,)),
            pltpu.SemaphoreType.DMA((3,)),
            pltpu.SemaphoreType.DMA,
        ],
        compiler_params=pltpu.CompilerParams(
            collective_id=2, has_side_effects=True, vmem_limit_bytes=VMEM_LIMIT
        ),
        name="attend",
    )(q, kv, zero)


def attend_back_kernel(
    n,
    q_ref,
    kvall_ref,
    do_ref,
    attn32_ref,
    lse_ref,
    bound_ref,
    attn_ref,
    dbranch_ref,
    proj_ref,
    inv_ref,
    gain_ref,
    tab_ref,
    dproj_ref,
    dgain_ref,
    own_out,
    x_out,
    y_out,
    dq_ref,
    part,
    got,
    acc,
    delta,
    dbranch,
    dbranch_s,
    attn_s,
    ring,
    got_o,
    tab,
    msg,
    send,
    recv,
    s_send,
    s_recv,
    local_sem,
    m_send,
    m_recv,
    o_send,
    o_recv,
    o_local,
):
    s, c, u = where_am_i()
    span, cols = q_ref.shape
    width = dbranch_ref.shape[1]
    heads = cols // HEAD_DIM
    xn, yn = (s, c ^ 1, u), (s, c ^ 2, u)
    bx, by, bd = c ^ 1, c ^ 2, c ^ 3
    load = [
        pltpu.make_async_copy(tab_ref.at[rows_of(c, span)], tab, local_sem.at[0]),
        pltpu.make_async_copy(half_columns(dbranch_ref, s), dbranch, local_sem.at[1]),
    ]
    for copy in load:
        copy.start()
    greet(plane_peers() + all_uly_peers(n) + [(None, (1 - s, c, u))])
    sibling = Sibling(s_send, s_recv)
    sibling.start(half_columns(dbranch_ref, 1 - s), dbranch_s)
    sibling.start(attn_ref, attn_s)
    bound = bound_ref[:1, :1]
    nq, tq = tiles(span, 512)
    nk, tk = tiles(span, 512)
    scale = HEAD_DIM ** (-0.5)
    dq_ref[...] = jnp.zeros_like(dq_ref)
    for h in range(heads):
        lanes = slice(h * HEAD_DIM, (h + 1) * HEAD_DIM)
        both = jnp.transpose(do_ref[:, lanes].astype(F32) * attn32_ref[:, lanes])
        delta[h, :1, :] = jnp.sum(both, axis=0, keepdims=True)

    def update(number, diagonal):
        acc[...] = jnp.zeros_like(acc)

        def over_queries(i, carry):
            first_q = c * span + i * tq
            starts = segment_starts(first_q, tq, bound)
            where_q = pl.ds(pl.multiple_of(i * tq, tq), tq)

            def over_keys(j, carry):
                first_k = number * span + j * tk
                where_k = pl.ds(pl.multiple_of(j * tk, tk), tk)
                for h in range(heads):
                    lanes = slice(h * HEAD_DIM, (h + 1) * HEAD_DIM)
                    keys = kvall_ref[number, 0, where_k, lanes]
                    values = kvall_ref[number, 1, where_k, lanes]
                    query, d_out = q_ref[where_q, lanes], do_ref[where_q, lanes]
                    scores = dot(keys, query, NT) * SCALE2
                    scores = score_mask(scores, first_k, first_q, starts, diagonal)
                    probs = jnp.exp2(scores - lse_ref[h, :1, where_q])
                    acc[1, where_k, lanes] += dot(probs.astype(BF16), d_out, NN)
                    d_probs = dot(values, d_out, NT)
                    d_scores = (probs * (d_probs - delta[h, :1, where_q])).astype(BF16)
                    acc[0, where_k, lanes] += dot(d_scores, query, NN) * scale
                    dq_ref[where_q, lanes] += dot(d_scores, keys, TN) * scale
                return carry

            return lax.fori_loop(0, nk, over_keys, carry)

        lax.fori_loop(0, nq, over_queries, 0)

    def work(number):
        @pl.when(number < c)
        def _():
            update(number, False)
            part[pl.ds(number, 1)] = acc[...].astype(BF16)[None]

        @pl.when(number > c)
        def _():
            part[pl.ds(number, 1)] = jnp.zeros_like(part[pl.ds(number, 1)])

    half = span // 2
    lo, hi = pl.ds(0, half), pl.ds(half, half)

    def sent(k, src, dst, peer):
        return remote(src, dst, send.at[k], recv.at[k], peer)

    def place(out, piece, part):
        size = cols if part is None else cols // 2
        return out.at[pl.ds((part or 0) * size, size)]

    weight = PlaneReduce(ring, got_o, (own_out, x_out, y_out), place, o_send, o_recv, o_local)
    pieces = Pieces(
        [
            (
                weight,
                0,
                wide_piece((attn_ref, dbranch), (attn_s, dbranch_s), lambda p: slice(None)),
            )
        ]
    )
    work(bd)
    copies = [
        sent(0, part.at[bd, :, lo], got.at[0, :, lo], xn),
        sent(1, part.at[bd, :, hi], got.at[0, :, hi], yn),
    ]
    for copy in copies:
        copy.start()
    work(bx)
    sent(1, part.at[bx, :, hi], got.at[0, :, hi], yn).wait_recv()
    part[bx, :, half:, :] = (
        part[bx, :, half:, :].astype(F32) + got[0, :, half:, :].astype(F32)
    ).astype(BF16)
    more = [sent(2, part.at[bx], got.at[1], xn)]
    more[0].start()
    copies += more
    work(by)
    sent(0, part.at[by, :, lo], got.at[0, :, lo], xn).wait_recv()
    part[by, :, :half, :] = (
        part[by, :, :half, :].astype(F32) + got[0, :, :half, :].astype(F32)
    ).astype(BF16)
    more = [sent(3, part.at[by], got.at[2], yn)]
    more[0].start()
    copies += more
    wait_all(load)
    sibling.wait(0)
    sibling.wait(1)
    pieces.step()
    update(c, True)

    cosine, sine = rope_factors(tab[...])

    def turn_back(i):
        inverse = inv_ref[:, i : i + 1]
        row_dot = jnp.zeros((span, 1), F32)
        for h in range(heads):
            lanes = slice(h * HEAD_DIM, (h + 1) * HEAD_DIM)
            source = dq_ref if i == 0 else acc.at[0]
            v = source[:, lanes]
            v = v * cosine - pltpu.roll(v, HALF, 1) * sine
            values = proj_ref[i, :, lanes]
            dgain_ref[i : i + 1, lanes] = jnp.sum(v * values * inverse, axis=0, keepdims=True)
            v = v * gain_ref[i : i + 1, lanes]
            source[:, lanes] = v
            row_dot = row_dot + jnp.sum(values * v, axis=-1, keepdims=True)
        return row_dot

    dots_q = turn_back(0)
    sent(2, part.at[bx], got.at[1], xn).wait_recv()
    sent(3, part.at[by], got.at[2], yn).wait_recv()
    acc[...] += got[1].astype(F32) + got[2].astype(F32)
    dproj_ref[2] = acc[1].astype(BF16)
    dots_k = turn_back(1)
    total = exchange_rows(n, to_rows(dots_q, dots_k), msg, m_send, m_recv)
    means = to_columns(total) / width
    for i in range(2):
        inverse = inv_ref[:, i : i + 1]
        factor = inverse**3 * means[:, i : i + 1]
        source = dq_ref if i == 0 else acc.at[0]
        dproj_ref[i] = (inverse * source[...] - proj_ref[i] * factor).astype(BF16)
    pieces.finish()
    weight.finish(1)
    sibling.finish()
    for copy in copies:
        copy.wait_send()


def attend_back(n, q, kvall, d_out, attn32, lse, bound, attn, dbranch, proj, inv, gain, table):
    span, cols = q.shape
    heads = cols // HEAD_DIM
    width = dbranch.shape[1]
    ring, sems = piece_scratch(1, 1, cols, width // 8)
    return pl.pallas_call(
        functools.partial(attend_back_kernel, n),
        out_shape=(shape((3, span, cols), BF16), shape((2, cols), F32))
        + (shape((cols, width // 8), BF16),) * 3,
        in_specs=[VM] * 7 + [HB, VM, VM, VM, HB],
        out_specs=(VM, VM, HB, HB, HB),
        scratch_shapes=[
            pltpu.VMEM((span, cols), F32),
            pltpu.VMEM((4, 2, span, cols), BF16),
            pltpu.VMEM((3, 2, span, cols), BF16),
            pltpu.VMEM((2, span, cols), F32),
            pltpu.VMEM((heads, 8, span), F32),
            pltpu.VMEM((span, width // 2), BF16),
            pltpu.VMEM((span, width // 2), BF16),
            pltpu.VMEM((span, cols), BF16),
            ring[0],
            ring[1],
            pltpu.VMEM((span, 128), F32),
            pltpu.VMEM((n, 8, span), F32),
            pltpu.SemaphoreType.DMA((4,)),
            pltpu.SemaphoreType.DMA((4,)),
            pltpu.SemaphoreType.DMA((2,)),
            pltpu.SemaphoreType.DMA((2,)),
            pltpu.SemaphoreType.DMA((2,)),
            pltpu.SemaphoreType.DMA((n - 1,)),
            pltpu.SemaphoreType.DMA((n - 1,)),
        ]
        + sems,
        compiler_params=pltpu.CompilerParams(
            collective_id=3, has_side_effects=True, vmem_limit_bytes=VMEM_LIMIT
        ),
        name="attend_back",
    )(q, kvall, d_out, attn32, lse, bound, attn, dbranch, proj, inv, gain, table)


def load_blocks(src, dst, sem, axis):
    blocks = src.shape[0]
    size = dst.shape[axis] // blocks
    copies = []
    for b in range(blocks):
        where = [slice(None)] * len(dst.shape)
        where[axis] = pl.ds(b * size, size)
        copies.append(pltpu.make_async_copy(src.at[b], dst.at[tuple(where)], sem.at[b]))
    for copy in copies:
        copy.start()
    return copies


def wait_all(copies):
    for copy in copies:
        copy.wait()


def mlp_in_kernel(
    n,
    attn_ref,
    wo_ref,
    x_ref,
    gain_ref,
    wga_ref,
    gu_ref,
    down_ref,
    branch_ref,
    resid_ref,
    group_out,
    gate_ref,
    up_ref,
    hidden_ref,
    wgb_out,
    wgc_out,
    wd_out,
    wo,
    wg,
    group,
    part,
    got_rows,
    sem_o,
    local_sem,
    w_send,
    w_recv,
    *sems,
):
    s, c, u = where_am_i()
    rows, width = x_ref.shape
    load_o = load_blocks(wo_ref, wo, sem_o, 1)
    half = wga_ref.shape[1]
    load_g = [
        pltpu.make_async_copy(wga_ref, wg.at[0, :, pl.ds(0, half)], local_sem.at[0]),
        pltpu.make_async_copy(wgb_out, wg.at[0, :, pl.ds(half, half)], local_sem.at[1]),
        pltpu.make_async_copy(wgc_out, wg.at[1], local_sem.at[2]),
    ]
    load_g[0].start()
    greet(line_peers(n) + plane_peers() + [(None, (1 - s, c, u))])

    def plane(k, src, out, half_rows):
        return PlaneGather(
            src, lambda b: out.at[b], half_rows, w_send.at[k], w_recv.at[k], local_sem.at[4 + k]
        )

    first = plane(0, gu_ref.at[0, pl.ds(half, half)], wgb_out, half // 2)
    second = plane(1, gu_ref.at[1], wgc_out, half)
    third = plane(2, down_ref, wd_out, down_ref.shape[0] // 2)
    first.start()
    wait_all(load_o)
    chunk_cols = width // part.shape[0]
    span = n * rows
    count, size = tiles(span, 512)

    def compute(chunk):
        def tile(i, carry):
            where = pl.ds(pl.multiple_of(i * size, size), size)
            part[chunk, where, :] = dot(
                attn_ref[where, :], wo[:, chunk * chunk_cols : (chunk + 1) * chunk_cols], NN
            ).astype(BF16)
            return carry

        lax.fori_loop(0, count, tile, 0)

    def reduce_hook(slot):
        if slot == 0:
            first.middle()
            second.start()
        if slot == 1:
            first.corner()
        if slot == 2:
            first.arrive()
            load_g[1].start()

    LineReduce(n, rows, part, got_rows, sems[:4]).run(compute, branch_ref, reduce_hook)
    branch = branch_ref[...]
    resid = x_ref[...].astype(F32) + branch * inverse_rms(branch) * gain_ref[0:1, :]
    resid_ref[...] = resid
    group[rows_of(u, rows), :] = resid.astype(BF16)
    gather = LineGather(n, rows, group, sems[4:])
    gather.send(0)
    second.middle()
    third.start()

    def gather_hook(slot):
        if slot == 1:
            second.corner()

    gather.run(gather_hook)
    second.arrive()
    load_g[2].start()
    keep = pltpu.make_async_copy(group, group_out, local_sem.at[3])
    keep.start()
    third.middle()
    wait_all(load_g)
    ff = gate_ref.shape[1]
    ntile, tsize = tiles(ff, 512)

    def body(i, carry):
        lanes = pl.ds(pl.multiple_of(i * tsize, tsize), tsize)

        def tile(j, carry):
            where = pl.ds(pl.multiple_of(j * size, size), size)
            gate = dot(group[where, :], wg[0, :, :, lanes].reshape(width, tsize), NN)
            up = dot(group[where, :], wg[1, :, :, lanes].reshape(width, tsize), NN)
            gate_ref[where, lanes] = gate.astype(BF16)
            up_ref[where, lanes] = up.astype(BF16)
            hidden_ref[where, lanes] = (gate * jax.nn.sigmoid(gate) * up).astype(BF16)
            return carry

        return lax.fori_loop(0, count, tile, carry)

    lax.fori_loop(0, ntile, body, 0)
    third.corner()
    third.arrive()
    for work in (first, second, third):
        work.finish()
    keep.wait()


def reduce_scratch(n, rows, width):
    cols = width // CHUNKS
    return [
        pltpu.VMEM((CHUNKS, n * rows, cols), BF16),
        pltpu.VMEM((CHUNKS, (n + 1) * rows, cols), BF16),
    ]


def mlp_in(n, attn, wo, x, gain, wga, gu, down):
    rows, width = x.shape
    span, cols = attn.shape
    kb, ff = gu.shape[1:]
    return pl.pallas_call(
        functools.partial(mlp_in_kernel, n),
        out_shape=(
            shape((rows, width), F32),
            shape((rows, width), F32),
            shape((span, width), BF16),
            shape((span, ff), BF16),
            shape((span, ff), BF16),
            shape((span, ff), BF16),
            shape((8, kb // 2, ff), BF16),
            shape((8, kb, ff), BF16),
            shape((8,) + down.shape, BF16),
        ),
        in_specs=[VM, HB, VM, VM, HB, HB, HB],
        out_specs=(VM, VM, HB, VM, VM, VM, HB, HB, HB),
        scratch_shapes=[
            pltpu.VMEM((cols, width), BF16),
            pltpu.VMEM((2, 8, kb, ff), BF16),
            pltpu.VMEM((span, width), BF16),
        ]
        + reduce_scratch(n, rows, width)
        + [
            pltpu.SemaphoreType.DMA((8,)),
            pltpu.SemaphoreType.DMA((7,)),
            pltpu.SemaphoreType.DMA((3, 9)),
            pltpu.SemaphoreType.DMA((3, 9)),
        ]
        + line_sems(n, CHUNKS)
        + line_sems(n),
        compiler_params=pltpu.CompilerParams(
            collective_id=4, has_side_effects=True, vmem_limit_bytes=VMEM_LIMIT
        ),
        name="mlp_in",
    )(attn, wo, x, gain, wga, gu, down)


def mlp_out_kernel(
    n,
    hidden_ref,
    wd_ref,
    resid_ref,
    gain_ref,
    cot_ref,
    gate_ref,
    up_ref,
    out_ref,
    group_out,
    dgu_ref,
    dgain_ref,
    wd,
    mlp,
    group,
    part,
    got_rows,
    sem_d,
    keep_sem,
    *sems,
):
    s, c, u = where_am_i()
    rows, width = resid_ref.shape
    load_d = load_blocks(wd_ref, wd, sem_d, 1)
    greet(line_peers(n))
    wait_all(load_d)
    chunk_cols = width // part.shape[0]
    span = n * rows
    count, size = tiles(span, 512)

    def compute(chunk):
        def tile(i, carry):
            where = pl.ds(pl.multiple_of(i * size, size), size)
            part[chunk, where, :] = dot(
                hidden_ref[where, :], wd[:, chunk * chunk_cols : (chunk + 1) * chunk_cols], NN
            ).astype(BF16)
            return carry

        lax.fori_loop(0, count, tile, 0)

    LineReduce(n, rows, part, got_rows, sems[:4]).run(compute, mlp)
    values = mlp[...]
    inverse = inverse_rms(values)
    grad = cot_ref[...].astype(F32)
    d_mlp = norm_back(values, inverse, grad * gain_ref[1:2, :], width)
    group[rows_of(u, rows), :] = d_mlp.astype(BF16)
    gather = LineGather(n, rows, group, sems[4:])
    gather.send(0)
    scaled = values * inverse
    out_ref[...] = (resid_ref[...] + scaled * gain_ref[1:2, :]).astype(BF16)
    dgain_ref[...] = jnp.sum(grad * scaled, axis=0, keepdims=True)
    for slot in range(n - 1):
        gather.wait(slot)
    gather.finish()
    keep = pltpu.make_async_copy(group, group_out, keep_sem)
    keep.start()
    ntile, tsize = tiles(gate_ref.shape[1], 512)

    def body(i, carry):
        lanes = pl.ds(pl.multiple_of(i * tsize, tsize), tsize)

        def tile(j, carry):
            where = pl.ds(pl.multiple_of(j * size, size), size)
            d_hidden = dot(group[where, :], wd[lanes, :], NT)
            gate = gate_ref[where, lanes].astype(F32)
            up = up_ref[where, lanes].astype(F32)
            sig = jax.nn.sigmoid(gate)
            slope = sig * (1.0 + gate * (1.0 - sig))
            dgu_ref[0, where, lanes] = (d_hidden * up * slope).astype(BF16)
            dgu_ref[1, where, lanes] = (d_hidden * (gate * sig)).astype(BF16)
            return carry

        return lax.fori_loop(0, count, tile, carry)

    lax.fori_loop(0, ntile, body, 0)
    keep.wait()


def mlp_out(n, hidden, wd, resid, gain, cot, gate, up):
    rows, width = resid.shape
    span, ff = hidden.shape
    return pl.pallas_call(
        functools.partial(mlp_out_kernel, n),
        out_shape=(
            shape((rows, width), BF16),
            shape((span, width), BF16),
            shape((2, span, ff), BF16),
            shape((1, width), F32),
        ),
        in_specs=[VM, HB, VM, VM, VM, VM, VM],
        out_specs=(VM, HB, VM, VM),
        scratch_shapes=[
            pltpu.VMEM((ff, width), BF16),
            pltpu.VMEM((rows, width), F32),
            pltpu.VMEM((span, width), BF16),
        ]
        + reduce_scratch(n, rows, width)
        + [pltpu.SemaphoreType.DMA((8,)), pltpu.SemaphoreType.DMA]
        + line_sems(n, CHUNKS)
        + line_sems(n),
        compiler_params=pltpu.CompilerParams(
            collective_id=5, has_side_effects=True, vmem_limit_bytes=VMEM_LIMIT
        ),
        name="mlp_out",
    )(hidden, wd, resid, gain, cot, gate, up)


def mlp_back_kernel(
    n,
    dgu_ref,
    wga_ref,
    wgb_ref,
    wgc_ref,
    cot_ref,
    branch_ref,
    gain_ref,
    wo_ref,
    hidden_ref,
    dmlp_ref,
    resid_ref,
    dresid_ref,
    group_out,
    dattn_ref,
    dgain_ref,
    gown_out,
    gx_out,
    gy_out,
    down_own_out,
    down_x_out,
    down_y_out,
    wo,
    wg,
    group,
    part,
    got_rows,
    dmlp,
    resid,
    hidden_s,
    dmlp_s,
    resid_s,
    dgu_s,
    ring_d,
    ring_g,
    got_d,
    got_g,
    sem_o,
    local_sem,
    s_send,
    s_recv,
    d_send,
    d_recv,
    d_local,
    g_send,
    g_recv,
    g_local,
    *sems,
):
    s, c, u = where_am_i()
    rows, width = cot_ref.shape
    half = wga_ref.shape[1]
    chunk_cols = width // part.shape[0]
    per_chunk = chunk_cols // (2 * half)
    chunks = part.shape[0]

    def load_chunk(chunk):
        slot = chunk % 2
        where = pl.ds(chunk * per_chunk, per_chunk)
        return [
            pltpu.make_async_copy(
                wga_ref.at[where], wg.at[slot, 0, :, pl.ds(0, half)], local_sem.at[slot, 0]
            ),
            pltpu.make_async_copy(
                wgb_ref.at[where], wg.at[slot, 0, :, pl.ds(half, half)], local_sem.at[slot, 1]
            ),
            pltpu.make_async_copy(wgc_ref.at[where], wg.at[slot, 1], local_sem.at[slot, 2]),
        ]

    def start_chunk(chunk):
        for copy in load_chunk(chunk):
            copy.start()

    start_chunk(0)
    start_chunk(1)
    load_m = [
        pltpu.make_async_copy(half_columns(dmlp_ref, s), dmlp, local_sem.at[2, 0]),
        pltpu.make_async_copy(half_columns(resid_ref, s), resid, local_sem.at[2, 1]),
    ]
    for copy in load_m:
        copy.start()
    load_o = load_blocks(wo_ref, wo, sem_o, 1)
    greet(line_peers(n) + plane_peers() + [(None, (1 - s, c, u))])
    sibling = Sibling(s_send, s_recv)
    sibling.start(half_columns(dmlp_ref, 1 - s), dmlp_s)
    sibling.start(hidden_ref, hidden_s)
    sibling.start(half_columns(resid_ref, 1 - s), resid_s)
    sibling.start(dgu_ref, dgu_s)
    span = n * rows
    count, size = tiles(span, 512)

    def compute(chunk):
        wait_all(load_chunk(chunk))
        slot = chunk % 2

        def tile(i, carry):
            where = pl.ds(pl.multiple_of(i * size, size), size)
            part[chunk, where, :] = (
                dot(dgu_ref[0, where, :], wg[slot, 0].reshape(chunk_cols, -1), NT)
                + dot(dgu_ref[1, where, :], wg[slot, 1].reshape(chunk_cols, -1), NT)
            ).astype(BF16)
            return carry

        lax.fori_loop(0, count, tile, 0)
        if chunk + 2 < chunks:
            start_chunk(chunk + 2)

    rows_d, cols_g = ring_d.shape[2], ring_g.shape[3]
    tiles_g = dgu_ref.shape[2] // cols_g

    def place_d(out, piece, part):
        size = rows_d if part is None else rows_d // 2
        return out.at[pl.ds(piece * rows_d + (part or 0) * size, size)]

    def place_g(out, piece, part):
        size = ring_g.shape[2] if part is None else ring_g.shape[2] // 2
        ci, tile = piece // tiles_g, piece % tiles_g
        return out.at[ci, pl.ds((part or 0) * size, size), pl.ds(tile * cols_g, cols_g)]

    down = PlaneReduce(
        ring_d, got_d, (down_own_out, down_x_out, down_y_out), place_d, d_send, d_recv, d_local
    )
    gate = PlaneReduce(ring_g, got_g, (gown_out, gx_out, gy_out), place_g, g_send, g_recv, g_local)
    down_piece = wide_piece(
        (hidden_ref, dmlp), (hidden_s, dmlp_s), lambda p: slice(p * rows_d, (p + 1) * rows_d)
    )

    def gate_right(ref, piece):
        tile = piece % tiles_g
        return ref[piece // tiles_g, :, tile * cols_g : (tile + 1) * cols_g]

    gate_piece = tall_piece((resid, dgu_ref), (resid_s, dgu_s), gate_right)
    n_d, n_g = got_d.shape[0], got_g.shape[0]
    pieces = Pieces(
        [(down, p, down_piece) for p in range(n_d)] + [(gate, p, gate_piece) for p in range(n_g)]
    )

    def reduce_hook(slot):
        if slot == 0:
            wait_all(load_m)
            sibling.wait(0)
            sibling.wait(1)
            pieces.step(2)
        if slot == 1:
            pieces.step()
        if slot == 2:
            pieces.step()

    LineReduce(n, rows, part, got_rows, sems[:4]).run(compute, dresid_ref, reduce_hook)
    d_resid = dresid_ref[...] + cot_ref[...].astype(F32)
    dresid_ref[...] = d_resid
    branch = branch_ref[...]
    inverse = inverse_rms(branch)
    d_branch = norm_back(branch, inverse, d_resid * gain_ref[0:1, :], width)
    small = group.shape[0] == span
    if small:
        group[rows_of(u, rows), :] = d_branch.astype(BF16)
        gather = LineGather(n, rows, group, sems[4:])
    else:
        group[:rows, :] = d_branch.astype(BF16)
        own = pltpu.make_async_copy(
            group.at[pl.ds(0, rows)], group_out.at[rows_of(u, rows)], local_sem.at[2, 2]
        )
        own.start()
        own.wait()
        gather = LineGather(n, rows, group_out, sems[4:])
    gather.send(0)
    dgain_ref[...] = jnp.sum(d_resid * branch * inverse, axis=0, keepdims=True)
    wait_all(load_o)
    sibling.wait(2)
    sibling.wait(3)
    pieces.step()

    def gather_hook(slot):
        if slot < 2:
            pieces.step()

    gather.run(gather_hook)
    if small:
        keep = pltpu.make_async_copy(group, group_out, local_sem.at[2, 2])
        keep.start()
    pieces.step()

    def tile(j, carry):
        where = pl.ds(pl.multiple_of(j * size, size), size)
        if small:
            rows_in = group[where, :]
        else:
            fetch = pltpu.make_async_copy(group_out.at[where], group, local_sem.at[2, 2])
            fetch.start()
            fetch.wait()
            rows_in = group[...]
        dattn_ref[where, :] = dot(rows_in, wo[...], NT).astype(BF16)
        return carry

    lax.fori_loop(0, count, tile, 0)
    pieces.finish()
    down.finish(n_d)
    gate.finish(n_g)
    sibling.finish()
    if small:
        keep.wait()


def piece_scratch(slots, pieces, rows, cols):
    return (
        [pltpu.VMEM((slots, 4, rows, cols), BF16), pltpu.VMEM((pieces, rows, cols), BF16)],
        [
            pltpu.SemaphoreType.DMA((pieces, 6)),
            pltpu.SemaphoreType.DMA((pieces, 6)),
            pltpu.SemaphoreType.DMA((pieces,)),
        ],
    )


def mlp_back(n, dgu, wga, wgb, wgc, cot, branch, gain, wo, hidden, dmlp, resid):
    rows, width = branch.shape
    span, ff = dgu.shape[1:]
    cols = wo.shape[1]
    kb, kc = width // 8, wo.shape[2]
    count, size = tiles(ff, 512)
    ring_d, sems_d = piece_scratch(min(3, count), count, size, kc)
    ring_g, sems_g = piece_scratch(3 if count > 1 else 2, 2 * count, kb, size)
    chunk_blocks = width // CHUNKS // kb
    return pl.pallas_call(
        functools.partial(mlp_back_kernel, n),
        out_shape=(
            shape((rows, width), F32),
            shape((span, width), BF16),
            shape((span, cols), BF16),
            shape((1, width), F32),
        )
        + (shape((2, kb, ff), BF16),) * 3
        + (shape((ff, kc), BF16),) * 3,
        in_specs=[VM, HB, HB, HB, VM, VM, VM, HB, VM, HB, HB],
        out_specs=(VM, HB, VM, VM) + (HB,) * 6,
        scratch_shapes=[
            pltpu.VMEM((cols, width), BF16),
            pltpu.VMEM((2, 2, chunk_blocks, kb, ff), BF16),
            pltpu.VMEM((min(span, 512), width), BF16),
        ]
        + reduce_scratch(n, rows, width)
        + [
            pltpu.VMEM((span, width // 2), BF16),
            pltpu.VMEM((span, width // 2), BF16),
            pltpu.VMEM((span, ff), BF16),
            pltpu.VMEM((span, width // 2), BF16),
            pltpu.VMEM((span, width // 2), BF16),
            pltpu.VMEM((2, span, ff), BF16),
            ring_d[0],
            ring_g[0],
            ring_d[1],
            ring_g[1],
            pltpu.SemaphoreType.DMA((8,)),
            pltpu.SemaphoreType.DMA((3, 3)),
            pltpu.SemaphoreType.DMA((4,)),
            pltpu.SemaphoreType.DMA((4,)),
        ]
        + sems_d
        + sems_g
        + line_sems(n, CHUNKS)
        + line_sems(n),
        compiler_params=pltpu.CompilerParams(
            collective_id=6, has_side_effects=True, vmem_limit_bytes=VMEM_LIMIT
        ),
        name="mlp_back",
    )(dgu, wga, wgb, wgc, cot, branch, gain, wo, hidden, dmlp, resid)


def proj_back_kernel(
    n,
    dproj_ref,
    wq_ref,
    dresid_ref,
    xg_ref,
    gcols_ref,
    gattn_ref,
    gmlp_ref,
    out_ref,
    gain_ref,
    own_out,
    x_out,
    y_out,
    wq,
    xs,
    xs_s,
    dproj_s,
    total,
    part,
    got_rows,
    ring,
    got,
    sums,
    local_sem,
    s_send,
    s_recv,
    q_send,
    q_recv,
    q_local,
    v_send,
    v_recv,
    m_send,
    m_recv,
    *sems,
):
    s, c, u = where_am_i()
    rows, width = dresid_ref.shape
    span = n * rows
    load = [
        pltpu.make_async_copy(wq_ref, wq, local_sem.at[0]),
        pltpu.make_async_copy(half_columns(xg_ref, s), xs, local_sem.at[1]),
    ]
    for copy in load:
        copy.start()
    corner = (s, c ^ 3, u)
    greet(all_uly_peers(n) + plane_peers() + [(None, corner), (None, (1 - s, c, u))])
    gains = GainSum(n, sums, (v_send, v_recv, m_send, m_recv))
    gains.start(gcols_ref, gattn_ref, gmlp_ref)
    sibling = Sibling(s_send, s_recv)
    sibling.start(half_columns(xg_ref, 1 - s), xs_s)
    sibling.start(dproj_ref, dproj_s)
    load[0].wait()
    chunk_cols = width // part.shape[0]
    count, size = tiles(span, 512)

    def compute(chunk):
        cols = slice(chunk * chunk_cols, (chunk + 1) * chunk_cols)

        def tile(i, carry):
            where = pl.ds(pl.multiple_of(i * size, size), size)
            part[chunk, where, :] = (
                dot(dproj_ref[0, where, :], wq[0, cols, :], NT)
                + dot(dproj_ref[1, where, :], wq[1, cols, :], NT)
                + dot(dproj_ref[2, where, :], wq[2, cols, :], NT)
            ).astype(BF16)
            return carry

        lax.fori_loop(0, count, tile, 0)

    def place(out, piece, part):
        size = ring.shape[2] if part is None else ring.shape[2] // 2
        return out.at[piece, pl.ds((part or 0) * size, size)]

    weight = PlaneReduce(ring, got, (own_out, x_out, y_out), place, q_send, q_recv, q_local)
    compute_piece = tall_piece((xs, dproj_ref), (xs_s, dproj_s), lambda ref, piece: ref[piece])
    pieces = Pieces([(weight, p, compute_piece) for p in range(3)])

    def hook(slot):
        if slot == 0:
            load[1].wait()
            sibling.wait(0)
            sibling.wait(1)
            pieces.step(3)
            gains.over_ctx()
        if slot == 1:
            pieces.catch_up()
            gains.over_uly()

    LineReduce(n, rows, part, got_rows, sems[:4]).run(compute, total, hook)
    out_ref[...] = (dresid_ref[...] + total[...]).astype(BF16)
    pieces.finish()
    gains.finish(gain_ref)
    weight.finish(3)
    sibling.finish()


class GainSum:
    def __init__(self, n, refs, sems):
        self.n = n
        self.all, self.core, self.plane, self.line = refs
        self.v_send, self.v_recv, self.m_send, self.m_recv = sems
        self.s, self.c, self.u = where_am_i()
        self.sent = []

    def copy(self, k, src, dst, peer):
        return remote(src, dst, self.v_send.at[k], self.v_recv.at[k], peer)

    def go(self, copy):
        copy.start()
        self.sent.append(copy)

    def start(self, cols, attn, mlp):
        half, local = self.all.shape[2], cols.shape[1]
        rows = jnp.zeros((8, half), F32)
        for h in range(2):
            self.all[h] = rows
        mine = self.u * local
        home = pl.ds(pl.multiple_of(lax.rem(mine, half), local), local)
        self.all[pl.ds(mine // half, 1), 0:2, home] = cols[...][None]
        for h in range(2):
            part = slice(h * half, (h + 1) * half)
            self.all[h, 2:3, :] = attn[:, part]
            self.all[h, 3:4, :] = mlp[:, part]
        self.go(self.copy(0, self.all.at[1 - self.s], self.core, (1 - self.s, self.c, self.u)))

    def over_ctx(self):
        s, c, u = self.s, self.c, self.u
        self.copy(0, self.all.at[s], self.core, (1 - s, c, u)).wait_recv()
        size = self.plane.shape[2]
        total = self.all[pl.ds(s, 1)][0] + self.core[...]
        for j in range(4):
            self.plane[j] = total[:, j * size : (j + 1) * size]
        for k in (1, 2, 3):
            self.go(self.copy(k, self.plane.at[c ^ k], self.line.at[k - 1], (s, c ^ k, u)))

    def over_uly(self):
        s, c, u = self.s, self.c, self.u
        total = self.plane[pl.ds(c, 1)][0]
        for k in (1, 2, 3):
            self.copy(k, self.plane.at[c ^ k], self.line.at[k - 1], (s, c ^ k, u)).wait_recv()
            total = total + self.line[k - 1]
        home = self.line.at[3 + u]
        self.line[pl.ds(3 + u, 1)] = total[None]
        for step in range(1, self.n):
            peer = (s, c, lax.rem(u + step, self.n))
            self.go(remote(home, home, self.m_send.at[step - 1], self.m_recv.at[step - 1], peer))

    def finish(self, out):
        s, c, u = self.s, self.c, self.u
        for step in range(1, self.n):
            source = lax.rem(u + self.n - step, self.n)
            place = self.line.at[3 + source]
            remote(
                place, place, self.m_send.at[step - 1], self.m_recv.at[step - 1], (s, c, source)
            ).wait_recv()
        total = self.line[3]
        for j in range(1, self.n):
            total = total + self.line[3 + j]
        out[...] = total[:4]
        for copy in self.sent:
            copy.wait_send()


def proj_back(n, dproj, wq, dresid, xg, gain_cols, gain_attn, gain_mlp):
    rows, width = dresid.shape
    span, cols = dproj.shape[1:]
    ring, sems = piece_scratch(3, 3, width // 8, cols)
    return pl.pallas_call(
        functools.partial(proj_back_kernel, n),
        out_shape=(shape((rows, width), BF16), shape((4, width // 8), F32))
        + (shape((3, width // 8, cols), BF16),) * 3,
        in_specs=[VM, HB, VM, HB, VM, VM, VM],
        out_specs=(VM, VM, HB, HB, HB),
        scratch_shapes=[
            pltpu.VMEM((3, width, cols), BF16),
            pltpu.VMEM((span, width // 2), BF16),
            pltpu.VMEM((span, width // 2), BF16),
            pltpu.VMEM((3, span, cols), BF16),
            pltpu.VMEM((rows, width), F32),
        ]
        + reduce_scratch(n, rows, width)
        + ring
        + [
            (
                pltpu.VMEM((2, 8, width // 2), F32),
                pltpu.VMEM((8, width // 2), F32),
                pltpu.VMEM((4, 8, width // 8), F32),
                pltpu.VMEM((3 + n, 8, width // 8), F32),
            ),
            pltpu.SemaphoreType.DMA((2,)),
            pltpu.SemaphoreType.DMA((2,)),
            pltpu.SemaphoreType.DMA((2,)),
        ]
        + sems
        + [
            pltpu.SemaphoreType.DMA((4,)),
            pltpu.SemaphoreType.DMA((4,)),
            pltpu.SemaphoreType.DMA((n - 1,)),
            pltpu.SemaphoreType.DMA((n - 1,)),
        ]
        + line_sems(n, CHUNKS),
        compiler_params=pltpu.CompilerParams(
            collective_id=7, has_side_effects=True, vmem_limit_bytes=VMEM_LIMIT
        ),
        name="proj_back",
    )(dproj, wq, dresid, xg, gain_cols, gain_attn, gain_mlp)


def rope_table(length):
    freqs = np.power(
        np.float32(ROPE_BASE), -(np.arange(HALF, dtype=np.float32) * 2.0 / HEAD_DIM)
    ).astype(np.float32)
    angles = (np.arange(length, dtype=np.float32)[:, None] * freqs[None, :]).astype(np.float64)
    return np.concatenate([np.cos(angles), np.sin(angles)], axis=1).astype(np.float32)


def on_device(
    n,
    table,
    tokens,
    segment_ids,
    qkv_weight,
    out_weight,
    gate_up,
    down_weight,
    qk_gain,
    post_gain,
    cotangent,
):
    x = tokens[0]
    width = x.shape[1]
    cot = cotangent[0]
    table = jnp.asarray(table)
    group_x, wq, wo, wga, proj, q, kv, inv, zero = project(
        n, x, qkv_weight, table, qk_gain, segment_ids, out_weight, gate_up
    )
    kvall, attn, attn32, lse, bound = attend(q, kv, zero)
    branch, resid, group_resid, gate, up, hidden, wgb, wgc, wd = mlp_in(
        n, attn, wo, x, post_gain, wga, gate_up, down_weight
    )
    block_out, group_dmlp, dgu, gain_mlp = mlp_out(n, hidden, wd, resid, post_gain, cot, gate, up)
    d_resid, group_dbranch, d_attn, gain_attn, *grads = mlp_back(
        n, dgu, wga, wgb, wgc, cot, branch, post_gain, wo, hidden, group_dmlp, group_resid
    )
    d_proj, gain_cols, *out_grads = attend_back(
        n, q, kvall, d_attn, attn32, lse, bound, attn, group_dbranch, proj, inv, qk_gain, table
    )
    input_grad, gain_part, *qkv_grads = proj_back(
        n, d_proj, wq, d_resid, group_x, gain_cols, gain_attn, gain_mlp
    )

    def total(parts):
        return parts[0].astype(F32) + parts[1].astype(F32) + parts[2].astype(F32)

    return (
        block_out[None],
        input_grad[None],
        total(qkv_grads),
        total(out_grads),
        total(grads[:3]),
        total(grads[3:]),
        gain_part,
    )


def solution(mesh):
    n = mesh.shape["uly"]
    in_specs = (
        P("slot", ("ctx", "uly"), None),
        P("slot", ("ctx", "uly")),
        P(None, ("slot", "ctx"), "uly"),
        P("uly", ("slot", "ctx")),
        P(None, ("slot", "ctx"), "uly"),
        P("uly", ("slot", "ctx")),
        P(None, "uly"),
        P(),
        P("slot", ("ctx", "uly"), None),
    )
    out_specs = (
        P("slot", ("ctx", "uly"), None),
        P("slot", ("ctx", "uly"), None),
        P(None, ("slot", "ctx"), "uly"),
        P("uly", ("slot", "ctx")),
        P(None, ("slot", "ctx"), "uly"),
        P("uly", ("slot", "ctx")),
        P(None, ("slot", "ctx")),
    )

    def whole(tokens, *rest):
        table = rope_table(tokens.shape[1])
        return jax.shard_map(
            functools.partial(on_device, n, table),
            mesh=mesh,
            in_specs=in_specs,
            out_specs=out_specs,
            check_vma=False,
        )(tokens, *rest)

    return whole
```

```python
import functools

import jax
import jax.numpy as jnp
import numpy as np
from jax import lax
from jax.experimental import pallas as pl
from jax.experimental.pallas import tpu as pltpu
from jax.sharding import PartitionSpec as P

HEAD_DIM = 128
HALF = HEAD_DIM // 2
EPS = 1e-06
ROPE_BASE = 500000.0
FLOOR = -1e30
LOG2E = 1.4426950408889634
SCALE2 = HEAD_DIM ** (-0.5) * LOG2E
MESH_ID = pl.DeviceIdType.MESH
BF16 = jnp.bfloat16
F32 = jnp.float32
VMEM_LIMIT = 62 * 1024 * 1024
CHUNKS = 4
LATER = 2

VM = pl.BlockSpec(memory_space=pltpu.VMEM)
HB = pl.BlockSpec(memory_space=pl.ANY)


def shape(dims, dtype):
    return jax.ShapeDtypeStruct(dims, dtype)


def where_am_i():
    return lax.axis_index("slot"), lax.axis_index("ctx"), lax.axis_index("uly")


def rows_of(index, rows):
    return pl.ds(pl.multiple_of(index * rows, rows), rows)


def greet(peers):
    barrier = pltpu.get_barrier_semaphore()
    total = 0
    for condition, peer in peers:
        if condition is None:
            pl.semaphore_signal(barrier, inc=1, device_id=peer, device_id_type=MESH_ID)
            total = total + 1
        else:

            @pl.when(condition)
            def _():
                pl.semaphore_signal(barrier, inc=1, device_id=peer, device_id_type=MESH_ID)

            total = total + condition.astype(jnp.int32)
    pl.semaphore_wait(barrier, total)


def line_peers(n):
    s, c, u = where_am_i()
    return [(u > 0, (s, c, u - 1)), (u < n - 1, (s, c, u + 1))]


def plane_peers():
    s, c, u = where_am_i()
    return [(None, (s, c ^ 1, u)), (None, (s, c ^ 2, u))]


def remote(src, dst, send, recv, peer):
    return pltpu.make_async_remote_copy(
        src_ref=src,
        dst_ref=dst,
        send_sem=send,
        recv_sem=recv,
        device_id=peer,
        device_id_type=MESH_ID,
    )


def line_sems(n, chunks=None):
    dims = (n - 1,) if chunks is None else (n - 1, chunks)
    return [pltpu.SemaphoreType.DMA(dims)] * 4


class LineGather:
    def __init__(self, n, rows, buf, sems):
        self.n, self.rows, self.buf, self.sems = n, rows, buf, sems

    def copy(self, right, slot, shard):
        s, c, u = where_am_i()
        send_r, recv_r, send_l, recv_l = self.sems
        view = self.buf.at[rows_of(shard, self.rows)]
        if right:
            return remote(view, view, send_r.at[slot], recv_r.at[slot], (s, c, u + 1))
        return remote(view, view, send_l.at[slot], recv_l.at[slot], (s, c, u - 1))

    def send(self, slot):
        u, n = lax.axis_index("uly"), self.n

        @pl.when((u < n - 1) & (u - slot >= 0))
        def _():
            self.copy(True, slot, u - slot).start()

        @pl.when((u > 0) & (u + slot <= n - 1))
        def _():
            self.copy(False, slot, u + slot).start()

    def wait(self, slot):
        u, n = lax.axis_index("uly"), self.n

        @pl.when(u - 1 - slot >= 0)
        def _():
            self.copy(True, slot, u - 1 - slot).wait_recv()

        @pl.when(u + 1 + slot <= n - 1)
        def _():
            self.copy(False, slot, u + 1 + slot).wait_recv()

        if slot + 1 < n - 1:
            self.send(slot + 1)

    def finish(self):
        u, n = lax.axis_index("uly"), self.n
        for slot in range(n - 1):

            @pl.when((u < n - 1) & (u - slot >= 0))
            def _():
                self.copy(True, slot, u - slot).wait_send()

            @pl.when((u > 0) & (u + slot <= n - 1))
            def _():
                self.copy(False, slot, u + slot).wait_send()

    def run(self, hook=None):
        for slot in range(self.n - 1):
            self.wait(slot)
            if hook is not None:
                hook(slot)
        self.finish()


class LineReduce:
    def __init__(self, n, rows, part, got, sems):
        self.n, self.rows, self.sems = n, rows, sems
        self.part, self.got = part, got
        self.chunks = part.shape[0]

    def copy(self, right, slot, chunk, block):
        s, c, u = where_am_i()
        send_r, recv_r, send_l, recv_l = self.sems
        where = rows_of(block, self.rows)
        src = self.part.at[chunk, where]
        if right:
            return remote(
                src,
                self.got.at[chunk, rows_of(block + 1, self.rows)],
                send_r.at[slot, chunk],
                recv_r.at[slot, chunk],
                (s, c, u + 1),
            )
        return remote(
            src,
            self.got.at[chunk, where],
            send_l.at[slot, chunk],
            recv_l.at[slot, chunk],
            (s, c, u - 1),
        )

    def add(self, chunk, block, place):
        where = rows_of(block, self.rows)
        self.part[chunk, where, :] = (
            self.part[chunk, where, :].astype(F32)
            + self.got[chunk, rows_of(place, self.rows), :].astype(F32)
        ).astype(BF16)

    def step(self, slot, chunk):
        u, n = lax.axis_index("uly"), self.n
        block_r = n - 1 - slot + u
        block_l = slot - (n - 1) + u

        @pl.when(u <= slot)
        def _():
            if slot > 0:

                @pl.when(u > 0)
                def _():
                    self.copy(True, slot - 1, chunk, block_r).wait_recv()
                    self.add(chunk, block_r, block_r + 1)

            self.copy(True, slot, chunk, block_r).start()

        @pl.when(u >= n - 1 - slot)
        def _():
            if slot > 0:

                @pl.when(u < n - 1)
                def _():
                    self.copy(False, slot - 1, chunk, block_l).wait_recv()
                    self.add(chunk, block_l, block_l)

            self.copy(False, slot, chunk, block_l).start()

    def last(self, out):
        u, n = lax.axis_index("uly"), self.n
        where = rows_of(u, self.rows)
        width = self.part.shape[2]
        for chunk in range(self.chunks):
            cols = slice(chunk * width, (chunk + 1) * width)
            out[:, cols] = self.part[chunk, where, :].astype(F32)

            @pl.when(u > 0)
            def _():
                self.copy(True, n - 2, chunk, u).wait_recv()
                out[:, cols] += self.got[chunk, rows_of(u + 1, self.rows), :].astype(F32)

            @pl.when(u < n - 1)
            def _():
                self.copy(False, n - 2, chunk, u).wait_recv()
                out[:, cols] += self.got[chunk, where, :].astype(F32)

    def finish(self):
        u, n = lax.axis_index("uly"), self.n
        for slot in range(n - 1):
            for chunk in range(self.chunks):

                @pl.when(u <= slot)
                def _():
                    self.copy(True, slot, chunk, n - 1 - slot + u).wait_send()

                @pl.when(u >= n - 1 - slot)
                def _():
                    self.copy(False, slot, chunk, slot - (n - 1) + u).wait_send()

    def run(self, compute, out, hook=None):
        for slot in range(self.n - 1):
            for chunk in range(self.chunks):
                if slot == 0:
                    compute(chunk)
                self.step(slot, chunk)
            if hook is not None:
                hook(slot)
        self.last(out)
        self.finish()


class PlaneGather:
    SEMS = 9

    def __init__(self, src, block, half_rows, send, recv, local):
        self.s, self.c, self.u = where_am_i()
        self.src, self.block, self.half_rows = src, block, half_rows
        self.send_sem, self.recv_sem = send, recv
        s, c, u = self.s, self.c, self.u
        self.xn, self.yn, self.sib = (s, c ^ 1, u), (s, c ^ 2, u), (1 - s, c, u)
        self.started = []
        self.own = pltpu.make_async_copy(src, block(s * 4 + c), local)

    def half(self, b, part):
        rows = self.half_rows
        view = self.block(b)
        where = [slice(None)] * len(view.shape)
        where[-2] = pl.ds(part * rows, rows)
        return view.at[tuple(where)]

    def copy(self, k, view, peer, src=None):
        return remote(
            view if src is None else src, view, self.send_sem.at[k], self.recv_sem.at[k], peer
        )

    def go(self, *copies):
        for copy in copies:
            copy.start()
            self.started.append(copy)

    def start(self):
        own = self.block(self.s * 4 + self.c)
        self.go(
            self.copy(0, own, self.xn, self.src),
            self.copy(1, own, self.yn, self.src),
            self.copy(2, own, self.sib, self.src),
        )
        self.own.start()

    def middle(self):
        bx, by = self.s * 4 + (self.c ^ 1), self.s * 4 + (self.c ^ 2)
        self.copy(0, self.block(bx), self.xn).wait_recv()
        self.go(
            self.copy(3, self.half(bx, 0), self.yn), self.copy(4, self.block(bx), self.sib)
        )
        self.copy(1, self.block(by), self.yn).wait_recv()
        self.go(
            self.copy(5, self.half(by, 1), self.xn), self.copy(6, self.block(by), self.sib)
        )

    def corner(self):
        bd = self.s * 4 + (self.c ^ 3)
        self.copy(3, self.half(bd, 0), self.yn).wait_recv()
        self.go(self.copy(7, self.half(bd, 0), self.sib))
        self.copy(5, self.half(bd, 1), self.xn).wait_recv()
        self.go(self.copy(8, self.half(bd, 1), self.sib))

    def arrive(self):
        far, c = (1 - self.s) * 4, self.c
        self.copy(2, self.block(far + c), self.sib).wait_recv()
        self.copy(4, self.block(far + (c ^ 1)), self.sib).wait_recv()
        self.copy(6, self.block(far + (c ^ 2)), self.sib).wait_recv()
        self.copy(7, self.half(far + (c ^ 3), 0), self.sib).wait_recv()
        self.copy(8, self.half(far + (c ^ 3), 1), self.sib).wait_recv()
        self.own.wait()

    def finish(self):
        for copy in self.started:
            copy.wait_send()


class PlaneReduce:
    SEMS = 6

    def __init__(self, ring, got, outs, place, send, recv, local):
        self.s, self.c, self.u = where_am_i()
        s, c, u = self.s, self.c, self.u
        self.xn, self.yn = (s, c ^ 1, u), (s, c ^ 2, u)
        self.ring, self.got, self.outs, self.place = ring, got, outs, place
        self.send_sem, self.recv_sem, self.local = send, recv, local
        self.slots, self.rows = ring.shape[0], ring.shape[2]
        self.open = {}

    def halves(self):
        h = self.rows // 2
        return pl.ds(0, h), pl.ds(h, h)

    def copy(self, piece, k, src, dst, peer):
        return remote(src, dst, self.send_sem.at[piece, k], self.recv_sem.at[piece, k], peer)

    def slot(self, piece):
        if piece >= self.slots:
            self.close(piece - self.slots)
        return self.ring.at[piece % self.slots]

    def close(self, piece):
        if piece in self.open:
            remotes, own = self.open.pop(piece)
            for copy in remotes:
                copy.wait_send()
            own.wait()

    def first(self, piece):
        c = self.c
        lo, hi = self.halves()
        blocks = self.ring.at[piece % self.slots]
        own_out, out_x, out_y = self.outs
        bx, by, bd = c ^ 1, c ^ 2, c ^ 3
        copies = [
            self.copy(piece, 0, blocks.at[bd, lo], self.got.at[piece, lo], self.xn),
            self.copy(piece, 1, blocks.at[bd, hi], self.got.at[piece, hi], self.yn),
            self.copy(piece, 2, blocks.at[bx, lo], self.place(out_x, piece, 0), self.xn),
            self.copy(piece, 3, blocks.at[by, hi], self.place(out_y, piece, 1), self.yn),
        ]
        for copy in copies:
            copy.start()
        own = pltpu.make_async_copy(
            blocks.at[c], self.place(own_out, piece, None), self.local.at[piece]
        )
        own.start()
        self.open[piece] = (copies, own)

    def second(self, piece):
        c, h = self.c, self.rows // 2
        lo, hi = self.halves()
        slot = piece % self.slots
        blocks = self.ring.at[slot]
        own_out, out_x, out_y = self.outs
        bx, by, bd = c ^ 1, c ^ 2, c ^ 3
        self.copy(piece, 0, blocks.at[bd, lo], self.got.at[piece, lo], self.xn).wait_recv()
        self.ring[slot, by, :h, :] = (
            self.ring[slot, by, :h, :].astype(F32) + self.got[piece, :h, :].astype(F32)
        ).astype(BF16)
        first = self.copy(piece, 4, blocks.at[by, lo], self.place(out_y, piece, 0), self.yn)
        first.start()
        self.copy(piece, 1, blocks.at[bd, hi], self.got.at[piece, hi], self.yn).wait_recv()
        self.ring[slot, bx, h:, :] = (
            self.ring[slot, bx, h:, :].astype(F32) + self.got[piece, h:, :].astype(F32)
        ).astype(BF16)
        second = self.copy(piece, 5, blocks.at[bx, hi], self.place(out_x, piece, 1), self.xn)
        second.start()
        self.open[piece][0].extend([first, second])

    def finish(self, pieces):
        own_out, out_x, out_y = self.outs
        slot = self.ring.at[0]
        lo, hi = self.halves()
        for piece in range(pieces):
            self.close(piece)
            for k, out, half, peer in (
                (2, out_x, 0, self.xn),
                (3, out_y, 1, self.yn),
                (4, out_y, 0, self.yn),
                (5, out_x, 1, self.xn),
            ):
                where = self.place(out, piece, half)
                self.copy(piece, k, where, where, peer).wait_recv()


class Pieces:
    def __init__(self, work):
        self.work, self.done, self.behind = work, 0, []

    def step(self, count=1):
        for _ in range(count):
            if self.done < len(self.work):
                plane, piece, compute = self.work[self.done]
                compute(plane.slot(piece), piece)
                plane.first(piece)
                self.behind.append((plane, piece))
                self.done += 1
                if len(self.behind) > 2:
                    self.catch_up()

    def catch_up(self):
        plane, piece = self.behind.pop(0)
        plane.second(piece)

    def finish(self):
        self.step(len(self.work))
        while self.behind:
            self.catch_up()


def wide_piece(own, other, lanes):
    def compute(out, piece):
        take = lanes(piece)
        cols = out.shape[2]

        def pair(i, carry):
            where = pl.ds(pl.multiple_of(i * 2 * cols, 2 * cols), 2 * cols)
            total = dot(own[0][:, take], own[1][:, where], TN) + dot(
                other[0][:, take], other[1][:, where], TN
            )
            total = total.astype(BF16)
            out[pl.ds(2 * i, 1)] = total[:, :cols][None]
            out[pl.ds(2 * i + 1, 1)] = total[:, cols:][None]
            return carry

        lax.fori_loop(0, 2, pair, 0)

    return compute


def tall_piece(own, other, right):
    def compute(out, piece):
        rows, cols = out.shape[1:]

        def pair(i, carry):
            where = pl.ds(pl.multiple_of(i * 2 * rows, 2 * rows), 2 * rows)
            total = dot(own[0][:, where], right(own[1], piece), TN) + dot(
                other[0][:, where], right(other[1], piece), TN
            )
            out[pl.ds(2 * i, 2)] = total.astype(BF16).reshape(2, rows, cols)
            return carry

        lax.fori_loop(0, 2, pair, 0)

    return compute


class LatePiece:
    def __init__(self, number, ins, outs, scratch, sems):
        s, c, u = where_am_i()
        resid_hbm, resid_s_hbm, dgu_hbm, dgu_s_hbm = ins
        resid, resid_s, right, right_s, ring, got = scratch
        send, recv, local, load_sem = sems
        cols = right.shape[1]
        ci, tile = divmod(number, dgu_hbm.shape[2] // cols)
        lanes = pl.ds(tile * cols, cols)
        pairs = (
            (half_columns(resid_hbm, s), resid),
            (resid_s_hbm, resid_s),
            (dgu_hbm.at[ci, :, lanes], right),
            (dgu_s_hbm.at[ci, :, lanes], right_s),
        )
        self.loads = [
            pltpu.make_async_copy(src, dst, load_sem.at[k]) for k, (src, dst) in enumerate(pairs)
        ]
        size = ring.shape[2]

        def place(out, piece, part):
            rows = size if part is None else size // 2
            return out.at[ci, pl.ds((part or 0) * rows, rows), lanes]

        self.plane = PlaneReduce(ring, got, outs, place, send, recv, local)
        self.compute = tall_piece(
            (resid, right), (resid_s, right_s), lambda ref, piece: ref[...]
        )

    def load(self):
        for copy in self.loads:
            copy.start()

    def work(self):
        def compute(out, piece):
            for copy in self.loads:
                copy.wait()
            self.compute(out, piece)

        return (self.plane, 0, compute)

    @staticmethod
    def scratch(span, width, ff):
        cols = min(ff, 512)
        ring, sems = piece_scratch(1, 1, width // 8, cols)
        buffers = (
            pltpu.VMEM((span, width // 2), BF16),
            pltpu.VMEM((span, width // 2), BF16),
            pltpu.VMEM((span, cols), BF16),
            pltpu.VMEM((span, cols), BF16),
            ring[0],
            ring[1],
        )
        return [buffers, tuple(sems) + (pltpu.SemaphoreType.DMA((4,)),)]


def half_columns(ref, s):
    half = ref.shape[1] // 2
    return ref.at[:, pl.ds(pl.multiple_of(s * half, half), half)]


class Sibling:
    def __init__(self, send, recv):
        s, c, u = where_am_i()
        self.peer, self.send, self.recv = (1 - s, c, u), send, recv
        self.copies = []

    def start(self, src, dst):
        k = len(self.copies)
        copy = remote(src, dst, self.send.at[k], self.recv.at[k], self.peer)
        copy.start()
        self.copies.append(copy)

    def wait(self, k):
        self.copies[k].wait_recv()

    def finish(self):
        for copy in self.copies:
            copy.wait_send()


def dot(a, b, dims):
    return lax.dot_general(a, b, ((dims[:1], dims[1:]), ((), ())), preferred_element_type=F32)


NN, NT, TN = (1, 0), (1, 1), (0, 0)


def tiles(total, size):
    size = min(total, size)
    return total // size, size


def inverse_rms(values):
    return lax.rsqrt(jnp.mean(values * values, axis=-1, keepdims=True) + EPS)


def norm_back(values, inverse, grad_scaled, width):
    return inverse * grad_scaled - values * inverse**3 * (
        jnp.sum(values * grad_scaled, axis=-1, keepdims=True) / width
    )


def rope_factors(table):
    lane = lax.broadcasted_iota(jnp.int32, table.shape, 1)
    turned = pltpu.roll(table, HALF, 1)
    cosine = jnp.where(lane < HALF, table, turned)
    sine = jnp.where(lane < HALF, -turned, table)
    return cosine, sine


def exchange_rows(n, mine, msg, send, recv):
    s, c, u = where_am_i()
    msg[pl.ds(u, 1)] = mine[None]
    copies = []
    for step in range(1, n):
        peer = lax.rem(u + step, n)
        copy = remote(msg.at[u], msg.at[u], send.at[step - 1], recv.at[step - 1], (s, c, peer))
        copy.start()
        copies.append(copy)
    for step in range(1, n):
        source = lax.rem(u + n - step, n)
        remote(
            msg.at[source], msg.at[source], send.at[step - 1], recv.at[step - 1], (s, c, source)
        ).wait_recv()
    total = msg[0]
    for j in range(1, n):
        total = total + msg[j]
    for copy in copies:
        copy.wait_send()
    return total


def to_rows(col0, col1):
    span = col0.shape[0]
    lane = lax.broadcasted_iota(jnp.int32, (span, 128), 1)
    both = jnp.where(lane == 0, col0, jnp.where(lane == 1, col1, 0.0))
    return jnp.transpose(both)[:8]


def to_columns(rows8):
    return jnp.transpose(jnp.concatenate([rows8] * 16, axis=0))


def all_uly_peers(n):
    s, c, u = where_am_i()
    return [(None, (s, c, lax.rem(u + k, n))) for k in range(1, n)]


def proj_kernel(
    n,
    x_ref,
    w_ref,
    tab_ref,
    gain_ref,
    seg_ref,
    wo_ref,
    gu_ref,
    xg_out,
    wq_out,
    wo_out,
    wga_out,
    proj_ref,
    q_ref,
    kv_ref,
    inv_ref,
    zero_ref,
    xg,
    wq,
    tab,
    msg,
    local_sem,
    w_send,
    w_recv,
    m_send,
    m_recv,
    *line,
):
    s, c, u = where_am_i()
    rows, width = x_ref.shape
    span = n * rows
    kb = w_ref.shape[1]
    sib = (1 - s, c, u)
    tab_copy = pltpu.make_async_copy(tab_ref.at[rows_of(c, span)], tab, local_sem.at[0])
    tab_copy.start()
    xg[rows_of(u, rows), :] = x_ref[...]
    greet(all_uly_peers(n) + plane_peers() + [(None, sib)])

    def plane(k, src, block, half_rows):
        return PlaneGather(
            src, block, half_rows, w_send.at[k], w_recv.at[k], local_sem.at[3 + k]
        )

    half = kb // 2
    gather = LineGather(n, rows, xg, line)
    first = plane(0, w_ref, lambda b: wq.at[:, rows_of(b, kb)], half)
    second = plane(1, wo_ref, lambda b: wo_out.at[b], wo_ref.shape[0] // 2)
    third = plane(2, gu_ref.at[0, pl.ds(0, half)], lambda b: wga_out.at[b], half // 2)
    gather.send(0)
    first.start()
    gather.wait(0)
    first.middle()
    second.start()
    if n > 2:
        gather.wait(1)
    first.corner()
    second.middle()
    third.start()
    for slot in range(2 if n > 2 else 1, n - 1):
        gather.wait(slot)
    first.arrive()
    tab_copy.wait()
    keep = [
        pltpu.make_async_copy(xg, xg_out, local_sem.at[1]),
        pltpu.make_async_copy(wq, wq_out, local_sem.at[2]),
    ]
    for copy in keep:
        copy.start()

    count, size = tiles(span, 512)

    def project(i, carry):
        where = pl.ds(pl.multiple_of(i * size, size), size)
        xs = xg[where, :]
        proj_ref[0, where, :] = dot(xs, wq[0], NN)
        proj_ref[1, where, :] = dot(xs, wq[1], NN)
        kv_ref[1, where, :] = dot(xs, wq[2], NN).astype(BF16)
        return carry

    lax.fori_loop(0, count, project, 0)
    squares = [jnp.sum(proj_ref[i] * proj_ref[i], axis=-1, keepdims=True) for i in range(2)]
    mine = to_rows(*squares)
    zeros = jnp.sum((1 - seg_ref[...]).astype(F32))
    row = lax.broadcasted_iota(jnp.int32, mine.shape, 0)
    mine = jnp.where(row == 2, zeros, mine)
    second.corner()
    third.middle()
    total = exchange_rows(n, mine, msg, m_send, m_recv)
    zero_ref[...] = jnp.broadcast_to(total[2:3, :128], (8, 128))
    inv = lax.rsqrt(to_columns(total) / width + EPS)
    inv_ref[...] = inv
    cosine, sine = rope_factors(tab[...])
    heads = proj_ref.shape[2] // HEAD_DIM
    for i in range(2):
        inverse = inv_ref[:, i : i + 1]
        for h in range(heads):
            cols = slice(h * HEAD_DIM, (h + 1) * HEAD_DIM)
            v = proj_ref[i, :, cols] * inverse * gain_ref[i : i + 1, cols]
            v = (v * cosine + pltpu.roll(v, HALF, 1) * sine).astype(BF16)
            if i == 0:
                q_ref[:, cols] = v
            else:
                kv_ref[0, :, cols] = v
    second.arrive()
    third.corner()
    third.arrive()
    for work in (first, second, third, gather):
        work.finish()
    for copy in keep:
        copy.wait()


def project(n, x, w, table, gain, seg, wo, gu):
    rows, width = x.shape
    span, cols = n * rows, w.shape[2]
    return pl.pallas_call(
        functools.partial(proj_kernel, n),
        out_shape=(
            shape((span, width), BF16),
            shape((3, width, cols), BF16),
            shape((8,) + wo.shape, BF16),
            shape((8, gu.shape[1] // 2, gu.shape[2]), BF16),
            shape((2, span, cols), F32),
            shape((span, cols), BF16),
            shape((2, span, cols), BF16),
            shape((span, 128), F32),
            shape((8, 128), F32),
        ),
        in_specs=[VM, HB, HB, VM, VM, HB, HB],
        out_specs=(HB, HB, HB, HB, VM, VM, VM, VM, VM),
        scratch_shapes=[
            pltpu.VMEM((span, width), BF16),
            pltpu.VMEM((3, width, cols), BF16),
            pltpu.VMEM((span, 128), F32),
            pltpu.VMEM((n, 8, span), F32),
            pltpu.SemaphoreType.DMA((6,)),
            pltpu.SemaphoreType.DMA((3, 9)),
            pltpu.SemaphoreType.DMA((3, 9)),
            pltpu.SemaphoreType.DMA((n - 1,)),
            pltpu.SemaphoreType.DMA((n - 1,)),
        ]
        + line_sems(n),
        compiler_params=pltpu.CompilerParams(
            collective_id=1, has_side_effects=True, vmem_limit_bytes=VMEM_LIMIT
        ),
        name="project",
    )(x, w, table, gain, seg, wo, gu)


def score_mask(scores, key_first, query_first, starts, diagonal):
    key_pos = key_first + lax.broadcasted_iota(jnp.int32, scores.shape, 0)
    keep = key_pos >= starts
    if diagonal:
        query_pos = query_first + lax.broadcasted_iota(jnp.int32, scores.shape, 1)
        keep = keep & (key_pos <= query_pos)
    return jnp.where(keep, scores, FLOOR)


def segment_starts(first, size, bound):
    pos = first + lax.broadcasted_iota(jnp.int32, (1, size), 1)
    return jnp.where(pos >= bound, bound, 0)


def attend_kernel(
    q_ref,
    kv_ref,
    zero_ref,
    kvall_out,
    attn_ref,
    attn32_ref,
    lse_ref,
    bound_ref,
    kvall,
    peaks,
    sums,
    acct,
    zmsg,
    send,
    recv,
    z_send,
    z_recv,
    keep_sem,
):
    s, c, u = where_am_i()
    span, cols = q_ref.shape
    heads = cols // HEAD_DIM
    xn, yn, dn = (s, c ^ 1, u), (s, c ^ 2, u), (s, c ^ 3, u)
    kvall[pl.ds(c, 1)] = kv_ref[...][None]
    zmsg[pl.ds(c, 1)] = zero_ref[...][None]
    greet(plane_peers() + [(None, dn)])

    def sent(k, view, peer):
        return remote(view, view, send.at[k], recv.at[k], peer)

    bx, by, bd = c ^ 1, c ^ 2, c ^ 3
    zs = [
        remote(zmsg.at[c], zmsg.at[c], z_send.at[k], z_recv.at[k], peer)
        for k, peer in enumerate((xn, yn, dn))
    ]
    for copy in zs:
        copy.start()
    copies = [sent(0, kvall.at[c], xn), sent(1, kvall.at[c], yn)]
    for copy in copies:
        copy.start()
    for k, (b, peer) in enumerate(((bx, xn), (by, yn), (bd, dn))):
        remote(zmsg.at[b], zmsg.at[b], z_send.at[k], z_recv.at[k], peer).wait_recv()
    ahead = jnp.zeros((8, 128), F32)
    for j in range(4):
        ahead = ahead + jnp.where(j <= c, zmsg[j], 0.0)
    bounds = ahead.astype(jnp.int32)
    bound_ref[...] = bounds
    bound = bounds[:1, :1]

    peaks[...] = jnp.full_like(peaks, FLOOR)
    sums[...] = jnp.zeros_like(sums)
    acct[...] = jnp.zeros_like(acct)
    nq, tq = tiles(span, 512)
    nk, tk = tiles(span, 512)

    def update(number, diagonal):
        def over_queries(i, carry):
            first_q = c * span + i * tq
            starts = segment_starts(first_q, tq, bound)
            where_q = pl.ds(pl.multiple_of(i * tq, tq), tq)

            def over_keys(j, carry):
                first_k = number * span + j * tk
                where_k = pl.ds(pl.multiple_of(j * tk, tk), tk)
                for h in range(heads):
                    lanes = slice(h * HEAD_DIM, (h + 1) * HEAD_DIM)
                    scores = dot(kvall[number, 0, where_k, lanes], q_ref[where_q, lanes], NT)
                    scores = score_mask(scores * SCALE2, first_k, first_q, starts, diagonal)
                    old = peaks[h, :1, where_q]
                    new = jnp.maximum(old, jnp.max(scores, axis=0, keepdims=True))
                    factor = jnp.exp2(old - new)
                    weights = jnp.exp2(scores - new)
                    peaks[h, :1, where_q] = new
                    sums[h, :1, where_q] = sums[h, :1, where_q] * factor + jnp.sum(
                        weights, axis=0, keepdims=True
                    )
                    acct[h, :, where_q] = acct[h, :, where_q] * factor + dot(
                        kvall[number, 1, where_k, lanes], weights.astype(BF16), TN
                    )
                return carry

            return lax.fori_loop(0, nk, over_keys, carry)

        lax.fori_loop(0, nq, over_queries, 0)

    update(c, True)
    half = span // 2
    sent(0, kvall.at[bx], xn).wait_recv()
    more = [sent(2, kvall.at[bx, :, pl.ds(0, half)], yn)]
    more[0].start()
    copies += more
    sent(1, kvall.at[by], yn).wait_recv()
    more = [sent(3, kvall.at[by, :, pl.ds(half, half)], xn)]
    more[0].start()
    copies += more
    for b in (bx, by):

        @pl.when(b < c)
        def _():
            update(b, False)

    sent(2, kvall.at[bd, :, pl.ds(0, half)], yn).wait_recv()
    sent(3, kvall.at[bd, :, pl.ds(half, half)], xn).wait_recv()
    keep = pltpu.make_async_copy(kvall, kvall_out, keep_sem)
    keep.start()

    @pl.when(bd < c)
    def _():
        update(bd, False)

    for h in range(heads):
        lanes = slice(h * HEAD_DIM, (h + 1) * HEAD_DIM)
        total = sums[h, :1, :]
        attention = jnp.transpose(acct[h] / total)
        attn32_ref[:, lanes] = attention
        attn_ref[:, lanes] = attention.astype(BF16)
        lse_ref[h, :1, :] = peaks[h, :1, :] + jnp.log2(total)
    for copy in copies + zs:
        copy.wait_send()
    keep.wait()


def attend(q, kv, zero):
    span, cols = q.shape
    heads = cols // HEAD_DIM
    return pl.pallas_call(
        attend_kernel,
        out_shape=(
            shape((4, 2, span, cols), BF16),
            shape((span, cols), BF16),
            shape((span, cols), F32),
            shape((heads, 8, span), F32),
            shape((8, 128), jnp.int32),
        ),
        in_specs=[VM] * 3,
        out_specs=(HB, VM, VM, VM, VM),
        scratch_shapes=[
            pltpu.VMEM((4, 2, span, cols), BF16),
            pltpu.VMEM((heads, 8, span), F32),
            pltpu.VMEM((heads, 8, span), F32),
            pltpu.VMEM((heads, HEAD_DIM, span), F32),
            pltpu.VMEM((4, 8, 128), F32),
            pltpu.SemaphoreType.DMA((4,)),
            pltpu.SemaphoreType.DMA((4,)),
            pltpu.SemaphoreType.DMA((3,)),
            pltpu.SemaphoreType.DMA((3,)),
            pltpu.SemaphoreType.DMA,
        ],
        compiler_params=pltpu.CompilerParams(
            collective_id=2, has_side_effects=True, vmem_limit_bytes=VMEM_LIMIT
        ),
        name="attend",
    )(q, kv, zero)


def attend_back_kernel(
    n,
    q_ref,
    kvall_ref,
    do_ref,
    attn32_ref,
    lse_ref,
    bound_ref,
    proj_ref,
    inv_ref,
    gain_ref,
    tab_ref,
    resid_hbm,
    resid_s_hbm,
    dgu_hbm,
    dgu_s_hbm,
    own_in,
    x_in,
    y_in,
    dproj_ref,
    dgain_ref,
    own_out,
    x_out,
    y_out,
    dq_ref,
    part,
    got,
    acc,
    delta,
    tab,
    msg,
    late_buffers,
    late_sems,
    send,
    recv,
    local_sem,
    m_send,
    m_recv,
):
    s, c, u = where_am_i()
    span, cols = q_ref.shape
    width = resid_hbm.shape[1]
    heads = cols // HEAD_DIM
    xn, yn = (s, c ^ 1, u), (s, c ^ 2, u)
    bx, by, bd = c ^ 1, c ^ 2, c ^ 3
    load = pltpu.make_async_copy(tab_ref.at[rows_of(c, span)], tab, local_sem)
    load.start()
    last = 2 * (dgu_hbm.shape[2] // late_buffers[2].shape[1])
    late = LatePiece(
        last - 2,
        (resid_hbm, resid_s_hbm, dgu_hbm, dgu_s_hbm),
        (own_out, x_out, y_out),
        late_buffers,
        late_sems,
    )
    late.load()
    pieces = Pieces([late.work()])
    greet(plane_peers() + all_uly_peers(n))
    bound = bound_ref[:1, :1]
    nq, tq = tiles(span, 512)
    nk, tk = tiles(span, 512)
    scale = HEAD_DIM ** (-0.5)
    dq_ref[...] = jnp.zeros_like(dq_ref)
    for h in range(heads):
        lanes = slice(h * HEAD_DIM, (h + 1) * HEAD_DIM)
        both = jnp.transpose(do_ref[:, lanes].astype(F32) * attn32_ref[:, lanes])
        delta[h, :1, :] = jnp.sum(both, axis=0, keepdims=True)

    def update(number, diagonal):
        acc[...] = jnp.zeros_like(acc)

        def over_queries(i, carry):
            first_q = c * span + i * tq
            starts = segment_starts(first_q, tq, bound)
            where_q = pl.ds(pl.multiple_of(i * tq, tq), tq)

            def over_keys(j, carry):
                first_k = number * span + j * tk
                where_k = pl.ds(pl.multiple_of(j * tk, tk), tk)
                for h in range(heads):
                    lanes = slice(h * HEAD_DIM, (h + 1) * HEAD_DIM)
                    keys = kvall_ref[number, 0, where_k, lanes]
                    values = kvall_ref[number, 1, where_k, lanes]
                    query, d_out = q_ref[where_q, lanes], do_ref[where_q, lanes]
                    scores = dot(keys, query, NT) * SCALE2
                    scores = score_mask(scores, first_k, first_q, starts, diagonal)
                    probs = jnp.exp2(scores - lse_ref[h, :1, where_q])
                    acc[1, where_k, lanes] += dot(probs.astype(BF16), d_out, NN)
                    d_probs = dot(values, d_out, NT)
                    d_scores = (probs * (d_probs - delta[h, :1, where_q])).astype(BF16)
                    acc[0, where_k, lanes] += dot(d_scores, query, NN) * scale
                    dq_ref[where_q, lanes] += dot(d_scores, keys, TN) * scale
                return carry

            return lax.fori_loop(0, nk, over_keys, carry)

        lax.fori_loop(0, nq, over_queries, 0)

    def work(number):
        @pl.when(number < c)
        def _():
            update(number, False)
            part[pl.ds(number, 1)] = acc[...].astype(BF16)[None]

        @pl.when(number > c)
        def _():
            part[pl.ds(number, 1)] = jnp.zeros_like(part[pl.ds(number, 1)])

    half = span // 2
    lo, hi = pl.ds(0, half), pl.ds(half, half)

    def sent(k, src, dst, peer):
        return remote(src, dst, send.at[k], recv.at[k], peer)

    pieces.step()
    work(bd)
    copies = [
        sent(0, part.at[bd, :, lo], got.at[0, :, lo], xn),
        sent(1, part.at[bd, :, hi], got.at[0, :, hi], yn),
    ]
    for copy in copies:
        copy.start()
    pieces.catch_up()
    work(bx)
    sent(1, part.at[bx, :, hi], got.at[0, :, hi], yn).wait_recv()
    part[bx, :, half:, :] = (
        part[bx, :, half:, :].astype(F32) + got[0, :, half:, :].astype(F32)
    ).astype(BF16)
    more = [sent(2, part.at[bx], got.at[1], xn)]
    more[0].start()
    copies += more
    work(by)
    sent(0, part.at[by, :, lo], got.at[0, :, lo], xn).wait_recv()
    part[by, :, :half, :] = (
        part[by, :, :half, :].astype(F32) + got[0, :, :half, :].astype(F32)
    ).astype(BF16)
    more = [sent(3, part.at[by], got.at[2], yn)]
    more[0].start()
    copies += more
    update(c, True)
    load.wait()

    cosine, sine = rope_factors(tab[...])

    def turn_back(i):
        inverse = inv_ref[:, i : i + 1]
        row_dot = jnp.zeros((span, 1), F32)
        for h in range(heads):
            lanes = slice(h * HEAD_DIM, (h + 1) * HEAD_DIM)
            source = dq_ref if i == 0 else acc.at[0]
            v = source[:, lanes]
            v = v * cosine - pltpu.roll(v, HALF, 1) * sine
            values = proj_ref[i, :, lanes]
            dgain_ref[i : i + 1, lanes] = jnp.sum(v * values * inverse, axis=0, keepdims=True)
            v = v * gain_ref[i : i + 1, lanes]
            source[:, lanes] = v
            row_dot = row_dot + jnp.sum(values * v, axis=-1, keepdims=True)
        return row_dot

    dots_q = turn_back(0)
    sent(2, part.at[bx], got.at[1], xn).wait_recv()
    sent(3, part.at[by], got.at[2], yn).wait_recv()
    acc[...] += got[1].astype(F32) + got[2].astype(F32)
    dproj_ref[2] = acc[1].astype(BF16)
    dots_k = turn_back(1)
    total = exchange_rows(n, to_rows(dots_q, dots_k), msg, m_send, m_recv)
    means = to_columns(total) / width
    for i in range(2):
        inverse = inv_ref[:, i : i + 1]
        factor = inverse**3 * means[:, i : i + 1]
        source = dq_ref if i == 0 else acc.at[0]
        dproj_ref[i] = (inverse * source[...] - proj_ref[i] * factor).astype(BF16)
    pieces.finish()
    late.plane.finish(1)
    for copy in copies:
        copy.wait_send()


def attend_back(
    n, q, kvall, d_out, attn32, lse, bound, proj, inv, gain, table, late, grads
):
    span, cols = q.shape
    heads = cols // HEAD_DIM
    width, ff = late[0].shape[1], late[2].shape[2]
    return pl.pallas_call(
        functools.partial(attend_back_kernel, n),
        out_shape=(shape((3, span, cols), BF16), shape((2, cols), F32))
        + tuple(shape(g.shape, BF16) for g in grads),
        in_specs=[VM] * 9 + [HB] * 8,
        out_specs=(VM, VM, HB, HB, HB),
        input_output_aliases={14: 2, 15: 3, 16: 4},
        scratch_shapes=[
            pltpu.VMEM((span, cols), F32),
            pltpu.VMEM((4, 2, span, cols), BF16),
            pltpu.VMEM((3, 2, span, cols), BF16),
            pltpu.VMEM((2, span, cols), F32),
            pltpu.VMEM((heads, 8, span), F32),
            pltpu.VMEM((span, 128), F32),
            pltpu.VMEM((n, 8, span), F32),
        ]
        + LatePiece.scratch(span, width, ff)
        + [
            pltpu.SemaphoreType.DMA((4,)),
            pltpu.SemaphoreType.DMA((4,)),
            pltpu.SemaphoreType.DMA,
            pltpu.SemaphoreType.DMA((n - 1,)),
            pltpu.SemaphoreType.DMA((n - 1,)),
        ],
        compiler_params=pltpu.CompilerParams(
            collective_id=3, has_side_effects=True, vmem_limit_bytes=VMEM_LIMIT
        ),
        name="attend_back",
    )(q, kvall, d_out, attn32, lse, bound, proj, inv, gain, table, *late, *grads)


def load_blocks(src, dst, sem, axis):
    blocks = src.shape[0]
    size = dst.shape[axis] // blocks
    copies = []
    for b in range(blocks):
        where = [slice(None)] * len(dst.shape)
        where[axis] = pl.ds(b * size, size)
        copies.append(pltpu.make_async_copy(src.at[b], dst.at[tuple(where)], sem.at[b]))
    for copy in copies:
        copy.start()
    return copies


def wait_all(copies):
    for copy in copies:
        copy.wait()


def mlp_in_kernel(
    n,
    attn_ref,
    wo_ref,
    x_ref,
    gain_ref,
    wga_ref,
    gu_ref,
    down_ref,
    branch_ref,
    resid_ref,
    group_out,
    gate_ref,
    up_ref,
    hidden_ref,
    wgb_out,
    wgc_out,
    wd_out,
    wo,
    wg,
    group,
    part,
    got_rows,
    sem_o,
    local_sem,
    w_send,
    w_recv,
    *sems,
):
    s, c, u = where_am_i()
    rows, width = x_ref.shape
    load_o = load_blocks(wo_ref, wo, sem_o, 1)
    half = wga_ref.shape[1]
    load_g = [
        pltpu.make_async_copy(wga_ref, wg.at[0, :, pl.ds(0, half)], local_sem.at[0]),
        pltpu.make_async_copy(wgb_out, wg.at[0, :, pl.ds(half, half)], local_sem.at[1]),
        pltpu.make_async_copy(wgc_out, wg.at[1], local_sem.at[2]),
    ]
    load_g[0].start()
    greet(line_peers(n) + plane_peers() + [(None, (1 - s, c, u))])

    def plane(k, src, out, half_rows):
        return PlaneGather(
            src, lambda b: out.at[b], half_rows, w_send.at[k], w_recv.at[k], local_sem.at[4 + k]
        )

    first = plane(0, gu_ref.at[0, pl.ds(half, half)], wgb_out, half // 2)
    second = plane(1, gu_ref.at[1], wgc_out, half)
    third = plane(2, down_ref, wd_out, down_ref.shape[0] // 2)
    first.start()
    wait_all(load_o)
    chunk_cols = width // part.shape[0]
    span = n * rows
    count, size = tiles(span, 512)

    def compute(chunk):
        def tile(i, carry):
            where = pl.ds(pl.multiple_of(i * size, size), size)
            part[chunk, where, :] = dot(
                attn_ref[where, :], wo[:, chunk * chunk_cols : (chunk + 1) * chunk_cols], NN
            ).astype(BF16)
            return carry

        lax.fori_loop(0, count, tile, 0)

    def reduce_hook(slot):
        if slot == 0:
            first.middle()
            second.start()
        if slot == 1:
            first.corner()
        if slot == 2:
            first.arrive()
            load_g[1].start()

    LineReduce(n, rows, part, got_rows, sems[:4]).run(compute, branch_ref, reduce_hook)
    branch = branch_ref[...]
    resid = x_ref[...].astype(F32) + branch * inverse_rms(branch) * gain_ref[0:1, :]
    resid_ref[...] = resid
    group[rows_of(u, rows), :] = resid.astype(BF16)
    gather = LineGather(n, rows, group, sems[4:])
    gather.send(0)
    second.middle()
    third.start()

    def gather_hook(slot):
        if slot == 1:
            second.corner()

    gather.run(gather_hook)
    second.arrive()
    load_g[2].start()
    keep = pltpu.make_async_copy(group, group_out, local_sem.at[3])
    keep.start()
    third.middle()
    wait_all(load_g)
    ff = gate_ref.shape[1]
    ntile, tsize = tiles(ff, 512)

    def body(i, carry):
        lanes = pl.ds(pl.multiple_of(i * tsize, tsize), tsize)

        def tile(j, carry):
            where = pl.ds(pl.multiple_of(j * size, size), size)
            gate = dot(group[where, :], wg[0, :, :, lanes].reshape(width, tsize), NN)
            up = dot(group[where, :], wg[1, :, :, lanes].reshape(width, tsize), NN)
            gate_ref[where, lanes] = gate.astype(BF16)
            up_ref[where, lanes] = up.astype(BF16)
            hidden_ref[where, lanes] = (gate * jax.nn.sigmoid(gate) * up).astype(BF16)
            return carry

        return lax.fori_loop(0, count, tile, carry)

    lax.fori_loop(0, ntile, body, 0)
    third.corner()
    third.arrive()
    for work in (first, second, third):
        work.finish()
    keep.wait()


def reduce_scratch(n, rows, width):
    cols = width // CHUNKS
    return [
        pltpu.VMEM((CHUNKS, n * rows, cols), BF16),
        pltpu.VMEM((CHUNKS, (n + 1) * rows, cols), BF16),
    ]


def mlp_in(n, attn, wo, x, gain, wga, gu, down):
    rows, width = x.shape
    span, cols = attn.shape
    kb, ff = gu.shape[1:]
    return pl.pallas_call(
        functools.partial(mlp_in_kernel, n),
        out_shape=(
            shape((rows, width), F32),
            shape((rows, width), F32),
            shape((span, width), BF16),
            shape((span, ff), BF16),
            shape((span, ff), BF16),
            shape((span, ff), BF16),
            shape((8, kb // 2, ff), BF16),
            shape((8, kb, ff), BF16),
            shape((8,) + down.shape, BF16),
        ),
        in_specs=[VM, HB, VM, VM, HB, HB, HB],
        out_specs=(VM, VM, HB, VM, VM, VM, HB, HB, HB),
        scratch_shapes=[
            pltpu.VMEM((cols, width), BF16),
            pltpu.VMEM((2, 8, kb, ff), BF16),
            pltpu.VMEM((span, width), BF16),
        ]
        + reduce_scratch(n, rows, width)
        + [
            pltpu.SemaphoreType.DMA((8,)),
            pltpu.SemaphoreType.DMA((7,)),
            pltpu.SemaphoreType.DMA((3, 9)),
            pltpu.SemaphoreType.DMA((3, 9)),
        ]
        + line_sems(n, CHUNKS)
        + line_sems(n),
        compiler_params=pltpu.CompilerParams(
            collective_id=4, has_side_effects=True, vmem_limit_bytes=VMEM_LIMIT
        ),
        name="mlp_in",
    )(attn, wo, x, gain, wga, gu, down)


def mlp_out_kernel(
    n,
    hidden_ref,
    wd_ref,
    resid_ref,
    gain_ref,
    cot_ref,
    gate_ref,
    up_ref,
    gresid_ref,
    out_ref,
    group_out,
    dgu_ref,
    dgain_ref,
    hidden_s,
    resid_s,
    dmlp_s,
    dgu_s,
    wd,
    mlp,
    group,
    part,
    got_rows,
    sem_d,
    keep_sem,
    s_send,
    s_recv,
    *sems,
):
    s, c, u = where_am_i()
    rows, width = resid_ref.shape
    load_d = load_blocks(wd_ref, wd, sem_d, 1)
    greet(line_peers(n) + [(None, (1 - s, c, u))])
    sibling = Sibling(s_send, s_recv)
    wait_all(load_d)
    chunk_cols = width // part.shape[0]
    span = n * rows
    count, size = tiles(span, 512)

    def compute(chunk):
        def tile(i, carry):
            where = pl.ds(pl.multiple_of(i * size, size), size)
            part[chunk, where, :] = dot(
                hidden_ref[where, :], wd[:, chunk * chunk_cols : (chunk + 1) * chunk_cols], NN
            ).astype(BF16)
            return carry

        lax.fori_loop(0, count, tile, 0)

    def hook(slot):
        if slot == 0:
            sibling.start(hidden_ref, hidden_s)
            sibling.start(half_columns(gresid_ref, 1 - s), resid_s)

    LineReduce(n, rows, part, got_rows, sems[:4]).run(compute, mlp, hook)
    values = mlp[...]
    inverse = inverse_rms(values)
    grad = cot_ref[...].astype(F32)
    d_mlp = norm_back(values, inverse, grad * gain_ref[1:2, :], width)
    group[rows_of(u, rows), :] = d_mlp.astype(BF16)
    gather = LineGather(n, rows, group, sems[4:])
    gather.send(0)
    scaled = values * inverse
    out_ref[...] = (resid_ref[...] + scaled * gain_ref[1:2, :]).astype(BF16)
    dgain_ref[...] = jnp.sum(grad * scaled, axis=0, keepdims=True)
    for slot in range(n - 1):
        gather.wait(slot)
    gather.finish()
    keep = pltpu.make_async_copy(group, group_out, keep_sem)
    keep.start()
    sibling.start(half_columns(group, 1 - s), dmlp_s)
    ntile, tsize = tiles(gate_ref.shape[1], 512)

    def body(i, carry):
        lanes = pl.ds(pl.multiple_of(i * tsize, tsize), tsize)

        def tile(j, carry):
            where = pl.ds(pl.multiple_of(j * size, size), size)
            d_hidden = dot(group[where, :], wd[lanes, :], NT)
            gate = gate_ref[where, lanes].astype(F32)
            up = up_ref[where, lanes].astype(F32)
            sig = jax.nn.sigmoid(gate)
            slope = sig * (1.0 + gate * (1.0 - sig))
            dgu_ref[0, where, lanes] = (d_hidden * up * slope).astype(BF16)
            dgu_ref[1, where, lanes] = (d_hidden * (gate * sig)).astype(BF16)
            return carry

        return lax.fori_loop(0, count, tile, carry)

    for i in range(ntile):
        body(i, 0)
        lanes = pl.ds(i * tsize, tsize)
        sibling.start(dgu_ref.at[:, :, lanes], dgu_s.at[:, :, lanes])
    for i in range(3 + ntile):
        sibling.wait(i)
    sibling.finish()
    keep.wait()


def mlp_out(n, hidden, wd, resid, gain, cot, gate, up, gresid):
    rows, width = resid.shape
    span, ff = hidden.shape
    return pl.pallas_call(
        functools.partial(mlp_out_kernel, n),
        out_shape=(
            shape((rows, width), BF16),
            shape((span, width), BF16),
            shape((2, span, ff), BF16),
            shape((1, width), F32),
            shape((span, ff), BF16),
            shape((span, width // 2), BF16),
            shape((span, width // 2), BF16),
            shape((2, span, ff), BF16),
        ),
        in_specs=[VM, HB, VM, VM, VM, VM, VM, HB],
        out_specs=(VM, HB, VM, VM, HB, HB, HB, HB),
        scratch_shapes=[
            pltpu.VMEM((ff, width), BF16),
            pltpu.VMEM((rows, width), F32),
            pltpu.VMEM((span, width), BF16),
        ]
        + reduce_scratch(n, rows, width)
        + [
            pltpu.SemaphoreType.DMA((8,)),
            pltpu.SemaphoreType.DMA,
            pltpu.SemaphoreType.DMA((3 + tiles(ff, 512)[0],)),
            pltpu.SemaphoreType.DMA((3 + tiles(ff, 512)[0],)),
        ]
        + line_sems(n, CHUNKS)
        + line_sems(n),
        compiler_params=pltpu.CompilerParams(
            collective_id=5, has_side_effects=True, vmem_limit_bytes=VMEM_LIMIT
        ),
        name="mlp_out",
    )(hidden, wd, resid, gain, cot, gate, up, gresid)


def mlp_back_kernel(
    n,
    dgu_hbm,
    wga_ref,
    wgb_ref,
    wgc_ref,
    cot_ref,
    branch_ref,
    gain_ref,
    wo_ref,
    hidden_hbm,
    dmlp_hbm,
    resid_hbm,
    hidden_s_hbm,
    dmlp_s_hbm,
    resid_s_hbm,
    dgu_s_hbm,
    dresid_ref,
    group_out,
    dattn_ref,
    dgain_ref,
    gown_out,
    gx_out,
    gy_out,
    down_own_out,
    down_x_out,
    down_y_out,
    wo,
    wg,
    group,
    part,
    got_rows,
    dgu_ref,
    hidden,
    hidden_s,
    dmlp,
    dmlp_s,
    gate_in,
    ring_d,
    ring_g,
    got_d,
    got_g,
    sem_o,
    sem_in,
    local_sem,
    d_send,
    d_recv,
    d_local,
    g_send,
    g_recv,
    g_local,
    *sems,
):
    s, c, u = where_am_i()
    rows, width = cot_ref.shape
    half = wga_ref.shape[1]
    chunk_cols = width // part.shape[0]
    per_chunk = chunk_cols // (2 * half)
    chunks = part.shape[0]

    def load_chunk(chunk):
        slot = chunk % 2
        where = pl.ds(chunk * per_chunk, per_chunk)
        return [
            pltpu.make_async_copy(
                wga_ref.at[where], wg.at[slot, 0, :, pl.ds(0, half)], local_sem.at[slot, 0]
            ),
            pltpu.make_async_copy(
                wgb_ref.at[where], wg.at[slot, 0, :, pl.ds(half, half)], local_sem.at[slot, 1]
            ),
            pltpu.make_async_copy(wgc_ref.at[where], wg.at[slot, 1], local_sem.at[slot, 2]),
        ]

    def start_chunk(chunk):
        for copy in load_chunk(chunk):
            copy.start()

    def fetch(k, src, dst):
        copy = pltpu.make_async_copy(src, dst, sem_in.at[k])
        copy.start()
        return copy

    load_dgu = fetch(0, dgu_hbm, dgu_ref)
    start_chunk(0)
    load_d = [
        fetch(1, hidden_hbm, hidden),
        fetch(2, half_columns(dmlp_hbm, s), dmlp),
        fetch(3, hidden_s_hbm, hidden_s),
        fetch(4, dmlp_s_hbm, dmlp_s),
    ]
    start_chunk(1)
    load_g = []
    if gate_in:
        resid, resid_s, dgu_s = gate_in
        load_g = [
            fetch(5, half_columns(resid_hbm, s), resid),
            fetch(6, resid_s_hbm, resid_s),
            fetch(7, dgu_s_hbm, dgu_s),
        ]
    load_o = load_blocks(wo_ref, wo, sem_o, 1)
    greet(line_peers(n) + plane_peers())
    load_dgu.wait()
    span = n * rows
    count, size = tiles(span, 512)

    def compute(chunk):
        wait_all(load_chunk(chunk))
        slot = chunk % 2

        def tile(i, carry):
            where = pl.ds(pl.multiple_of(i * size, size), size)
            part[chunk, where, :] = (
                dot(dgu_ref[0, where, :], wg[slot, 0].reshape(chunk_cols, -1), NT)
                + dot(dgu_ref[1, where, :], wg[slot, 1].reshape(chunk_cols, -1), NT)
            ).astype(BF16)
            return carry

        lax.fori_loop(0, count, tile, 0)
        if chunk + 2 < chunks:
            start_chunk(chunk + 2)

    rows_d, cols_g = ring_d.shape[2], ring_g.shape[3]
    tiles_g = dgu_hbm.shape[2] // cols_g

    def place_d(out, piece, part):
        size = rows_d if part is None else rows_d // 2
        return out.at[pl.ds(piece * rows_d + (part or 0) * size, size)]

    def place_g(out, piece, part):
        size = ring_g.shape[2] if part is None else ring_g.shape[2] // 2
        ci, tile = piece // tiles_g, piece % tiles_g
        return out.at[ci, pl.ds((part or 0) * size, size), pl.ds(tile * cols_g, cols_g)]

    down = PlaneReduce(
        ring_d, got_d, (down_own_out, down_x_out, down_y_out), place_d, d_send, d_recv, d_local
    )
    gate = PlaneReduce(ring_g, got_g, (gown_out, gx_out, gy_out), place_g, g_send, g_recv, g_local)
    down_piece = wide_piece(
        (hidden, dmlp), (hidden_s, dmlp_s), lambda p: slice(p * rows_d, (p + 1) * rows_d)
    )

    def gate_right(ref, piece):
        tile = piece % tiles_g
        return ref[piece // tiles_g, :, tile * cols_g : (tile + 1) * cols_g]

    n_d, n_g = got_d.shape[0], got_g.shape[0] if gate_in else 0
    work = [(down, p, down_piece) for p in range(n_d)]
    if gate_in:
        gate_piece = tall_piece((resid, dgu_ref), (resid_s, dgu_s), gate_right)
        work += [(gate, p, gate_piece) for p in range(n_g)]
    pieces = Pieces(work)

    def compute_and_piece(chunk):
        compute(chunk)
        if chunk == 0:
            wait_all(load_d)
        if chunk < 2:
            pieces.step()

    def reduce_hook(slot):
        if slot == 0:
            wait_all(load_g)
        pieces.step()

    LineReduce(n, rows, part, got_rows, sems[:4]).run(compute_and_piece, dresid_ref, reduce_hook)
    d_resid = dresid_ref[...] + cot_ref[...].astype(F32)
    dresid_ref[...] = d_resid
    branch = branch_ref[...]
    inverse = inverse_rms(branch)
    d_branch = norm_back(branch, inverse, d_resid * gain_ref[0:1, :], width)
    small = group.shape[0] == span
    if small:
        group[rows_of(u, rows), :] = d_branch.astype(BF16)
        gather = LineGather(n, rows, group, sems[4:])
    else:
        group[:rows, :] = d_branch.astype(BF16)
        own = pltpu.make_async_copy(
            group.at[pl.ds(0, rows)], group_out.at[rows_of(u, rows)], local_sem.at[2, 2]
        )
        own.start()
        own.wait()
        gather = LineGather(n, rows, group_out, sems[4:])
    gather.send(0)
    dgain_ref[...] = jnp.sum(d_resid * branch * inverse, axis=0, keepdims=True)
    wait_all(load_o)
    pieces.step()

    def gather_hook(slot):
        pieces.step()

    gather.run(gather_hook)
    if small:
        keep = pltpu.make_async_copy(group, group_out, local_sem.at[2, 2])
        keep.start()

    def tile(j, carry):
        where = pl.ds(pl.multiple_of(j * size, size), size)
        if small:
            rows_in = group[where, :]
        else:
            fetch = pltpu.make_async_copy(group_out.at[where], group, local_sem.at[2, 2])
            fetch.start()
            fetch.wait()
            rows_in = group[...]
        dattn_ref[where, :] = dot(rows_in, wo[...], NT).astype(BF16)
        return carry

    lax.fori_loop(0, count, tile, 0)
    pieces.finish()
    down.finish(n_d)
    gate.finish(n_g)
    if small:
        keep.wait()


def piece_scratch(slots, pieces, rows, cols):
    return (
        [pltpu.VMEM((slots, 4, rows, cols), BF16), pltpu.VMEM((pieces, rows, cols), BF16)],
        [
            pltpu.SemaphoreType.DMA((pieces, 6)),
            pltpu.SemaphoreType.DMA((pieces, 6)),
            pltpu.SemaphoreType.DMA((pieces,)),
        ],
    )


def mlp_back(
    n,
    dgu,
    wga,
    wgb,
    wgc,
    cot,
    branch,
    gain,
    wo,
    hidden,
    dmlp,
    resid,
    hidden_s,
    resid_s,
    dmlp_s,
    dgu_s,
):
    rows, width = branch.shape
    span, ff = dgu.shape[1:]
    cols = wo.shape[1]
    kb, kc = width // 8, wo.shape[2]
    count, size = tiles(ff, 512)
    ring_d, sems_d = piece_scratch(min(3, count), count, size, kc)
    here = 2 * count - LATER
    ring_g, sems_g = piece_scratch(min(3, max(here, 1)), max(here, 1), kb, size)
    chunk_blocks = width // CHUNKS // kb
    return pl.pallas_call(
        functools.partial(mlp_back_kernel, n),
        out_shape=(
            shape((rows, width), F32),
            shape((span, width), BF16),
            shape((span, cols), BF16),
            shape((1, width), F32),
        )
        + (shape((2, kb, ff), BF16),) * 3
        + (shape((ff, kc), BF16),) * 3,
        in_specs=[HB, HB, HB, HB, VM, VM, VM] + [HB] * 8,
        out_specs=(VM, HB, VM, VM) + (HB,) * 6,
        scratch_shapes=[
            pltpu.VMEM((cols, width), BF16),
            pltpu.VMEM((2, 2, chunk_blocks, kb, ff), BF16),
            pltpu.VMEM((min(span, 512), width), BF16),
        ]
        + reduce_scratch(n, rows, width)
        + [
            pltpu.VMEM((2, span, ff), BF16),
            pltpu.VMEM((span, ff), BF16),
            pltpu.VMEM((span, ff), BF16),
            pltpu.VMEM((span, width // 2), BF16),
            pltpu.VMEM((span, width // 2), BF16),
            (
                pltpu.VMEM((span, width // 2), BF16),
                pltpu.VMEM((span, width // 2), BF16),
                pltpu.VMEM((2, span, ff), BF16),
            )
            if here > 0
            else (),
            ring_d[0],
            ring_g[0],
            ring_d[1],
            ring_g[1],
            pltpu.SemaphoreType.DMA((8,)),
            pltpu.SemaphoreType.DMA((8,)),
            pltpu.SemaphoreType.DMA((3, 3)),
        ]
        + sems_d
        + sems_g
        + line_sems(n, CHUNKS)
        + line_sems(n),
        compiler_params=pltpu.CompilerParams(
            collective_id=6, has_side_effects=True, vmem_limit_bytes=VMEM_LIMIT
        ),
        name="mlp_back",
    )(
        dgu,
        wga,
        wgb,
        wgc,
        cot,
        branch,
        gain,
        wo,
        hidden,
        dmlp,
        resid,
        hidden_s,
        dmlp_s,
        resid_s,
        dgu_s,
    )


def proj_back_kernel(
    n,
    dproj_ref,
    wq_ref,
    dresid_ref,
    xg_ref,
    gcols_ref,
    gattn_ref,
    gmlp_ref,
    attn_ref,
    dbranch_ref,
    resid_hbm,
    resid_s_hbm,
    dgu_hbm,
    dgu_s_hbm,
    own_in,
    x_in,
    y_in,
    out_ref,
    gain_ref,
    own_out,
    x_out,
    y_out,
    oown_out,
    ox_out,
    oy_out,
    gown_out,
    gx_out,
    gy_out,
    wq,
    xs,
    xs_s,
    dproj_s,
    dbranch,
    dbranch_s,
    attn_s,
    total,
    part,
    got_rows,
    ring,
    got,
    sums,
    ring_o,
    got_o,
    late_buffers,
    late_sems,
    o_sems,
    local_sem,
    s_send,
    s_recv,
    q_send,
    q_recv,
    q_local,
    v_send,
    v_recv,
    m_send,
    m_recv,
    *sems,
):
    s, c, u = where_am_i()
    rows, width = dresid_ref.shape
    span = n * rows
    load = [
        pltpu.make_async_copy(wq_ref, wq, local_sem.at[0]),
        pltpu.make_async_copy(half_columns(xg_ref, s), xs, local_sem.at[1]),
        pltpu.make_async_copy(half_columns(dbranch_ref, s), dbranch, local_sem.at[2]),
    ]
    last = 2 * (dgu_hbm.shape[2] // late_buffers[2].shape[1])
    late = LatePiece(
        last - 1,
        (resid_hbm, resid_s_hbm, dgu_hbm, dgu_s_hbm),
        (gown_out, gx_out, gy_out),
        late_buffers,
        late_sems,
    )
    late.load()
    for copy in load:
        copy.start()
    corner = (s, c ^ 3, u)
    greet(all_uly_peers(n) + plane_peers() + [(None, corner), (None, (1 - s, c, u))])
    gains = GainSum(n, sums, (v_send, v_recv, m_send, m_recv))
    gains.start(gcols_ref, gattn_ref, gmlp_ref)
    sibling = Sibling(s_send, s_recv)
    sibling.start(attn_ref, attn_s)
    sibling.start(half_columns(dbranch_ref, 1 - s), dbranch_s)
    sibling.start(half_columns(xg_ref, 1 - s), xs_s)
    sibling.start(dproj_ref, dproj_s)
    load[0].wait()
    chunk_cols = width // part.shape[0]
    count, size = tiles(span, 512)

    def compute(chunk):
        cols = slice(chunk * chunk_cols, (chunk + 1) * chunk_cols)

        def tile(i, carry):
            where = pl.ds(pl.multiple_of(i * size, size), size)
            part[chunk, where, :] = (
                dot(dproj_ref[0, where, :], wq[0, cols, :], NT)
                + dot(dproj_ref[1, where, :], wq[1, cols, :], NT)
                + dot(dproj_ref[2, where, :], wq[2, cols, :], NT)
            ).astype(BF16)
            return carry

        lax.fori_loop(0, count, tile, 0)

    def place(out, piece, part):
        size = ring.shape[2] if part is None else ring.shape[2] // 2
        return out.at[piece, pl.ds((part or 0) * size, size)]

    weight = PlaneReduce(ring, got, (own_out, x_out, y_out), place, q_send, q_recv, q_local)
    compute_piece = tall_piece((xs, dproj_ref), (xs_s, dproj_s), lambda ref, piece: ref[piece])

    def place_o(out, piece, part):
        size = ring_o.shape[2] if part is None else ring_o.shape[2] // 2
        return out.at[pl.ds((part or 0) * size, size)]

    out_weight = PlaneReduce(ring_o, got_o, (oown_out, ox_out, oy_out), place_o, *o_sems)
    out_piece = wide_piece((attn_ref, dbranch), (attn_s, dbranch_s), lambda p: slice(None))
    pieces = Pieces(
        [late.work(), (out_weight, 0, out_piece)] + [(weight, p, compute_piece) for p in range(3)]
    )

    def compute_and_piece(chunk):
        compute(chunk)
        if chunk == 0:
            pieces.step()
        if chunk == 2:
            load[2].wait()
            sibling.wait(0)
            sibling.wait(1)
            pieces.step()

    def hook(slot):
        if slot == 0:
            load[1].wait()
            sibling.wait(2)
            sibling.wait(3)
            pieces.step()
            gains.over_ctx()
        if slot == 1:
            pieces.step()
            gains.over_uly()
        if slot == 2:
            pieces.step()

    LineReduce(n, rows, part, got_rows, sems[:4]).run(compute_and_piece, total, hook)
    out_ref[...] = (dresid_ref[...] + total[...]).astype(BF16)
    pieces.finish()
    gains.finish(gain_ref)
    weight.finish(3)
    out_weight.finish(1)
    late.plane.finish(1)
    sibling.finish()


class GainSum:
    def __init__(self, n, refs, sems):
        self.n = n
        self.all, self.core, self.plane, self.line = refs
        self.v_send, self.v_recv, self.m_send, self.m_recv = sems
        self.s, self.c, self.u = where_am_i()
        self.sent = []

    def copy(self, k, src, dst, peer):
        return remote(src, dst, self.v_send.at[k], self.v_recv.at[k], peer)

    def go(self, copy):
        copy.start()
        self.sent.append(copy)

    def start(self, cols, attn, mlp):
        half, local = self.all.shape[2], cols.shape[1]
        rows = jnp.zeros((8, half), F32)
        for h in range(2):
            self.all[h] = rows
        mine = self.u * local
        home = pl.ds(pl.multiple_of(lax.rem(mine, half), local), local)
        self.all[pl.ds(mine // half, 1), 0:2, home] = cols[...][None]
        for h in range(2):
            part = slice(h * half, (h + 1) * half)
            self.all[h, 2:3, :] = attn[:, part]
            self.all[h, 3:4, :] = mlp[:, part]
        self.go(self.copy(0, self.all.at[1 - self.s], self.core, (1 - self.s, self.c, self.u)))

    def over_ctx(self):
        s, c, u = self.s, self.c, self.u
        self.copy(0, self.all.at[s], self.core, (1 - s, c, u)).wait_recv()
        size = self.plane.shape[2]
        total = self.all[pl.ds(s, 1)][0] + self.core[...]
        for j in range(4):
            self.plane[j] = total[:, j * size : (j + 1) * size]
        for k in (1, 2, 3):
            self.go(self.copy(k, self.plane.at[c ^ k], self.line.at[k - 1], (s, c ^ k, u)))

    def over_uly(self):
        s, c, u = self.s, self.c, self.u
        total = self.plane[pl.ds(c, 1)][0]
        for k in (1, 2, 3):
            self.copy(k, self.plane.at[c ^ k], self.line.at[k - 1], (s, c ^ k, u)).wait_recv()
            total = total + self.line[k - 1]
        home = self.line.at[3 + u]
        self.line[pl.ds(3 + u, 1)] = total[None]
        for step in range(1, self.n):
            peer = (s, c, lax.rem(u + step, self.n))
            self.go(remote(home, home, self.m_send.at[step - 1], self.m_recv.at[step - 1], peer))

    def finish(self, out):
        s, c, u = self.s, self.c, self.u
        for step in range(1, self.n):
            source = lax.rem(u + self.n - step, self.n)
            place = self.line.at[3 + source]
            remote(
                place, place, self.m_send.at[step - 1], self.m_recv.at[step - 1], (s, c, source)
            ).wait_recv()
        total = self.line[3]
        for j in range(1, self.n):
            total = total + self.line[3 + j]
        out[...] = total[:4]
        for copy in self.sent:
            copy.wait_send()


def proj_back(
    n, dproj, wq, dresid, xg, gain_cols, gain_attn, gain_mlp, attn, dbranch, late, grads
):
    rows, width = dresid.shape
    span, cols = dproj.shape[1:]
    ring, sems = piece_scratch(3, 3, width // 8, cols)
    ring_o, sems_o = piece_scratch(1, 1, cols, width // 8)
    ff = late[2].shape[2]
    return pl.pallas_call(
        functools.partial(proj_back_kernel, n),
        out_shape=(shape((rows, width), BF16), shape((4, width // 8), F32))
        + (shape((3, width // 8, cols), BF16),) * 3
        + (shape((cols, width // 8), BF16),) * 3
        + tuple(shape(g.shape, BF16) for g in grads),
        in_specs=[VM, HB, VM, HB, VM, VM, VM, VM] + [HB] * 8,
        out_specs=(VM, VM) + (HB,) * 9,
        input_output_aliases={13: 8, 14: 9, 15: 10},
        scratch_shapes=[
            pltpu.VMEM((3, width, cols), BF16),
            pltpu.VMEM((span, width // 2), BF16),
            pltpu.VMEM((span, width // 2), BF16),
            pltpu.VMEM((3, span, cols), BF16),
            pltpu.VMEM((span, width // 2), BF16),
            pltpu.VMEM((span, width // 2), BF16),
            pltpu.VMEM((span, cols), BF16),
            pltpu.VMEM((rows, width), F32),
        ]
        + reduce_scratch(n, rows, width)
        + ring
        + [
            (
                pltpu.VMEM((2, 8, width // 2), F32),
                pltpu.VMEM((8, width // 2), F32),
                pltpu.VMEM((4, 8, width // 8), F32),
                pltpu.VMEM((3 + n, 8, width // 8), F32),
            ),
        ]
        + ring_o
        + LatePiece.scratch(span, width, ff)
        + [
            tuple(sems_o),
            pltpu.SemaphoreType.DMA((3,)),
            pltpu.SemaphoreType.DMA((4,)),
            pltpu.SemaphoreType.DMA((4,)),
        ]
        + sems
        + [
            pltpu.SemaphoreType.DMA((4,)),
            pltpu.SemaphoreType.DMA((4,)),
            pltpu.SemaphoreType.DMA((n - 1,)),
            pltpu.SemaphoreType.DMA((n - 1,)),
        ]
        + line_sems(n, CHUNKS),
        compiler_params=pltpu.CompilerParams(
            collective_id=7, has_side_effects=True, vmem_limit_bytes=VMEM_LIMIT
        ),
        name="proj_back",
    )(
        dproj,
        wq,
        dresid,
        xg,
        gain_cols,
        gain_attn,
        gain_mlp,
        attn,
        dbranch,
        *late,
        *grads,
    )


def rope_table(length):
    freqs = np.power(
        np.float32(ROPE_BASE), -(np.arange(HALF, dtype=np.float32) * 2.0 / HEAD_DIM)
    ).astype(np.float32)
    angles = (np.arange(length, dtype=np.float32)[:, None] * freqs[None, :]).astype(np.float64)
    return np.concatenate([np.cos(angles), np.sin(angles)], axis=1).astype(np.float32)


def on_device(
    n,
    table,
    tokens,
    segment_ids,
    qkv_weight,
    out_weight,
    gate_up,
    down_weight,
    qk_gain,
    post_gain,
    cotangent,
):
    x = tokens[0]
    width = x.shape[1]
    cot = cotangent[0]
    table = jnp.asarray(table)
    group_x, wq, wo, wga, proj, q, kv, inv, zero = project(
        n, x, qkv_weight, table, qk_gain, segment_ids, out_weight, gate_up
    )
    kvall, attn, attn32, lse, bound = attend(q, kv, zero)
    branch, resid, group_resid, gate, up, hidden, wgb, wgc, wd = mlp_in(
        n, attn, wo, x, post_gain, wga, gate_up, down_weight
    )
    block_out, group_dmlp, dgu, gain_mlp, hidden_s, resid_s, dmlp_s, dgu_s = mlp_out(
        n, hidden, wd, resid, post_gain, cot, gate, up, group_resid
    )
    d_resid, group_dbranch, d_attn, gain_attn, *grads = mlp_back(
        n,
        dgu,
        wga,
        wgb,
        wgc,
        cot,
        branch,
        post_gain,
        wo,
        hidden,
        group_dmlp,
        group_resid,
        hidden_s,
        resid_s,
        dmlp_s,
        dgu_s,
    )
    gate_grads, down_grads = grads[:3], grads[3:]
    late = (group_resid, resid_s, dgu, dgu_s)
    d_proj, gain_cols, *gate_grads = attend_back(
        n, q, kvall, d_attn, attn32, lse, bound, proj, inv, qk_gain, table, late, gate_grads
    )
    input_grad, gain_part, *grads = proj_back(
        n,
        d_proj,
        wq,
        d_resid,
        group_x,
        gain_cols,
        gain_attn,
        gain_mlp,
        attn,
        group_dbranch,
        late,
        gate_grads,
    )
    qkv_grads, out_grads, gate_grads = grads[:3], grads[3:6], grads[6:]

    def total(parts):
        return parts[0].astype(F32) + parts[1].astype(F32) + parts[2].astype(F32)

    return (
        block_out[None],
        input_grad[None],
        total(qkv_grads),
        total(out_grads),
        total(gate_grads),
        total(down_grads),
        gain_part,
    )


def solution(mesh):
    n = mesh.shape["uly"]
    in_specs = (
        P("slot", ("ctx", "uly"), None),
        P("slot", ("ctx", "uly")),
        P(None, ("slot", "ctx"), "uly"),
        P("uly", ("slot", "ctx")),
        P(None, ("slot", "ctx"), "uly"),
        P("uly", ("slot", "ctx")),
        P(None, "uly"),
        P(),
        P("slot", ("ctx", "uly"), None),
    )
    out_specs = (
        P("slot", ("ctx", "uly"), None),
        P("slot", ("ctx", "uly"), None),
        P(None, ("slot", "ctx"), "uly"),
        P("uly", ("slot", "ctx")),
        P(None, ("slot", "ctx"), "uly"),
        P("uly", ("slot", "ctx")),
        P(None, ("slot", "ctx")),
    )

    def whole(tokens, *rest):
        table = rope_table(tokens.shape[1])
        return jax.shard_map(
            functools.partial(on_device, n, table),
            mesh=mesh,
            in_specs=in_specs,
            out_specs=out_specs,
            check_vma=False,
        )(tokens, *rest)

    return whole
```

```python
import functools

import jax
import jax.numpy as jnp
import numpy as np
from jax import lax
from jax.experimental import pallas as pl
from jax.experimental.pallas import tpu as pltpu
from jax.sharding import PartitionSpec as P

HEAD_DIM = 128
HALF = HEAD_DIM // 2
EPS = 1e-06
ROPE_BASE = 500000.0
FLOOR = -1e30
LOG2E = 1.4426950408889634
SCALE2 = HEAD_DIM ** (-0.5) * LOG2E
MESH_ID = pl.DeviceIdType.MESH
BF16 = jnp.bfloat16
F32 = jnp.float32
VMEM_LIMIT = 62 * 1024 * 1024
CHUNKS = 4
LATER = 2

VM = pl.BlockSpec(memory_space=pltpu.VMEM)
HB = pl.BlockSpec(memory_space=pl.ANY)


def shape(dims, dtype):
    return jax.ShapeDtypeStruct(dims, dtype)


def where_am_i():
    return lax.axis_index("slot"), lax.axis_index("ctx"), lax.axis_index("uly")


def rows_of(index, rows):
    return pl.ds(pl.multiple_of(index * rows, rows), rows)


def greet(peers):
    barrier = pltpu.get_barrier_semaphore()
    total = 0
    for condition, peer in peers:
        if condition is None:
            pl.semaphore_signal(barrier, inc=1, device_id=peer, device_id_type=MESH_ID)
            total = total + 1
        else:

            @pl.when(condition)
            def _():
                pl.semaphore_signal(barrier, inc=1, device_id=peer, device_id_type=MESH_ID)

            total = total + condition.astype(jnp.int32)
    pl.semaphore_wait(barrier, total)


def line_peers(n):
    s, c, u = where_am_i()
    return [(u > 0, (s, c, u - 1)), (u < n - 1, (s, c, u + 1))]


def plane_peers():
    s, c, u = where_am_i()
    return [(None, (s, c ^ 1, u)), (None, (s, c ^ 2, u))]


def remote(src, dst, send, recv, peer):
    return pltpu.make_async_remote_copy(
        src_ref=src,
        dst_ref=dst,
        send_sem=send,
        recv_sem=recv,
        device_id=peer,
        device_id_type=MESH_ID,
    )


def line_sems(n, chunks=None):
    dims = (n - 1,) if chunks is None else (n - 1, chunks)
    return [pltpu.SemaphoreType.DMA(dims)] * 4


class LineGather:
    def __init__(self, n, rows, buf, sems, part=None):
        self.n, self.rows, self.buf, self.sems, self.part = n, rows, buf, sems, part

    def copy(self, right, slot, shard):
        s, c, u = where_am_i()
        send_r, recv_r, send_l, recv_l = self.sems
        if self.part is None:
            view = self.buf.at[rows_of(shard, self.rows)]
        else:
            index, size = self.part
            view = self.buf.at[shard, pl.ds(index * size, size)]
            send_r, recv_r, send_l, recv_l = [sem.at[:, index] for sem in self.sems]
        if right:
            return remote(view, view, send_r.at[slot], recv_r.at[slot], (s, c, u + 1))
        return remote(view, view, send_l.at[slot], recv_l.at[slot], (s, c, u - 1))

    def send(self, slot):
        u, n = lax.axis_index("uly"), self.n

        @pl.when((u < n - 1) & (u - slot >= 0))
        def _():
            self.copy(True, slot, u - slot).start()

        @pl.when((u > 0) & (u + slot <= n - 1))
        def _():
            self.copy(False, slot, u + slot).start()

    def wait(self, slot):
        u, n = lax.axis_index("uly"), self.n

        @pl.when(u - 1 - slot >= 0)
        def _():
            self.copy(True, slot, u - 1 - slot).wait_recv()

        @pl.when(u + 1 + slot <= n - 1)
        def _():
            self.copy(False, slot, u + 1 + slot).wait_recv()

        if slot + 1 < n - 1:
            self.send(slot + 1)

    def finish(self):
        u, n = lax.axis_index("uly"), self.n
        for slot in range(n - 1):

            @pl.when((u < n - 1) & (u - slot >= 0))
            def _():
                self.copy(True, slot, u - slot).wait_send()

            @pl.when((u > 0) & (u + slot <= n - 1))
            def _():
                self.copy(False, slot, u + slot).wait_send()

    def run(self, hook=None):
        for slot in range(self.n - 1):
            self.wait(slot)
            if hook is not None:
                hook(slot)
        self.finish()


class LineReduce:
    def __init__(self, n, rows, part, got, sems):
        self.n, self.rows, self.sems = n, rows, sems
        self.part, self.got = part, got
        self.chunks = part.shape[0]

    def copy(self, right, slot, chunk, block):
        s, c, u = where_am_i()
        send_r, recv_r, send_l, recv_l = self.sems
        where = rows_of(block, self.rows)
        src = self.part.at[chunk, where]
        if right:
            return remote(
                src,
                self.got.at[chunk, rows_of(block + 1, self.rows)],
                send_r.at[slot, chunk],
                recv_r.at[slot, chunk],
                (s, c, u + 1),
            )
        return remote(
            src,
            self.got.at[chunk, where],
            send_l.at[slot, chunk],
            recv_l.at[slot, chunk],
            (s, c, u - 1),
        )

    def add(self, chunk, block, place):
        where = rows_of(block, self.rows)
        self.part[chunk, where, :] = (
            self.part[chunk, where, :].astype(F32)
            + self.got[chunk, rows_of(place, self.rows), :].astype(F32)
        ).astype(BF16)

    def step(self, slot, chunk):
        u, n = lax.axis_index("uly"), self.n
        block_r = n - 1 - slot + u
        block_l = slot - (n - 1) + u

        @pl.when(u <= slot)
        def _():
            if slot > 0:

                @pl.when(u > 0)
                def _():
                    self.copy(True, slot - 1, chunk, block_r).wait_recv()
                    self.add(chunk, block_r, block_r + 1)

            self.copy(True, slot, chunk, block_r).start()

        @pl.when(u >= n - 1 - slot)
        def _():
            if slot > 0:

                @pl.when(u < n - 1)
                def _():
                    self.copy(False, slot - 1, chunk, block_l).wait_recv()
                    self.add(chunk, block_l, block_l)

            self.copy(False, slot, chunk, block_l).start()

    def last(self, out, chunks=None):
        u, n = lax.axis_index("uly"), self.n
        where = rows_of(u, self.rows)
        width = self.part.shape[2]
        chunks = range(self.chunks) if chunks is None else chunks
        for number, chunk in enumerate(chunks):
            cols = slice(number * width, (number + 1) * width)
            out[:, cols] = self.part[chunk, where, :].astype(F32)

            @pl.when(u > 0)
            def _():
                self.copy(True, n - 2, chunk, u).wait_recv()
                out[:, cols] += self.got[chunk, rows_of(u + 1, self.rows), :].astype(F32)

            @pl.when(u < n - 1)
            def _():
                self.copy(False, n - 2, chunk, u).wait_recv()
                out[:, cols] += self.got[chunk, where, :].astype(F32)

    def finish(self):
        u, n = lax.axis_index("uly"), self.n
        for slot in range(n - 1):
            for chunk in range(self.chunks):

                @pl.when(u <= slot)
                def _():
                    self.copy(True, slot, chunk, n - 1 - slot + u).wait_send()

                @pl.when(u >= n - 1 - slot)
                def _():
                    self.copy(False, slot, chunk, slot - (n - 1) + u).wait_send()

    def run(self, compute, out, hook=None):
        for slot in range(self.n - 1):
            for chunk in range(self.chunks):
                if slot == 0:
                    compute(chunk)
                self.step(slot, chunk)
            if hook is not None:
                hook(slot)
        self.last(out)
        self.finish()


def reduce_norm_gather(n, reduce, gathers, compute, finish, consume, hook):
    per_half = reduce.chunks // 2
    slots = n - 1
    chunks = [range(h * per_half, (h + 1) * per_half) for h in range(2)]
    for chunk in chunks[0]:
        compute(chunk)
        reduce.step(0, chunk)
    for chunk in chunks[1]:
        compute(chunk)
    for slot in range(1, slots):
        for chunk in chunks[0]:
            reduce.step(slot, chunk)
    for chunk in chunks[1]:
        reduce.step(0, chunk)
    hook("sent")
    finish(0)
    gathers[0].send(0)
    hook("half")
    for slot in range(1, slots):
        for chunk in chunks[1]:
            reduce.step(slot, chunk)
        gathers[0].wait(slot - 1)
        hook(f"b{slot}")
    finish(1)
    gathers[1].send(0)
    gathers[0].wait(slots - 1)
    hook("first")
    tiles = consume.tiles
    done = 0
    for slot in range(slots):
        while done < tiles * (slot + 1) // slots:
            consume(0, done)
            done += 1
        gathers[1].wait(slot)
        hook(f"g{slot}")
    for tile in range(tiles):
        consume(1, tile)
        hook(f"t{tile}")
    reduce.finish()
    for gather in gathers:
        gather.finish()


class Halves:
    def __init__(self, n, rows):
        self.n, self.half = n, rows // 2
        self.per_tile = min(n, max(512 // self.half, 1))
        self.count = n // self.per_tile

    def each(self, half, body):
        size = self.per_tile * self.half
        for t in range(self.count):
            index = (pl.ds(t * self.per_tile, self.per_tile), pl.ds(half * self.half, self.half))
            body(index, t * size, size)

    def load(self, ref, index, lanes=slice(None)):
        value = ref[index[0], index[1], lanes]
        return value.reshape(value.shape[0] * value.shape[1], value.shape[2])

    def store(self, ref, index, lanes, value):
        ref[index[0], index[1], lanes] = value.reshape(
            self.per_tile, self.half, value.shape[1]
        )


class Consume:
    def __init__(self, tiles, body):
        self.tiles, self.body = tiles, body

    def __call__(self, half, tile):
        self.body(half, tile)


class PlaneGather:
    SEMS = 9

    def __init__(self, src, block, half_rows, send, recv, local):
        self.s, self.c, self.u = where_am_i()
        self.src, self.block, self.half_rows = src, block, half_rows
        self.send_sem, self.recv_sem = send, recv
        s, c, u = self.s, self.c, self.u
        self.xn, self.yn, self.sib = (s, c ^ 1, u), (s, c ^ 2, u), (1 - s, c, u)
        self.started = []
        self.own = pltpu.make_async_copy(src, block(s * 4 + c), local)

    def half(self, b, part):
        rows = self.half_rows
        view = self.block(b)
        where = [slice(None)] * len(view.shape)
        where[-2] = pl.ds(part * rows, rows)
        return view.at[tuple(where)]

    def copy(self, k, view, peer, src=None):
        return remote(
            view if src is None else src, view, self.send_sem.at[k], self.recv_sem.at[k], peer
        )

    def go(self, *copies):
        for copy in copies:
            copy.start()
            self.started.append(copy)

    def start(self):
        own = self.block(self.s * 4 + self.c)
        self.go(
            self.copy(0, own, self.xn, self.src),
            self.copy(1, own, self.yn, self.src),
            self.copy(2, own, self.sib, self.src),
        )
        self.own.start()

    def middle(self):
        bx, by = self.s * 4 + (self.c ^ 1), self.s * 4 + (self.c ^ 2)
        self.copy(0, self.block(bx), self.xn).wait_recv()
        self.go(
            self.copy(3, self.half(bx, 0), self.yn), self.copy(4, self.block(bx), self.sib)
        )
        self.copy(1, self.block(by), self.yn).wait_recv()
        self.go(
            self.copy(5, self.half(by, 1), self.xn), self.copy(6, self.block(by), self.sib)
        )

    def corner(self):
        bd = self.s * 4 + (self.c ^ 3)
        self.copy(3, self.half(bd, 0), self.yn).wait_recv()
        self.go(self.copy(7, self.half(bd, 0), self.sib))
        self.copy(5, self.half(bd, 1), self.xn).wait_recv()
        self.go(self.copy(8, self.half(bd, 1), self.sib))

    def arrive(self):
        far, c = (1 - self.s) * 4, self.c
        self.copy(2, self.block(far + c), self.sib).wait_recv()
        self.copy(4, self.block(far + (c ^ 1)), self.sib).wait_recv()
        self.copy(6, self.block(far + (c ^ 2)), self.sib).wait_recv()
        self.copy(7, self.half(far + (c ^ 3), 0), self.sib).wait_recv()
        self.copy(8, self.half(far + (c ^ 3), 1), self.sib).wait_recv()
        self.own.wait()

    def finish(self):
        for copy in self.started:
            copy.wait_send()


class PlaneReduce:
    SEMS = 6

    def __init__(self, ring, got, outs, place, send, recv, local):
        self.s, self.c, self.u = where_am_i()
        s, c, u = self.s, self.c, self.u
        self.xn, self.yn = (s, c ^ 1, u), (s, c ^ 2, u)
        self.ring, self.got, self.outs, self.place = ring, got, outs, place
        self.send_sem, self.recv_sem, self.local = send, recv, local
        self.slots, self.rows = ring.shape[0], ring.shape[2]
        self.open = {}

    def halves(self):
        h = self.rows // 2
        return pl.ds(0, h), pl.ds(h, h)

    def copy(self, piece, k, src, dst, peer):
        return remote(src, dst, self.send_sem.at[piece, k], self.recv_sem.at[piece, k], peer)

    def slot(self, piece):
        if piece >= self.slots:
            self.close(piece - self.slots)
        return self.ring.at[piece % self.slots]

    def close(self, piece):
        if piece in self.open:
            remotes, own = self.open.pop(piece)
            for copy in remotes:
                copy.wait_send()
            own.wait()

    def first(self, piece):
        c = self.c
        lo, hi = self.halves()
        blocks = self.ring.at[piece % self.slots]
        own_out, out_x, out_y = self.outs
        bx, by, bd = c ^ 1, c ^ 2, c ^ 3
        copies = [
            self.copy(piece, 0, blocks.at[bd, lo], self.got.at[piece, lo], self.xn),
            self.copy(piece, 1, blocks.at[bd, hi], self.got.at[piece, hi], self.yn),
            self.copy(piece, 2, blocks.at[bx, lo], self.place(out_x, piece, 0), self.xn),
            self.copy(piece, 3, blocks.at[by, hi], self.place(out_y, piece, 1), self.yn),
        ]
        for copy in copies:
            copy.start()
        own = pltpu.make_async_copy(
            blocks.at[c], self.place(own_out, piece, None), self.local.at[piece]
        )
        own.start()
        self.open[piece] = (copies, own)

    def second(self, piece):
        c, h = self.c, self.rows // 2
        lo, hi = self.halves()
        slot = piece % self.slots
        blocks = self.ring.at[slot]
        own_out, out_x, out_y = self.outs
        bx, by, bd = c ^ 1, c ^ 2, c ^ 3
        self.copy(piece, 0, blocks.at[bd, lo], self.got.at[piece, lo], self.xn).wait_recv()
        self.ring[slot, by, :h, :] = (
            self.ring[slot, by, :h, :].astype(F32) + self.got[piece, :h, :].astype(F32)
        ).astype(BF16)
        first = self.copy(piece, 4, blocks.at[by, lo], self.place(out_y, piece, 0), self.yn)
        first.start()
        self.copy(piece, 1, blocks.at[bd, hi], self.got.at[piece, hi], self.yn).wait_recv()
        self.ring[slot, bx, h:, :] = (
            self.ring[slot, bx, h:, :].astype(F32) + self.got[piece, h:, :].astype(F32)
        ).astype(BF16)
        second = self.copy(piece, 5, blocks.at[bx, hi], self.place(out_x, piece, 1), self.xn)
        second.start()
        self.open[piece][0].extend([first, second])

    def finish(self, pieces):
        own_out, out_x, out_y = self.outs
        slot = self.ring.at[0]
        lo, hi = self.halves()
        for piece in range(pieces):
            self.close(piece)
            for k, out, half, peer in (
                (2, out_x, 0, self.xn),
                (3, out_y, 1, self.yn),
                (4, out_y, 0, self.yn),
                (5, out_x, 1, self.xn),
            ):
                where = self.place(out, piece, half)
                self.copy(piece, k, where, where, peer).wait_recv()


class Pieces:
    def __init__(self, work):
        self.work, self.done, self.behind = work, 0, []

    def step(self, count=1):
        for _ in range(count):
            if self.done < len(self.work):
                plane, piece, compute = self.work[self.done]
                compute(plane.slot(piece), piece)
                plane.first(piece)
                self.behind.append((plane, piece))
                self.done += 1
                if len(self.behind) > 2:
                    self.catch_up()

    def catch_up(self):
        plane, piece = self.behind.pop(0)
        plane.second(piece)

    def finish(self):
        self.step(len(self.work))
        while self.behind:
            self.catch_up()


def wide_piece(own, other, lanes):
    def compute(out, piece):
        take = lanes(piece)
        cols = out.shape[2]

        def pair(i, carry):
            where = pl.ds(pl.multiple_of(i * 2 * cols, 2 * cols), 2 * cols)
            total = dot(own[0][:, take], own[1][:, where], TN) + dot(
                other[0][:, take], other[1][:, where], TN
            )
            total = total.astype(BF16)
            out[pl.ds(2 * i, 1)] = total[:, :cols][None]
            out[pl.ds(2 * i + 1, 1)] = total[:, cols:][None]
            return carry

        lax.fori_loop(0, 2, pair, 0)

    return compute


def tall_piece(own, other, right):
    def compute(out, piece):
        rows, cols = out.shape[1:]

        def pair(i, carry):
            where = pl.ds(pl.multiple_of(i * 2 * rows, 2 * rows), 2 * rows)
            total = dot(own[0][:, where], right(own[1], piece), TN) + dot(
                other[0][:, where], right(other[1], piece), TN
            )
            out[pl.ds(2 * i, 2)] = total.astype(BF16).reshape(2, rows, cols)
            return carry

        lax.fori_loop(0, 2, pair, 0)

    return compute


class LatePiece:
    def __init__(self, number, ins, outs, scratch, sems):
        s, c, u = where_am_i()
        resid_hbm, resid_s_hbm, dgu_hbm, dgu_s_hbm = ins
        resid, resid_s, right, right_s, ring, got = scratch
        send, recv, local, load_sem = sems
        cols = right.shape[1]
        ci, tile = divmod(number, dgu_hbm.shape[2] // cols)
        lanes = pl.ds(tile * cols, cols)
        pairs = (
            (half_columns(resid_hbm, s), resid),
            (resid_s_hbm, resid_s),
            (dgu_hbm.at[ci, :, lanes], right),
            (dgu_s_hbm.at[ci, :, lanes], right_s),
        )
        self.loads = [
            pltpu.make_async_copy(src, dst, load_sem.at[k]) for k, (src, dst) in enumerate(pairs)
        ]
        size = ring.shape[2]

        def place(out, piece, part):
            rows = size if part is None else size // 2
            return out.at[ci, pl.ds((part or 0) * rows, rows), lanes]

        self.plane = PlaneReduce(ring, got, outs, place, send, recv, local)
        self.compute = tall_piece(
            (resid, right), (resid_s, right_s), lambda ref, piece: ref[...]
        )

    def load(self):
        for copy in self.loads:
            copy.start()

    def work(self):
        def compute(out, piece):
            for copy in self.loads:
                copy.wait()
            self.compute(out, piece)

        return (self.plane, 0, compute)

    @staticmethod
    def scratch(span, width, ff):
        cols = min(ff, 512)
        ring, sems = piece_scratch(1, 1, width // 8, cols)
        buffers = (
            pltpu.VMEM((span, width // 2), BF16),
            pltpu.VMEM((span, width // 2), BF16),
            pltpu.VMEM((span, cols), BF16),
            pltpu.VMEM((span, cols), BF16),
            ring[0],
            ring[1],
        )
        return [buffers, tuple(sems) + (pltpu.SemaphoreType.DMA((4,)),)]


def half_columns(ref, s):
    half = ref.shape[1] // 2
    return ref.at[:, pl.ds(pl.multiple_of(s * half, half), half)]


class Sibling:
    def __init__(self, send, recv):
        s, c, u = where_am_i()
        self.peer, self.send, self.recv = (1 - s, c, u), send, recv
        self.copies = []

    def start(self, src, dst):
        k = len(self.copies)
        copy = remote(src, dst, self.send.at[k], self.recv.at[k], self.peer)
        copy.start()
        self.copies.append(copy)

    def wait(self, k):
        self.copies[k].wait_recv()

    def finish(self):
        for copy in self.copies:
            copy.wait_send()


def dot(a, b, dims):
    return lax.dot_general(a, b, ((dims[:1], dims[1:]), ((), ())), preferred_element_type=F32)


NN, NT, TN = (1, 0), (1, 1), (0, 0)


def tiles(total, size):
    size = min(total, size)
    return total // size, size


def inverse_rms(values):
    return lax.rsqrt(jnp.mean(values * values, axis=-1, keepdims=True) + EPS)


def norm_back(values, inverse, grad_scaled, width):
    return inverse * grad_scaled - values * inverse**3 * (
        jnp.sum(values * grad_scaled, axis=-1, keepdims=True) / width
    )


def rope_factors(table):
    lane = lax.broadcasted_iota(jnp.int32, table.shape, 1)
    turned = pltpu.roll(table, HALF, 1)
    cosine = jnp.where(lane < HALF, table, turned)
    sine = jnp.where(lane < HALF, -turned, table)
    return cosine, sine


def exchange_rows(n, mine, msg, send, recv):
    s, c, u = where_am_i()
    msg[pl.ds(u, 1)] = mine[None]
    copies = []
    for step in range(1, n):
        peer = lax.rem(u + step, n)
        copy = remote(msg.at[u], msg.at[u], send.at[step - 1], recv.at[step - 1], (s, c, peer))
        copy.start()
        copies.append(copy)
    for step in range(1, n):
        source = lax.rem(u + n - step, n)
        remote(
            msg.at[source], msg.at[source], send.at[step - 1], recv.at[step - 1], (s, c, source)
        ).wait_recv()
    total = msg[0]
    for j in range(1, n):
        total = total + msg[j]
    for copy in copies:
        copy.wait_send()
    return total


def to_rows(col0, col1):
    span = col0.shape[0]
    lane = lax.broadcasted_iota(jnp.int32, (span, 128), 1)
    both = jnp.where(lane == 0, col0, jnp.where(lane == 1, col1, 0.0))
    return jnp.transpose(both)[:8]


def to_columns(rows8):
    return jnp.transpose(jnp.concatenate([rows8] * 16, axis=0))


def all_uly_peers(n):
    s, c, u = where_am_i()
    return [(None, (s, c, lax.rem(u + k, n))) for k in range(1, n)]


def spread_heads(cols):
    return cols % (4 * HEAD_DIM) == 0


def proj_kernel(
    n,
    x_ref,
    w_ref,
    tab_ref,
    gain_ref,
    seg_ref,
    wo_ref,
    gu_ref,
    xg_out,
    wq_out,
    wo_out,
    wga_out,
    proj_ref,
    qkv_refs,
    inv_ref,
    zero_ref,
    xg,
    wq,
    tab,
    msg,
    local_sem,
    w_send,
    w_recv,
    m_send,
    m_recv,
    *line,
):
    s, c, u = where_am_i()
    rows, width = x_ref.shape
    span = n * rows
    kb = w_ref.shape[1]
    sib = (1 - s, c, u)
    tab_copy = pltpu.make_async_copy(tab_ref.at[rows_of(c, span)], tab, local_sem.at[0])
    tab_copy.start()
    xg[rows_of(u, rows), :] = x_ref[...]
    greet(all_uly_peers(n) + plane_peers() + [(None, sib)])

    def plane(k, src, block, half_rows):
        return PlaneGather(
            src, block, half_rows, w_send.at[k], w_recv.at[k], local_sem.at[3 + k]
        )

    half = kb // 2
    gather = LineGather(n, rows, xg, line)
    first = plane(0, w_ref, lambda b: wq.at[:, rows_of(b, kb)], half)
    second = plane(1, wo_ref, lambda b: wo_out.at[b], wo_ref.shape[0] // 2)
    third = plane(2, gu_ref.at[0, pl.ds(0, half)], lambda b: wga_out.at[b], half // 2)
    gather.send(0)
    first.start()
    gather.wait(0)
    first.middle()
    second.start()
    if n > 2:
        gather.wait(1)
    first.corner()
    second.middle()
    third.start()
    for slot in range(2 if n > 2 else 1, n - 1):
        gather.wait(slot)
    first.arrive()
    tab_copy.wait()
    keep = [
        pltpu.make_async_copy(xg, xg_out, local_sem.at[1]),
        pltpu.make_async_copy(wq, wq_out, local_sem.at[2]),
    ]
    for copy in keep:
        copy.start()

    count, size = tiles(span, 512)

    def store(i, where, first, values):
        if len(qkv_refs) == 1:
            (ref,) = qkv_refs
            size = ref.shape[3]
            for at in range(0, values.shape[1], min(size, values.shape[1])):
                group, inside = divmod(first + at, size)
                part = values[:, at : at + size]
                ref[group, i, where, inside : inside + part.shape[1]] = part
        else:
            ref = qkv_refs[0] if i == 0 else qkv_refs[1].at[i - 1]
            ref[where, first : first + values.shape[1]] = values

    def project(i, carry):
        where = pl.ds(pl.multiple_of(i * size, size), size)
        xs = xg[where, :]
        proj_ref[0, where, :] = dot(xs, wq[0], NN)
        proj_ref[1, where, :] = dot(xs, wq[1], NN)
        store(2, where, 0, dot(xs, wq[2], NN).astype(BF16))
        return carry

    lax.fori_loop(0, count, project, 0)
    squares = [jnp.sum(proj_ref[i] * proj_ref[i], axis=-1, keepdims=True) for i in range(2)]
    mine = to_rows(*squares)
    zeros = jnp.sum((1 - seg_ref[...]).astype(F32))
    row = lax.broadcasted_iota(jnp.int32, mine.shape, 0)
    mine = jnp.where(row == 2, zeros, mine)
    second.corner()
    third.middle()
    total = exchange_rows(n, mine, msg, m_send, m_recv)
    zero_ref[...] = jnp.broadcast_to(total[2:3, :128], (8, 128))
    inv = lax.rsqrt(to_columns(total) / width + EPS)
    inv_ref[...] = inv
    cosine, sine = rope_factors(tab[...])
    heads = proj_ref.shape[2] // HEAD_DIM
    for i in range(2):
        inverse = inv_ref[:, i : i + 1]
        for h in range(heads):
            cols = slice(h * HEAD_DIM, (h + 1) * HEAD_DIM)
            v = proj_ref[i, :, cols] * inverse * gain_ref[i : i + 1, cols]
            v = (v * cosine + pltpu.roll(v, HALF, 1) * sine).astype(BF16)
            store(i, slice(None), h * HEAD_DIM, v)
    second.arrive()
    third.corner()
    third.arrive()
    for work in (first, second, third, gather):
        work.finish()
    for copy in keep:
        copy.wait()


def project(n, x, w, table, gain, seg, wo, gu):
    rows, width = x.shape
    span, cols = n * rows, w.shape[2]
    if spread_heads(cols):
        qkv = (shape((4, 3, span, cols // 4), BF16),)
    else:
        qkv = (shape((span, cols), BF16), shape((2, span, cols), BF16))
    return pl.pallas_call(
        functools.partial(proj_kernel, n),
        out_shape=(
            shape((span, width), BF16),
            shape((3, width, cols), BF16),
            shape((8,) + wo.shape, BF16),
            shape((8, gu.shape[1] // 2, gu.shape[2]), BF16),
            shape((2, span, cols), F32),
            qkv,
            shape((span, 128), F32),
            shape((8, 128), F32),
        ),
        in_specs=[VM, HB, HB, VM, VM, HB, HB],
        out_specs=(HB, HB, HB, HB, VM, (VM,) * len(qkv), VM, VM),
        scratch_shapes=[
            pltpu.VMEM((span, width), BF16),
            pltpu.VMEM((3, width, cols), BF16),
            pltpu.VMEM((span, 128), F32),
            pltpu.VMEM((n, 8, span), F32),
            pltpu.SemaphoreType.DMA((6,)),
            pltpu.SemaphoreType.DMA((3, 9)),
            pltpu.SemaphoreType.DMA((3, 9)),
            pltpu.SemaphoreType.DMA((n - 1,)),
            pltpu.SemaphoreType.DMA((n - 1,)),
        ]
        + line_sems(n),
        compiler_params=pltpu.CompilerParams(
            collective_id=1, has_side_effects=True, vmem_limit_bytes=VMEM_LIMIT
        ),
        name="project",
    )(x, w, table, gain, seg, wo, gu)


def score_mask(scores, key_first, query_first, starts, diagonal):
    key_pos = key_first + lax.broadcasted_iota(jnp.int32, scores.shape, 0)
    keep = key_pos >= starts
    if diagonal:
        query_pos = query_first + lax.broadcasted_iota(jnp.int32, scores.shape, 1)
        keep = keep & (key_pos <= query_pos)
    return jnp.where(keep, scores, FLOOR)


def segment_starts(first, size, bound):
    pos = first + lax.broadcasted_iota(jnp.int32, (1, size), 1)
    return jnp.where(pos >= bound, bound, 0)


def attend_kernel(
    q_ref,
    kv_ref,
    zero_ref,
    gu_ref,
    kvall_out,
    wgb_out,
    attn_ref,
    attn32_ref,
    lse_ref,
    bound_ref,
    kvall,
    peaks,
    sums,
    acct,
    zmsg,
    send,
    recv,
    z_send,
    z_recv,
    w_send,
    w_recv,
    keep_sem,
    w_local,
):
    s, c, u = where_am_i()
    span, cols = q_ref.shape
    heads = cols // HEAD_DIM
    xn, yn, dn = (s, c ^ 1, u), (s, c ^ 2, u), (s, c ^ 3, u)
    kvall[pl.ds(c, 1)] = kv_ref[...][None]
    zmsg[pl.ds(c, 1)] = zero_ref[...][None]
    greet(plane_peers() + [(None, dn), (None, (1 - s, c, u))])
    weight = upper_gate(gu_ref, wgb_out, w_send, w_recv, w_local)

    def sent(k, view, peer):
        return remote(view, view, send.at[k], recv.at[k], peer)

    bx, by, bd = c ^ 1, c ^ 2, c ^ 3
    zs = [
        remote(zmsg.at[c], zmsg.at[c], z_send.at[k], z_recv.at[k], peer)
        for k, peer in enumerate((xn, yn, dn))
    ]
    for copy in zs:
        copy.start()
    copies = [sent(0, kvall.at[c], xn), sent(1, kvall.at[c], yn)]
    for copy in copies:
        copy.start()
    for k, (b, peer) in enumerate(((bx, xn), (by, yn), (bd, dn))):
        remote(zmsg.at[b], zmsg.at[b], z_send.at[k], z_recv.at[k], peer).wait_recv()
    ahead = jnp.zeros((8, 128), F32)
    for j in range(4):
        ahead = ahead + jnp.where(j <= c, zmsg[j], 0.0)
    bounds = ahead.astype(jnp.int32)
    bound_ref[...] = bounds
    bound = bounds[:1, :1]

    peaks[...] = jnp.full_like(peaks, FLOOR)
    sums[...] = jnp.zeros_like(sums)
    acct[...] = jnp.zeros_like(acct)
    nq, tq = tiles(span, 512)
    nk, tk = tiles(span, 512)

    def update(number, diagonal):
        def over_queries(i, carry):
            first_q = c * span + i * tq
            starts = segment_starts(first_q, tq, bound)
            where_q = pl.ds(pl.multiple_of(i * tq, tq), tq)

            def over_keys(j, carry):
                first_k = number * span + j * tk
                where_k = pl.ds(pl.multiple_of(j * tk, tk), tk)
                for h in range(heads):
                    lanes = slice(h * HEAD_DIM, (h + 1) * HEAD_DIM)
                    scores = dot(kvall[number, 0, where_k, lanes], q_ref[where_q, lanes], NT)
                    scores = score_mask(scores * SCALE2, first_k, first_q, starts, diagonal)
                    old = peaks[h, :1, where_q]
                    new = jnp.maximum(old, jnp.max(scores, axis=0, keepdims=True))
                    factor = jnp.exp2(old - new)
                    weights = jnp.exp2(scores - new)
                    peaks[h, :1, where_q] = new
                    sums[h, :1, where_q] = sums[h, :1, where_q] * factor + jnp.sum(
                        weights, axis=0, keepdims=True
                    )
                    acct[h, :, where_q] = acct[h, :, where_q] * factor + dot(
                        kvall[number, 1, where_k, lanes], weights.astype(BF16), TN
                    )
                return carry

            return lax.fori_loop(0, nk, over_keys, carry)

        lax.fori_loop(0, nq, over_queries, 0)

    update(c, True)
    half = span // 2
    sent(0, kvall.at[bx], xn).wait_recv()
    more = [sent(2, kvall.at[bx, :, pl.ds(0, half)], yn)]
    more[0].start()
    copies += more
    sent(1, kvall.at[by], yn).wait_recv()
    more = [sent(3, kvall.at[by, :, pl.ds(half, half)], xn)]
    more[0].start()
    copies += more
    for b in (bx, by):

        @pl.when(b < c)
        def _():
            update(b, False)

    sent(2, kvall.at[bd, :, pl.ds(0, half)], yn).wait_recv()
    sent(3, kvall.at[bd, :, pl.ds(half, half)], xn).wait_recv()
    keep = pltpu.make_async_copy(kvall, kvall_out, keep_sem)
    keep.start()
    weight.start()

    @pl.when(bd < c)
    def _():
        update(bd, False)

    for h in range(heads):
        lanes = slice(h * HEAD_DIM, (h + 1) * HEAD_DIM)
        total = sums[h, :1, :]
        attention = jnp.transpose(acct[h] / total)
        attn32_ref[:, lanes] = attention
        attn_ref[:, lanes] = attention.astype(BF16)
        lse_ref[h, :1, :] = peaks[h, :1, :] + jnp.log2(total)
    for copy in copies + zs:
        copy.wait_send()
    weight.middle()
    weight.corner()
    weight.arrive()
    weight.finish()
    keep.wait()


def attend(q, kv, zero, gu):
    span, cols = q.shape
    heads = cols // HEAD_DIM
    return pl.pallas_call(
        attend_kernel,
        out_shape=(
            shape((4, 2, span, cols), BF16),
            shape((8, gu.shape[1] // 2, gu.shape[2]), BF16),
            shape((span, cols), BF16),
            shape((span, cols), F32),
            shape((heads, 8, span), F32),
            shape((8, 128), jnp.int32),
        ),
        in_specs=[VM] * 3 + [HB],
        out_specs=(HB, HB, VM, VM, VM, VM),
        scratch_shapes=[
            pltpu.VMEM((4, 2, span, cols), BF16),
            pltpu.VMEM((heads, 8, span), F32),
            pltpu.VMEM((heads, 8, span), F32),
            pltpu.VMEM((heads, HEAD_DIM, span), F32),
            pltpu.VMEM((4, 8, 128), F32),
            pltpu.SemaphoreType.DMA((4,)),
            pltpu.SemaphoreType.DMA((4,)),
            pltpu.SemaphoreType.DMA((3,)),
            pltpu.SemaphoreType.DMA((3,)),
            pltpu.SemaphoreType.DMA((9,)),
            pltpu.SemaphoreType.DMA((9,)),
            pltpu.SemaphoreType.DMA,
            pltpu.SemaphoreType.DMA,
        ],
        compiler_params=pltpu.CompilerParams(
            collective_id=2, has_side_effects=True, vmem_limit_bytes=VMEM_LIMIT
        ),
        name="attend",
    )(q, kv, zero, gu)


def attend_spread_kernel(
    qkv_ref,
    zero_ref,
    gu_ref,
    all_out,
    wgb_out,
    attn_ref,
    att_ref,
    lse_ref,
    bound_ref,
    every,
    peaks,
    sums,
    acct,
    back,
    zmsg,
    send,
    recv,
    z_send,
    z_recv,
    b_send,
    b_recv,
    w_send,
    w_recv,
    keep_sem,
    w_local,
):
    s, c, u = where_am_i()
    span, cols = every.shape[2:]
    heads = cols // HEAD_DIM
    peers = [(s, c ^ k, u) for k in (1, 2, 3)]
    greet([(None, peer) for peer in peers] + [(None, (1 - s, c, u))])
    weight = upper_gate(gu_ref, wgb_out, w_send, w_recv, w_local)
    copies, arrivals = [], []
    zmsg[pl.ds(c, 1)] = zero_ref[...][None]
    for k, peer in enumerate(peers):
        there = peer[1]
        copy = remote(qkv_ref.at[there], every.at[c], send.at[k], recv.at[k], peer)
        copy.start()
        small = remote(zmsg.at[c], zmsg.at[c], z_send.at[k], z_recv.at[k], peer)
        small.start()
        copies += [copy, small]
        arrivals.append(remote(every.at[there], every.at[there], send.at[k], recv.at[k], peer))
        arrivals.append(remote(zmsg.at[there], zmsg.at[there], z_send.at[k], z_recv.at[k], peer))
    every[pl.ds(c, 1)] = qkv_ref[pl.ds(c, 1)]
    for arrival in arrivals:
        arrival.wait_recv()
    weight.start()
    keep = pltpu.make_async_copy(every, all_out, keep_sem)
    keep.start()
    bounds = (zmsg[0] + zmsg[1] + zmsg[2] + zmsg[3]).astype(jnp.int32)
    bound_ref[...] = bounds
    bound = bounds[:1, :1]

    def step(k, carry):
        i = c ^ (3 - k)
        first_q = i * span
        starts = segment_starts(first_q, span, bound)
        for h in range(heads):
            lanes = slice(h * HEAD_DIM, (h + 1) * HEAD_DIM)
            peaks[...] = jnp.full_like(peaks, FLOOR)
            sums[...] = jnp.zeros_like(sums)
            acct[...] = jnp.zeros_like(acct)

            def update(j, diagonal):
                scores = dot(every[j, 1, :, lanes], every[i, 0, :, lanes], NT) * SCALE2
                scores = score_mask(scores, j * span, first_q, starts, diagonal)
                old = peaks[:1, :]
                new = jnp.maximum(old, jnp.max(scores, axis=0, keepdims=True))
                factor = jnp.exp2(old - new)
                weights = jnp.exp2(scores - new)
                peaks[:1, :] = new
                sums[:1, :] = sums[:1, :] * factor + jnp.sum(weights, axis=0, keepdims=True)
                acct[...] = acct[...] * factor + dot(
                    every[j, 2, :, lanes], weights.astype(BF16), TN
                )

            def before(j, carry):
                update(j, False)
                return carry

            lax.fori_loop(0, i, before, 0)
            update(i, True)
            total = sums[:1, :]
            attention = acct[...] / total
            att_ref[pl.ds(i, 1), lanes, :] = attention[None]
            back[pl.ds(k, 1), :, lanes] = jnp.transpose(attention).astype(BF16)[None]
            lse_ref[pl.ds(i, 1), h, :1, :] = (peaks[:1, :] + jnp.log2(total))[None]

        @pl.when(k < 3)
        def _():
            home(k, i).start()

        return carry

    def home(k, i):
        return remote(
            back.at[k],
            attn_ref.at[:, pl.ds(pl.multiple_of(c * cols, cols), cols)],
            b_send.at[k],
            b_recv.at[k],
            (s, i, u),
        )

    lax.fori_loop(0, 4, step, 0)
    attn_ref[:, pl.ds(pl.multiple_of(c * cols, cols), cols)] = back[3]
    for k in range(3):
        i = c ^ (3 - k)
        remote(
            back.at[k],
            attn_ref.at[:, pl.ds(pl.multiple_of(i * cols, cols), cols)],
            b_send.at[k],
            b_recv.at[k],
            (s, i, u),
        ).wait_recv()
        home(k, i).wait_send()
    for copy in copies:
        copy.wait_send()
    weight.middle()
    weight.corner()
    weight.arrive()
    weight.finish()
    keep.wait()


def upper_gate(gu_ref, out, send, recv, local):
    half = gu_ref.shape[1] // 2
    return PlaneGather(
        gu_ref.at[0, pl.ds(half, half)], lambda b: out.at[b], half // 2, send, recv, local
    )


def attend_spread(qkv, zero, gu):
    span, cols = qkv.shape[2:]
    heads = cols // HEAD_DIM
    return pl.pallas_call(
        attend_spread_kernel,
        out_shape=(
            shape(qkv.shape, BF16),
            shape((8, gu.shape[1] // 2, gu.shape[2]), BF16),
            shape((span, 4 * cols), BF16),
            shape((4, cols, span), F32),
            shape((4, heads, 8, span), F32),
            shape((8, 128), jnp.int32),
        ),
        in_specs=[VM, VM, HB],
        out_specs=(HB, HB, VM, VM, VM, VM),
        scratch_shapes=[
            pltpu.VMEM(qkv.shape, BF16),
            pltpu.VMEM((8, span), F32),
            pltpu.VMEM((8, span), F32),
            pltpu.VMEM((HEAD_DIM, span), F32),
            pltpu.VMEM((4, span, cols), BF16),
            pltpu.VMEM((4, 8, 128), F32),
        ]
        + [pltpu.SemaphoreType.DMA((3,))] * 6
        + [pltpu.SemaphoreType.DMA((9,))] * 2
        + [pltpu.SemaphoreType.DMA] * 2,
        compiler_params=pltpu.CompilerParams(
            collective_id=8, has_side_effects=True, vmem_limit_bytes=VMEM_LIMIT
        ),
        name="attend_spread",
    )(qkv, zero, gu)


def norms_back(n, source, keep, proj_ref, inv_ref, gain_ref, tab, dgain_ref):
    cosine, sine = rope_factors(tab[...])
    span, cols = keep.shape[1:]
    dots = []
    for i in range(2):
        inverse = inv_ref[:, i : i + 1]
        row_dot = jnp.zeros((span, 1), F32)
        for h in range(cols // HEAD_DIM):
            lanes = slice(h * HEAD_DIM, (h + 1) * HEAD_DIM)
            v = source(i, h)
            v = v * cosine - pltpu.roll(v, HALF, 1) * sine
            values = proj_ref[i, :, lanes]
            dgain_ref[i : i + 1, lanes] = jnp.sum(v * values * inverse, axis=0, keepdims=True)
            v = v * gain_ref[i : i + 1, lanes]
            keep[i, :, lanes] = v
            row_dot = row_dot + jnp.sum(values * v, axis=-1, keepdims=True)
        dots.append(row_dot)
    return to_rows(*dots)


def attend_spread_back_kernel(
    n,
    all_hbm,
    do_ref,
    att_hbm,
    lse_ref,
    bound_ref,
    proj_hbm,
    inv_ref,
    gain_ref,
    tab_ref,
    resid_hbm,
    resid_s_hbm,
    dgu_hbm,
    dgu_s_hbm,
    own_in,
    x_in,
    y_in,
    dproj_ref,
    dgain_ref,
    own_out,
    x_out,
    y_out,
    every,
    att,
    proj,
    d_out,
    dq,
    acc,
    delta,
    back,
    got,
    scaled,
    tab,
    msg,
    late_buffers,
    late_sems,
    send,
    recv,
    b_send,
    b_recv,
    local_sem,
    m_send,
    m_recv,
):
    s, c, u = where_am_i()
    span, cols = every.shape[2:]
    width = resid_hbm.shape[1]
    heads = cols // HEAD_DIM
    load = [
        pltpu.make_async_copy(all_hbm, every, local_sem.at[0]),
        pltpu.make_async_copy(att_hbm, att, local_sem.at[1]),
        pltpu.make_async_copy(tab_ref.at[rows_of(c, span)], tab, local_sem.at[2]),
        pltpu.make_async_copy(proj_hbm, proj, local_sem.at[3]),
    ]
    last = 2 * (dgu_hbm.shape[2] // late_buffers[2].shape[1])
    late = LatePiece(
        last - 2,
        (resid_hbm, resid_s_hbm, dgu_hbm, dgu_s_hbm),
        (own_out, x_out, y_out),
        late_buffers,
        late_sems,
    )
    late.load()
    for copy in load:
        copy.start()
    peers = [(s, c ^ k, u) for k in (1, 2, 3)]
    greet([(None, peer) for peer in peers] + all_uly_peers(n))
    copies = []
    for k, peer in enumerate(peers):
        copy = remote(do_ref.at[peer[1]], d_out.at[c], send.at[k], recv.at[k], peer)
        copy.start()
        copies.append(copy)
    pieces = Pieces([late.work()])
    d_out[pl.ds(c, 1)] = do_ref[pl.ds(c, 1)]
    dq[...] = jnp.zeros_like(dq)
    bound = bound_ref[:1, :1]
    scale = HEAD_DIM ** (-0.5)
    load[0].wait()
    load[1].wait()
    for k, peer in enumerate(peers):
        there = d_out.at[peer[1]]
        remote(there, there, send.at[k], recv.at[k], peer).wait_recv()
    pieces.step()
    for i in range(4):
        for h in range(heads):
            lanes = slice(h * HEAD_DIM, (h + 1) * HEAD_DIM)
            both = jnp.transpose(d_out[i, :, lanes].astype(F32)) * att[i, lanes, :]
            delta[i, h, :1, :] = jnp.sum(both, axis=0, keepdims=True)

    def home(j):
        return remote(back.at[j], got.at[c], b_send.at[j], b_recv.at[c], (s, j, u))

    def step(j, carry):
        acc[...] = jnp.zeros_like(acc)
        for h in range(heads):
            lanes = slice(h * HEAD_DIM, (h + 1) * HEAD_DIM)

            def update(i, diagonal):
                starts = segment_starts(i * span, span, bound)
                keys, values = every[j, 1, :, lanes], every[j, 2, :, lanes]
                query, grad = every[i, 0, :, lanes], d_out[i, :, lanes]
                scores = dot(keys, query, NT) * SCALE2
                scores = score_mask(scores, j * span, i * span, starts, diagonal)
                probs = jnp.exp2(scores - lse_ref[i, h, :1, :])
                acc[1, :, lanes] += dot(probs.astype(BF16), grad, NN)
                d_probs = dot(values, grad, NT)
                d_scores = (probs * (d_probs - delta[i, h, :1, :])).astype(BF16)
                acc[0, :, lanes] += dot(d_scores, query, NN) * scale
                dq[i, :, lanes] += dot(d_scores, keys, TN) * scale

            def after(i, carry):
                update(i, False)
                return carry

            update(j, True)
            lax.fori_loop(j + 1, 4, after, 0)
        back[j, 0] = dq[j].astype(BF16)
        back[j, 1] = acc[0].astype(BF16)
        back[j, 2] = acc[1].astype(BF16)

        @pl.when(j != c)
        def _():
            home(j).start()

        return carry

    lax.fori_loop(0, 4, step, 0)
    pieces.finish()
    got[pl.ds(c, 1)] = back[pl.ds(c, 1)]
    load[2].wait()
    load[3].wait()
    for k in (1, 2, 3):
        j = c ^ k
        remote(got.at[j], got.at[j], b_send.at[c], b_recv.at[j], (s, j, u)).wait_recv()
    for j in range(4):
        dproj_ref[2, :, j * cols : (j + 1) * cols] = got[j, 2]

    def source(i, h):
        group, inside = divmod(h, heads)
        lanes = slice(inside * HEAD_DIM, (inside + 1) * HEAD_DIM)
        return got[group, i, :, lanes].astype(F32)

    rows = norms_back(n, source, scaled, proj, inv_ref, gain_ref, tab, dgain_ref)
    total = exchange_rows(n, rows, msg, m_send, m_recv)
    means = to_columns(total) / width
    for i in range(2):
        inverse = inv_ref[:, i : i + 1]
        factor = inverse**3 * means[:, i : i + 1]
        dproj_ref[i] = (inverse * scaled[i] - proj[i] * factor).astype(BF16)
    late.plane.finish(1)
    for j in range(4):

        @pl.when(j != c)
        def _():
            home(j).wait_send()

    for copy in copies:
        copy.wait_send()


def attend_spread_back(
    n, every, d_out, att, lse, bound, proj, inv, gain, table, late, grads
):
    span, cols = every.shape[2:]
    heads = cols // HEAD_DIM
    width, ff = late[0].shape[1], late[2].shape[2]
    return pl.pallas_call(
        functools.partial(attend_spread_back_kernel, n),
        out_shape=(shape((3, span, 4 * cols), BF16), shape((2, 4 * cols), F32))
        + tuple(shape(g.shape, BF16) for g in grads),
        in_specs=[HB, VM, HB, VM, VM, HB, VM, VM] + [HB] * 8,
        out_specs=(VM, VM, HB, HB, HB),
        input_output_aliases={13: 2, 14: 3, 15: 4},
        scratch_shapes=[
            pltpu.VMEM(every.shape, BF16),
            pltpu.VMEM(att.shape, F32),
            pltpu.VMEM(proj.shape, F32),
            pltpu.VMEM((4, span, cols), BF16),
            pltpu.VMEM((4, span, cols), F32),
            pltpu.VMEM((2, span, cols), F32),
            pltpu.VMEM((4, heads, 8, span), F32),
            pltpu.VMEM((4, 3, span, cols), BF16),
            pltpu.VMEM((4, 3, span, cols), BF16),
            pltpu.VMEM((2, span, 4 * cols), F32),
            pltpu.VMEM((span, 128), F32),
            pltpu.VMEM((n, 8, span), F32),
        ]
        + LatePiece.scratch(span, width, ff)
        + [
            pltpu.SemaphoreType.DMA((3,)),
            pltpu.SemaphoreType.DMA((3,)),
            pltpu.SemaphoreType.DMA((4,)),
            pltpu.SemaphoreType.DMA((4,)),
            pltpu.SemaphoreType.DMA((4,)),
            pltpu.SemaphoreType.DMA((n - 1,)),
            pltpu.SemaphoreType.DMA((n - 1,)),
        ],
        compiler_params=pltpu.CompilerParams(
            collective_id=9, has_side_effects=True, vmem_limit_bytes=VMEM_LIMIT
        ),
        name="attend_spread_back",
    )(every, d_out, att, lse, bound, proj, inv, gain, table, *late, *grads)


def attend_back_kernel(
    n,
    q_ref,
    kvall_ref,
    do_ref,
    attn32_ref,
    lse_ref,
    bound_ref,
    proj_ref,
    inv_ref,
    gain_ref,
    tab_ref,
    resid_hbm,
    resid_s_hbm,
    dgu_hbm,
    dgu_s_hbm,
    own_in,
    x_in,
    y_in,
    dproj_ref,
    dgain_ref,
    own_out,
    x_out,
    y_out,
    dq_ref,
    part,
    got,
    acc,
    delta,
    tab,
    msg,
    late_buffers,
    late_sems,
    send,
    recv,
    local_sem,
    m_send,
    m_recv,
):
    s, c, u = where_am_i()
    span, cols = q_ref.shape
    width = resid_hbm.shape[1]
    heads = cols // HEAD_DIM
    xn, yn = (s, c ^ 1, u), (s, c ^ 2, u)
    bx, by, bd = c ^ 1, c ^ 2, c ^ 3
    load = pltpu.make_async_copy(tab_ref.at[rows_of(c, span)], tab, local_sem)
    load.start()
    last = 2 * (dgu_hbm.shape[2] // late_buffers[2].shape[1])
    late = LatePiece(
        last - 2,
        (resid_hbm, resid_s_hbm, dgu_hbm, dgu_s_hbm),
        (own_out, x_out, y_out),
        late_buffers,
        late_sems,
    )
    late.load()
    pieces = Pieces([late.work()])
    greet(plane_peers() + all_uly_peers(n))
    bound = bound_ref[:1, :1]
    nq, tq = tiles(span, 512)
    nk, tk = tiles(span, 512)
    scale = HEAD_DIM ** (-0.5)
    dq_ref[...] = jnp.zeros_like(dq_ref)
    for h in range(heads):
        lanes = slice(h * HEAD_DIM, (h + 1) * HEAD_DIM)
        both = jnp.transpose(do_ref[:, lanes].astype(F32) * attn32_ref[:, lanes])
        delta[h, :1, :] = jnp.sum(both, axis=0, keepdims=True)

    def update(number, diagonal):
        acc[...] = jnp.zeros_like(acc)

        def over_queries(i, carry):
            first_q = c * span + i * tq
            starts = segment_starts(first_q, tq, bound)
            where_q = pl.ds(pl.multiple_of(i * tq, tq), tq)

            def over_keys(j, carry):
                first_k = number * span + j * tk
                where_k = pl.ds(pl.multiple_of(j * tk, tk), tk)
                for h in range(heads):
                    lanes = slice(h * HEAD_DIM, (h + 1) * HEAD_DIM)
                    keys = kvall_ref[number, 0, where_k, lanes]
                    values = kvall_ref[number, 1, where_k, lanes]
                    query, d_out = q_ref[where_q, lanes], do_ref[where_q, lanes]
                    scores = dot(keys, query, NT) * SCALE2
                    scores = score_mask(scores, first_k, first_q, starts, diagonal)
                    probs = jnp.exp2(scores - lse_ref[h, :1, where_q])
                    acc[1, where_k, lanes] += dot(probs.astype(BF16), d_out, NN)
                    d_probs = dot(values, d_out, NT)
                    d_scores = (probs * (d_probs - delta[h, :1, where_q])).astype(BF16)
                    acc[0, where_k, lanes] += dot(d_scores, query, NN) * scale
                    dq_ref[where_q, lanes] += dot(d_scores, keys, TN) * scale
                return carry

            return lax.fori_loop(0, nk, over_keys, carry)

        lax.fori_loop(0, nq, over_queries, 0)

    def work(number):
        @pl.when(number < c)
        def _():
            update(number, False)
            part[pl.ds(number, 1)] = acc[...].astype(BF16)[None]

        @pl.when(number > c)
        def _():
            part[pl.ds(number, 1)] = jnp.zeros_like(part[pl.ds(number, 1)])

    half = span // 2
    lo, hi = pl.ds(0, half), pl.ds(half, half)

    def sent(k, src, dst, peer):
        return remote(src, dst, send.at[k], recv.at[k], peer)

    pieces.step()
    work(bd)
    copies = [
        sent(0, part.at[bd, :, lo], got.at[0, :, lo], xn),
        sent(1, part.at[bd, :, hi], got.at[0, :, hi], yn),
    ]
    for copy in copies:
        copy.start()
    pieces.catch_up()
    work(bx)
    sent(1, part.at[bx, :, hi], got.at[0, :, hi], yn).wait_recv()
    part[bx, :, half:, :] = (
        part[bx, :, half:, :].astype(F32) + got[0, :, half:, :].astype(F32)
    ).astype(BF16)
    more = [sent(2, part.at[bx], got.at[1], xn)]
    more[0].start()
    copies += more
    work(by)
    sent(0, part.at[by, :, lo], got.at[0, :, lo], xn).wait_recv()
    part[by, :, :half, :] = (
        part[by, :, :half, :].astype(F32) + got[0, :, :half, :].astype(F32)
    ).astype(BF16)
    more = [sent(3, part.at[by], got.at[2], yn)]
    more[0].start()
    copies += more
    update(c, True)
    load.wait()

    cosine, sine = rope_factors(tab[...])

    def turn_back(i):
        inverse = inv_ref[:, i : i + 1]
        row_dot = jnp.zeros((span, 1), F32)
        for h in range(heads):
            lanes = slice(h * HEAD_DIM, (h + 1) * HEAD_DIM)
            source = dq_ref if i == 0 else acc.at[0]
            v = source[:, lanes]
            v = v * cosine - pltpu.roll(v, HALF, 1) * sine
            values = proj_ref[i, :, lanes]
            dgain_ref[i : i + 1, lanes] = jnp.sum(v * values * inverse, axis=0, keepdims=True)
            v = v * gain_ref[i : i + 1, lanes]
            source[:, lanes] = v
            row_dot = row_dot + jnp.sum(values * v, axis=-1, keepdims=True)
        return row_dot

    dots_q = turn_back(0)
    sent(2, part.at[bx], got.at[1], xn).wait_recv()
    sent(3, part.at[by], got.at[2], yn).wait_recv()
    acc[...] += got[1].astype(F32) + got[2].astype(F32)
    dproj_ref[2] = acc[1].astype(BF16)
    dots_k = turn_back(1)
    total = exchange_rows(n, to_rows(dots_q, dots_k), msg, m_send, m_recv)
    means = to_columns(total) / width
    for i in range(2):
        inverse = inv_ref[:, i : i + 1]
        factor = inverse**3 * means[:, i : i + 1]
        source = dq_ref if i == 0 else acc.at[0]
        dproj_ref[i] = (inverse * source[...] - proj_ref[i] * factor).astype(BF16)
    pieces.finish()
    late.plane.finish(1)
    for copy in copies:
        copy.wait_send()


def attend_back(
    n, q, kvall, d_out, attn32, lse, bound, proj, inv, gain, table, late, grads
):
    span, cols = q.shape
    heads = cols // HEAD_DIM
    width, ff = late[0].shape[1], late[2].shape[2]
    return pl.pallas_call(
        functools.partial(attend_back_kernel, n),
        out_shape=(shape((3, span, cols), BF16), shape((2, cols), F32))
        + tuple(shape(g.shape, BF16) for g in grads),
        in_specs=[VM] * 9 + [HB] * 8,
        out_specs=(VM, VM, HB, HB, HB),
        input_output_aliases={14: 2, 15: 3, 16: 4},
        scratch_shapes=[
            pltpu.VMEM((span, cols), F32),
            pltpu.VMEM((4, 2, span, cols), BF16),
            pltpu.VMEM((3, 2, span, cols), BF16),
            pltpu.VMEM((2, span, cols), F32),
            pltpu.VMEM((heads, 8, span), F32),
            pltpu.VMEM((span, 128), F32),
            pltpu.VMEM((n, 8, span), F32),
        ]
        + LatePiece.scratch(span, width, ff)
        + [
            pltpu.SemaphoreType.DMA((4,)),
            pltpu.SemaphoreType.DMA((4,)),
            pltpu.SemaphoreType.DMA,
            pltpu.SemaphoreType.DMA((n - 1,)),
            pltpu.SemaphoreType.DMA((n - 1,)),
        ],
        compiler_params=pltpu.CompilerParams(
            collective_id=3, has_side_effects=True, vmem_limit_bytes=VMEM_LIMIT
        ),
        name="attend_back",
    )(q, kvall, d_out, attn32, lse, bound, proj, inv, gain, table, *late, *grads)


def load_blocks(src, dst, sem, axis):
    blocks = src.shape[0]
    size = dst.shape[axis] // blocks
    copies = []
    for b in range(blocks):
        where = [slice(None)] * len(dst.shape)
        where[axis] = pl.ds(b * size, size)
        copies.append(pltpu.make_async_copy(src.at[b], dst.at[tuple(where)], sem.at[b]))
    for copy in copies:
        copy.start()
    return copies


def wait_all(copies):
    for copy in copies:
        copy.wait()


def mlp_in_kernel(
    n,
    attn_ref,
    wo_ref,
    x_ref,
    gain_ref,
    wga_ref,
    wgb_ref,
    gu_ref,
    down_ref,
    branch_out,
    resid_out,
    group_out,
    gate_out,
    up_out,
    hidden_out,
    wgc_out,
    wd_out,
    wo,
    wg,
    group,
    branch,
    resid,
    gate,
    up,
    hidden,
    part,
    got_rows,
    sem_o,
    local_sem,
    keep_sem,
    w_send,
    w_recv,
    *sems,
):
    s, c, u = where_am_i()
    rows, width = x_ref.shape
    load_o = load_blocks(wo_ref, wo, sem_o, 1)
    kb = wgc_out.shape[1]
    load_g = [
        pltpu.make_async_copy(wga_ref, wg.at[0, :, pl.ds(0, kb // 2)], local_sem.at[0]),
        pltpu.make_async_copy(wgb_ref, wg.at[0, :, pl.ds(kb // 2, kb // 2)], local_sem.at[1]),
        pltpu.make_async_copy(wgc_out, wg.at[1], local_sem.at[2]),
    ]
    greet(line_peers(n) + plane_peers() + [(None, (1 - s, c, u))])

    def plane(k, src, out, half_rows):
        return PlaneGather(
            src, lambda b: out.at[b], half_rows, w_send.at[k], w_recv.at[k], local_sem.at[3 + k]
        )

    first = plane(0, gu_ref.at[1], wgc_out, kb // 2)
    second = plane(1, down_ref, wd_out, down_ref.shape[0] // 2)
    first.start()
    load_g[0].start()
    load_g[1].start()
    wait_all(load_o)
    halves = Halves(n, rows)
    half = rows // 2
    per_half = part.shape[0] // 2
    chunk_cols = part.shape[2]

    def compute(chunk):
        h, q = divmod(chunk, per_half)
        cols = slice(q * chunk_cols, (q + 1) * chunk_cols)

        def tile(index, start, size):
            part[chunk, start : start + size, :] = dot(
                halves.load(attn_ref, index), wo[:, cols], NN
            ).astype(BF16)

        halves.each(h, tile)

    reduce = LineReduce(n, half, part, got_rows, sems[:4])
    gathers = [LineGather(n, rows, group, sems[4:], (h, half)) for h in range(2)]
    kept = []

    def keep(src, dst):
        copy = pltpu.make_async_copy(src, dst, keep_sem.at[len(kept)])
        copy.start()
        kept.append(copy)

    def finish(h):
        where = slice(h * half, (h + 1) * half)
        reduce.last(branch.at[h], range(h * per_half, (h + 1) * per_half))
        values = branch[h]
        total = x_ref[where, :].astype(F32) + values * inverse_rms(values) * gain_ref[0:1, :]
        resid[h] = total
        group[pl.ds(u, 1), where, :] = total.astype(BF16)[None]

    ff = gate.shape[2]
    ntile, tsize = tiles(ff, 512)

    def body(h, t):
        lanes = slice(t * tsize, (t + 1) * tsize)

        def tile(index, start, size):
            inputs = halves.load(group, index)
            gates = dot(inputs, wg[0, :, :, lanes].reshape(width, tsize), NN)
            ups = dot(inputs, wg[1, :, :, lanes].reshape(width, tsize), NN)
            halves.store(gate, index, lanes, gates.astype(BF16))
            halves.store(up, index, lanes, ups.astype(BF16))
            halves.store(
                hidden, index, lanes, (gates * jax.nn.sigmoid(gates) * ups).astype(BF16)
            )

        halves.each(h, tile)
        if h == 1:
            for src, dst in ((hidden, hidden_out), (gate, gate_out), (up, up_out)):
                keep(src.at[:, :, lanes], dst.at[:, :, lanes])

    def hook(label):
        if label == "b1":
            first.middle()
            second.start()
        if label == "first":
            keep(branch, branch_out)
            keep(resid, resid_out)
            first.corner()
            first.arrive()
            load_g[2].start()
            wait_all(load_g)
        if label == f"g{n - 2}":
            keep(group, group_out)
        if label == "t0":
            second.middle()

    reduce_norm_gather(n, reduce, gathers, compute, finish, Consume(ntile, body), hook)
    second.corner()
    second.arrive()
    for work in (first, second):
        work.finish()
    wait_all(kept)


def reduce_scratch(n, rows, width):
    cols = width // CHUNKS
    return [
        pltpu.VMEM((CHUNKS, n * rows, cols), BF16),
        pltpu.VMEM((CHUNKS, (n + 1) * rows, cols), BF16),
    ]


def half_scratch(n, rows, width):
    half, cols = rows // 2, width // 2
    return [
        pltpu.VMEM((4, n * half, cols), BF16),
        pltpu.VMEM((4, (n + 1) * half, cols), BF16),
    ]


def mlp_in(n, attn, wo, x, gain, wga, wgb, gu, down):
    rows, width = x.shape
    span, cols = attn.shape
    kb, ff = gu.shape[1:]
    ntile = tiles(ff, 512)[0]
    outs = pl.pallas_call(
        functools.partial(mlp_in_kernel, n),
        out_shape=(
            shape((2, rows // 2, width), F32),
            shape((2, rows // 2, width), F32),
            shape((n, rows, width), BF16),
            shape((n, rows, ff), BF16),
            shape((n, rows, ff), BF16),
            shape((n, rows, ff), BF16),
            shape((8, kb, ff), BF16),
            shape((8,) + down.shape, BF16),
        ),
        in_specs=[VM, HB, VM, VM, HB, HB, HB, HB],
        out_specs=(HB,) * 8,
        scratch_shapes=[
            pltpu.VMEM((cols, width), BF16),
            pltpu.VMEM((2, 8, kb, ff), BF16),
            pltpu.VMEM((n, rows, width), BF16),
            pltpu.VMEM((2, rows // 2, width), F32),
            pltpu.VMEM((2, rows // 2, width), F32),
            pltpu.VMEM((n, rows, ff), BF16),
            pltpu.VMEM((n, rows, ff), BF16),
            pltpu.VMEM((n, rows, ff), BF16),
        ]
        + half_scratch(n, rows, width)
        + [
            pltpu.SemaphoreType.DMA((8,)),
            pltpu.SemaphoreType.DMA((5,)),
            pltpu.SemaphoreType.DMA((3 + 3 * ntile,)),
            pltpu.SemaphoreType.DMA((2, 9)),
            pltpu.SemaphoreType.DMA((2, 9)),
        ]
        + line_sems(n, 4)
        + line_sems(n, 2),
        compiler_params=pltpu.CompilerParams(
            collective_id=4, has_side_effects=True, vmem_limit_bytes=VMEM_LIMIT
        ),
        name="mlp_in",
    )(attn.reshape(n, rows, cols), wo, x, gain, wga, wgb, gu, down)
    return outs


def mlp_out_kernel(
    n,
    hidden_ref,
    wd_ref,
    resid_ref,
    gain_ref,
    cot_ref,
    gate_hbm,
    up_hbm,
    gresid_ref,
    out_ref,
    group_out,
    dgu_out,
    dgain_ref,
    hidden_s,
    resid_s,
    dmlp_s,
    dgu_s,
    wd,
    mlp,
    group,
    gate_ref,
    up_ref,
    dgu,
    part,
    got_rows,
    sem_d,
    local_sem,
    keep_sem,
    s_send,
    s_recv,
    *sems,
):
    s, c, u = where_am_i()
    rows, width = cot_ref.shape
    load_d = load_blocks(wd_ref, wd, sem_d, 1)
    load_g = [
        pltpu.make_async_copy(gate_hbm, gate_ref, local_sem.at[0]),
        pltpu.make_async_copy(up_hbm, up_ref, local_sem.at[1]),
    ]
    greet(line_peers(n) + [(None, (1 - s, c, u))])
    sibling = Sibling(s_send, s_recv)
    halves = Halves(n, rows)
    half = rows // 2
    per_half = part.shape[0] // 2
    chunk_cols = part.shape[2]

    def compute(chunk):
        h, q = divmod(chunk, per_half)
        cols = slice(q * chunk_cols, (q + 1) * chunk_cols)
        if h == 0:
            wait_all(load_d[q * (8 // per_half) : (q + 1) * (8 // per_half)])

        def tile(index, start, size):
            part[chunk, start : start + size, :] = dot(
                halves.load(hidden_ref, index), wd[:, cols], NN
            ).astype(BF16)

        halves.each(h, tile)

    reduce = LineReduce(n, half, part, got_rows, sems[:4])
    gathers = [LineGather(n, rows, group, sems[4:], (h, half)) for h in range(2)]
    dgain_ref[...] = jnp.zeros_like(dgain_ref)

    def finish(h):
        where = slice(h * half, (h + 1) * half)
        reduce.last(mlp.at[h], range(h * per_half, (h + 1) * per_half))
        values = mlp[h]
        grad = cot_ref[where, :].astype(F32)
        d_mlp = norm_back(values, inverse_rms(values), grad * gain_ref[1:2, :], width)
        group[pl.ds(u, 1), where, :] = d_mlp.astype(BF16)[None]

    def rest(h):
        where = slice(h * half, (h + 1) * half)
        values = mlp[h]
        scaled = values * inverse_rms(values)
        out_ref[where, :] = (resid_ref[h] + scaled * gain_ref[1:2, :]).astype(BF16)
        dgain_ref[...] += jnp.sum(cot_ref[where, :].astype(F32) * scaled, axis=0, keepdims=True)

    ff = gate_ref.shape[2]
    ntile, tsize = tiles(ff, 512)
    kept = []

    def keep(src, dst):
        copy = pltpu.make_async_copy(src, dst, keep_sem.at[len(kept)])
        copy.start()
        kept.append(copy)

    def body(h, t):
        lanes = slice(t * tsize, (t + 1) * tsize)

        def tile(index, start, size):
            d_hidden = dot(halves.load(group, index), wd[lanes, :], NT)
            gate = halves.load(gate_ref, index, lanes).astype(F32)
            up = halves.load(up_ref, index, lanes).astype(F32)
            sig = jax.nn.sigmoid(gate)
            slope = sig * (1.0 + gate * (1.0 - sig))
            halves.store(dgu.at[0], index, lanes, (d_hidden * up * slope).astype(BF16))
            halves.store(dgu.at[1], index, lanes, (d_hidden * (gate * sig)).astype(BF16))

        halves.each(h, tile)
        where = pl.ds(h * half, half)
        view = dgu.at[:, :, where, lanes]
        sibling.start(view, dgu_s.at[:, :, where, lanes])
        keep(view, dgu_out.at[:, :, where, lanes])

    def hook(label):
        if label == "sent":
            sibling.start(hidden_ref, hidden_s)
            lanes = pl.ds(pl.multiple_of((1 - s) * (width // 2), width // 2), width // 2)
            sibling.start(gresid_ref.at[:, :, lanes], resid_s)
            for copy in load_g:
                copy.start()
        if label == "half":
            rest(0)
        if label == "first":
            rest(1)
            wait_all(load_g)
        if label == f"g{n - 2}":
            lanes = pl.ds(pl.multiple_of((1 - s) * (width // 2), width // 2), width // 2)
            sibling.start(group.at[:, :, lanes], dmlp_s)
            keep(group, group_out)

    reduce_norm_gather(n, reduce, gathers, compute, finish, Consume(ntile, body), hook)
    for i in range(3 + 2 * ntile):
        sibling.wait(i)
    sibling.finish()
    wait_all(kept)


def mlp_out(n, hidden, wd, resid, gain, cot, gate, up, gresid):
    rows, width = cot.shape
    ff = hidden.shape[2]
    ntile = tiles(ff, 512)[0]
    return pl.pallas_call(
        functools.partial(mlp_out_kernel, n),
        out_shape=(
            shape((rows, width), BF16),
            shape((n, rows, width), BF16),
            shape((2, n, rows, ff), BF16),
            shape((1, width), F32),
            shape((n, rows, ff), BF16),
            shape((n, rows, width // 2), BF16),
            shape((n, rows, width // 2), BF16),
            shape((2, n, rows, ff), BF16),
        ),
        in_specs=[VM, HB, VM, VM, VM, HB, HB, HB],
        out_specs=(VM, HB, HB, VM, HB, HB, HB, HB),
        scratch_shapes=[
            pltpu.VMEM((ff, width), BF16),
            pltpu.VMEM((2, rows // 2, width), F32),
            pltpu.VMEM((n, rows, width), BF16),
            pltpu.VMEM((n, rows, ff), BF16),
            pltpu.VMEM((n, rows, ff), BF16),
            pltpu.VMEM((2, n, rows, ff), BF16),
        ]
        + half_scratch(n, rows, width)
        + [
            pltpu.SemaphoreType.DMA((8,)),
            pltpu.SemaphoreType.DMA((2,)),
            pltpu.SemaphoreType.DMA((1 + 2 * ntile,)),
            pltpu.SemaphoreType.DMA((3 + 2 * ntile,)),
            pltpu.SemaphoreType.DMA((3 + 2 * ntile,)),
        ]
        + line_sems(n, 4)
        + line_sems(n, 2),
        compiler_params=pltpu.CompilerParams(
            collective_id=5, has_side_effects=True, vmem_limit_bytes=VMEM_LIMIT
        ),
        name="mlp_out",
    )(hidden, wd, resid, gain, cot, gate, up, gresid)


def mlp_back_kernel(
    n,
    dgu_hbm,
    wga_ref,
    wgb_ref,
    wgc_ref,
    cot_ref,
    branch_ref,
    gain_ref,
    wo_ref,
    hidden_hbm,
    dmlp_hbm,
    resid_hbm,
    hidden_s_hbm,
    dmlp_s_hbm,
    resid_s_hbm,
    dgu_s_hbm,
    dresid_ref,
    group_out,
    dattn_ref,
    dgain_ref,
    gown_out,
    gx_out,
    gy_out,
    down_own_out,
    down_x_out,
    down_y_out,
    wo,
    wg,
    group,
    part,
    got_rows,
    dgu_ref,
    hidden,
    hidden_s,
    dmlp,
    dmlp_s,
    gate_in,
    ring_d,
    ring_g,
    got_d,
    got_g,
    sem_o,
    sem_in,
    local_sem,
    d_send,
    d_recv,
    d_local,
    g_send,
    g_recv,
    g_local,
    *sems,
):
    s, c, u = where_am_i()
    rows, width = cot_ref.shape
    half = wga_ref.shape[1]
    chunk_cols = width // part.shape[0]
    per_chunk = chunk_cols // (2 * half)
    chunks = part.shape[0]

    def load_chunk(chunk):
        slot = chunk % 2
        where = pl.ds(chunk * per_chunk, per_chunk)
        return [
            pltpu.make_async_copy(
                wga_ref.at[where], wg.at[slot, 0, :, pl.ds(0, half)], local_sem.at[slot, 0]
            ),
            pltpu.make_async_copy(
                wgb_ref.at[where], wg.at[slot, 0, :, pl.ds(half, half)], local_sem.at[slot, 1]
            ),
            pltpu.make_async_copy(wgc_ref.at[where], wg.at[slot, 1], local_sem.at[slot, 2]),
        ]

    def start_chunk(chunk):
        for copy in load_chunk(chunk):
            copy.start()

    def fetch(k, src, dst):
        copy = pltpu.make_async_copy(src, dst, sem_in.at[k])
        copy.start()
        return copy

    load_dgu = fetch(0, dgu_hbm, dgu_ref)
    start_chunk(0)
    load_d = [
        fetch(1, hidden_hbm, hidden),
        fetch(2, half_columns(dmlp_hbm, s), dmlp),
        fetch(3, hidden_s_hbm, hidden_s),
        fetch(4, dmlp_s_hbm, dmlp_s),
    ]
    start_chunk(1)
    load_g = []
    if gate_in:
        resid, resid_s, dgu_s = gate_in
        load_g = [
            fetch(5, half_columns(resid_hbm, s), resid),
            fetch(6, resid_s_hbm, resid_s),
            fetch(7, dgu_s_hbm, dgu_s),
        ]
    load_o = load_blocks(wo_ref, wo, sem_o, 1)
    greet(line_peers(n) + plane_peers())
    load_dgu.wait()
    span = n * rows
    count, size = tiles(span, 512)

    def compute(chunk):
        wait_all(load_chunk(chunk))
        slot = chunk % 2

        def tile(i, carry):
            where = pl.ds(pl.multiple_of(i * size, size), size)
            part[chunk, where, :] = (
                dot(dgu_ref[0, where, :], wg[slot, 0].reshape(chunk_cols, -1), NT)
                + dot(dgu_ref[1, where, :], wg[slot, 1].reshape(chunk_cols, -1), NT)
            ).astype(BF16)
            return carry

        lax.fori_loop(0, count, tile, 0)
        if chunk + 2 < chunks:
            start_chunk(chunk + 2)

    rows_d, cols_g = ring_d.shape[2], ring_g.shape[3]
    tiles_g = dgu_hbm.shape[2] // cols_g

    def place_d(out, piece, part):
        size = rows_d if part is None else rows_d // 2
        return out.at[pl.ds(piece * rows_d + (part or 0) * size, size)]

    def place_g(out, piece, part):
        size = ring_g.shape[2] if part is None else ring_g.shape[2] // 2
        ci, tile = piece // tiles_g, piece % tiles_g
        return out.at[ci, pl.ds((part or 0) * size, size), pl.ds(tile * cols_g, cols_g)]

    down = PlaneReduce(
        ring_d, got_d, (down_own_out, down_x_out, down_y_out), place_d, d_send, d_recv, d_local
    )
    gate = PlaneReduce(ring_g, got_g, (gown_out, gx_out, gy_out), place_g, g_send, g_recv, g_local)
    down_piece = wide_piece(
        (hidden, dmlp), (hidden_s, dmlp_s), lambda p: slice(p * rows_d, (p + 1) * rows_d)
    )

    def gate_right(ref, piece):
        tile = piece % tiles_g
        return ref[piece // tiles_g, :, tile * cols_g : (tile + 1) * cols_g]

    n_d, n_g = got_d.shape[0], got_g.shape[0] if gate_in else 0
    work = [(down, p, down_piece) for p in range(n_d)]
    if gate_in:
        gate_piece = tall_piece((resid, dgu_ref), (resid_s, dgu_s), gate_right)
        work += [(gate, p, gate_piece) for p in range(n_g)]
    pieces = Pieces(work)

    def compute_and_piece(chunk):
        compute(chunk)
        if chunk == 0:
            wait_all(load_d)
        if chunk < 2:
            pieces.step()

    def reduce_hook(slot):
        if slot == 0:
            wait_all(load_g)
        pieces.step()

    LineReduce(n, rows, part, got_rows, sems[:4]).run(compute_and_piece, dresid_ref, reduce_hook)
    d_resid = dresid_ref[...] + cot_ref[...].astype(F32)
    dresid_ref[...] = d_resid
    branch = branch_ref[...]
    inverse = inverse_rms(branch)
    d_branch = norm_back(branch, inverse, d_resid * gain_ref[0:1, :], width)
    small = group.shape[0] == span
    if small:
        group[rows_of(u, rows), :] = d_branch.astype(BF16)
        gather = LineGather(n, rows, group, sems[4:])
    else:
        group[:rows, :] = d_branch.astype(BF16)
        own = pltpu.make_async_copy(
            group.at[pl.ds(0, rows)], group_out.at[rows_of(u, rows)], local_sem.at[2, 2]
        )
        own.start()
        own.wait()
        gather = LineGather(n, rows, group_out, sems[4:])
    gather.send(0)
    dgain_ref[...] = jnp.sum(d_resid * branch * inverse, axis=0, keepdims=True)
    wait_all(load_o)
    pieces.step()

    def gather_hook(slot):
        pieces.step()

    gather.run(gather_hook)
    if small:
        keep = pltpu.make_async_copy(group, group_out, local_sem.at[2, 2])
        keep.start()

    def tile(j, carry):
        where = pl.ds(pl.multiple_of(j * size, size), size)
        if small:
            rows_in = group[where, :]
        else:
            fetch = pltpu.make_async_copy(group_out.at[where], group, local_sem.at[2, 2])
            fetch.start()
            fetch.wait()
            rows_in = group[...]
        d_attn = dot(rows_in, wo[...], NT).astype(BF16)
        if len(dattn_ref.shape) == 3:
            cols = dattn_ref.shape[2]
            for q in range(4):
                dattn_ref[q, where, :] = d_attn[:, q * cols : (q + 1) * cols]
        else:
            dattn_ref[where, :] = d_attn
        return carry

    lax.fori_loop(0, count, tile, 0)
    pieces.finish()
    down.finish(n_d)
    gate.finish(n_g)
    if small:
        keep.wait()


def piece_scratch(slots, pieces, rows, cols):
    return (
        [pltpu.VMEM((slots, 4, rows, cols), BF16), pltpu.VMEM((pieces, rows, cols), BF16)],
        [
            pltpu.SemaphoreType.DMA((pieces, 6)),
            pltpu.SemaphoreType.DMA((pieces, 6)),
            pltpu.SemaphoreType.DMA((pieces,)),
        ],
    )


def mlp_back(
    n,
    dgu,
    wga,
    wgb,
    wgc,
    cot,
    branch,
    gain,
    wo,
    hidden,
    dmlp,
    resid,
    hidden_s,
    resid_s,
    dmlp_s,
    dgu_s,
):
    rows, width = branch.shape
    span, ff = dgu.shape[1:]
    cols = wo.shape[1]
    kb, kc = width // 8, wo.shape[2]
    count, size = tiles(ff, 512)
    ring_d, sems_d = piece_scratch(min(3, count), count, size, kc)
    here = 2 * count - LATER
    ring_g, sems_g = piece_scratch(min(3, max(here, 1)), max(here, 1), kb, size)
    chunk_blocks = width // CHUNKS // kb
    return pl.pallas_call(
        functools.partial(mlp_back_kernel, n),
        out_shape=(
            shape((rows, width), F32),
            shape((span, width), BF16),
            shape((4, span, cols // 4) if spread_heads(cols) else (span, cols), BF16),
            shape((1, width), F32),
        )
        + (shape((2, kb, ff), BF16),) * 3
        + (shape((ff, kc), BF16),) * 3,
        in_specs=[HB, HB, HB, HB, VM, VM, VM] + [HB] * 8,
        out_specs=(VM, HB, VM, VM) + (HB,) * 6,
        scratch_shapes=[
            pltpu.VMEM((cols, width), BF16),
            pltpu.VMEM((2, 2, chunk_blocks, kb, ff), BF16),
            pltpu.VMEM((min(span, 512), width), BF16),
        ]
        + reduce_scratch(n, rows, width)
        + [
            pltpu.VMEM((2, span, ff), BF16),
            pltpu.VMEM((span, ff), BF16),
            pltpu.VMEM((span, ff), BF16),
            pltpu.VMEM((span, width // 2), BF16),
            pltpu.VMEM((span, width // 2), BF16),
            (
                pltpu.VMEM((span, width // 2), BF16),
                pltpu.VMEM((span, width // 2), BF16),
                pltpu.VMEM((2, span, ff), BF16),
            )
            if here > 0
            else (),
            ring_d[0],
            ring_g[0],
            ring_d[1],
            ring_g[1],
            pltpu.SemaphoreType.DMA((8,)),
            pltpu.SemaphoreType.DMA((8,)),
            pltpu.SemaphoreType.DMA((3, 3)),
        ]
        + sems_d
        + sems_g
        + line_sems(n, CHUNKS)
        + line_sems(n),
        compiler_params=pltpu.CompilerParams(
            collective_id=6, has_side_effects=True, vmem_limit_bytes=VMEM_LIMIT
        ),
        name="mlp_back",
    )(
        dgu,
        wga,
        wgb,
        wgc,
        cot,
        branch,
        gain,
        wo,
        hidden,
        dmlp,
        resid,
        hidden_s,
        dmlp_s,
        resid_s,
        dgu_s,
    )


def proj_back_kernel(
    n,
    dproj_ref,
    wq_ref,
    dresid_ref,
    xg_ref,
    gcols_ref,
    gattn_ref,
    gmlp_ref,
    attn_ref,
    dbranch_ref,
    resid_hbm,
    resid_s_hbm,
    dgu_hbm,
    dgu_s_hbm,
    own_in,
    x_in,
    y_in,
    out_ref,
    gain_ref,
    own_out,
    x_out,
    y_out,
    oown_out,
    ox_out,
    oy_out,
    gown_out,
    gx_out,
    gy_out,
    wq,
    xs,
    xs_s,
    dproj_s,
    dbranch,
    dbranch_s,
    attn_s,
    total,
    part,
    got_rows,
    ring,
    got,
    sums,
    ring_o,
    got_o,
    late_buffers,
    late_sems,
    o_sems,
    local_sem,
    s_send,
    s_recv,
    q_send,
    q_recv,
    q_local,
    v_send,
    v_recv,
    m_send,
    m_recv,
    *sems,
):
    s, c, u = where_am_i()
    rows, width = dresid_ref.shape
    span = n * rows
    load = [
        pltpu.make_async_copy(wq_ref, wq, local_sem.at[0]),
        pltpu.make_async_copy(half_columns(xg_ref, s), xs, local_sem.at[1]),
        pltpu.make_async_copy(half_columns(dbranch_ref, s), dbranch, local_sem.at[2]),
    ]
    last = 2 * (dgu_hbm.shape[2] // late_buffers[2].shape[1])
    late = LatePiece(
        last - 1,
        (resid_hbm, resid_s_hbm, dgu_hbm, dgu_s_hbm),
        (gown_out, gx_out, gy_out),
        late_buffers,
        late_sems,
    )
    late.load()
    for copy in load:
        copy.start()
    corner = (s, c ^ 3, u)
    greet(all_uly_peers(n) + plane_peers() + [(None, corner), (None, (1 - s, c, u))])
    gains = GainSum(n, sums, (v_send, v_recv, m_send, m_recv))
    gains.start(gcols_ref, gattn_ref, gmlp_ref)
    sibling = Sibling(s_send, s_recv)
    sibling.start(attn_ref, attn_s)
    sibling.start(half_columns(dbranch_ref, 1 - s), dbranch_s)
    sibling.start(half_columns(xg_ref, 1 - s), xs_s)
    sibling.start(dproj_ref, dproj_s)
    load[0].wait()
    chunk_cols = width // part.shape[0]
    count, size = tiles(span, 512)

    def compute(chunk):
        cols = slice(chunk * chunk_cols, (chunk + 1) * chunk_cols)

        def tile(i, carry):
            where = pl.ds(pl.multiple_of(i * size, size), size)
            part[chunk, where, :] = (
                dot(dproj_ref[0, where, :], wq[0, cols, :], NT)
                + dot(dproj_ref[1, where, :], wq[1, cols, :], NT)
                + dot(dproj_ref[2, where, :], wq[2, cols, :], NT)
            ).astype(BF16)
            return carry

        lax.fori_loop(0, count, tile, 0)

    def place(out, piece, part):
        size = ring.shape[2] if part is None else ring.shape[2] // 2
        return out.at[piece, pl.ds((part or 0) * size, size)]

    weight = PlaneReduce(ring, got, (own_out, x_out, y_out), place, q_send, q_recv, q_local)
    compute_piece = tall_piece((xs, dproj_ref), (xs_s, dproj_s), lambda ref, piece: ref[piece])

    def place_o(out, piece, part):
        size = ring_o.shape[2] if part is None else ring_o.shape[2] // 2
        return out.at[pl.ds((part or 0) * size, size)]

    out_weight = PlaneReduce(ring_o, got_o, (oown_out, ox_out, oy_out), place_o, *o_sems)
    out_piece = wide_piece((attn_ref, dbranch), (attn_s, dbranch_s), lambda p: slice(None))
    pieces = Pieces(
        [late.work(), (out_weight, 0, out_piece)] + [(weight, p, compute_piece) for p in range(3)]
    )

    def compute_and_piece(chunk):
        compute(chunk)
        if chunk == 0:
            pieces.step()
        if chunk == 2:
            load[2].wait()
            sibling.wait(0)
            sibling.wait(1)
            pieces.step()

    def hook(slot):
        if slot == 0:
            load[1].wait()
            sibling.wait(2)
            sibling.wait(3)
            pieces.step()
            gains.over_ctx()
        if slot == 1:
            pieces.step()
            gains.over_uly()
        if slot == 2:
            pieces.step()

    LineReduce(n, rows, part, got_rows, sems[:4]).run(compute_and_piece, total, hook)
    out_ref[...] = (dresid_ref[...] + total[...]).astype(BF16)
    pieces.finish()
    gains.finish(gain_ref)
    weight.finish(3)
    out_weight.finish(1)
    late.plane.finish(1)
    sibling.finish()


class GainSum:
    def __init__(self, n, refs, sems):
        self.n = n
        self.all, self.core, self.plane, self.line = refs
        self.v_send, self.v_recv, self.m_send, self.m_recv = sems
        self.s, self.c, self.u = where_am_i()
        self.sent = []

    def copy(self, k, src, dst, peer):
        return remote(src, dst, self.v_send.at[k], self.v_recv.at[k], peer)

    def go(self, copy):
        copy.start()
        self.sent.append(copy)

    def start(self, cols, attn, mlp):
        half, local = self.all.shape[2], cols.shape[1]
        rows = jnp.zeros((8, half), F32)
        for h in range(2):
            self.all[h] = rows
        mine = self.u * local
        home = pl.ds(pl.multiple_of(lax.rem(mine, half), local), local)
        self.all[pl.ds(mine // half, 1), 0:2, home] = cols[...][None]
        for h in range(2):
            part = slice(h * half, (h + 1) * half)
            self.all[h, 2:3, :] = attn[:, part]
            self.all[h, 3:4, :] = mlp[:, part]
        self.go(self.copy(0, self.all.at[1 - self.s], self.core, (1 - self.s, self.c, self.u)))

    def over_ctx(self):
        s, c, u = self.s, self.c, self.u
        self.copy(0, self.all.at[s], self.core, (1 - s, c, u)).wait_recv()
        size = self.plane.shape[2]
        total = self.all[pl.ds(s, 1)][0] + self.core[...]
        for j in range(4):
            self.plane[j] = total[:, j * size : (j + 1) * size]
        for k in (1, 2, 3):
            self.go(self.copy(k, self.plane.at[c ^ k], self.line.at[k - 1], (s, c ^ k, u)))

    def over_uly(self):
        s, c, u = self.s, self.c, self.u
        total = self.plane[pl.ds(c, 1)][0]
        for k in (1, 2, 3):
            self.copy(k, self.plane.at[c ^ k], self.line.at[k - 1], (s, c ^ k, u)).wait_recv()
            total = total + self.line[k - 1]
        home = self.line.at[3 + u]
        self.line[pl.ds(3 + u, 1)] = total[None]
        for step in range(1, self.n):
            peer = (s, c, lax.rem(u + step, self.n))
            self.go(remote(home, home, self.m_send.at[step - 1], self.m_recv.at[step - 1], peer))

    def finish(self, out):
        s, c, u = self.s, self.c, self.u
        for step in range(1, self.n):
            source = lax.rem(u + self.n - step, self.n)
            place = self.line.at[3 + source]
            remote(
                place, place, self.m_send.at[step - 1], self.m_recv.at[step - 1], (s, c, source)
            ).wait_recv()
        total = self.line[3]
        for j in range(1, self.n):
            total = total + self.line[3 + j]
        out[...] = total[:4]
        for copy in self.sent:
            copy.wait_send()


def proj_back(
    n, dproj, wq, dresid, xg, gain_cols, gain_attn, gain_mlp, attn, dbranch, late, grads
):
    rows, width = dresid.shape
    span, cols = dproj.shape[1:]
    ring, sems = piece_scratch(3, 3, width // 8, cols)
    ring_o, sems_o = piece_scratch(1, 1, cols, width // 8)
    ff = late[2].shape[2]
    return pl.pallas_call(
        functools.partial(proj_back_kernel, n),
        out_shape=(shape((rows, width), BF16), shape((4, width // 8), F32))
        + (shape((3, width // 8, cols), BF16),) * 3
        + (shape((cols, width // 8), BF16),) * 3
        + tuple(shape(g.shape, BF16) for g in grads),
        in_specs=[VM, HB, VM, HB, VM, VM, VM, VM] + [HB] * 8,
        out_specs=(VM, VM) + (HB,) * 9,
        input_output_aliases={13: 8, 14: 9, 15: 10},
        scratch_shapes=[
            pltpu.VMEM((3, width, cols), BF16),
            pltpu.VMEM((span, width // 2), BF16),
            pltpu.VMEM((span, width // 2), BF16),
            pltpu.VMEM((3, span, cols), BF16),
            pltpu.VMEM((span, width // 2), BF16),
            pltpu.VMEM((span, width // 2), BF16),
            pltpu.VMEM((span, cols), BF16),
            pltpu.VMEM((rows, width), F32),
        ]
        + reduce_scratch(n, rows, width)
        + ring
        + [
            (
                pltpu.VMEM((2, 8, width // 2), F32),
                pltpu.VMEM((8, width // 2), F32),
                pltpu.VMEM((4, 8, width // 8), F32),
                pltpu.VMEM((3 + n, 8, width // 8), F32),
            ),
        ]
        + ring_o
        + LatePiece.scratch(span, width, ff)
        + [
            tuple(sems_o),
            pltpu.SemaphoreType.DMA((3,)),
            pltpu.SemaphoreType.DMA((4,)),
            pltpu.SemaphoreType.DMA((4,)),
        ]
        + sems
        + [
            pltpu.SemaphoreType.DMA((4,)),
            pltpu.SemaphoreType.DMA((4,)),
            pltpu.SemaphoreType.DMA((n - 1,)),
            pltpu.SemaphoreType.DMA((n - 1,)),
        ]
        + line_sems(n, CHUNKS),
        compiler_params=pltpu.CompilerParams(
            collective_id=7, has_side_effects=True, vmem_limit_bytes=VMEM_LIMIT
        ),
        name="proj_back",
    )(
        dproj,
        wq,
        dresid,
        xg,
        gain_cols,
        gain_attn,
        gain_mlp,
        attn,
        dbranch,
        *late,
        *grads,
    )


def rope_table(length):
    freqs = np.power(
        np.float32(ROPE_BASE), -(np.arange(HALF, dtype=np.float32) * 2.0 / HEAD_DIM)
    ).astype(np.float32)
    angles = (np.arange(length, dtype=np.float32)[:, None] * freqs[None, :]).astype(np.float64)
    return np.concatenate([np.cos(angles), np.sin(angles)], axis=1).astype(np.float32)


def on_device(
    n,
    table,
    tokens,
    segment_ids,
    qkv_weight,
    out_weight,
    gate_up,
    down_weight,
    qk_gain,
    post_gain,
    cotangent,
):
    x = tokens[0]
    width = x.shape[1]
    cot = cotangent[0]
    table = jnp.asarray(table)
    group_x, wq, wo, wga, proj, qkv, inv, zero = project(
        n, x, qkv_weight, table, qk_gain, segment_ids, out_weight, gate_up
    )
    if len(qkv) == 1:
        every, wgb, attn, att, lse, bound = attend_spread(qkv[0], zero, gate_up)
        seen, back = (every,), attend_spread_back
    else:
        every, wgb, attn, att, lse, bound = attend(*qkv, zero, gate_up)
        seen, back = (qkv[0], every), attend_back
    branch, resid, group_resid, gate, up, hidden, wgc, wd = mlp_in(
        n, attn, wo, x, post_gain, wga, wgb, gate_up, down_weight
    )
    block_out, group_dmlp, dgu, gain_mlp, hidden_s, resid_s, dmlp_s, dgu_s = mlp_out(
        n, hidden, wd, resid, post_gain, cot, gate, up, group_resid
    )
    span, ff = n * x.shape[0], hidden.shape[2]
    branch = branch.reshape(x.shape)
    dgu, dgu_s = dgu.reshape(2, span, ff), dgu_s.reshape(2, span, ff)
    hidden, hidden_s = hidden.reshape(span, ff), hidden_s.reshape(span, ff)
    group_resid, group_dmlp = group_resid.reshape(span, width), group_dmlp.reshape(span, width)
    resid_s, dmlp_s = resid_s.reshape(span, width // 2), dmlp_s.reshape(span, width // 2)
    d_resid, group_dbranch, d_attn, gain_attn, *grads = mlp_back(
        n,
        dgu,
        wga,
        wgb,
        wgc,
        cot,
        branch,
        post_gain,
        wo,
        hidden,
        group_dmlp,
        group_resid,
        hidden_s,
        resid_s,
        dmlp_s,
        dgu_s,
    )
    gate_grads, down_grads = grads[:3], grads[3:]
    late = (group_resid, resid_s, dgu, dgu_s)
    d_proj, gain_cols, *gate_grads = back(
        n, *seen, d_attn, att, lse, bound, proj, inv, qk_gain, table, late, gate_grads
    )
    input_grad, gain_part, *grads = proj_back(
        n,
        d_proj,
        wq,
        d_resid,
        group_x,
        gain_cols,
        gain_attn,
        gain_mlp,
        attn,
        group_dbranch,
        late,
        gate_grads,
    )
    qkv_grads, out_grads, gate_grads = grads[:3], grads[3:6], grads[6:]

    def total(parts):
        return parts[0].astype(F32) + parts[1].astype(F32) + parts[2].astype(F32)

    return (
        block_out[None],
        input_grad[None],
        total(qkv_grads),
        total(out_grads),
        total(gate_grads),
        total(down_grads),
        gain_part,
    )


def solution(mesh):
    n = mesh.shape["uly"]
    in_specs = (
        P("slot", ("ctx", "uly"), None),
        P("slot", ("ctx", "uly")),
        P(None, ("slot", "ctx"), "uly"),
        P("uly", ("slot", "ctx")),
        P(None, ("slot", "ctx"), "uly"),
        P("uly", ("slot", "ctx")),
        P(None, "uly"),
        P(),
        P("slot", ("ctx", "uly"), None),
    )
    out_specs = (
        P("slot", ("ctx", "uly"), None),
        P("slot", ("ctx", "uly"), None),
        P(None, ("slot", "ctx"), "uly"),
        P("uly", ("slot", "ctx")),
        P(None, ("slot", "ctx"), "uly"),
        P("uly", ("slot", "ctx")),
        P(None, ("slot", "ctx")),
    )

    def whole(tokens, *rest):
        table = rope_table(tokens.shape[1])
        return jax.shard_map(
            functools.partial(on_device, n, table),
            mesh=mesh,
            in_specs=in_specs,
            out_specs=out_specs,
            check_vma=False,
        )(tokens, *rest)

    return whole
```

```python
import functools

import jax
import jax.numpy as jnp
import numpy as np
from jax import lax
from jax.experimental import pallas as pl
from jax.experimental.pallas import tpu as pltpu
from jax.sharding import PartitionSpec as P

HEAD_DIM = 128
HALF = HEAD_DIM // 2
EPS = 1e-06
ROPE_BASE = 500000.0
FLOOR = -1e30
LOG2E = 1.4426950408889634
SCALE2 = HEAD_DIM ** (-0.5) * LOG2E
MESH_ID = pl.DeviceIdType.MESH
BF16 = jnp.bfloat16
F32 = jnp.float32
VMEM_LIMIT = 62 * 1024 * 1024
CHUNKS = 4
AHEAD = 1
LATER = 2

VM = pl.BlockSpec(memory_space=pltpu.VMEM)
HB = pl.BlockSpec(memory_space=pl.ANY)


def shape(dims, dtype):
    return jax.ShapeDtypeStruct(dims, dtype)


def where_am_i():
    return lax.axis_index("slot"), lax.axis_index("ctx"), lax.axis_index("uly")


def rows_of(index, rows):
    return pl.ds(pl.multiple_of(index * rows, rows), rows)


def greet(peers):
    barrier = pltpu.get_barrier_semaphore()
    total = 0
    for condition, peer in peers:
        if condition is None:
            pl.semaphore_signal(barrier, inc=1, device_id=peer, device_id_type=MESH_ID)
            total = total + 1
        else:

            @pl.when(condition)
            def _():
                pl.semaphore_signal(barrier, inc=1, device_id=peer, device_id_type=MESH_ID)

            total = total + condition.astype(jnp.int32)
    pl.semaphore_wait(barrier, total)


def line_peers(n):
    s, c, u = where_am_i()
    return [(u > 0, (s, c, u - 1)), (u < n - 1, (s, c, u + 1))]


def plane_peers():
    s, c, u = where_am_i()
    return [(None, (s, c ^ 1, u)), (None, (s, c ^ 2, u))]


def remote(src, dst, send, recv, peer):
    return pltpu.make_async_remote_copy(
        src_ref=src,
        dst_ref=dst,
        send_sem=send,
        recv_sem=recv,
        device_id=peer,
        device_id_type=MESH_ID,
    )


def line_sems(n, chunks=None):
    dims = (n - 1,) if chunks is None else (n - 1, chunks)
    return [pltpu.SemaphoreType.DMA(dims)] * 4


class LineGather:
    def __init__(self, n, rows, buf, sems, part=None):
        self.n, self.rows, self.buf, self.sems, self.part = n, rows, buf, sems, part

    def copy(self, right, slot, shard):
        s, c, u = where_am_i()
        send_r, recv_r, send_l, recv_l = self.sems
        if self.part is None:
            view = self.buf.at[rows_of(shard, self.rows)]
        else:
            index, size = self.part
            view = self.buf.at[shard, pl.ds(index * size, size)]
            send_r, recv_r, send_l, recv_l = [sem.at[:, index] for sem in self.sems]
        if right:
            return remote(view, view, send_r.at[slot], recv_r.at[slot], (s, c, u + 1))
        return remote(view, view, send_l.at[slot], recv_l.at[slot], (s, c, u - 1))

    def send(self, slot):
        u, n = lax.axis_index("uly"), self.n

        @pl.when((u < n - 1) & (u - slot >= 0))
        def _():
            self.copy(True, slot, u - slot).start()

        @pl.when((u > 0) & (u + slot <= n - 1))
        def _():
            self.copy(False, slot, u + slot).start()

    def wait(self, slot):
        u, n = lax.axis_index("uly"), self.n

        @pl.when(u - 1 - slot >= 0)
        def _():
            self.copy(True, slot, u - 1 - slot).wait_recv()

        @pl.when(u + 1 + slot <= n - 1)
        def _():
            self.copy(False, slot, u + 1 + slot).wait_recv()

        if slot + 1 < n - 1:
            self.send(slot + 1)

    def finish(self):
        u, n = lax.axis_index("uly"), self.n
        for slot in range(n - 1):

            @pl.when((u < n - 1) & (u - slot >= 0))
            def _():
                self.copy(True, slot, u - slot).wait_send()

            @pl.when((u > 0) & (u + slot <= n - 1))
            def _():
                self.copy(False, slot, u + slot).wait_send()

    def run(self, hook=None):
        for slot in range(self.n - 1):
            self.wait(slot)
            if hook is not None:
                hook(slot)
        self.finish()


class LineReduce:
    def __init__(self, n, rows, part, got, sems):
        self.n, self.rows, self.sems = n, rows, sems
        self.part, self.got = part, got
        self.chunks = part.shape[0]

    def copy(self, right, slot, chunk, block):
        s, c, u = where_am_i()
        send_r, recv_r, send_l, recv_l = self.sems
        where = rows_of(block, self.rows)
        src = self.part.at[chunk, where]
        if right:
            return remote(
                src,
                self.got.at[chunk, rows_of(block + 1, self.rows)],
                send_r.at[slot, chunk],
                recv_r.at[slot, chunk],
                (s, c, u + 1),
            )
        return remote(
            src,
            self.got.at[chunk, where],
            send_l.at[slot, chunk],
            recv_l.at[slot, chunk],
            (s, c, u - 1),
        )

    def add(self, chunk, block, place):
        where = rows_of(block, self.rows)
        self.part[chunk, where, :] = (
            self.part[chunk, where, :].astype(F32)
            + self.got[chunk, rows_of(place, self.rows), :].astype(F32)
        ).astype(BF16)

    def step(self, slot, chunk):
        u, n = lax.axis_index("uly"), self.n
        block_r = n - 1 - slot + u
        block_l = slot - (n - 1) + u

        @pl.when(u <= slot)
        def _():
            if slot > 0:

                @pl.when(u > 0)
                def _():
                    self.copy(True, slot - 1, chunk, block_r).wait_recv()
                    self.add(chunk, block_r, block_r + 1)

            self.copy(True, slot, chunk, block_r).start()

        @pl.when(u >= n - 1 - slot)
        def _():
            if slot > 0:

                @pl.when(u < n - 1)
                def _():
                    self.copy(False, slot - 1, chunk, block_l).wait_recv()
                    self.add(chunk, block_l, block_l)

            self.copy(False, slot, chunk, block_l).start()

    def last(self, out, chunks=None):
        u, n = lax.axis_index("uly"), self.n
        where = rows_of(u, self.rows)
        width = self.part.shape[2]
        chunks = range(self.chunks) if chunks is None else chunks
        for number, chunk in enumerate(chunks):
            cols = slice(number * width, (number + 1) * width)
            out[:, cols] = self.part[chunk, where, :].astype(F32)

            @pl.when(u > 0)
            def _():
                self.copy(True, n - 2, chunk, u).wait_recv()
                out[:, cols] += self.got[chunk, rows_of(u + 1, self.rows), :].astype(F32)

            @pl.when(u < n - 1)
            def _():
                self.copy(False, n - 2, chunk, u).wait_recv()
                out[:, cols] += self.got[chunk, where, :].astype(F32)

    def finish(self):
        u, n = lax.axis_index("uly"), self.n
        for slot in range(n - 1):
            for chunk in range(self.chunks):

                @pl.when(u <= slot)
                def _():
                    self.copy(True, slot, chunk, n - 1 - slot + u).wait_send()

                @pl.when(u >= n - 1 - slot)
                def _():
                    self.copy(False, slot, chunk, slot - (n - 1) + u).wait_send()

    def run(self, compute, out, hook=None):
        for slot in range(self.n - 1):
            for chunk in range(self.chunks):
                if slot == 0:
                    compute(chunk)
                self.step(slot, chunk)
            if hook is not None:
                hook(slot)
        self.last(out)
        self.finish()


def reduce_norm_gather(n, reduce, gathers, compute, finish, consume, hook):
    per_half = reduce.chunks // 2
    slots = n - 1
    chunks = [range(h * per_half, (h + 1) * per_half) for h in range(2)]
    for chunk in chunks[0]:
        compute(chunk)
        reduce.step(0, chunk)
    for chunk in chunks[1]:
        compute(chunk)
    hook("started")
    for slot in range(1, slots):
        for chunk in chunks[0]:
            reduce.step(slot, chunk)
    for chunk in chunks[1]:
        reduce.step(0, chunk)
    hook("sent")
    finish(0)
    gathers[0].send(0)
    hook("half")
    for slot in range(1, slots):
        for chunk in chunks[1]:
            reduce.step(slot, chunk)
        gathers[0].wait(slot - 1)
        hook(f"b{slot}")
    finish(1)
    gathers[1].send(0)
    gathers[0].wait(slots - 1)
    hook("first")
    tiles = consume.tiles
    done = 0
    for slot in range(slots):
        while done < tiles * (slot + 1) // slots:
            consume(0, done)
            done += 1
        gathers[1].wait(slot)
        hook(f"g{slot}")
    for tile in range(tiles):
        consume(1, tile)
        hook(f"t{tile}")
    reduce.finish()
    for gather in gathers:
        gather.finish()


class Halves:
    def __init__(self, n, rows):
        self.n, self.half = n, rows // 2
        self.per_tile = min(n, max(512 // self.half, 1))
        self.count = n // self.per_tile

    def each(self, half, body):
        size = self.per_tile * self.half
        for t in range(self.count):
            index = (pl.ds(t * self.per_tile, self.per_tile), pl.ds(half * self.half, self.half))
            body(index, t * size, size)

    def load(self, ref, index, lanes=slice(None)):
        value = ref[index[0], index[1], lanes]
        return value.reshape(value.shape[0] * value.shape[1], value.shape[2])

    def store(self, ref, index, lanes, value):
        ref[index[0], index[1], lanes] = value.reshape(
            self.per_tile, self.half, value.shape[1]
        )


class Consume:
    def __init__(self, tiles, body):
        self.tiles, self.body = tiles, body

    def __call__(self, half, tile):
        self.body(half, tile)


class PlaneGather:
    SEMS = 9

    def __init__(self, src, block, half_rows, send, recv, local):
        self.s, self.c, self.u = where_am_i()
        self.src, self.block, self.half_rows = src, block, half_rows
        self.send_sem, self.recv_sem = send, recv
        s, c, u = self.s, self.c, self.u
        self.xn, self.yn, self.sib = (s, c ^ 1, u), (s, c ^ 2, u), (1 - s, c, u)
        self.started = []
        self.own = pltpu.make_async_copy(src, block(s * 4 + c), local)

    def half(self, b, part):
        rows = self.half_rows
        view = self.block(b)
        where = [slice(None)] * len(view.shape)
        where[-2] = pl.ds(part * rows, rows)
        return view.at[tuple(where)]

    def copy(self, k, view, peer, src=None):
        return remote(
            view if src is None else src, view, self.send_sem.at[k], self.recv_sem.at[k], peer
        )

    def go(self, *copies):
        for copy in copies:
            copy.start()
            self.started.append(copy)

    def start(self):
        own = self.block(self.s * 4 + self.c)
        self.go(
            self.copy(0, own, self.xn, self.src),
            self.copy(1, own, self.yn, self.src),
            self.copy(2, own, self.sib, self.src),
        )
        self.own.start()

    def middle(self):
        bx, by = self.s * 4 + (self.c ^ 1), self.s * 4 + (self.c ^ 2)
        self.copy(0, self.block(bx), self.xn).wait_recv()
        self.go(
            self.copy(3, self.half(bx, 0), self.yn), self.copy(4, self.block(bx), self.sib)
        )
        self.copy(1, self.block(by), self.yn).wait_recv()
        self.go(
            self.copy(5, self.half(by, 1), self.xn), self.copy(6, self.block(by), self.sib)
        )

    def corner(self):
        bd = self.s * 4 + (self.c ^ 3)
        self.copy(3, self.half(bd, 0), self.yn).wait_recv()
        self.go(self.copy(7, self.half(bd, 0), self.sib))
        self.copy(5, self.half(bd, 1), self.xn).wait_recv()
        self.go(self.copy(8, self.half(bd, 1), self.sib))

    def arrive(self):
        far, c = (1 - self.s) * 4, self.c
        self.copy(2, self.block(far + c), self.sib).wait_recv()
        self.copy(4, self.block(far + (c ^ 1)), self.sib).wait_recv()
        self.copy(6, self.block(far + (c ^ 2)), self.sib).wait_recv()
        self.copy(7, self.half(far + (c ^ 3), 0), self.sib).wait_recv()
        self.copy(8, self.half(far + (c ^ 3), 1), self.sib).wait_recv()
        self.own.wait()

    def finish(self):
        for copy in self.started:
            copy.wait_send()


class PlaneReduce:
    SEMS = 6

    def __init__(self, ring, got, outs, place, send, recv, local):
        self.s, self.c, self.u = where_am_i()
        s, c, u = self.s, self.c, self.u
        self.xn, self.yn = (s, c ^ 1, u), (s, c ^ 2, u)
        self.ring, self.got, self.outs, self.place = ring, got, outs, place
        self.send_sem, self.recv_sem, self.local = send, recv, local
        self.slots, self.rows = ring.shape[0], ring.shape[2]
        self.open = {}

    def halves(self):
        h = self.rows // 2
        return pl.ds(0, h), pl.ds(h, h)

    def copy(self, piece, k, src, dst, peer):
        return remote(src, dst, self.send_sem.at[piece, k], self.recv_sem.at[piece, k], peer)

    def slot(self, piece):
        if piece >= self.slots:
            self.close(piece - self.slots)
        return self.ring.at[piece % self.slots]

    def close(self, piece):
        if piece in self.open:
            remotes, own = self.open.pop(piece)
            for copy in remotes:
                copy.wait_send()
            wait_all(own)

    def first(self, piece):
        c = self.c
        lo, hi = self.halves()
        blocks = self.ring.at[piece % self.slots]
        own_out, out_x, out_y = self.outs
        bx, by, bd = c ^ 1, c ^ 2, c ^ 3
        copies = [
            self.copy(piece, 0, blocks.at[bd, lo], self.got.at[piece, lo], self.xn),
            self.copy(piece, 1, blocks.at[bd, hi], self.got.at[piece, hi], self.yn),
            self.copy(piece, 2, blocks.at[bx, lo], self.place(out_x, piece, 0), self.xn),
            self.copy(piece, 3, blocks.at[by, hi], self.place(out_y, piece, 1), self.yn),
        ]
        for copy in copies:
            copy.start()
        own = self.own_copies(piece, blocks)
        for copy in own:
            copy.start()
        self.open[piece] = (copies, own)

    def own_copies(self, piece, blocks):
        place = self.place(self.outs[0], piece, None)
        return [pltpu.make_async_copy(blocks.at[self.c], place, self.local.at[piece])]

    def add(self, slot, block, half, piece):
        h = self.rows // 2
        where = slice(half * h, (half + 1) * h)
        self.ring[slot, block, where, :] = (
            self.ring[slot, block, where, :].astype(F32) + self.got[piece, where, :].astype(F32)
        ).astype(BF16)

    def second(self, piece):
        c = self.c
        lo, hi = self.halves()
        slot = piece % self.slots
        blocks = self.ring.at[slot]
        own_out, out_x, out_y = self.outs
        bx, by, bd = c ^ 1, c ^ 2, c ^ 3
        self.copy(piece, 0, blocks.at[bd, lo], self.got.at[piece, lo], self.xn).wait_recv()
        self.add(slot, by, 0, piece)
        first = self.copy(piece, 4, blocks.at[by, lo], self.place(out_y, piece, 0), self.yn)
        first.start()
        self.copy(piece, 1, blocks.at[bd, hi], self.got.at[piece, hi], self.yn).wait_recv()
        self.add(slot, bx, 1, piece)
        second = self.copy(piece, 5, blocks.at[bx, hi], self.place(out_x, piece, 1), self.xn)
        second.start()
        self.open[piece][0].extend([first, second])

    def finish(self, pieces):
        own_out, out_x, out_y = self.outs
        slot = self.ring.at[0]
        lo, hi = self.halves()
        for piece in range(pieces):
            self.close(piece)
            for k, out, half, peer in (
                (2, out_x, 0, self.xn),
                (3, out_y, 1, self.yn),
                (4, out_y, 0, self.yn),
                (5, out_x, 1, self.xn),
            ):
                where = self.place(out, piece, half)
                self.copy(piece, k, where, where, peer).wait_recv()


class Pieces:
    def __init__(self, work, ahead=2):
        self.work, self.done, self.behind, self.ahead = work, 0, [], ahead

    def step(self, count=1):
        for _ in range(count):
            if self.done < len(self.work):
                plane, piece, compute = self.work[self.done]
                compute(plane.slot(piece), piece)
                plane.first(piece)
                self.behind.append((plane, piece))
                self.done += 1
                if len(self.behind) > self.ahead:
                    self.catch_up()

    def catch_up(self):
        plane, piece = self.behind.pop(0)
        plane.second(piece)

    def finish(self):
        self.step(len(self.work))
        while self.behind:
            self.catch_up()


def wide_piece(own, other, lanes):
    def compute(out, piece):
        take = lanes(piece)
        cols = out.shape[2]

        def pair(i, carry):
            where = pl.ds(pl.multiple_of(i * 2 * cols, 2 * cols), 2 * cols)
            total = dot(own[0][:, take], own[1][:, where], TN) + dot(
                other[0][:, take], other[1][:, where], TN
            )
            total = total.astype(BF16)
            out[pl.ds(2 * i, 1)] = total[:, :cols][None]
            out[pl.ds(2 * i + 1, 1)] = total[:, cols:][None]
            return carry

        lax.fori_loop(0, 2, pair, 0)

    return compute


def tall_piece(own, other, right):
    def compute(out, piece):
        rows, cols = out.shape[1:]

        def pair(i, carry):
            where = pl.ds(pl.multiple_of(i * 2 * rows, 2 * rows), 2 * rows)
            total = dot(own[0][:, where], right(own[1], piece), TN) + dot(
                other[0][:, where], right(other[1], piece), TN
            )
            out[pl.ds(2 * i, 2)] = total.astype(BF16).reshape(2, rows, cols)
            return carry

        lax.fori_loop(0, 2, pair, 0)

    return compute


class LatePiece:
    def __init__(self, number, ins, outs, scratch, sems):
        s, c, u = where_am_i()
        resid_hbm, resid_s_hbm, dgu_hbm, dgu_s_hbm = ins
        resid, resid_s, right, right_s, ring, got = scratch
        send, recv, local, load_sem = sems
        cols = right.shape[1]
        ci, tile = divmod(number, dgu_hbm.shape[2] // cols)
        lanes = pl.ds(tile * cols, cols)
        pairs = (
            (half_columns(resid_hbm, s), resid),
            (resid_s_hbm, resid_s),
            (dgu_hbm.at[ci, :, lanes], right),
            (dgu_s_hbm.at[ci, :, lanes], right_s),
        )
        self.loads = [
            pltpu.make_async_copy(src, dst, load_sem.at[k]) for k, (src, dst) in enumerate(pairs)
        ]
        size = ring.shape[2]

        def place(out, piece, part):
            rows = size if part is None else size // 2
            return out.at[ci, pl.ds((part or 0) * rows, rows), lanes]

        self.plane = PlaneReduce(ring, got, outs, place, send, recv, local)
        self.compute = tall_piece(
            (resid, right), (resid_s, right_s), lambda ref, piece: ref[...]
        )

    def load(self):
        for copy in self.loads:
            copy.start()

    def work(self):
        def compute(out, piece):
            for copy in self.loads:
                copy.wait()
            self.compute(out, piece)

        return (self.plane, 0, compute)

    @staticmethod
    def scratch(span, width, ff):
        cols = min(ff, 512)
        ring, sems = piece_scratch(1, 1, width // 8, cols)
        buffers = (
            pltpu.VMEM((span, width // 2), BF16),
            pltpu.VMEM((span, width // 2), BF16),
            pltpu.VMEM((span, cols), BF16),
            pltpu.VMEM((span, cols), BF16),
            ring[0],
            ring[1],
        )
        return [buffers, tuple(sems) + (pltpu.SemaphoreType.DMA((4,)),)]


def half_columns(ref, s):
    half = ref.shape[1] // 2
    return ref.at[:, pl.ds(pl.multiple_of(s * half, half), half)]


class Sibling:
    def __init__(self, send, recv):
        s, c, u = where_am_i()
        self.peer, self.send, self.recv = (1 - s, c, u), send, recv
        self.copies = []

    def start(self, src, dst):
        k = len(self.copies)
        copy = remote(src, dst, self.send.at[k], self.recv.at[k], self.peer)
        copy.start()
        self.copies.append(copy)

    def wait(self, k):
        self.copies[k].wait_recv()

    def finish(self):
        for copy in self.copies:
            copy.wait_send()


def dot(a, b, dims):
    return lax.dot_general(a, b, ((dims[:1], dims[1:]), ((), ())), preferred_element_type=F32)


NN, NT, TN = (1, 0), (1, 1), (0, 0)


def tiles(total, size):
    size = min(total, size)
    return total // size, size


def inverse_rms(values):
    return lax.rsqrt(jnp.mean(values * values, axis=-1, keepdims=True) + EPS)


def norm_back(values, inverse, grad_scaled, width):
    return inverse * grad_scaled - values * inverse**3 * (
        jnp.sum(values * grad_scaled, axis=-1, keepdims=True) / width
    )


def rope_factors(table):
    lane = lax.broadcasted_iota(jnp.int32, table.shape, 1)
    turned = pltpu.roll(table, HALF, 1)
    cosine = jnp.where(lane < HALF, table, turned)
    sine = jnp.where(lane < HALF, -turned, table)
    return cosine, sine


def exchange_rows(n, mine, msg, send, recv):
    s, c, u = where_am_i()
    msg[pl.ds(u, 1)] = mine[None]
    copies = []
    for step in range(1, n):
        peer = lax.rem(u + step, n)
        copy = remote(msg.at[u], msg.at[u], send.at[step - 1], recv.at[step - 1], (s, c, peer))
        copy.start()
        copies.append(copy)
    for step in range(1, n):
        source = lax.rem(u + n - step, n)
        remote(
            msg.at[source], msg.at[source], send.at[step - 1], recv.at[step - 1], (s, c, source)
        ).wait_recv()
    total = msg[0]
    for j in range(1, n):
        total = total + msg[j]
    for copy in copies:
        copy.wait_send()
    return total


def to_rows(col0, col1):
    span = col0.shape[0]
    lane = lax.broadcasted_iota(jnp.int32, (span, 128), 1)
    both = jnp.where(lane == 0, col0, jnp.where(lane == 1, col1, 0.0))
    return jnp.transpose(both)[:8]


def to_columns(rows8):
    return jnp.transpose(jnp.concatenate([rows8] * 16, axis=0))


def all_uly_peers(n):
    s, c, u = where_am_i()
    return [(None, (s, c, lax.rem(u + k, n))) for k in range(1, n)]


def spread_heads(cols):
    return cols % (4 * HEAD_DIM) == 0


def proj_kernel(
    n,
    x_ref,
    w_ref,
    tab_ref,
    gain_ref,
    seg_ref,
    wo_ref,
    gu_ref,
    xg_out,
    wq_out,
    wo_out,
    wga_out,
    proj_ref,
    qkv_refs,
    inv_ref,
    zero_ref,
    xg,
    wq,
    tab,
    msg,
    local_sem,
    w_send,
    w_recv,
    m_send,
    m_recv,
    *line,
):
    s, c, u = where_am_i()
    rows, width = x_ref.shape
    span = n * rows
    kb = w_ref.shape[1]
    sib = (1 - s, c, u)
    tab_copy = pltpu.make_async_copy(tab_ref.at[rows_of(c, span)], tab, local_sem.at[0])
    tab_copy.start()
    xg[rows_of(u, rows), :] = x_ref[...]
    greet(all_uly_peers(n) + plane_peers() + [(None, sib)])

    def plane(k, src, block, half_rows):
        return PlaneGather(
            src, block, half_rows, w_send.at[k], w_recv.at[k], local_sem.at[3 + k]
        )

    half = kb // 2
    gather = LineGather(n, rows, xg, line)
    first = plane(0, w_ref, lambda b: wq.at[:, rows_of(b, kb)], half)
    second = plane(1, wo_ref, lambda b: wo_out.at[b], wo_ref.shape[0] // 2)
    third = plane(2, gu_ref.at[0, pl.ds(0, half)], lambda b: wga_out.at[b], half // 2)
    gather.send(0)
    first.start()
    gather.wait(0)
    first.middle()
    second.start()
    if n > 2:
        gather.wait(1)
    first.corner()
    second.middle()
    third.start()
    for slot in range(2 if n > 2 else 1, n - 1):
        gather.wait(slot)
    first.arrive()
    tab_copy.wait()
    keep = [
        pltpu.make_async_copy(xg, xg_out, local_sem.at[1]),
        pltpu.make_async_copy(wq, wq_out, local_sem.at[2]),
    ]
    for copy in keep:
        copy.start()

    count, size = tiles(span, 512)

    def store(i, where, first, values):
        if len(qkv_refs) == 1:
            (ref,) = qkv_refs
            size = ref.shape[3]
            for at in range(0, values.shape[1], min(size, values.shape[1])):
                group, inside = divmod(first + at, size)
                part = values[:, at : at + size]
                ref[group, i, where, inside : inside + part.shape[1]] = part
        else:
            ref = qkv_refs[0] if i == 0 else qkv_refs[1].at[i - 1]
            ref[where, first : first + values.shape[1]] = values

    def project(i, carry):
        where = pl.ds(pl.multiple_of(i * size, size), size)
        xs = xg[where, :]
        proj_ref[0, where, :] = dot(xs, wq[0], NN)
        proj_ref[1, where, :] = dot(xs, wq[1], NN)
        store(2, where, 0, dot(xs, wq[2], NN).astype(BF16))
        return carry

    lax.fori_loop(0, count, project, 0)
    squares = [jnp.sum(proj_ref[i] * proj_ref[i], axis=-1, keepdims=True) for i in range(2)]
    mine = to_rows(*squares)
    zeros = jnp.sum((1 - seg_ref[...]).astype(F32))
    row = lax.broadcasted_iota(jnp.int32, mine.shape, 0)
    mine = jnp.where(row == 2, zeros, mine)
    second.corner()
    third.middle()
    total = exchange_rows(n, mine, msg, m_send, m_recv)
    zero_ref[...] = jnp.broadcast_to(total[2:3, :128], (8, 128))
    inv = lax.rsqrt(to_columns(total) / width + EPS)
    inv_ref[...] = inv
    cosine, sine = rope_factors(tab[...])
    heads = proj_ref.shape[2] // HEAD_DIM
    for i in range(2):
        inverse = inv_ref[:, i : i + 1]
        for h in range(heads):
            cols = slice(h * HEAD_DIM, (h + 1) * HEAD_DIM)
            v = proj_ref[i, :, cols] * inverse * gain_ref[i : i + 1, cols]
            v = (v * cosine + pltpu.roll(v, HALF, 1) * sine).astype(BF16)
            store(i, slice(None), h * HEAD_DIM, v)
    second.arrive()
    third.corner()
    third.arrive()
    for work in (first, second, third, gather):
        work.finish()
    for copy in keep:
        copy.wait()


def project(n, x, w, table, gain, seg, wo, gu):
    rows, width = x.shape
    span, cols = n * rows, w.shape[2]
    if spread_heads(cols):
        qkv = (shape((4, 3, span, cols // 4), BF16),)
    else:
        qkv = (shape((span, cols), BF16), shape((2, span, cols), BF16))
    return pl.pallas_call(
        functools.partial(proj_kernel, n),
        out_shape=(
            shape((span, width), BF16),
            shape((3, width, cols), BF16),
            shape((8,) + wo.shape, BF16),
            shape((8, gu.shape[1] // 2, gu.shape[2]), BF16),
            shape((2, span, cols), F32),
            qkv,
            shape((span, 128), F32),
            shape((8, 128), F32),
        ),
        in_specs=[VM, HB, HB, VM, VM, HB, HB],
        out_specs=(HB, HB, HB, HB, VM, (VM,) * len(qkv), VM, VM),
        scratch_shapes=[
            pltpu.VMEM((span, width), BF16),
            pltpu.VMEM((3, width, cols), BF16),
            pltpu.VMEM((span, 128), F32),
            pltpu.VMEM((n, 8, span), F32),
            pltpu.SemaphoreType.DMA((6,)),
            pltpu.SemaphoreType.DMA((3, 9)),
            pltpu.SemaphoreType.DMA((3, 9)),
            pltpu.SemaphoreType.DMA((n - 1,)),
            pltpu.SemaphoreType.DMA((n - 1,)),
        ]
        + line_sems(n),
        compiler_params=pltpu.CompilerParams(
            collective_id=1, has_side_effects=True, vmem_limit_bytes=VMEM_LIMIT
        ),
        name="project",
    )(x, w, table, gain, seg, wo, gu)


def score_mask(scores, key_first, query_first, starts, diagonal):
    key_pos = key_first + lax.broadcasted_iota(jnp.int32, scores.shape, 0)
    keep = key_pos >= starts
    if diagonal:
        query_pos = query_first + lax.broadcasted_iota(jnp.int32, scores.shape, 1)
        keep = keep & (key_pos <= query_pos)
    return jnp.where(keep, scores, FLOOR)


def segment_starts(first, size, bound):
    pos = first + lax.broadcasted_iota(jnp.int32, (1, size), 1)
    return jnp.where(pos >= bound, bound, 0)


def attend_kernel(
    q_ref,
    kv_ref,
    zero_ref,
    gu_ref,
    kvall_out,
    wgb_out,
    attn_ref,
    attn32_ref,
    lse_ref,
    bound_ref,
    kvall,
    peaks,
    sums,
    acct,
    zmsg,
    send,
    recv,
    z_send,
    z_recv,
    w_send,
    w_recv,
    keep_sem,
    w_local,
):
    s, c, u = where_am_i()
    span, cols = q_ref.shape
    heads = cols // HEAD_DIM
    xn, yn, dn = (s, c ^ 1, u), (s, c ^ 2, u), (s, c ^ 3, u)
    kvall[pl.ds(c, 1)] = kv_ref[...][None]
    zmsg[pl.ds(c, 1)] = zero_ref[...][None]
    greet(plane_peers() + [(None, dn), (None, (1 - s, c, u))])
    weight = upper_gate(gu_ref, wgb_out, w_send, w_recv, w_local)

    def sent(k, view, peer):
        return remote(view, view, send.at[k], recv.at[k], peer)

    bx, by, bd = c ^ 1, c ^ 2, c ^ 3
    zs = [
        remote(zmsg.at[c], zmsg.at[c], z_send.at[k], z_recv.at[k], peer)
        for k, peer in enumerate((xn, yn, dn))
    ]
    for copy in zs:
        copy.start()
    copies = [sent(0, kvall.at[c], xn), sent(1, kvall.at[c], yn)]
    for copy in copies:
        copy.start()
    for k, (b, peer) in enumerate(((bx, xn), (by, yn), (bd, dn))):
        remote(zmsg.at[b], zmsg.at[b], z_send.at[k], z_recv.at[k], peer).wait_recv()
    ahead = jnp.zeros((8, 128), F32)
    for j in range(4):
        ahead = ahead + jnp.where(j <= c, zmsg[j], 0.0)
    bounds = ahead.astype(jnp.int32)
    bound_ref[...] = bounds
    bound = bounds[:1, :1]

    peaks[...] = jnp.full_like(peaks, FLOOR)
    sums[...] = jnp.zeros_like(sums)
    acct[...] = jnp.zeros_like(acct)
    nq, tq = tiles(span, 512)
    nk, tk = tiles(span, 512)

    def update(number, diagonal):
        def over_queries(i, carry):
            first_q = c * span + i * tq
            starts = segment_starts(first_q, tq, bound)
            where_q = pl.ds(pl.multiple_of(i * tq, tq), tq)

            def over_keys(j, carry):
                first_k = number * span + j * tk
                where_k = pl.ds(pl.multiple_of(j * tk, tk), tk)
                for h in range(heads):
                    lanes = slice(h * HEAD_DIM, (h + 1) * HEAD_DIM)
                    scores = dot(kvall[number, 0, where_k, lanes], q_ref[where_q, lanes], NT)
                    scores = score_mask(scores * SCALE2, first_k, first_q, starts, diagonal)
                    old = peaks[h, :1, where_q]
                    new = jnp.maximum(old, jnp.max(scores, axis=0, keepdims=True))
                    factor = jnp.exp2(old - new)
                    weights = jnp.exp2(scores - new)
                    peaks[h, :1, where_q] = new
                    sums[h, :1, where_q] = sums[h, :1, where_q] * factor + jnp.sum(
                        weights, axis=0, keepdims=True
                    )
                    acct[h, :, where_q] = acct[h, :, where_q] * factor + dot(
                        kvall[number, 1, where_k, lanes], weights.astype(BF16), TN
                    )
                return carry

            return lax.fori_loop(0, nk, over_keys, carry)

        lax.fori_loop(0, nq, over_queries, 0)

    update(c, True)
    half = span // 2
    sent(0, kvall.at[bx], xn).wait_recv()
    more = [sent(2, kvall.at[bx, :, pl.ds(0, half)], yn)]
    more[0].start()
    copies += more
    sent(1, kvall.at[by], yn).wait_recv()
    more = [sent(3, kvall.at[by, :, pl.ds(half, half)], xn)]
    more[0].start()
    copies += more
    for b in (bx, by):

        @pl.when(b < c)
        def _():
            update(b, False)

    sent(2, kvall.at[bd, :, pl.ds(0, half)], yn).wait_recv()
    sent(3, kvall.at[bd, :, pl.ds(half, half)], xn).wait_recv()
    keep = pltpu.make_async_copy(kvall, kvall_out, keep_sem)
    keep.start()
    weight.start()

    @pl.when(bd < c)
    def _():
        update(bd, False)

    for h in range(heads):
        lanes = slice(h * HEAD_DIM, (h + 1) * HEAD_DIM)
        total = sums[h, :1, :]
        attention = jnp.transpose(acct[h] / total)
        attn32_ref[:, lanes] = attention
        attn_ref[:, lanes] = attention.astype(BF16)
        lse_ref[h, :1, :] = peaks[h, :1, :] + jnp.log2(total)
    for copy in copies + zs:
        copy.wait_send()
    weight.middle()
    weight.corner()
    weight.arrive()
    weight.finish()
    keep.wait()


def attend(q, kv, zero, gu):
    span, cols = q.shape
    heads = cols // HEAD_DIM
    return pl.pallas_call(
        attend_kernel,
        out_shape=(
            shape((4, 2, span, cols), BF16),
            shape((8, gu.shape[1] // 2, gu.shape[2]), BF16),
            shape((span, cols), BF16),
            shape((span, cols), F32),
            shape((heads, 8, span), F32),
            shape((8, 128), jnp.int32),
        ),
        in_specs=[VM] * 3 + [HB],
        out_specs=(HB, HB, VM, VM, VM, VM),
        scratch_shapes=[
            pltpu.VMEM((4, 2, span, cols), BF16),
            pltpu.VMEM((heads, 8, span), F32),
            pltpu.VMEM((heads, 8, span), F32),
            pltpu.VMEM((heads, HEAD_DIM, span), F32),
            pltpu.VMEM((4, 8, 128), F32),
            pltpu.SemaphoreType.DMA((4,)),
            pltpu.SemaphoreType.DMA((4,)),
            pltpu.SemaphoreType.DMA((3,)),
            pltpu.SemaphoreType.DMA((3,)),
            pltpu.SemaphoreType.DMA((9,)),
            pltpu.SemaphoreType.DMA((9,)),
            pltpu.SemaphoreType.DMA,
            pltpu.SemaphoreType.DMA,
        ],
        compiler_params=pltpu.CompilerParams(
            collective_id=2, has_side_effects=True, vmem_limit_bytes=VMEM_LIMIT
        ),
        name="attend",
    )(q, kv, zero, gu)


def upper_gate(gu_ref, out, send, recv, local):
    half = gu_ref.shape[1] // 2
    return PlaneGather(
        gu_ref.at[0, pl.ds(half, half)], lambda b: out.at[b], half // 2, send, recv, local
    )


def norms_back(source, keep, proj_ref, inv_ref, gain_ref, tab, dgain_ref):
    cosine, sine = rope_factors(tab[...])
    span, cols = proj_ref.shape[1:]
    dots = []
    for i in range(2):
        inverse = inv_ref[:, i : i + 1]
        row_dot = jnp.zeros((span, 1), F32)
        for h in range(cols // HEAD_DIM):
            lanes = slice(h * HEAD_DIM, (h + 1) * HEAD_DIM)
            v = source(i, h)
            v = v * cosine - pltpu.roll(v, HALF, 1) * sine
            values = proj_ref[i, :, lanes]
            dgain_ref[i : i + 1, lanes] = jnp.sum(v * values * inverse, axis=0, keepdims=True)
            v = v * gain_ref[i : i + 1, lanes]
            keep(i, h, v)
            row_dot = row_dot + jnp.sum(values * v, axis=-1, keepdims=True)
        dots.append(row_dot)
    return to_rows(*dots)


def attend_back_kernel(
    n,
    q_ref,
    kvall_ref,
    do_ref,
    attn32_ref,
    lse_ref,
    bound_ref,
    proj_ref,
    inv_ref,
    gain_ref,
    tab_ref,
    resid_hbm,
    resid_s_hbm,
    dgu_hbm,
    dgu_s_hbm,
    own_in,
    x_in,
    y_in,
    dproj_ref,
    dgain_ref,
    own_out,
    x_out,
    y_out,
    dq_ref,
    part,
    got,
    acc,
    delta,
    tab,
    msg,
    late_buffers,
    late_sems,
    send,
    recv,
    local_sem,
    m_send,
    m_recv,
):
    s, c, u = where_am_i()
    span, cols = q_ref.shape
    width = resid_hbm.shape[1]
    heads = cols // HEAD_DIM
    xn, yn = (s, c ^ 1, u), (s, c ^ 2, u)
    bx, by, bd = c ^ 1, c ^ 2, c ^ 3
    load = pltpu.make_async_copy(tab_ref.at[rows_of(c, span)], tab, local_sem)
    load.start()
    last = 2 * (dgu_hbm.shape[2] // late_buffers[2].shape[1])
    late = LatePiece(
        last - 2,
        (resid_hbm, resid_s_hbm, dgu_hbm, dgu_s_hbm),
        (own_out, x_out, y_out),
        late_buffers,
        late_sems,
    )
    late.load()
    pieces = Pieces([late.work()])
    greet(plane_peers() + all_uly_peers(n))
    bound = bound_ref[:1, :1]
    nq, tq = tiles(span, 512)
    nk, tk = tiles(span, 512)
    scale = HEAD_DIM ** (-0.5)
    dq_ref[...] = jnp.zeros_like(dq_ref)
    for h in range(heads):
        lanes = slice(h * HEAD_DIM, (h + 1) * HEAD_DIM)
        both = jnp.transpose(do_ref[:, lanes].astype(F32) * attn32_ref[:, lanes])
        delta[h, :1, :] = jnp.sum(both, axis=0, keepdims=True)

    def update(number, diagonal):
        acc[...] = jnp.zeros_like(acc)

        def over_queries(i, carry):
            first_q = c * span + i * tq
            starts = segment_starts(first_q, tq, bound)
            where_q = pl.ds(pl.multiple_of(i * tq, tq), tq)

            def over_keys(j, carry):
                first_k = number * span + j * tk
                where_k = pl.ds(pl.multiple_of(j * tk, tk), tk)
                for h in range(heads):
                    lanes = slice(h * HEAD_DIM, (h + 1) * HEAD_DIM)
                    keys = kvall_ref[number, 0, where_k, lanes]
                    values = kvall_ref[number, 1, where_k, lanes]
                    query, d_out = q_ref[where_q, lanes], do_ref[where_q, lanes]
                    scores = dot(keys, query, NT) * SCALE2
                    scores = score_mask(scores, first_k, first_q, starts, diagonal)
                    probs = jnp.exp2(scores - lse_ref[h, :1, where_q])
                    acc[1, where_k, lanes] += dot(probs.astype(BF16), d_out, NN)
                    d_probs = dot(values, d_out, NT)
                    d_scores = (probs * (d_probs - delta[h, :1, where_q])).astype(BF16)
                    acc[0, where_k, lanes] += dot(d_scores, query, NN) * scale
                    dq_ref[where_q, lanes] += dot(d_scores, keys, TN) * scale
                return carry

            return lax.fori_loop(0, nk, over_keys, carry)

        lax.fori_loop(0, nq, over_queries, 0)

    def work(number):
        @pl.when(number < c)
        def _():
            update(number, False)
            part[pl.ds(number, 1)] = acc[...].astype(BF16)[None]

        @pl.when(number > c)
        def _():
            part[pl.ds(number, 1)] = jnp.zeros_like(part[pl.ds(number, 1)])

    half = span // 2
    lo, hi = pl.ds(0, half), pl.ds(half, half)

    def sent(k, src, dst, peer):
        return remote(src, dst, send.at[k], recv.at[k], peer)

    pieces.step()
    work(bd)
    copies = [
        sent(0, part.at[bd, :, lo], got.at[0, :, lo], xn),
        sent(1, part.at[bd, :, hi], got.at[0, :, hi], yn),
    ]
    for copy in copies:
        copy.start()
    pieces.catch_up()
    work(bx)
    sent(1, part.at[bx, :, hi], got.at[0, :, hi], yn).wait_recv()
    part[bx, :, half:, :] = (
        part[bx, :, half:, :].astype(F32) + got[0, :, half:, :].astype(F32)
    ).astype(BF16)
    more = [sent(2, part.at[bx], got.at[1], xn)]
    more[0].start()
    copies += more
    work(by)
    sent(0, part.at[by, :, lo], got.at[0, :, lo], xn).wait_recv()
    part[by, :, :half, :] = (
        part[by, :, :half, :].astype(F32) + got[0, :, :half, :].astype(F32)
    ).astype(BF16)
    more = [sent(3, part.at[by], got.at[2], yn)]
    more[0].start()
    copies += more
    update(c, True)
    load.wait()

    cosine, sine = rope_factors(tab[...])

    def turn_back(i):
        inverse = inv_ref[:, i : i + 1]
        row_dot = jnp.zeros((span, 1), F32)
        for h in range(heads):
            lanes = slice(h * HEAD_DIM, (h + 1) * HEAD_DIM)
            source = dq_ref if i == 0 else acc.at[0]
            v = source[:, lanes]
            v = v * cosine - pltpu.roll(v, HALF, 1) * sine
            values = proj_ref[i, :, lanes]
            dgain_ref[i : i + 1, lanes] = jnp.sum(v * values * inverse, axis=0, keepdims=True)
            v = v * gain_ref[i : i + 1, lanes]
            source[:, lanes] = v
            row_dot = row_dot + jnp.sum(values * v, axis=-1, keepdims=True)
        return row_dot

    dots_q = turn_back(0)
    sent(2, part.at[bx], got.at[1], xn).wait_recv()
    sent(3, part.at[by], got.at[2], yn).wait_recv()
    acc[...] += got[1].astype(F32) + got[2].astype(F32)
    dproj_ref[2] = acc[1].astype(BF16)
    dots_k = turn_back(1)
    total = exchange_rows(n, to_rows(dots_q, dots_k), msg, m_send, m_recv)
    means = to_columns(total) / width
    for i in range(2):
        inverse = inv_ref[:, i : i + 1]
        factor = inverse**3 * means[:, i : i + 1]
        source = dq_ref if i == 0 else acc.at[0]
        dproj_ref[i] = (inverse * source[...] - proj_ref[i] * factor).astype(BF16)
    pieces.finish()
    late.plane.finish(1)
    for copy in copies:
        copy.wait_send()


def attend_back(
    n, q, kvall, d_out, attn32, lse, bound, proj, inv, gain, table, late, grads
):
    span, cols = q.shape
    heads = cols // HEAD_DIM
    width, ff = late[0].shape[1], late[2].shape[2]
    return pl.pallas_call(
        functools.partial(attend_back_kernel, n),
        out_shape=(shape((3, span, cols), BF16), shape((2, cols), F32))
        + tuple(shape(g.shape, BF16) for g in grads),
        in_specs=[VM] * 9 + [HB] * 8,
        out_specs=(VM, VM, HB, HB, HB),
        input_output_aliases={14: 2, 15: 3, 16: 4},
        scratch_shapes=[
            pltpu.VMEM((span, cols), F32),
            pltpu.VMEM((4, 2, span, cols), BF16),
            pltpu.VMEM((3, 2, span, cols), BF16),
            pltpu.VMEM((2, span, cols), F32),
            pltpu.VMEM((heads, 8, span), F32),
            pltpu.VMEM((span, 128), F32),
            pltpu.VMEM((n, 8, span), F32),
        ]
        + LatePiece.scratch(span, width, ff)
        + [
            pltpu.SemaphoreType.DMA((4,)),
            pltpu.SemaphoreType.DMA((4,)),
            pltpu.SemaphoreType.DMA,
            pltpu.SemaphoreType.DMA((n - 1,)),
            pltpu.SemaphoreType.DMA((n - 1,)),
        ],
        compiler_params=pltpu.CompilerParams(
            collective_id=3, has_side_effects=True, vmem_limit_bytes=VMEM_LIMIT
        ),
        name="attend_back",
    )(q, kvall, d_out, attn32, lse, bound, proj, inv, gain, table, *late, *grads)


class Keep:
    def __init__(self, sems):
        self.sems, self.copies = sems, []

    def __call__(self, src, dst):
        copy = pltpu.make_async_copy(src, dst, self.sems.at[len(self.copies)])
        copy.start()
        self.copies.append(copy)
        return copy

    def finish(self, but=()):
        for copy in self.copies:
            if not any(copy is done for done in but):
                copy.wait()


def forward_kernel(n, names, *refs):
    ref = dict(zip(names, refs))
    (x_ref, w_ref, tab_ref, gain_ref, seg_ref, wo_ref, gu_ref, down_ref, post_ref) = [
        ref[name] for name in ("x", "w", "table", "gain", "seg", "wo", "gu", "down", "post")
    ]
    s, c, u = where_am_i()
    rows, width = x_ref.shape
    span, half = n * rows, rows // 2
    kb = w_ref.shape[1]
    xg, wq, proj, qkv = ref["v_xg"], ref["v_wq"], ref["v_proj"], ref["v_qkv"]
    every, back, attn = ref["v_every"], ref["v_back"], ref["v_attn"]
    cols = proj.shape[2]
    quarter = cols // 4
    keep, load = Keep(ref["keep_sem"]), Keep(ref["load_sem"])
    table = load(tab_ref.at[rows_of(c, span)], ref["v_tab"])
    xg[rows_of(u, rows), :] = x_ref[...]
    peers = [(s, c ^ k, u) for k in (1, 2, 3)]
    greet(all_uly_peers(n) + [(None, peer) for peer in peers] + [(None, (1 - s, c, u))])

    def plane(k, src, block, half_rows):
        return PlaneGather(
            src, block, half_rows, ref["w_send"].at[k], ref["w_recv"].at[k], ref["w_local"].at[k]
        )

    def plane_to(k, src, out):
        return plane(k, src, lambda b: out.at[b], src.shape[0] // 2)

    lower, upper = pl.ds(0, kb // 2), pl.ds(kb // 2, kb // 2)
    w_qkv = plane(0, w_ref, lambda b: wq.at[:, rows_of(b, kb)], kb // 2)
    w_out = plane_to(1, wo_ref, ref["o_wo"])
    w_a = plane_to(2, gu_ref.at[0, lower], ref["o_wga"])
    w_b = plane_to(3, gu_ref.at[0, upper], ref["o_wgb"])
    w_c = plane_to(4, gu_ref.at[1], ref["o_wgc"])
    w_d = plane_to(5, down_ref, ref["o_wd"])

    gather = LineGather(n, rows, xg, [ref[f"x_sem{i}"] for i in range(4)])
    gather.send(0)
    w_qkv.start()
    gather.wait(0)
    w_qkv.middle()
    w_out.start()
    if n > 2:
        gather.wait(1)
    w_qkv.corner()
    w_a.start()
    w_out.middle()
    for slot in range(2 if n > 2 else 1, n - 1):
        gather.wait(slot)
    w_qkv.arrive()
    keep(xg, ref["o_xg"])
    keep(wq, ref["o_wq"])
    count, size = tiles(span, 512)

    def project(i, carry):
        where = pl.ds(pl.multiple_of(i * size, size), size)
        xs = xg[where, :]
        proj[0, where, :] = dot(xs, wq[0], NN)
        proj[1, where, :] = dot(xs, wq[1], NN)
        value = dot(xs, wq[2], NN).astype(BF16)
        for q in range(4):
            qkv[q, 2, where, :] = value[:, q * quarter : (q + 1) * quarter]
        return carry

    lax.fori_loop(0, count, project, 0)
    keep(proj, ref["o_proj"])
    squares = [jnp.sum(proj[i] * proj[i], axis=-1, keepdims=True) for i in range(2)]
    mine = to_rows(*squares)
    zeros = jnp.sum((1 - seg_ref[...]).astype(F32))
    row = lax.broadcasted_iota(jnp.int32, mine.shape, 0)
    mine = jnp.where(row == 2, zeros, mine)
    total = exchange_rows(n, mine, ref["v_msg"], ref["m_send"], ref["m_recv"])
    zmsg = ref["v_zmsg"]
    zmsg[pl.ds(c, 1)] = jnp.broadcast_to(total[2:3, :128], (1, 8, 128))
    inv = ref["v_inv"]
    inv[...] = lax.rsqrt(to_columns(total) / width + EPS)
    table.wait()
    cosine, sine = rope_factors(ref["v_tab"][...])
    for i in range(2):
        inverse = inv[:, i : i + 1]
        for h in range(cols // HEAD_DIM):
            lanes = slice(h * HEAD_DIM, (h + 1) * HEAD_DIM)
            v = proj[i, :, lanes] * inverse * gain_ref[i : i + 1, lanes]
            v = (v * cosine + pltpu.roll(v, HALF, 1) * sine).astype(BF16)
            group, inside = divmod(h * HEAD_DIM, quarter)
            qkv[group, i, :, inside : inside + HEAD_DIM] = v

    copies, arrivals = [], []
    a_send, a_recv, z_send, z_recv = ref["a_send"], ref["a_recv"], ref["z_send"], ref["z_recv"]
    for k, peer in enumerate(peers):
        there = peer[1]
        copy = remote(qkv.at[there], every.at[c], a_send.at[k], a_recv.at[k], peer)
        copy.start()
        small = remote(zmsg.at[c], zmsg.at[c], z_send.at[k], z_recv.at[k], peer)
        small.start()
        copies += [copy, small]
        arrivals.append(remote(every.at[there], every.at[there], a_send.at[k], a_recv.at[k], peer))
        arrivals.append(remote(zmsg.at[there], zmsg.at[there], z_send.at[k], z_recv.at[k], peer))
    every[pl.ds(c, 1)] = qkv[pl.ds(c, 1)]
    keep(inv, ref["o_inv"])
    w_a.middle()
    w_out.corner()
    w_out.arrive()
    load_o = load_blocks(ref["o_wo"], ref["v_wo"], ref["wo_sem"], 1)
    for arrival in arrivals:
        arrival.wait_recv()
    w_b.start()
    keep(every, ref["o_every"])
    bounds = (zmsg[0] + zmsg[1] + zmsg[2] + zmsg[3]).astype(jnp.int32)
    ref["v_bound"][...] = bounds
    bound = bounds[:1, :1]
    peaks, sums, acct = ref["v_peaks"], ref["v_sums"], ref["v_acct"]
    att, lse = ref["v_att"], ref["v_lse"]

    def attend(k, carry):
        i = c ^ (3 - k)
        first_q = i * span
        starts = segment_starts(first_q, span, bound)
        for h in range(quarter // HEAD_DIM):
            lanes = slice(h * HEAD_DIM, (h + 1) * HEAD_DIM)
            peaks[...] = jnp.full_like(peaks, FLOOR)
            sums[...] = jnp.zeros_like(sums)
            acct[...] = jnp.zeros_like(acct)

            def update(j, diagonal):
                scores = dot(every[j, 1, :, lanes], every[i, 0, :, lanes], NT) * SCALE2
                scores = score_mask(scores, j * span, first_q, starts, diagonal)
                old = peaks[:1, :]
                new = jnp.maximum(old, jnp.max(scores, axis=0, keepdims=True))
                factor = jnp.exp2(old - new)
                weights = jnp.exp2(scores - new)
                peaks[:1, :] = new
                sums[:1, :] = sums[:1, :] * factor + jnp.sum(weights, axis=0, keepdims=True)
                acct[...] = acct[...] * factor + dot(
                    every[j, 2, :, lanes], weights.astype(BF16), TN
                )

            def before(j, carry):
                update(j, False)
                return carry

            lax.fori_loop(0, i, before, 0)
            update(i, True)
            total = sums[:1, :]
            attention = acct[...] / total
            att[pl.ds(i, 1), lanes, :] = attention[None]
            back[pl.ds(k, 1), :, :, lanes] = (
                jnp.transpose(attention).astype(BF16).reshape(1, n, rows, HEAD_DIM)
            )
            lse[pl.ds(i, 1), h, :1, :] = (peaks[:1, :] + jnp.log2(total))[None]

        @pl.when(k < 3)
        def _():
            home(k, i, c).start()

        return carry

    def home(k, i, owner):
        return remote(
            back.at[k],
            attn.at[:, :, pl.ds(pl.multiple_of(owner * quarter, quarter), quarter)],
            ref["b_send"].at[k],
            ref["b_recv"].at[k],
            (s, i, u),
        )

    lax.fori_loop(0, 4, attend, 0)
    attn[:, :, pl.ds(pl.multiple_of(c * quarter, quarter), quarter)] = back[3]
    keep(att, ref["o_att"])
    keep(lse, ref["o_lse"])
    keep(ref["v_bound"], ref["o_bound"])
    w_a.corner()
    for k in range(3):
        i = c ^ (3 - k)
        home(k, i, i).wait_recv()
    keep(attn, ref["o_attn"])
    wait_all(load_o)
    w_a.arrive()
    wg = ref["v_wg"]
    load(ref["o_wga"], wg.at[0, :, lower])

    wo, part, group = ref["v_wo"], ref["v_part"], ref["v_group"]
    halves = Halves(n, rows)
    per_half, chunk_cols = part.shape[0] // 2, part.shape[2]

    def compute(chunk):
        h, q = divmod(chunk, per_half)
        lanes = slice(q * chunk_cols, (q + 1) * chunk_cols)

        def tile(index, start, size):
            part[chunk, start : start + size, :] = dot(
                halves.load(attn, index), wo[:, lanes], NN
            ).astype(BF16)

        halves.each(h, tile)

    reduce = LineReduce(n, half, part, ref["v_got"], [ref[f"r_sem{i}"] for i in range(4)])
    g_sems = [ref[f"g_sem{i}"] for i in range(4)]
    gathers = [LineGather(n, rows, group, g_sems, (h, half)) for h in range(2)]
    branch, resid = ref["v_branch"], ref["v_resid"]
    gate, up, hidden = ref["v_gate"], ref["v_up"], ref["v_hidden"]

    def finish(h):
        where = slice(h * half, (h + 1) * half)
        reduce.last(branch.at[h], range(h * per_half, (h + 1) * per_half))
        values = branch[h]
        total = x_ref[where, :].astype(F32) + values * inverse_rms(values) * post_ref[0:1, :]
        resid[h] = total
        group[pl.ds(u, 1), where, :] = total.astype(BF16)[None]

    ff = gate.shape[2]
    ntile, tsize = tiles(ff, 512)

    def body(h, t):
        lanes = slice(t * tsize, (t + 1) * tsize)

        def tile(index, start, size):
            inputs = halves.load(group, index)
            gates = dot(inputs, wg[0, :, :, lanes].reshape(width, tsize), NN)
            ups = dot(inputs, wg[1, :, :, lanes].reshape(width, tsize), NN)
            halves.store(gate, index, lanes, gates.astype(BF16))
            halves.store(up, index, lanes, ups.astype(BF16))
            halves.store(
                hidden, index, lanes, (gates * jax.nn.sigmoid(gates) * ups).astype(BF16)
            )

        halves.each(h, tile)
        if h == 1:
            for name, src in (("o_hidden", hidden), ("o_gate", gate), ("o_up", up)):
                keep(src.at[:, :, lanes], ref[name].at[:, :, lanes])

    def hook(label):
        if label == "started":
            w_b.middle()
            w_c.start()
        if label == "sent":
            w_b.corner()
        if label == "b1":
            w_b.arrive()
            load(ref["o_wgb"], wg.at[0, :, upper])
        if label == f"b{n - 2}":
            w_c.middle()
        if label == "first":
            keep(branch, ref["o_branch"])
            keep(resid, ref["o_resid"])
            w_c.corner()
            w_d.start()
            w_c.arrive()
            load(ref["o_wgc"], wg.at[1])
            load.finish((table,))
        if label == f"g{n - 2}":
            keep(group, ref["o_group"])

    reduce_norm_gather(n, reduce, gathers, compute, finish, Consume(ntile, body), hook)
    w_d.middle()
    w_d.corner()
    w_d.arrive()
    for k in range(3):
        home(k, c ^ (3 - k), c).wait_send()
    for copy in copies:
        copy.wait_send()
    for work in (w_qkv, w_out, w_a, w_b, w_c, w_d, gather):
        work.finish()
    keep.finish()


def forward(n, x, w, table, gain, seg, wo, gu, down, post):
    rows, width = x.shape
    span, cols, half = n * rows, w.shape[2], rows // 2
    quarter = cols // 4
    kb, ff = gu.shape[1:]
    ntile = tiles(ff, 512)[0]
    dma = pltpu.SemaphoreType.DMA
    ins = {
        "x": (x, VM),
        "w": (w, HB),
        "table": (table, HB),
        "gain": (gain, VM),
        "seg": (seg, VM),
        "wo": (wo, HB),
        "gu": (gu, HB),
        "down": (down, HB),
        "post": (post, VM),
    }
    outs = {
        "o_xg": ((span, width), BF16),
        "o_wq": ((3, width, cols), BF16),
        "o_wo": ((8,) + wo.shape, BF16),
        "o_wga": ((8, kb // 2, ff), BF16),
        "o_wgb": ((8, kb // 2, ff), BF16),
        "o_wgc": ((8, kb, ff), BF16),
        "o_wd": ((8,) + down.shape, BF16),
        "o_proj": ((2, span, cols), F32),
        "o_inv": ((span, 128), F32),
        "o_every": ((4, 3, span, quarter), BF16),
        "o_att": ((4, quarter, span), F32),
        "o_lse": ((4, quarter // HEAD_DIM, 8, span), F32),
        "o_bound": ((8, 128), jnp.int32),
        "o_attn": ((n, rows, cols), BF16),
        "o_branch": ((2, half, width), F32),
        "o_resid": ((2, half, width), F32),
        "o_group": ((n, rows, width), BF16),
        "o_gate": ((n, rows, ff), BF16),
        "o_up": ((n, rows, ff), BF16),
        "o_hidden": ((n, rows, ff), BF16),
    }
    buffers = {
        "v_xg": ((span, width), BF16),
        "v_wq": ((3, width, cols), BF16),
        "v_tab": ((span, 128), F32),
        "v_proj": ((2, span, cols), F32),
        "v_inv": ((span, 128), F32),
        "v_msg": ((n, 8, span), F32),
        "v_qkv": ((4, 3, span, quarter), BF16),
        "v_every": ((4, 3, span, quarter), BF16),
        "v_back": ((4, n, rows, quarter), BF16),
        "v_zmsg": ((4, 8, 128), F32),
        "v_bound": ((8, 128), jnp.int32),
        "v_peaks": ((8, span), F32),
        "v_sums": ((8, span), F32),
        "v_acct": ((HEAD_DIM, span), F32),
        "v_att": ((4, quarter, span), F32),
        "v_lse": ((4, quarter // HEAD_DIM, 8, span), F32),
        "v_attn": ((n, rows, cols), BF16),
        "v_wo": ((cols, width), BF16),
        "v_wg": ((2, 8, kb, ff), BF16),
        "v_group": ((n, rows, width), BF16),
        "v_branch": ((2, half, width), F32),
        "v_resid": ((2, half, width), F32),
        "v_gate": ((n, rows, ff), BF16),
        "v_up": ((n, rows, ff), BF16),
        "v_hidden": ((n, rows, ff), BF16),
        "v_part": ((4, n * half, width // 2), BF16),
        "v_got": ((4, (n + 1) * half, width // 2), BF16),
    }
    sems = {
        "keep_sem": (12 + 3 * ntile,),
        "load_sem": (4,),
        "wo_sem": (8,),
        "w_send": (6, 9),
        "w_recv": (6, 9),
        "w_local": (6,),
        "m_send": (n - 1,),
        "m_recv": (n - 1,),
    }
    for name in ("a_send", "a_recv", "z_send", "z_recv", "b_send", "b_recv"):
        sems[name] = (3,)
    for i in range(4):
        sems[f"x_sem{i}"] = (n - 1,)
        sems[f"r_sem{i}"] = (n - 1, 4)
        sems[f"g_sem{i}"] = (n - 1, 2)
    names = [*ins, *outs, *buffers, *sems]
    results = pl.pallas_call(
        functools.partial(forward_kernel, n, names),
        out_shape=[shape(*out) for out in outs.values()],
        in_specs=[spec for value, spec in ins.values()],
        out_specs=[HB] * len(outs),
        scratch_shapes=[pltpu.VMEM(*buffer) for buffer in buffers.values()]
        + [dma(dims) for dims in sems.values()],
        compiler_params=pltpu.CompilerParams(
            collective_id=10, has_side_effects=True, vmem_limit_bytes=VMEM_LIMIT
        ),
        name="forward",
    )(*[value for value, spec in ins.values()])
    return dict(zip(outs, results))


def load_blocks(src, dst, sem, axis):
    blocks = src.shape[0]
    size = dst.shape[axis] // blocks
    copies = []
    for b in range(blocks):
        where = [slice(None)] * len(dst.shape)
        where[axis] = pl.ds(b * size, size)
        copies.append(pltpu.make_async_copy(src.at[b], dst.at[tuple(where)], sem.at[b]))
    for copy in copies:
        copy.start()
    return copies


def wait_all(copies):
    for copy in copies:
        copy.wait()


def mlp_in_kernel(
    n,
    attn_ref,
    wo_ref,
    x_ref,
    gain_ref,
    wga_ref,
    wgb_ref,
    gu_ref,
    down_ref,
    branch_out,
    resid_out,
    group_out,
    gate_out,
    up_out,
    hidden_out,
    wgc_out,
    wd_out,
    wo,
    wg,
    group,
    branch,
    resid,
    gate,
    up,
    hidden,
    part,
    got_rows,
    sem_o,
    local_sem,
    keep_sem,
    w_send,
    w_recv,
    *sems,
):
    s, c, u = where_am_i()
    rows, width = x_ref.shape
    load_o = load_blocks(wo_ref, wo, sem_o, 1)
    kb = wgc_out.shape[1]
    load_g = [
        pltpu.make_async_copy(wga_ref, wg.at[0, :, pl.ds(0, kb // 2)], local_sem.at[0]),
        pltpu.make_async_copy(wgb_ref, wg.at[0, :, pl.ds(kb // 2, kb // 2)], local_sem.at[1]),
        pltpu.make_async_copy(wgc_out, wg.at[1], local_sem.at[2]),
    ]
    greet(line_peers(n) + plane_peers() + [(None, (1 - s, c, u))])

    def plane(k, src, out, half_rows):
        return PlaneGather(
            src, lambda b: out.at[b], half_rows, w_send.at[k], w_recv.at[k], local_sem.at[3 + k]
        )

    first = plane(0, gu_ref.at[1], wgc_out, kb // 2)
    second = plane(1, down_ref, wd_out, down_ref.shape[0] // 2)
    first.start()
    load_g[0].start()
    load_g[1].start()
    wait_all(load_o)
    halves = Halves(n, rows)
    half = rows // 2
    per_half = part.shape[0] // 2
    chunk_cols = part.shape[2]

    def compute(chunk):
        h, q = divmod(chunk, per_half)
        cols = slice(q * chunk_cols, (q + 1) * chunk_cols)

        def tile(index, start, size):
            part[chunk, start : start + size, :] = dot(
                halves.load(attn_ref, index), wo[:, cols], NN
            ).astype(BF16)

        halves.each(h, tile)

    reduce = LineReduce(n, half, part, got_rows, sems[:4])
    gathers = [LineGather(n, rows, group, sems[4:], (h, half)) for h in range(2)]
    kept = []

    def keep(src, dst):
        copy = pltpu.make_async_copy(src, dst, keep_sem.at[len(kept)])
        copy.start()
        kept.append(copy)

    def finish(h):
        where = slice(h * half, (h + 1) * half)
        reduce.last(branch.at[h], range(h * per_half, (h + 1) * per_half))
        values = branch[h]
        total = x_ref[where, :].astype(F32) + values * inverse_rms(values) * gain_ref[0:1, :]
        resid[h] = total
        group[pl.ds(u, 1), where, :] = total.astype(BF16)[None]

    ff = gate.shape[2]
    ntile, tsize = tiles(ff, 512)

    def body(h, t):
        lanes = slice(t * tsize, (t + 1) * tsize)

        def tile(index, start, size):
            inputs = halves.load(group, index)
            gates = dot(inputs, wg[0, :, :, lanes].reshape(width, tsize), NN)
            ups = dot(inputs, wg[1, :, :, lanes].reshape(width, tsize), NN)
            halves.store(gate, index, lanes, gates.astype(BF16))
            halves.store(up, index, lanes, ups.astype(BF16))
            halves.store(
                hidden, index, lanes, (gates * jax.nn.sigmoid(gates) * ups).astype(BF16)
            )

        halves.each(h, tile)
        if h == 1:
            for src, dst in ((hidden, hidden_out), (gate, gate_out), (up, up_out)):
                keep(src.at[:, :, lanes], dst.at[:, :, lanes])

    def hook(label):
        if label == "b1":
            first.middle()
            second.start()
        if label == "first":
            keep(branch, branch_out)
            keep(resid, resid_out)
            first.corner()
            first.arrive()
            load_g[2].start()
            wait_all(load_g)
        if label == f"g{n - 2}":
            keep(group, group_out)
        if label == "t0":
            second.middle()

    reduce_norm_gather(n, reduce, gathers, compute, finish, Consume(ntile, body), hook)
    second.corner()
    second.arrive()
    for work in (first, second):
        work.finish()
    wait_all(kept)


def reduce_scratch(n, rows, width):
    cols = width // CHUNKS
    return [
        pltpu.VMEM((CHUNKS, n * rows, cols), BF16),
        pltpu.VMEM((CHUNKS, (n + 1) * rows, cols), BF16),
    ]


def half_scratch(n, rows, width):
    half, cols = rows // 2, width // 2
    return [
        pltpu.VMEM((4, n * half, cols), BF16),
        pltpu.VMEM((4, (n + 1) * half, cols), BF16),
    ]


def mlp_in(n, attn, wo, x, gain, wga, wgb, gu, down):
    rows, width = x.shape
    span, cols = attn.shape
    kb, ff = gu.shape[1:]
    ntile = tiles(ff, 512)[0]
    outs = pl.pallas_call(
        functools.partial(mlp_in_kernel, n),
        out_shape=(
            shape((2, rows // 2, width), F32),
            shape((2, rows // 2, width), F32),
            shape((n, rows, width), BF16),
            shape((n, rows, ff), BF16),
            shape((n, rows, ff), BF16),
            shape((n, rows, ff), BF16),
            shape((8, kb, ff), BF16),
            shape((8,) + down.shape, BF16),
        ),
        in_specs=[VM, HB, VM, VM, HB, HB, HB, HB],
        out_specs=(HB,) * 8,
        scratch_shapes=[
            pltpu.VMEM((cols, width), BF16),
            pltpu.VMEM((2, 8, kb, ff), BF16),
            pltpu.VMEM((n, rows, width), BF16),
            pltpu.VMEM((2, rows // 2, width), F32),
            pltpu.VMEM((2, rows // 2, width), F32),
            pltpu.VMEM((n, rows, ff), BF16),
            pltpu.VMEM((n, rows, ff), BF16),
            pltpu.VMEM((n, rows, ff), BF16),
        ]
        + half_scratch(n, rows, width)
        + [
            pltpu.SemaphoreType.DMA((8,)),
            pltpu.SemaphoreType.DMA((5,)),
            pltpu.SemaphoreType.DMA((3 + 3 * ntile,)),
            pltpu.SemaphoreType.DMA((2, 9)),
            pltpu.SemaphoreType.DMA((2, 9)),
        ]
        + line_sems(n, 4)
        + line_sems(n, 2),
        compiler_params=pltpu.CompilerParams(
            collective_id=4, has_side_effects=True, vmem_limit_bytes=VMEM_LIMIT
        ),
        name="mlp_in",
    )(attn.reshape(n, rows, cols), wo, x, gain, wga, wgb, gu, down)
    return outs


def mlp_out_kernel(
    n,
    hidden_ref,
    wd_ref,
    resid_ref,
    gain_ref,
    cot_ref,
    gate_hbm,
    up_hbm,
    gresid_ref,
    out_ref,
    group_out,
    dgu_out,
    dgain_ref,
    hidden_s,
    resid_s,
    dmlp_s,
    dgu_s,
    wd,
    mlp,
    group,
    gate_ref,
    up_ref,
    dgu,
    part,
    got_rows,
    sem_d,
    local_sem,
    keep_sem,
    s_send,
    s_recv,
    *sems,
):
    s, c, u = where_am_i()
    rows, width = cot_ref.shape
    load_d = load_blocks(wd_ref, wd, sem_d, 1)
    load_g = [
        pltpu.make_async_copy(gate_hbm, gate_ref, local_sem.at[0]),
        pltpu.make_async_copy(up_hbm, up_ref, local_sem.at[1]),
    ]
    greet(line_peers(n) + [(None, (1 - s, c, u))])
    sibling = Sibling(s_send, s_recv)
    halves = Halves(n, rows)
    half = rows // 2
    per_half = part.shape[0] // 2
    chunk_cols = part.shape[2]

    def compute(chunk):
        h, q = divmod(chunk, per_half)
        cols = slice(q * chunk_cols, (q + 1) * chunk_cols)
        if h == 0:
            wait_all(load_d[q * (8 // per_half) : (q + 1) * (8 // per_half)])

        def tile(index, start, size):
            part[chunk, start : start + size, :] = dot(
                halves.load(hidden_ref, index), wd[:, cols], NN
            ).astype(BF16)

        halves.each(h, tile)

    reduce = LineReduce(n, half, part, got_rows, sems[:4])
    gathers = [LineGather(n, rows, group, sems[4:], (h, half)) for h in range(2)]
    dgain_ref[...] = jnp.zeros_like(dgain_ref)

    def finish(h):
        where = slice(h * half, (h + 1) * half)
        reduce.last(mlp.at[h], range(h * per_half, (h + 1) * per_half))
        values = mlp[h]
        grad = cot_ref[where, :].astype(F32)
        d_mlp = norm_back(values, inverse_rms(values), grad * gain_ref[1:2, :], width)
        group[pl.ds(u, 1), where, :] = d_mlp.astype(BF16)[None]

    def rest(h):
        where = slice(h * half, (h + 1) * half)
        values = mlp[h]
        scaled = values * inverse_rms(values)
        out_ref[where, :] = (resid_ref[h] + scaled * gain_ref[1:2, :]).astype(BF16)
        dgain_ref[...] += jnp.sum(cot_ref[where, :].astype(F32) * scaled, axis=0, keepdims=True)

    ff = gate_ref.shape[2]
    ntile, tsize = tiles(ff, 512)
    kept = []

    def keep(src, dst):
        copy = pltpu.make_async_copy(src, dst, keep_sem.at[len(kept)])
        copy.start()
        kept.append(copy)

    def body(h, t):
        lanes = slice(t * tsize, (t + 1) * tsize)

        def tile(index, start, size):
            d_hidden = dot(halves.load(group, index), wd[lanes, :], NT)
            gate = halves.load(gate_ref, index, lanes).astype(F32)
            up = halves.load(up_ref, index, lanes).astype(F32)
            sig = jax.nn.sigmoid(gate)
            slope = sig * (1.0 + gate * (1.0 - sig))
            halves.store(dgu.at[0], index, lanes, (d_hidden * up * slope).astype(BF16))
            halves.store(dgu.at[1], index, lanes, (d_hidden * (gate * sig)).astype(BF16))

        halves.each(h, tile)
        where = pl.ds(h * half, half)
        view = dgu.at[:, :, where, lanes]
        sibling.start(view, dgu_s.at[:, :, where, lanes])
        keep(view, dgu_out.at[:, :, where, lanes])

    def hook(label):
        if label == "sent":
            sibling.start(hidden_ref, hidden_s)
            lanes = pl.ds(pl.multiple_of((1 - s) * (width // 2), width // 2), width // 2)
            sibling.start(gresid_ref.at[:, :, lanes], resid_s)
            for copy in load_g:
                copy.start()
        if label == "half":
            rest(0)
        if label == "first":
            rest(1)
            wait_all(load_g)
        if label == f"g{n - 2}":
            lanes = pl.ds(pl.multiple_of((1 - s) * (width // 2), width // 2), width // 2)
            sibling.start(group.at[:, :, lanes], dmlp_s)
            keep(group, group_out)

    reduce_norm_gather(n, reduce, gathers, compute, finish, Consume(ntile, body), hook)
    for i in range(3 + 2 * ntile):
        sibling.wait(i)
    sibling.finish()
    wait_all(kept)


def mlp_out(n, hidden, wd, resid, gain, cot, gate, up, gresid):
    rows, width = cot.shape
    ff = hidden.shape[2]
    ntile = tiles(ff, 512)[0]
    return pl.pallas_call(
        functools.partial(mlp_out_kernel, n),
        out_shape=(
            shape((rows, width), BF16),
            shape((n, rows, width), BF16),
            shape((2, n, rows, ff), BF16),
            shape((1, width), F32),
            shape((n, rows, ff), BF16),
            shape((n, rows, width // 2), BF16),
            shape((n, rows, width // 2), BF16),
            shape((2, n, rows, ff), BF16),
        ),
        in_specs=[VM, HB, VM, VM, VM, HB, HB, HB],
        out_specs=(VM, HB, HB, VM, HB, HB, HB, HB),
        scratch_shapes=[
            pltpu.VMEM((ff, width), BF16),
            pltpu.VMEM((2, rows // 2, width), F32),
            pltpu.VMEM((n, rows, width), BF16),
            pltpu.VMEM((n, rows, ff), BF16),
            pltpu.VMEM((n, rows, ff), BF16),
            pltpu.VMEM((2, n, rows, ff), BF16),
        ]
        + half_scratch(n, rows, width)
        + [
            pltpu.SemaphoreType.DMA((8,)),
            pltpu.SemaphoreType.DMA((2,)),
            pltpu.SemaphoreType.DMA((1 + 2 * ntile,)),
            pltpu.SemaphoreType.DMA((3 + 2 * ntile,)),
            pltpu.SemaphoreType.DMA((3 + 2 * ntile,)),
        ]
        + line_sems(n, 4)
        + line_sems(n, 2),
        compiler_params=pltpu.CompilerParams(
            collective_id=5, has_side_effects=True, vmem_limit_bytes=VMEM_LIMIT
        ),
        name="mlp_out",
    )(hidden, wd, resid, gain, cot, gate, up, gresid)


def mlp_back_kernel(
    n,
    dgu_hbm,
    wga_ref,
    wgb_ref,
    wgc_ref,
    cot_ref,
    branch_ref,
    gain_ref,
    wo_ref,
    hidden_hbm,
    dmlp_hbm,
    resid_hbm,
    hidden_s_hbm,
    dmlp_s_hbm,
    resid_s_hbm,
    dgu_s_hbm,
    dresid_ref,
    group_out,
    dattn_ref,
    dgain_ref,
    gown_out,
    gx_out,
    gy_out,
    down_own_out,
    down_x_out,
    down_y_out,
    wo,
    wg,
    group,
    part,
    got_rows,
    dgu_ref,
    hidden,
    hidden_s,
    dmlp,
    dmlp_s,
    gate_in,
    ring_d,
    ring_g,
    got_d,
    got_g,
    sem_o,
    sem_in,
    local_sem,
    d_send,
    d_recv,
    d_local,
    g_send,
    g_recv,
    g_local,
    *sems,
):
    s, c, u = where_am_i()
    rows, width = cot_ref.shape
    half = wga_ref.shape[1]
    chunk_cols = width // part.shape[0]
    per_chunk = chunk_cols // (2 * half)
    chunks = part.shape[0]

    def load_chunk(chunk):
        slot = chunk % 2
        where = pl.ds(chunk * per_chunk, per_chunk)
        return [
            pltpu.make_async_copy(
                wga_ref.at[where], wg.at[slot, 0, :, pl.ds(0, half)], local_sem.at[slot, 0]
            ),
            pltpu.make_async_copy(
                wgb_ref.at[where], wg.at[slot, 0, :, pl.ds(half, half)], local_sem.at[slot, 1]
            ),
            pltpu.make_async_copy(wgc_ref.at[where], wg.at[slot, 1], local_sem.at[slot, 2]),
        ]

    def start_chunk(chunk):
        for copy in load_chunk(chunk):
            copy.start()

    def fetch(k, src, dst):
        copy = pltpu.make_async_copy(src, dst, sem_in.at[k])
        copy.start()
        return copy

    load_dgu = fetch(0, dgu_hbm, dgu_ref)
    start_chunk(0)
    load_d = [
        fetch(1, hidden_hbm, hidden),
        fetch(2, half_columns(dmlp_hbm, s), dmlp),
        fetch(3, hidden_s_hbm, hidden_s),
        fetch(4, dmlp_s_hbm, dmlp_s),
    ]
    start_chunk(1)
    load_g = []
    if gate_in:
        resid, resid_s, dgu_s = gate_in
        load_g = [
            fetch(5, half_columns(resid_hbm, s), resid),
            fetch(6, resid_s_hbm, resid_s),
            fetch(7, dgu_s_hbm, dgu_s),
        ]
    load_o = load_blocks(wo_ref, wo, sem_o, 1)
    greet(line_peers(n) + plane_peers())
    load_dgu.wait()
    span = n * rows
    count, size = tiles(span, 512)

    def compute(chunk):
        wait_all(load_chunk(chunk))
        slot = chunk % 2

        def tile(i, carry):
            where = pl.ds(pl.multiple_of(i * size, size), size)
            part[chunk, where, :] = (
                dot(dgu_ref[0, where, :], wg[slot, 0].reshape(chunk_cols, -1), NT)
                + dot(dgu_ref[1, where, :], wg[slot, 1].reshape(chunk_cols, -1), NT)
            ).astype(BF16)
            return carry

        lax.fori_loop(0, count, tile, 0)
        if chunk + 2 < chunks:
            start_chunk(chunk + 2)

    rows_d, cols_g = ring_d.shape[2], ring_g.shape[3]
    tiles_g = dgu_hbm.shape[2] // cols_g

    def place_d(out, piece, part):
        size = rows_d if part is None else rows_d // 2
        return out.at[pl.ds(piece * rows_d + (part or 0) * size, size)]

    def place_g(out, piece, part):
        size = ring_g.shape[2] if part is None else ring_g.shape[2] // 2
        ci, tile = piece // tiles_g, piece % tiles_g
        return out.at[ci, pl.ds((part or 0) * size, size), pl.ds(tile * cols_g, cols_g)]

    down = PlaneReduce(
        ring_d, got_d, (down_own_out, down_x_out, down_y_out), place_d, d_send, d_recv, d_local
    )
    gate = PlaneReduce(ring_g, got_g, (gown_out, gx_out, gy_out), place_g, g_send, g_recv, g_local)
    down_piece = wide_piece(
        (hidden, dmlp), (hidden_s, dmlp_s), lambda p: slice(p * rows_d, (p + 1) * rows_d)
    )

    def gate_right(ref, piece):
        tile = piece % tiles_g
        return ref[piece // tiles_g, :, tile * cols_g : (tile + 1) * cols_g]

    n_d, n_g = got_d.shape[0], got_g.shape[0] if gate_in else 0
    work = [(down, p, down_piece) for p in range(n_d)]
    if gate_in:
        gate_piece = tall_piece((resid, dgu_ref), (resid_s, dgu_s), gate_right)
        work += [(gate, p, gate_piece) for p in range(n_g)]
    pieces = Pieces(work)

    def compute_and_piece(chunk):
        compute(chunk)
        if chunk == 0:
            wait_all(load_d)
        if chunk < 2:
            pieces.step()

    def reduce_hook(slot):
        if slot == 0:
            wait_all(load_g)
        pieces.step()

    LineReduce(n, rows, part, got_rows, sems[:4]).run(compute_and_piece, dresid_ref, reduce_hook)
    d_resid = dresid_ref[...] + cot_ref[...].astype(F32)
    dresid_ref[...] = d_resid
    branch = branch_ref[...]
    inverse = inverse_rms(branch)
    d_branch = norm_back(branch, inverse, d_resid * gain_ref[0:1, :], width)
    small = group.shape[0] == span
    if small:
        group[rows_of(u, rows), :] = d_branch.astype(BF16)
        gather = LineGather(n, rows, group, sems[4:])
    else:
        group[:rows, :] = d_branch.astype(BF16)
        own = pltpu.make_async_copy(
            group.at[pl.ds(0, rows)], group_out.at[rows_of(u, rows)], local_sem.at[2, 2]
        )
        own.start()
        own.wait()
        gather = LineGather(n, rows, group_out, sems[4:])
    gather.send(0)
    dgain_ref[...] = jnp.sum(d_resid * branch * inverse, axis=0, keepdims=True)
    wait_all(load_o)
    pieces.step()

    def gather_hook(slot):
        pieces.step()

    gather.run(gather_hook)
    if small:
        keep = pltpu.make_async_copy(group, group_out, local_sem.at[2, 2])
        keep.start()

    def tile(j, carry):
        where = pl.ds(pl.multiple_of(j * size, size), size)
        if small:
            rows_in = group[where, :]
        else:
            fetch = pltpu.make_async_copy(group_out.at[where], group, local_sem.at[2, 2])
            fetch.start()
            fetch.wait()
            rows_in = group[...]
        d_attn = dot(rows_in, wo[...], NT).astype(BF16)
        if len(dattn_ref.shape) == 3:
            cols = dattn_ref.shape[2]
            for q in range(4):
                dattn_ref[q, where, :] = d_attn[:, q * cols : (q + 1) * cols]
        else:
            dattn_ref[where, :] = d_attn
        return carry

    lax.fori_loop(0, count, tile, 0)
    pieces.finish()
    down.finish(n_d)
    gate.finish(n_g)
    if small:
        keep.wait()


def piece_scratch(slots, pieces, rows, cols):
    return (
        [pltpu.VMEM((slots, 4, rows, cols), BF16), pltpu.VMEM((pieces, rows, cols), BF16)],
        [
            pltpu.SemaphoreType.DMA((pieces, 6)),
            pltpu.SemaphoreType.DMA((pieces, 6)),
            pltpu.SemaphoreType.DMA((pieces,)),
        ],
    )


def mlp_back(
    n,
    dgu,
    wga,
    wgb,
    wgc,
    cot,
    branch,
    gain,
    wo,
    hidden,
    dmlp,
    resid,
    hidden_s,
    resid_s,
    dmlp_s,
    dgu_s,
):
    rows, width = branch.shape
    span, ff = dgu.shape[1:]
    cols = wo.shape[1]
    kb, kc = width // 8, wo.shape[2]
    count, size = tiles(ff, 512)
    ring_d, sems_d = piece_scratch(min(3, count), count, size, kc)
    here = 2 * count - LATER
    ring_g, sems_g = piece_scratch(min(3, max(here, 1)), max(here, 1), kb, size)
    chunk_blocks = width // CHUNKS // kb
    return pl.pallas_call(
        functools.partial(mlp_back_kernel, n),
        out_shape=(
            shape((rows, width), F32),
            shape((span, width), BF16),
            shape((4, span, cols // 4) if spread_heads(cols) else (span, cols), BF16),
            shape((1, width), F32),
        )
        + (shape((2, kb, ff), BF16),) * 3
        + (shape((ff, kc), BF16),) * 3,
        in_specs=[HB, HB, HB, HB, VM, VM, VM] + [HB] * 8,
        out_specs=(VM, HB, VM, VM) + (HB,) * 6,
        scratch_shapes=[
            pltpu.VMEM((cols, width), BF16),
            pltpu.VMEM((2, 2, chunk_blocks, kb, ff), BF16),
            pltpu.VMEM((min(span, 512), width), BF16),
        ]
        + reduce_scratch(n, rows, width)
        + [
            pltpu.VMEM((2, span, ff), BF16),
            pltpu.VMEM((span, ff), BF16),
            pltpu.VMEM((span, ff), BF16),
            pltpu.VMEM((span, width // 2), BF16),
            pltpu.VMEM((span, width // 2), BF16),
            (
                pltpu.VMEM((span, width // 2), BF16),
                pltpu.VMEM((span, width // 2), BF16),
                pltpu.VMEM((2, span, ff), BF16),
            )
            if here > 0
            else (),
            ring_d[0],
            ring_g[0],
            ring_d[1],
            ring_g[1],
            pltpu.SemaphoreType.DMA((8,)),
            pltpu.SemaphoreType.DMA((8,)),
            pltpu.SemaphoreType.DMA((3, 3)),
        ]
        + sems_d
        + sems_g
        + line_sems(n, CHUNKS)
        + line_sems(n),
        compiler_params=pltpu.CompilerParams(
            collective_id=6, has_side_effects=True, vmem_limit_bytes=VMEM_LIMIT
        ),
        name="mlp_back",
    )(
        dgu,
        wga,
        wgb,
        wgc,
        cot,
        branch,
        gain,
        wo,
        hidden,
        dmlp,
        resid,
        hidden_s,
        dmlp_s,
        resid_s,
        dgu_s,
    )


def proj_back_kernel(
    n,
    dproj_ref,
    wq_ref,
    dresid_ref,
    xg_ref,
    gcols_ref,
    gattn_ref,
    gmlp_ref,
    attn_ref,
    dbranch_ref,
    resid_hbm,
    resid_s_hbm,
    dgu_hbm,
    dgu_s_hbm,
    own_in,
    x_in,
    y_in,
    out_ref,
    gain_ref,
    own_out,
    x_out,
    y_out,
    oown_out,
    ox_out,
    oy_out,
    gown_out,
    gx_out,
    gy_out,
    wq,
    xs,
    xs_s,
    dproj_s,
    dbranch,
    dbranch_s,
    attn_s,
    total,
    part,
    got_rows,
    ring,
    got,
    sums,
    ring_o,
    got_o,
    late_buffers,
    late_sems,
    o_sems,
    local_sem,
    s_send,
    s_recv,
    q_send,
    q_recv,
    q_local,
    v_send,
    v_recv,
    m_send,
    m_recv,
    *sems,
):
    s, c, u = where_am_i()
    rows, width = dresid_ref.shape
    span = n * rows
    load = [
        pltpu.make_async_copy(wq_ref, wq, local_sem.at[0]),
        pltpu.make_async_copy(half_columns(xg_ref, s), xs, local_sem.at[1]),
        pltpu.make_async_copy(half_columns(dbranch_ref, s), dbranch, local_sem.at[2]),
    ]
    last = 2 * (dgu_hbm.shape[2] // late_buffers[2].shape[1])
    late = LatePiece(
        last - 1,
        (resid_hbm, resid_s_hbm, dgu_hbm, dgu_s_hbm),
        (gown_out, gx_out, gy_out),
        late_buffers,
        late_sems,
    )
    late.load()
    for copy in load:
        copy.start()
    corner = (s, c ^ 3, u)
    greet(all_uly_peers(n) + plane_peers() + [(None, corner), (None, (1 - s, c, u))])
    gains = GainSum(n, sums, (v_send, v_recv, m_send, m_recv))
    gains.start(gcols_ref, gattn_ref, gmlp_ref)
    sibling = Sibling(s_send, s_recv)
    sibling.start(attn_ref, attn_s)
    sibling.start(half_columns(dbranch_ref, 1 - s), dbranch_s)
    sibling.start(half_columns(xg_ref, 1 - s), xs_s)
    sibling.start(dproj_ref, dproj_s)
    load[0].wait()
    chunk_cols = width // part.shape[0]
    count, size = tiles(span, 512)

    def compute(chunk):
        cols = slice(chunk * chunk_cols, (chunk + 1) * chunk_cols)

        def tile(i, carry):
            where = pl.ds(pl.multiple_of(i * size, size), size)
            part[chunk, where, :] = (
                dot(dproj_ref[0, where, :], wq[0, cols, :], NT)
                + dot(dproj_ref[1, where, :], wq[1, cols, :], NT)
                + dot(dproj_ref[2, where, :], wq[2, cols, :], NT)
            ).astype(BF16)
            return carry

        lax.fori_loop(0, count, tile, 0)

    def place(out, piece, part):
        size = ring.shape[2] if part is None else ring.shape[2] // 2
        return out.at[piece, pl.ds((part or 0) * size, size)]

    weight = PlaneReduce(ring, got, (own_out, x_out, y_out), place, q_send, q_recv, q_local)
    compute_piece = tall_piece((xs, dproj_ref), (xs_s, dproj_s), lambda ref, piece: ref[piece])

    def place_o(out, piece, part):
        size = ring_o.shape[2] if part is None else ring_o.shape[2] // 2
        return out.at[pl.ds((part or 0) * size, size)]

    out_weight = PlaneReduce(ring_o, got_o, (oown_out, ox_out, oy_out), place_o, *o_sems)
    out_piece = wide_piece((attn_ref, dbranch), (attn_s, dbranch_s), lambda p: slice(None))
    pieces = Pieces(
        [late.work(), (out_weight, 0, out_piece)] + [(weight, p, compute_piece) for p in range(3)]
    )

    def compute_and_piece(chunk):
        compute(chunk)
        if chunk == 0:
            pieces.step()
        if chunk == 2:
            load[2].wait()
            sibling.wait(0)
            sibling.wait(1)
            pieces.step()

    def hook(slot):
        if slot == 0:
            load[1].wait()
            sibling.wait(2)
            sibling.wait(3)
            pieces.step()
            gains.over_ctx()
        if slot == 1:
            pieces.step()
            gains.over_uly()
        if slot == 2:
            pieces.step()

    LineReduce(n, rows, part, got_rows, sems[:4]).run(compute_and_piece, total, hook)
    out_ref[...] = (dresid_ref[...] + total[...]).astype(BF16)
    pieces.finish()
    gains.finish(gain_ref)
    weight.finish(3)
    out_weight.finish(1)
    late.plane.finish(1)
    sibling.finish()


class GainSum:
    def __init__(self, n, refs, sems):
        self.n = n
        self.all, self.core, self.plane, self.line = refs
        self.v_send, self.v_recv, self.m_send, self.m_recv = sems
        self.s, self.c, self.u = where_am_i()
        self.sent = []

    def copy(self, k, src, dst, peer):
        return remote(src, dst, self.v_send.at[k], self.v_recv.at[k], peer)

    def go(self, copy):
        copy.start()
        self.sent.append(copy)

    def start(self, cols, attn, mlp):
        half, local = self.all.shape[2], cols.shape[1]
        rows = jnp.zeros((8, half), F32)
        for h in range(2):
            self.all[h] = rows
        mine = self.u * local
        home = pl.ds(pl.multiple_of(lax.rem(mine, half), local), local)
        self.all[pl.ds(mine // half, 1), 0:2, home] = cols[...][None]
        for h in range(2):
            part = slice(h * half, (h + 1) * half)
            self.all[h, 2:3, :] = attn[:, part]
            self.all[h, 3:4, :] = mlp[:, part]
        self.go(self.copy(0, self.all.at[1 - self.s], self.core, (1 - self.s, self.c, self.u)))

    def over_ctx(self):
        s, c, u = self.s, self.c, self.u
        self.copy(0, self.all.at[s], self.core, (1 - s, c, u)).wait_recv()
        size = self.plane.shape[2]
        total = self.all[pl.ds(s, 1)][0] + self.core[...]
        for j in range(4):
            self.plane[j] = total[:, j * size : (j + 1) * size]
        for k in (1, 2, 3):
            self.go(self.copy(k, self.plane.at[c ^ k], self.line.at[k - 1], (s, c ^ k, u)))

    def over_uly(self):
        s, c, u = self.s, self.c, self.u
        total = self.plane[pl.ds(c, 1)][0]
        for k in (1, 2, 3):
            self.copy(k, self.plane.at[c ^ k], self.line.at[k - 1], (s, c ^ k, u)).wait_recv()
            total = total + self.line[k - 1]
        home = self.line.at[3 + u]
        self.line[pl.ds(3 + u, 1)] = total[None]
        for step in range(1, self.n):
            peer = (s, c, lax.rem(u + step, self.n))
            self.go(remote(home, home, self.m_send.at[step - 1], self.m_recv.at[step - 1], peer))

    def finish(self, out):
        s, c, u = self.s, self.c, self.u
        for step in range(1, self.n):
            source = lax.rem(u + self.n - step, self.n)
            place = self.line.at[3 + source]
            remote(
                place, place, self.m_send.at[step - 1], self.m_recv.at[step - 1], (s, c, source)
            ).wait_recv()
        total = self.line[3]
        for j in range(1, self.n):
            total = total + self.line[3 + j]
        out[...] = total[:4]
        for copy in self.sent:
            copy.wait_send()


def proj_back(
    n, dproj, wq, dresid, xg, gain_cols, gain_attn, gain_mlp, attn, dbranch, late, grads
):
    rows, width = dresid.shape
    span, cols = dproj.shape[1:]
    ring, sems = piece_scratch(3, 3, width // 8, cols)
    ring_o, sems_o = piece_scratch(1, 1, cols, width // 8)
    ff = late[2].shape[2]
    return pl.pallas_call(
        functools.partial(proj_back_kernel, n),
        out_shape=(shape((rows, width), BF16), shape((4, width // 8), F32))
        + (shape((3, width // 8, cols), BF16),) * 3
        + (shape((cols, width // 8), BF16),) * 3
        + tuple(shape(g.shape, BF16) for g in grads),
        in_specs=[VM, HB, VM, HB, VM, VM, VM, VM] + [HB] * 8,
        out_specs=(VM, VM) + (HB,) * 9,
        input_output_aliases={13: 8, 14: 9, 15: 10},
        scratch_shapes=[
            pltpu.VMEM((3, width, cols), BF16),
            pltpu.VMEM((span, width // 2), BF16),
            pltpu.VMEM((span, width // 2), BF16),
            pltpu.VMEM((3, span, cols), BF16),
            pltpu.VMEM((span, width // 2), BF16),
            pltpu.VMEM((span, width // 2), BF16),
            pltpu.VMEM((span, cols), BF16),
            pltpu.VMEM((rows, width), F32),
        ]
        + reduce_scratch(n, rows, width)
        + ring
        + [
            (
                pltpu.VMEM((2, 8, width // 2), F32),
                pltpu.VMEM((8, width // 2), F32),
                pltpu.VMEM((4, 8, width // 8), F32),
                pltpu.VMEM((3 + n, 8, width // 8), F32),
            ),
        ]
        + ring_o
        + LatePiece.scratch(span, width, ff)
        + [
            tuple(sems_o),
            pltpu.SemaphoreType.DMA((3,)),
            pltpu.SemaphoreType.DMA((4,)),
            pltpu.SemaphoreType.DMA((4,)),
        ]
        + sems
        + [
            pltpu.SemaphoreType.DMA((4,)),
            pltpu.SemaphoreType.DMA((4,)),
            pltpu.SemaphoreType.DMA((n - 1,)),
            pltpu.SemaphoreType.DMA((n - 1,)),
        ]
        + line_sems(n, CHUNKS),
        compiler_params=pltpu.CompilerParams(
            collective_id=7, has_side_effects=True, vmem_limit_bytes=VMEM_LIMIT
        ),
        name="proj_back",
    )(
        dproj,
        wq,
        dresid,
        xg,
        gain_cols,
        gain_attn,
        gain_mlp,
        attn,
        dbranch,
        *late,
        *grads,
    )


class PiecePlane(PlaneReduce):
    def __init__(self, ring, got, place, send, recv, local):
        super().__init__(ring, got, (0, 1, 2), place, send, recv, local)

    def halves(self):
        return 0, 1

    def own_copies(self, piece, blocks):
        return [
            pltpu.make_async_copy(
                blocks.at[self.c, h], self.place(0, piece, h), self.local.at[piece, h]
            )
            for h in range(2)
        ]

    def add(self, slot, block, half, piece):
        self.ring[slot, block, half] = (
            self.ring[slot, block, half].astype(F32) + self.got[piece, half].astype(F32)
        ).astype(BF16)


class Stream:
    def __init__(self, slots, sem, source, count):
        self.slots, self.sem, self.source, self.count = slots, sem, source, count
        for tile in range(slots.shape[0]):
            self.start(tile)

    def copy(self, tile):
        slot = tile % self.slots.shape[0]
        return pltpu.make_async_copy(self.source(tile), self.slots.at[slot], self.sem.at[slot])

    def start(self, tile):
        if tile < self.count:
            self.copy(tile).start()

    def wait(self, tile):
        self.copy(tile).wait()


def wide_blocks(own, other, out):
    rows = out.shape[2]

    def pair(i, carry):
        where = pl.ds(pl.multiple_of(i * 2 * rows, 2 * rows), 2 * rows)
        total = dot(own[0][...], own[1][:, where], TN) + dot(other[0][...], other[1][:, where], TN)
        total = total.astype(BF16)
        for j in range(2):
            part = total[:, j * rows : (j + 1) * rows]
            out[pl.ds(2 * i + j, 1)] = part.reshape(1, 2, rows, rows)
        return carry

    lax.fori_loop(0, 2, pair, 0)


def tall_blocks(own, other, out):
    rows = out.shape[2]

    def pair(i, carry):
        where = pl.ds(pl.multiple_of(i * 2 * rows, 2 * rows), 2 * rows)
        total = dot(own[0][:, where], own[1][...], TN) + dot(other[0][:, where], other[1][...], TN)
        total = total.astype(BF16)
        for j in range(2):
            for h in range(2):
                out[pl.ds(2 * i + j, 1), h] = total[
                    j * rows : (j + 1) * rows, h * rows : (h + 1) * rows
                ][None]
        return carry

    lax.fori_loop(0, 2, pair, 0)


def backward_kernel(n, names, *refs):
    ref = dict(zip(names, refs))
    s, c, u = where_am_i()
    cot_ref, gain_ref, qk_gain_ref = ref["cot"], ref["post"], ref["gain"]
    rows, width = cot_ref.shape
    span = n * rows
    weights, dgu, dgu_s = ref["v_weights"], ref["v_dgu"], ref["v_dgu_s"]
    hidden, hidden_s, dmlp, dmlp_s = [
        ref[f"v_{k}"] for k in ("hidden", "hidden_s", "dmlp", "dmlp_s")
    ]
    resid, resid_s, branch, attn = [ref[f"v_{k}"] for k in ("resid", "resid_s", "branch", "attn")]
    part, group, dresid = ref["v_part"], ref["v_group"], ref["v_dresid"]
    load = Keep(ref["load_sem"])
    chunks, chunk_cols = part.shape[0], part.shape[2]
    kb = ref["wgc"].shape[1]
    per_chunk = chunk_cols // kb
    lower, upper = kb // 2, kb // 2


    rows_g = ref["v_ring"].shape[3]
    rows_d = cols_g = 2 * rows_g
    tiles_g = dgu.shape[2] // cols_g
    n_d, n_g = hidden.shape[1] // rows_d, 2 * tiles_g

    def hidden_tile(view, piece):
        return view.at[:, pl.ds(piece * rows_d, rows_d)]

    def gate_tile(view, piece):
        ci, tile = divmod(piece, tiles_g)
        return view.at[ci, :, pl.ds(tile * cols_g, cols_g)]

    def load_chunk(chunk):
        slot, copies = chunk % 2, []
        for b in range(per_chunk):
            block = chunk * per_chunk + b
            at = slot * 2 * chunk_cols + b * kb
            for k, (src, first, size) in enumerate(
                (
                    (ref["wga"], at, lower),
                    (ref["wgb"], at + lower, upper),
                    (ref["wgc"], at + chunk_cols, kb),
                )
            ):
                copies.append(
                    pltpu.make_async_copy(
                        src.at[block],
                        weights.at[pl.ds(first, size)],
                        ref["chunk_sem"].at[slot, 3 * b + k],
                    )
                )
        return copies

    def start_chunk(chunk):
        for copy in load_chunk(chunk):
            copy.start()

    load_dgu = load(ref["dgu"], dgu)
    start_chunk(0)
    load_d = [
        load(ref["hidden"], hidden),
        load(half_columns(ref["dmlp"], s), dmlp),
        load(ref["dmlp_s"], dmlp_s),
    ]
    stream_d = Stream(hidden_s, ref["hs_sem"], lambda p: hidden_tile(ref["hidden_s"], p), n_d)
    start_chunk(1)
    load_g = [
        load(half_columns(ref["resid"], s), resid),
        load(ref["resid_s"], resid_s),
        load(ref["branch"], branch),
        load(ref["attn"], attn),
    ]
    stream_g = Stream(dgu_s, ref["ds_sem"], lambda p: gate_tile(ref["dgu_s"], p), n_g)
    wo_row = 4 * chunk_cols
    wo_cols = ref["wo"].shape[1]
    wo_view = weights.at[pl.ds(wo_row, wo_cols)]
    load_o = load_blocks(ref["wo"], wo_view, ref["wo_sem"], 1)
    peers = [(s, c ^ k, u) for k in (1, 2, 3)]
    greet(all_uly_peers(n) + [(None, peer) for peer in peers] + [(None, (1 - s, c, u))])
    sibling = Sibling(ref["s_send"], ref["s_recv"])
    sibling.start(half_columns(ref["xg"], 1 - s), ref["v_xs_s"])
    load_dgu.wait()
    count, size = tiles(span, 512)

    def compute(chunk):
        wait_all(load_chunk(chunk))
        at = (chunk % 2) * 2 * chunk_cols

        def tile(i, carry):
            where = pl.ds(pl.multiple_of(i * size, size), size)
            part[chunk, where, :] = (
                dot(dgu[0, where, :], weights[at : at + chunk_cols, :], NT)
                + dot(dgu[1, where, :], weights[at + chunk_cols : at + 2 * chunk_cols, :], NT)
            ).astype(BF16)
            return carry

        lax.fori_loop(0, count, tile, 0)
        if chunk + 2 < chunks:
            start_chunk(chunk + 2)

    def place(index, piece, half):
        if piece < n_d or piece == n_d + n_g:
            name, first = ("down", piece * rows_d) if piece < n_d else ("out", 0)
            rows = pl.ds(first + half * rows_g, rows_g)
            return ref[f"o_{name}{index}"].at[rows]
        if piece < n_d + n_g:
            ci, tile = divmod(piece - n_d, tiles_g)
            lanes = pl.ds(tile * cols_g + half * rows_g, rows_g)
            return ref[f"o_gate{index}"].at[ci, :, lanes]
        lanes = pl.ds(half * rows_g, rows_g)
        return ref[f"o_qkv{index}"].at[piece - n_d - n_g - 1, :, lanes]

    plane = PiecePlane(
        ref["v_ring"], ref["v_got_p"], place, ref["p_send"], ref["p_recv"], ref["p_local"]
    )
    def down_piece(out, piece):
        stream_d.wait(piece)
        own, other = hidden_tile(hidden, piece), hidden_s.at[piece % hidden_s.shape[0]]
        wide_blocks((own, dmlp), (other, dmlp_s), out)
        stream_d.start(piece + hidden_s.shape[0])

    def gate_piece(out, piece):
        number = piece - n_d
        stream_g.wait(number)
        own, other = gate_tile(dgu, number), dgu_s.at[number % dgu_s.shape[0]]
        tall_blocks((resid, own), (resid_s, other), out)
        stream_g.start(number + dgu_s.shape[0])

    def out_piece(out, piece):
        own = (attn, half_columns(group, s))
        wide_blocks(own, (ref["v_attn_s"], ref["v_dbranch_s"]), out)

    cols = attn.shape[1]
    dproj = hidden.at[:, pl.ds(0, 3 * cols)]

    def qkv_piece(out, piece):
        lanes = pl.ds((piece - n_d - n_g - 1) * cols, cols)
        own = (dmlp, hidden.at[:, lanes])
        tall_blocks(own, (ref["v_xs_s"], ref["v_dproj_s"].at[:, lanes]), out)

    kinds = [down_piece] * n_d + [gate_piece] * n_g + [out_piece] + [qkv_piece] * 3
    pieces = Pieces([(plane, p, kind) for p, kind in enumerate(kinds)], AHEAD)

    def compute_and_piece(chunk):
        compute(chunk)
        if chunk == 0:
            wait_all(load_d)
        if chunk < 2:
            pieces.step()

    def reduce_hook(slot):
        if slot == 0:
            wait_all(load_g)
        pieces.step()

    sem_r = [ref[f"r_sem{i}"] for i in range(4)]
    sem_b = [ref[f"b_sem{i}"] for i in range(4)]
    LineReduce(n, rows, part, ref["v_got"], sem_r).run(compute_and_piece, dresid, reduce_hook)
    d_resid = dresid[...] + cot_ref[...].astype(F32)
    dresid[...] = d_resid
    values = branch[...]
    inverse = inverse_rms(values)
    d_branch = norm_back(values, inverse, d_resid * gain_ref[0:1, :], width)
    group[rows_of(u, rows), :] = d_branch.astype(BF16)
    gather = LineGather(n, rows, group, [ref[f"g_sem{i}"] for i in range(4)])
    gather.send(0)
    gain_attn = jnp.sum(d_resid * values * inverse, axis=0, keepdims=True)
    ref["v_gattn"][...] = gain_attn
    quarter = cols // 4
    load_a = [
        load(ref["every"].at[i, t], weights.at[pl.ds(0, span), pl.ds((3 * i + t) * quarter, quarter)])
        for i in range(4)
        for t in range(3)
    ]
    att, proj, tab = ref["v_att"], ref["v_proj"], ref["v_tab"]
    load_a.append(load(ref["att"], att))
    load_p = [load(ref["proj"], proj), load(ref["table"].at[rows_of(c, span)], tab)]
    pieces.step()

    def gather_hook(slot):
        if slot == 0:
            pieces.step(2)
        if slot == 1:
            pieces.step()

    gather.run(gather_hook)
    wait_all(load_o)
    dattn, d_out = ref["v_dattn"], ref["v_d_out"]

    def tile(j, carry):
        where = pl.ds(pl.multiple_of(j * size, size), size)
        d_attn = dot(group[where, :], weights[wo_row : wo_row + wo_cols, :], NT).astype(BF16)
        for q in range(4):
            dattn[q, where, :] = d_attn[:, q * quarter : (q + 1) * quarter]
        return carry

    lax.fori_loop(0, count, tile, 0)

    a_send, a_recv, h_send, h_recv = ref["a_send"], ref["a_recv"], ref["h_send"], ref["h_recv"]
    copies = []
    for k, peer in enumerate(peers):
        copy = remote(dattn.at[peer[1]], d_out.at[c], a_send.at[k], a_recv.at[k], peer)
        copy.start()
        copies.append(copy)
    sibling.start(attn, ref["v_attn_s"])
    sibling.start(half_columns(group, 1 - s), ref["v_dbranch_s"])
    d_out[pl.ds(c, 1)] = dattn[pl.ds(c, 1)]
    dq, acc, delta, got = ref["v_dq"], ref["v_acc"], ref["v_delta"], ref["v_home"]
    lse_ref = ref["lse"]
    dq[...] = jnp.zeros_like(dq)
    bound = ref["bound"][:1, :1]
    scale = HEAD_DIM ** (-0.5)
    heads = quarter // HEAD_DIM
    wait_all(load_a)
    for k, peer in enumerate(peers):
        there = d_out.at[peer[1]]
        remote(there, there, a_send.at[k], a_recv.at[k], peer).wait_recv()
    pieces.step()
    for i in range(4):
        for h in range(heads):
            lanes = slice(h * HEAD_DIM, (h + 1) * HEAD_DIM)
            both = jnp.transpose(d_out[i, :, lanes].astype(F32)) * att[i, lanes, :]
            delta[i, h, :1, :] = jnp.sum(both, axis=0, keepdims=True)

    def seen(i, t, h):
        first = (3 * i + t) * quarter + h * HEAD_DIM
        return weights[:span, pl.ds(pl.multiple_of(first, HEAD_DIM), HEAD_DIM)]

    def going(j):
        first = pl.multiple_of(3 * j * quarter, 3 * quarter)
        return weights.at[pl.ds(wo_row, span), pl.ds(first, 3 * quarter)]

    def home(j):
        return remote(going(j), got.at[c], h_send.at[j], h_recv.at[c], (s, j, u))

    def step(j, carry):
        acc[...] = jnp.zeros_like(acc)
        for h in range(heads):
            lanes = slice(h * HEAD_DIM, (h + 1) * HEAD_DIM)

            def update(i, diagonal):
                starts = segment_starts(i * span, span, bound)
                keys, values = seen(j, 1, h), seen(j, 2, h)
                query, grad = seen(i, 0, h), d_out[i, :, lanes]
                scores = dot(keys, query, NT) * SCALE2
                scores = score_mask(scores, j * span, i * span, starts, diagonal)
                probs = jnp.exp2(scores - lse_ref[i, h, :1, :])
                acc[1, :, lanes] += dot(probs.astype(BF16), grad, NN)
                d_probs = dot(values, grad, NT)
                d_scores = (probs * (d_probs - delta[i, h, :1, :])).astype(BF16)
                acc[0, :, lanes] += dot(d_scores, query, NN) * scale
                dq[i, :, lanes] += dot(d_scores, keys, TN) * scale

            def after(i, carry):
                update(i, False)
                return carry

            update(j, True)
            lax.fori_loop(j + 1, 4, after, 0)
        first = pl.multiple_of(3 * j * quarter, 3 * quarter)
        weights[wo_row : wo_row + span, pl.ds(first, 3 * quarter)] = jnp.concatenate(
            [dq[j].astype(BF16), acc[0].astype(BF16), acc[1].astype(BF16)], axis=1
        )

        @pl.when(j != c)
        def _():
            home(j).start()

        return carry

    lax.fori_loop(0, 4, step, 0)
    load_q = [
        load(ref["wq"].at[i], weights.at[pl.ds(0, width), pl.ds(i * cols, cols)]) for i in range(3)
    ]
    load_x = load(half_columns(ref["xg"], s), dmlp)
    got[pl.ds(c, 1)] = going(c)[...][None]
    wait_all(load_p)
    for k in (1, 2, 3):
        j = c ^ k
        remote(got.at[j], got.at[j], h_send.at[c], h_recv.at[j], (s, j, u)).wait_recv()
    pieces.step()
    kept, inv_ref = (dq, ref["v_dk"]), ref["inv"]
    for j in range(4):
        hidden[:, 2 * cols + j * quarter : 2 * cols + (j + 1) * quarter] = got[
            j, :, 2 * quarter : 3 * quarter
        ]

    def source(i, h):
        group, inside = divmod(h, heads)
        first = i * quarter + inside * HEAD_DIM
        return got[group, :, first : first + HEAD_DIM].astype(F32)

    gcols = ref["v_gcols"]

    def store(i, h, values):
        group, inside = divmod(h, heads)
        kept[i][group, :, inside * HEAD_DIM : (inside + 1) * HEAD_DIM] = values

    dots = norms_back(source, store, proj, inv_ref, qk_gain_ref, tab, gcols)
    total = exchange_rows(n, dots, ref["v_msg"], ref["m_send"], ref["m_recv"])
    means = to_columns(total) / width
    for i in range(2):
        inverse = inv_ref[:, i : i + 1]
        factor = inverse**3 * means[:, i : i + 1]
        for j in range(4):
            lanes = slice(j * quarter, (j + 1) * quarter)
            hidden[:, i * cols + j * quarter : i * cols + (j + 1) * quarter] = (
                inverse * kept[i][j] - proj[i, :, lanes] * factor
            ).astype(BF16)
    sibling.start(dproj, ref["v_dproj_s"])
    gains = GainSum(
        n,
        [ref[f"v_sum{i}"] for i in range(4)],
        (ref["v_send"], ref["v_recv"], ref["n_send"], ref["n_recv"]),
    )
    gains.start(gcols, ref["v_gattn"], ref["gmlp"])
    wait_all(load_q)

    def compute_input(chunk):
        lanes = slice(chunk * chunk_cols, (chunk + 1) * chunk_cols)

        def tile(i, carry):
            where = pl.ds(pl.multiple_of(i * size, size), size)
            part[chunk, where, :] = dot(
                hidden[where, : 3 * cols], weights[lanes, : 3 * cols], NT
            ).astype(BF16)
            return carry

        lax.fori_loop(0, count, tile, 0)
        if chunk == 0:
            pieces.step()
        if chunk == 2:
            sibling.wait(1)
            sibling.wait(2)
            pieces.step()

    def input_hook(slot):
        if slot == 0:
            load_x.wait()
            sibling.wait(0)
            sibling.wait(3)
            gains.over_ctx()
        if slot == 1:
            gains.over_uly()
        pieces.step()

    LineReduce(n, rows, part, ref["v_got"], sem_b).run(compute_input, branch, input_hook)
    ref["o_input"][...] = (dresid[...] + branch[...]).astype(BF16)
    pieces.finish()
    gains.finish(ref["o_gain"])
    plane.finish(len(kinds))
    sibling.finish()
    for j in range(4):

        @pl.when(j != c)
        def _():
            home(j).wait_send()

    for copy in copies:
        copy.wait_send()


def backward(n, ins):
    rows, width = ins["cot"][0].shape
    span, ff = n * rows, ins["hidden"][0].shape[1]
    cols = ins["attn"][0].shape[1]
    quarter = cols // 4
    kb, kc = width // 8, ins["wo"][0].shape[2]
    n_d, size = tiles(ff, 512)
    dma = pltpu.SemaphoreType.DMA
    outs = {"o_input": ((rows, width), BF16), "o_gain": ((4, width // 8), F32)}
    for i in range(3):
        outs[f"o_down{i}"] = ((ff, kc), BF16)
        outs[f"o_gate{i}"] = ((2, kb, ff), BF16)
        outs[f"o_out{i}"] = ((cols, kc), BF16)
        outs[f"o_qkv{i}"] = ((3, kb, cols), BF16)
    buffers = {
        "v_weights": ((width + cols, width), BF16),
        "v_dgu": ((2, span, ff), BF16),
        "v_dgu_s": ((3, span, size), BF16),
        "v_hidden": ((span, ff), BF16),
        "v_hidden_s": ((2, span, size), BF16),
        "v_dmlp": ((span, width // 2), BF16),
        "v_dmlp_s": ((span, width // 2), BF16),
        "v_resid": ((span, width // 2), BF16),
        "v_resid_s": ((span, width // 2), BF16),
        "v_branch": ((rows, width), F32),
        "v_attn": ((span, cols), BF16),
        "v_dresid": ((rows, width), F32),
        "v_group": ((span, width), BF16),
        "v_part": ((CHUNKS, span, width // CHUNKS), BF16),
        "v_got": ((CHUNKS, span + rows, width // CHUNKS), BF16),
        "v_ring": ((AHEAD + 1, 4, 2, kb, kb), BF16),
        "v_got_p": ((3 * n_d + 4, 2, kb, kb), BF16),
        "v_gattn": ((1, width), F32),
        "v_att": ((4, quarter, span), F32),
        "v_proj": ((2, span, cols), F32),
        "v_tab": ((span, 128), F32),
        "v_dattn": ((4, span, quarter), BF16),
        "v_d_out": ((4, span, quarter), BF16),
        "v_dq": ((4, span, quarter), F32),
        "v_acc": ((2, span, quarter), F32),
        "v_delta": ((4, quarter // HEAD_DIM, 8, span), F32),
        "v_home": ((4, span, 3 * quarter), BF16),
        "v_dk": ((4, span, quarter), F32),
        "v_gcols": ((2, cols), F32),
        "v_msg": ((n, 8, span), F32),
        "v_xs_s": ((span, width // 2), BF16),
        "v_attn_s": ((span, cols), BF16),
        "v_dbranch_s": ((span, width // 2), BF16),
        "v_dproj_s": ((span, 3 * cols), BF16),
        "v_sum0": ((2, 8, width // 2), F32),
        "v_sum1": ((8, width // 2), F32),
        "v_sum2": ((4, 8, width // 8), F32),
        "v_sum3": ((3 + n, 8, width // 8), F32),
    }
    sems = {
        "load_sem": (32,),
        "chunk_sem": (2, 3 * (width // CHUNKS // kb)),
        "wo_sem": (8,),
        "hs_sem": (2,),
        "ds_sem": (3,),
        "p_send": (3 * n_d + 4, 6),
        "p_recv": (3 * n_d + 4, 6),
        "p_local": (3 * n_d + 4, 2),
        "a_send": (3,),
        "a_recv": (3,),
    }
    for name in ("s_send", "s_recv", "h_send", "h_recv", "v_send", "v_recv"):
        sems[name] = (4,)
    for name in ("m_send", "m_recv", "n_send", "n_recv"):
        sems[name] = (n - 1,)
    for i in range(4):
        sems[f"r_sem{i}"] = (n - 1, CHUNKS)
        sems[f"b_sem{i}"] = (n - 1, CHUNKS)
        sems[f"g_sem{i}"] = (n - 1,)
    names = [*ins, *outs, *buffers, *sems]
    results = pl.pallas_call(
        functools.partial(backward_kernel, n, names),
        out_shape=[shape(*out) for out in outs.values()],
        in_specs=[spec for value, spec in ins.values()],
        out_specs=[VM, VM] + [HB] * 12,
        scratch_shapes=[pltpu.VMEM(*buffer) for buffer in buffers.values()]
        + [dma(dims) for dims in sems.values()],
        compiler_params=pltpu.CompilerParams(
            collective_id=11, has_side_effects=True, vmem_limit_bytes=63 * 1024 * 1024
        ),
        name="backward",
    )(*[value for value, spec in ins.values()])
    return dict(zip(outs, results))


def rope_table(length):
    freqs = np.power(
        np.float32(ROPE_BASE), -(np.arange(HALF, dtype=np.float32) * 2.0 / HEAD_DIM)
    ).astype(np.float32)
    angles = (np.arange(length, dtype=np.float32)[:, None] * freqs[None, :]).astype(np.float64)
    return np.concatenate([np.cos(angles), np.sin(angles)], axis=1).astype(np.float32)


def on_device(
    n,
    table,
    tokens,
    segment_ids,
    qkv_weight,
    out_weight,
    gate_up,
    down_weight,
    qk_gain,
    post_gain,
    cotangent,
):
    x = tokens[0]
    width = x.shape[1]
    cot = cotangent[0]
    table = jnp.asarray(table)
    if spread_heads(qkv_weight.shape[2]):
        o = forward(
            n,
            x,
            qkv_weight,
            table,
            qk_gain,
            segment_ids,
            out_weight,
            gate_up,
            down_weight,
            post_gain,
        )
        group_x, wq, wo, proj, inv = [o[f"o_{k}"] for k in ("xg", "wq", "wo", "proj", "inv")]
        wga, wgb, wgc, wd = [o[f"o_{k}"] for k in ("wga", "wgb", "wgc", "wd")]
        att, lse, bound, attn = [o[f"o_{k}"] for k in ("att", "lse", "bound", "attn")]
        branch, resid, group_resid = [o[f"o_{k}"] for k in ("branch", "resid", "group")]
        gate, up, hidden = [o[f"o_{k}"] for k in ("gate", "up", "hidden")]
        attn = attn.reshape(group_x.shape[0], -1)
        seen = (o["o_every"],)
    else:
        group_x, wq, wo, wga, proj, qkv, inv, zero = project(
            n, x, qkv_weight, table, qk_gain, segment_ids, out_weight, gate_up
        )
        every, wgb, attn, att, lse, bound = attend(*qkv, zero, gate_up)
        seen, back = (qkv[0], every), attend_back
        branch, resid, group_resid, gate, up, hidden, wgc, wd = mlp_in(
            n, attn, wo, x, post_gain, wga, wgb, gate_up, down_weight
        )
    block_out, group_dmlp, dgu, gain_mlp, hidden_s, resid_s, dmlp_s, dgu_s = mlp_out(
        n, hidden, wd, resid, post_gain, cot, gate, up, group_resid
    )
    span, ff = n * x.shape[0], hidden.shape[2]
    branch = branch.reshape(x.shape)
    dgu, dgu_s = dgu.reshape(2, span, ff), dgu_s.reshape(2, span, ff)
    hidden, hidden_s = hidden.reshape(span, ff), hidden_s.reshape(span, ff)
    group_resid, group_dmlp = group_resid.reshape(span, width), group_dmlp.reshape(span, width)
    resid_s, dmlp_s = resid_s.reshape(span, width // 2), dmlp_s.reshape(span, width // 2)
    if spread_heads(qkv_weight.shape[2]):
        o = backward(
            n,
            {
                "dgu": (dgu, HB),
                "dgu_s": (dgu_s, HB),
                "wga": (wga, HB),
                "wgb": (wgb, HB),
                "wgc": (wgc, HB),
                "cot": (cot, VM),
                "branch": (branch, HB),
                "post": (post_gain, VM),
                "gain": (qk_gain, VM),
                "wo": (wo, HB),
                "hidden": (hidden, HB),
                "hidden_s": (hidden_s, HB),
                "dmlp": (group_dmlp, HB),
                "dmlp_s": (dmlp_s, HB),
                "resid": (group_resid, HB),
                "resid_s": (resid_s, HB),
                "every": (seen[0], HB),
                "att": (att, HB),
                "lse": (lse, VM),
                "bound": (bound, VM),
                "attn": (attn, HB),
                "proj": (proj, HB),
                "inv": (inv, VM),
                "table": (table, HB),
                "wq": (wq, HB),
                "xg": (group_x, HB),
                "gmlp": (gain_mlp, VM),
            },
        )
        input_grad, gain_part = o["o_input"], o["o_gain"]
        qkv_grads, out_grads, gate_grads, down_grads = [
            [o[f"o_{k}{i}"] for i in range(3)] for k in ("qkv", "out", "gate", "down")
        ]
    else:
        d_resid, group_dbranch, d_attn, gain_attn, *grads = mlp_back(
            n,
            dgu,
            wga,
            wgb,
            wgc,
            cot,
            branch,
            post_gain,
            wo,
            hidden,
            group_dmlp,
            group_resid,
            hidden_s,
            resid_s,
            dmlp_s,
            dgu_s,
        )
        gate_grads, down_grads = grads[:3], grads[3:]
        late = (group_resid, resid_s, dgu, dgu_s)
        d_proj, gain_cols, *gate_grads = back(
            n, *seen, d_attn, att, lse, bound, proj, inv, qk_gain, table, late, gate_grads
        )
        input_grad, gain_part, *grads = proj_back(
            n,
            d_proj,
            wq,
            d_resid,
            group_x,
            gain_cols,
            gain_attn,
            gain_mlp,
            attn,
            group_dbranch,
            late,
            gate_grads,
        )
        qkv_grads, out_grads, gate_grads = grads[:3], grads[3:6], grads[6:]

    def total(parts):
        return parts[0].astype(F32) + parts[1].astype(F32) + parts[2].astype(F32)

    return (
        block_out[None],
        input_grad[None],
        total(qkv_grads),
        total(out_grads),
        total(gate_grads),
        total(down_grads),
        gain_part,
    )


def solution(mesh):
    n = mesh.shape["uly"]
    in_specs = (
        P("slot", ("ctx", "uly"), None),
        P("slot", ("ctx", "uly")),
        P(None, ("slot", "ctx"), "uly"),
        P("uly", ("slot", "ctx")),
        P(None, ("slot", "ctx"), "uly"),
        P("uly", ("slot", "ctx")),
        P(None, "uly"),
        P(),
        P("slot", ("ctx", "uly"), None),
    )
    out_specs = (
        P("slot", ("ctx", "uly"), None),
        P("slot", ("ctx", "uly"), None),
        P(None, ("slot", "ctx"), "uly"),
        P("uly", ("slot", "ctx")),
        P(None, ("slot", "ctx"), "uly"),
        P("uly", ("slot", "ctx")),
        P(None, ("slot", "ctx")),
    )

    def whole(tokens, *rest):
        table = rope_table(tokens.shape[1])
        return jax.shard_map(
            functools.partial(on_device, n, table),
            mesh=mesh,
            in_specs=in_specs,
            out_specs=out_specs,
            check_vma=False,
        )(tokens, *rest)

    return whole
```

```python
import functools
from types import SimpleNamespace

import jax
import jax.numpy as jnp
import numpy as np
from jax import lax
from jax.experimental import pallas as pl
from jax.experimental.pallas import tpu as pltpu
from jax.sharding import PartitionSpec as P

HEAD_DIM = 128
HALF = HEAD_DIM // 2
EPS = 1e-06
ROPE_BASE = 500000.0
FLOOR = -1e30
LOG2E = 1.4426950408889634
SCALE2 = HEAD_DIM ** (-0.5) * LOG2E
MESH_ID = pl.DeviceIdType.MESH
BF16 = jnp.bfloat16
F32 = jnp.float32
VMEM_LIMIT = 62 * 1024 * 1024
CHUNKS = 4
AHEAD = 1
LATER = 2

VM = pl.BlockSpec(memory_space=pltpu.VMEM)
HB = pl.BlockSpec(memory_space=pl.ANY)


def shape(dims, dtype):
    return jax.ShapeDtypeStruct(dims, dtype)


def where_am_i():
    return lax.axis_index("slot"), lax.axis_index("ctx"), lax.axis_index("uly")


def rows_of(index, rows):
    return pl.ds(pl.multiple_of(index * rows, rows), rows)


def greet(peers):
    barrier = pltpu.get_barrier_semaphore()
    total = 0
    for condition, peer in peers:
        if condition is None:
            pl.semaphore_signal(barrier, inc=1, device_id=peer, device_id_type=MESH_ID)
            total = total + 1
        else:

            @pl.when(condition)
            def _():
                pl.semaphore_signal(barrier, inc=1, device_id=peer, device_id_type=MESH_ID)

            total = total + condition.astype(jnp.int32)
    pl.semaphore_wait(barrier, total)


def line_peers(n):
    s, c, u = where_am_i()
    return [(u > 0, (s, c, u - 1)), (u < n - 1, (s, c, u + 1))]


def plane_peers():
    s, c, u = where_am_i()
    return [(None, (s, c ^ 1, u)), (None, (s, c ^ 2, u))]


def remote(src, dst, send, recv, peer):
    return pltpu.make_async_remote_copy(
        src_ref=src,
        dst_ref=dst,
        send_sem=send,
        recv_sem=recv,
        device_id=peer,
        device_id_type=MESH_ID,
    )


def line_sems(n, chunks=None):
    dims = (n - 1,) if chunks is None else (n - 1, chunks)
    return [pltpu.SemaphoreType.DMA(dims)] * 4


class LineGather:
    def __init__(self, n, rows, buf, sems, part=None):
        self.n, self.rows, self.buf, self.sems, self.part = n, rows, buf, sems, part

    def copy(self, right, slot, shard):
        s, c, u = where_am_i()
        send_r, recv_r, send_l, recv_l = self.sems
        if self.part is None:
            view = self.buf.at[rows_of(shard, self.rows)]
        else:
            index, size = self.part
            view = self.buf.at[shard, pl.ds(index * size, size)]
            send_r, recv_r, send_l, recv_l = [sem.at[:, index] for sem in self.sems]
        if right:
            return remote(view, view, send_r.at[slot], recv_r.at[slot], (s, c, u + 1))
        return remote(view, view, send_l.at[slot], recv_l.at[slot], (s, c, u - 1))

    def send(self, slot):
        u, n = lax.axis_index("uly"), self.n

        @pl.when((u < n - 1) & (u - slot >= 0))
        def _():
            self.copy(True, slot, u - slot).start()

        @pl.when((u > 0) & (u + slot <= n - 1))
        def _():
            self.copy(False, slot, u + slot).start()

    def wait(self, slot):
        u, n = lax.axis_index("uly"), self.n

        @pl.when(u - 1 - slot >= 0)
        def _():
            self.copy(True, slot, u - 1 - slot).wait_recv()

        @pl.when(u + 1 + slot <= n - 1)
        def _():
            self.copy(False, slot, u + 1 + slot).wait_recv()

        if slot + 1 < n - 1:
            self.send(slot + 1)

    def finish(self):
        u, n = lax.axis_index("uly"), self.n
        for slot in range(n - 1):

            @pl.when((u < n - 1) & (u - slot >= 0))
            def _():
                self.copy(True, slot, u - slot).wait_send()

            @pl.when((u > 0) & (u + slot <= n - 1))
            def _():
                self.copy(False, slot, u + slot).wait_send()

    def run(self, hook=None):
        for slot in range(self.n - 1):
            self.wait(slot)
            if hook is not None:
                hook(slot)
        self.finish()


class LineReduce:
    def __init__(self, n, rows, part, got, sems):
        self.n, self.rows, self.sems = n, rows, sems
        self.part, self.got = part, got
        self.chunks = part.shape[0]

    def copy(self, right, slot, chunk, block):
        s, c, u = where_am_i()
        send_r, recv_r, send_l, recv_l = self.sems
        where = rows_of(block, self.rows)
        src = self.part.at[chunk, where]
        if right:
            return remote(
                src,
                self.got.at[chunk, rows_of(block + 1, self.rows)],
                send_r.at[slot, chunk],
                recv_r.at[slot, chunk],
                (s, c, u + 1),
            )
        return remote(
            src,
            self.got.at[chunk, where],
            send_l.at[slot, chunk],
            recv_l.at[slot, chunk],
            (s, c, u - 1),
        )

    def add(self, chunk, block, place):
        where = rows_of(block, self.rows)
        self.part[chunk, where, :] = (
            self.part[chunk, where, :].astype(F32)
            + self.got[chunk, rows_of(place, self.rows), :].astype(F32)
        ).astype(BF16)

    def step(self, slot, chunk):
        u, n = lax.axis_index("uly"), self.n
        block_r = n - 1 - slot + u
        block_l = slot - (n - 1) + u

        @pl.when(u <= slot)
        def _():
            if slot > 0:

                @pl.when(u > 0)
                def _():
                    self.copy(True, slot - 1, chunk, block_r).wait_recv()
                    self.add(chunk, block_r, block_r + 1)

            self.copy(True, slot, chunk, block_r).start()

        @pl.when(u >= n - 1 - slot)
        def _():
            if slot > 0:

                @pl.when(u < n - 1)
                def _():
                    self.copy(False, slot - 1, chunk, block_l).wait_recv()
                    self.add(chunk, block_l, block_l)

            self.copy(False, slot, chunk, block_l).start()

    def last(self, out, chunks=None):
        u, n = lax.axis_index("uly"), self.n
        where = rows_of(u, self.rows)
        width = self.part.shape[2]
        chunks = range(self.chunks) if chunks is None else chunks
        for number, chunk in enumerate(chunks):
            cols = slice(number * width, (number + 1) * width)
            out[:, cols] = self.part[chunk, where, :].astype(F32)

            @pl.when(u > 0)
            def _():
                self.copy(True, n - 2, chunk, u).wait_recv()
                out[:, cols] += self.got[chunk, rows_of(u + 1, self.rows), :].astype(F32)

            @pl.when(u < n - 1)
            def _():
                self.copy(False, n - 2, chunk, u).wait_recv()
                out[:, cols] += self.got[chunk, where, :].astype(F32)

    def finish(self):
        u, n = lax.axis_index("uly"), self.n
        for slot in range(n - 1):
            for chunk in range(self.chunks):

                @pl.when(u <= slot)
                def _():
                    self.copy(True, slot, chunk, n - 1 - slot + u).wait_send()

                @pl.when(u >= n - 1 - slot)
                def _():
                    self.copy(False, slot, chunk, slot - (n - 1) + u).wait_send()

    def run(self, compute, out, hook=None):
        for slot in range(self.n - 1):
            for chunk in range(self.chunks):
                if slot == 0:
                    compute(chunk)
                self.step(slot, chunk)
            if hook is not None:
                hook(slot)
        self.last(out)
        self.finish()


def reduce_norm_gather(n, reduce, gathers, compute, finish, consume, hook):
    per_half = reduce.chunks // 2
    slots = n - 1
    chunks = [range(h * per_half, (h + 1) * per_half) for h in range(2)]
    for chunk in chunks[0]:
        compute(chunk)
        reduce.step(0, chunk)
    for chunk in chunks[1]:
        compute(chunk)
    hook("started")
    for slot in range(1, slots):
        for chunk in chunks[0]:
            reduce.step(slot, chunk)
    for chunk in chunks[1]:
        reduce.step(0, chunk)
    hook("sent")
    finish(0)
    gathers[0].send(0)
    hook("half")
    for slot in range(1, slots):
        for chunk in chunks[1]:
            reduce.step(slot, chunk)
        gathers[0].wait(slot - 1)
        hook(f"b{slot}")
    finish(1)
    gathers[1].send(0)
    gathers[0].wait(slots - 1)
    hook("first")
    tiles = consume.tiles
    done = 0
    for slot in range(slots):
        while done < tiles * (slot + 1) // slots:
            consume(0, done)
            done += 1
        gathers[1].wait(slot)
        hook(f"g{slot}")
    for tile in range(tiles):
        consume(1, tile)
        hook(f"t{tile}")
    reduce.finish()
    for gather in gathers:
        gather.finish()


class Halves:
    def __init__(self, n, rows):
        self.n, self.half = n, rows // 2
        self.per_tile = min(n, max(512 // self.half, 1))
        self.count = n // self.per_tile

    def each(self, half, body):
        size = self.per_tile * self.half
        for t in range(self.count):
            index = (pl.ds(t * self.per_tile, self.per_tile), pl.ds(half * self.half, self.half))
            body(index, t * size, size)

    def load(self, ref, index, lanes=slice(None)):
        value = ref[index[0], index[1], lanes]
        return value.reshape(value.shape[0] * value.shape[1], value.shape[2])

    def store(self, ref, index, lanes, value):
        ref[index[0], index[1], lanes] = value.reshape(
            self.per_tile, self.half, value.shape[1]
        )


class Consume:
    def __init__(self, tiles, body):
        self.tiles, self.body = tiles, body

    def __call__(self, half, tile):
        self.body(half, tile)


class PlaneGather:
    SEMS = 9

    def __init__(self, src, block, half_rows, send, recv, local):
        self.s, self.c, self.u = where_am_i()
        self.src, self.block, self.half_rows = src, block, half_rows
        self.send_sem, self.recv_sem = send, recv
        s, c, u = self.s, self.c, self.u
        self.xn, self.yn, self.sib = (s, c ^ 1, u), (s, c ^ 2, u), (1 - s, c, u)
        self.started = []
        self.own = pltpu.make_async_copy(src, block(s * 4 + c), local)

    def half(self, b, part):
        rows = self.half_rows
        view = self.block(b)
        where = [slice(None)] * len(view.shape)
        where[-2] = pl.ds(part * rows, rows)
        return view.at[tuple(where)]

    def copy(self, k, view, peer, src=None):
        return remote(
            view if src is None else src, view, self.send_sem.at[k], self.recv_sem.at[k], peer
        )

    def go(self, *copies):
        for copy in copies:
            copy.start()
            self.started.append(copy)

    def start(self):
        own = self.block(self.s * 4 + self.c)
        self.go(
            self.copy(0, own, self.xn, self.src),
            self.copy(1, own, self.yn, self.src),
            self.copy(2, own, self.sib, self.src),
        )
        self.own.start()

    def middle(self):
        bx, by = self.s * 4 + (self.c ^ 1), self.s * 4 + (self.c ^ 2)
        self.copy(0, self.block(bx), self.xn).wait_recv()
        self.go(
            self.copy(3, self.half(bx, 0), self.yn), self.copy(4, self.block(bx), self.sib)
        )
        self.copy(1, self.block(by), self.yn).wait_recv()
        self.go(
            self.copy(5, self.half(by, 1), self.xn), self.copy(6, self.block(by), self.sib)
        )

    def corner(self):
        bd = self.s * 4 + (self.c ^ 3)
        self.copy(3, self.half(bd, 0), self.yn).wait_recv()
        self.go(self.copy(7, self.half(bd, 0), self.sib))
        self.copy(5, self.half(bd, 1), self.xn).wait_recv()
        self.go(self.copy(8, self.half(bd, 1), self.sib))

    def arrive(self):
        far, c = (1 - self.s) * 4, self.c
        self.copy(2, self.block(far + c), self.sib).wait_recv()
        self.copy(4, self.block(far + (c ^ 1)), self.sib).wait_recv()
        self.copy(6, self.block(far + (c ^ 2)), self.sib).wait_recv()
        self.copy(7, self.half(far + (c ^ 3), 0), self.sib).wait_recv()
        self.copy(8, self.half(far + (c ^ 3), 1), self.sib).wait_recv()
        self.own.wait()

    def finish(self):
        for copy in self.started:
            copy.wait_send()


class PlaneReduce:
    SEMS = 6

    def __init__(self, ring, got, outs, place, send, recv, local):
        self.s, self.c, self.u = where_am_i()
        s, c, u = self.s, self.c, self.u
        self.xn, self.yn = (s, c ^ 1, u), (s, c ^ 2, u)
        self.ring, self.got, self.outs, self.place = ring, got, outs, place
        self.send_sem, self.recv_sem, self.local = send, recv, local
        self.slots, self.rows = ring.shape[0], ring.shape[2]
        self.open = {}

    def halves(self):
        h = self.rows // 2
        return pl.ds(0, h), pl.ds(h, h)

    def copy(self, piece, k, src, dst, peer):
        return remote(src, dst, self.send_sem.at[piece, k], self.recv_sem.at[piece, k], peer)

    def slot(self, piece):
        if piece >= self.slots:
            self.close(piece - self.slots)
        return self.ring.at[piece % self.slots]

    def close(self, piece):
        if piece in self.open:
            remotes, own = self.open.pop(piece)
            for copy in remotes:
                copy.wait_send()
            wait_all(own)

    def first(self, piece):
        c = self.c
        lo, hi = self.halves()
        blocks = self.ring.at[piece % self.slots]
        own_out, out_x, out_y = self.outs
        bx, by, bd = c ^ 1, c ^ 2, c ^ 3
        copies = [
            self.copy(piece, 0, blocks.at[bd, lo], self.got.at[piece, lo], self.xn),
            self.copy(piece, 1, blocks.at[bd, hi], self.got.at[piece, hi], self.yn),
            self.copy(piece, 2, blocks.at[bx, lo], self.place(out_x, piece, 0), self.xn),
            self.copy(piece, 3, blocks.at[by, hi], self.place(out_y, piece, 1), self.yn),
        ]
        for copy in copies:
            copy.start()
        own = self.own_copies(piece, blocks)
        for copy in own:
            copy.start()
        self.open[piece] = (copies, own)

    def own_copies(self, piece, blocks):
        place = self.place(self.outs[0], piece, None)
        return [pltpu.make_async_copy(blocks.at[self.c], place, self.local.at[piece])]

    def add(self, slot, block, half, piece):
        h = self.rows // 2
        where = slice(half * h, (half + 1) * h)
        self.ring[slot, block, where, :] = (
            self.ring[slot, block, where, :].astype(F32) + self.got[piece, where, :].astype(F32)
        ).astype(BF16)

    def second(self, piece):
        c = self.c
        lo, hi = self.halves()
        slot = piece % self.slots
        blocks = self.ring.at[slot]
        own_out, out_x, out_y = self.outs
        bx, by, bd = c ^ 1, c ^ 2, c ^ 3
        self.copy(piece, 0, blocks.at[bd, lo], self.got.at[piece, lo], self.xn).wait_recv()
        self.add(slot, by, 0, piece)
        first = self.copy(piece, 4, blocks.at[by, lo], self.place(out_y, piece, 0), self.yn)
        first.start()
        self.copy(piece, 1, blocks.at[bd, hi], self.got.at[piece, hi], self.yn).wait_recv()
        self.add(slot, bx, 1, piece)
        second = self.copy(piece, 5, blocks.at[bx, hi], self.place(out_x, piece, 1), self.xn)
        second.start()
        self.open[piece][0].extend([first, second])

    def finish(self, pieces):
        own_out, out_x, out_y = self.outs
        slot = self.ring.at[0]
        lo, hi = self.halves()
        for piece in range(pieces):
            self.close(piece)
            for k, out, half, peer in (
                (2, out_x, 0, self.xn),
                (3, out_y, 1, self.yn),
                (4, out_y, 0, self.yn),
                (5, out_x, 1, self.xn),
            ):
                where = self.place(out, piece, half)
                self.copy(piece, k, where, where, peer).wait_recv()


class Pieces:
    def __init__(self, work, ahead=2):
        self.work, self.done, self.behind, self.ahead = work, 0, [], ahead

    def step(self, count=1):
        for _ in range(count):
            if self.done < len(self.work):
                plane, piece, compute = self.work[self.done]
                compute(plane.slot(piece), piece)
                plane.first(piece)
                self.behind.append((plane, piece))
                self.done += 1
                if len(self.behind) > self.ahead:
                    self.catch_up()

    def catch_up(self):
        plane, piece = self.behind.pop(0)
        plane.second(piece)

    def finish(self):
        self.step(len(self.work))
        while self.behind:
            self.catch_up()


def wide_piece(own, other, lanes):
    def compute(out, piece):
        take = lanes(piece)
        cols = out.shape[2]

        def pair(i, carry):
            where = pl.ds(pl.multiple_of(i * 2 * cols, 2 * cols), 2 * cols)
            total = dot(own[0][:, take], own[1][:, where], TN) + dot(
                other[0][:, take], other[1][:, where], TN
            )
            total = total.astype(BF16)
            out[pl.ds(2 * i, 1)] = total[:, :cols][None]
            out[pl.ds(2 * i + 1, 1)] = total[:, cols:][None]
            return carry

        lax.fori_loop(0, 2, pair, 0)

    return compute


def tall_piece(own, other, right):
    def compute(out, piece):
        rows, cols = out.shape[1:]

        def pair(i, carry):
            where = pl.ds(pl.multiple_of(i * 2 * rows, 2 * rows), 2 * rows)
            total = dot(own[0][:, where], right(own[1], piece), TN) + dot(
                other[0][:, where], right(other[1], piece), TN
            )
            out[pl.ds(2 * i, 2)] = total.astype(BF16).reshape(2, rows, cols)
            return carry

        lax.fori_loop(0, 2, pair, 0)

    return compute


class LatePiece:
    def __init__(self, number, ins, outs, scratch, sems):
        s, c, u = where_am_i()
        resid_hbm, resid_s_hbm, dgu_hbm, dgu_s_hbm = ins
        resid, resid_s, right, right_s, ring, got = scratch
        send, recv, local, load_sem = sems
        cols = right.shape[1]
        ci, tile = divmod(number, dgu_hbm.shape[2] // cols)
        lanes = pl.ds(tile * cols, cols)
        pairs = (
            (half_columns(resid_hbm, s), resid),
            (resid_s_hbm, resid_s),
            (dgu_hbm.at[ci, :, lanes], right),
            (dgu_s_hbm.at[ci, :, lanes], right_s),
        )
        self.loads = [
            pltpu.make_async_copy(src, dst, load_sem.at[k]) for k, (src, dst) in enumerate(pairs)
        ]
        size = ring.shape[2]

        def place(out, piece, part):
            rows = size if part is None else size // 2
            return out.at[ci, pl.ds((part or 0) * rows, rows), lanes]

        self.plane = PlaneReduce(ring, got, outs, place, send, recv, local)
        self.compute = tall_piece(
            (resid, right), (resid_s, right_s), lambda ref, piece: ref[...]
        )

    def load(self):
        for copy in self.loads:
            copy.start()

    def work(self):
        def compute(out, piece):
            for copy in self.loads:
                copy.wait()
            self.compute(out, piece)

        return (self.plane, 0, compute)

    @staticmethod
    def scratch(span, width, ff):
        cols = min(ff, 512)
        ring, sems = piece_scratch(1, 1, width // 8, cols)
        buffers = (
            pltpu.VMEM((span, width // 2), BF16),
            pltpu.VMEM((span, width // 2), BF16),
            pltpu.VMEM((span, cols), BF16),
            pltpu.VMEM((span, cols), BF16),
            ring[0],
            ring[1],
        )
        return [buffers, tuple(sems) + (pltpu.SemaphoreType.DMA((4,)),)]


def half_columns(ref, s):
    half = ref.shape[1] // 2
    return ref.at[:, pl.ds(pl.multiple_of(s * half, half), half)]


class Sibling:
    def __init__(self, send, recv):
        s, c, u = where_am_i()
        self.peer, self.send, self.recv = (1 - s, c, u), send, recv
        self.copies = []

    def start(self, src, dst):
        k = len(self.copies)
        copy = remote(src, dst, self.send.at[k], self.recv.at[k], self.peer)
        copy.start()
        self.copies.append(copy)

    def wait(self, k):
        self.copies[k].wait_recv()

    def finish(self):
        for copy in self.copies:
            copy.wait_send()


def dot(a, b, dims):
    return lax.dot_general(a, b, ((dims[:1], dims[1:]), ((), ())), preferred_element_type=F32)


NN, NT, TN = (1, 0), (1, 1), (0, 0)


def tiles(total, size):
    size = min(total, size)
    return total // size, size


def inverse_rms(values):
    return lax.rsqrt(jnp.mean(values * values, axis=-1, keepdims=True) + EPS)


def norm_back(values, inverse, grad_scaled, width):
    return inverse * grad_scaled - values * inverse**3 * (
        jnp.sum(values * grad_scaled, axis=-1, keepdims=True) / width
    )


def rope_factors(table):
    lane = lax.broadcasted_iota(jnp.int32, table.shape, 1)
    turned = pltpu.roll(table, HALF, 1)
    cosine = jnp.where(lane < HALF, table, turned)
    sine = jnp.where(lane < HALF, -turned, table)
    return cosine, sine


def exchange_rows(n, mine, msg, send, recv):
    s, c, u = where_am_i()
    msg[pl.ds(u, 1)] = mine[None]
    copies = []
    for step in range(1, n):
        peer = lax.rem(u + step, n)
        copy = remote(msg.at[u], msg.at[u], send.at[step - 1], recv.at[step - 1], (s, c, peer))
        copy.start()
        copies.append(copy)
    for step in range(1, n):
        source = lax.rem(u + n - step, n)
        remote(
            msg.at[source], msg.at[source], send.at[step - 1], recv.at[step - 1], (s, c, source)
        ).wait_recv()
    total = msg[0]
    for j in range(1, n):
        total = total + msg[j]
    for copy in copies:
        copy.wait_send()
    return total


def to_rows(col0, col1):
    span = col0.shape[0]
    lane = lax.broadcasted_iota(jnp.int32, (span, 128), 1)
    both = jnp.where(lane == 0, col0, jnp.where(lane == 1, col1, 0.0))
    return jnp.transpose(both)[:8]


def to_columns(rows8):
    return jnp.transpose(jnp.concatenate([rows8] * 16, axis=0))


def all_uly_peers(n):
    s, c, u = where_am_i()
    return [(None, (s, c, lax.rem(u + k, n))) for k in range(1, n)]


def spread_heads(cols):
    return cols % (4 * HEAD_DIM) == 0


def proj_kernel(
    n,
    x_ref,
    w_ref,
    tab_ref,
    gain_ref,
    seg_ref,
    wo_ref,
    gu_ref,
    xg_out,
    wq_out,
    wo_out,
    wga_out,
    proj_ref,
    qkv_refs,
    inv_ref,
    zero_ref,
    xg,
    wq,
    tab,
    msg,
    local_sem,
    w_send,
    w_recv,
    m_send,
    m_recv,
    *line,
):
    s, c, u = where_am_i()
    rows, width = x_ref.shape
    span = n * rows
    kb = w_ref.shape[1]
    sib = (1 - s, c, u)
    tab_copy = pltpu.make_async_copy(tab_ref.at[rows_of(c, span)], tab, local_sem.at[0])
    tab_copy.start()
    xg[rows_of(u, rows), :] = x_ref[...]
    greet(all_uly_peers(n) + plane_peers() + [(None, sib)])

    def plane(k, src, block, half_rows):
        return PlaneGather(
            src, block, half_rows, w_send.at[k], w_recv.at[k], local_sem.at[3 + k]
        )

    half = kb // 2
    gather = LineGather(n, rows, xg, line)
    first = plane(0, w_ref, lambda b: wq.at[:, rows_of(b, kb)], half)
    second = plane(1, wo_ref, lambda b: wo_out.at[b], wo_ref.shape[0] // 2)
    third = plane(2, gu_ref.at[0, pl.ds(0, half)], lambda b: wga_out.at[b], half // 2)
    gather.send(0)
    first.start()
    gather.wait(0)
    first.middle()
    second.start()
    if n > 2:
        gather.wait(1)
    first.corner()
    second.middle()
    third.start()
    for slot in range(2 if n > 2 else 1, n - 1):
        gather.wait(slot)
    first.arrive()
    tab_copy.wait()
    keep = [
        pltpu.make_async_copy(xg, xg_out, local_sem.at[1]),
        pltpu.make_async_copy(wq, wq_out, local_sem.at[2]),
    ]
    for copy in keep:
        copy.start()

    count, size = tiles(span, 512)

    def store(i, where, first, values):
        if len(qkv_refs) == 1:
            (ref,) = qkv_refs
            size = ref.shape[3]
            for at in range(0, values.shape[1], min(size, values.shape[1])):
                group, inside = divmod(first + at, size)
                part = values[:, at : at + size]
                ref[group, i, where, inside : inside + part.shape[1]] = part
        else:
            ref = qkv_refs[0] if i == 0 else qkv_refs[1].at[i - 1]
            ref[where, first : first + values.shape[1]] = values

    def project(i, carry):
        where = pl.ds(pl.multiple_of(i * size, size), size)
        xs = xg[where, :]
        proj_ref[0, where, :] = dot(xs, wq[0], NN)
        proj_ref[1, where, :] = dot(xs, wq[1], NN)
        store(2, where, 0, dot(xs, wq[2], NN).astype(BF16))
        return carry

    lax.fori_loop(0, count, project, 0)
    squares = [jnp.sum(proj_ref[i] * proj_ref[i], axis=-1, keepdims=True) for i in range(2)]
    mine = to_rows(*squares)
    zeros = jnp.sum((1 - seg_ref[...]).astype(F32))
    row = lax.broadcasted_iota(jnp.int32, mine.shape, 0)
    mine = jnp.where(row == 2, zeros, mine)
    second.corner()
    third.middle()
    total = exchange_rows(n, mine, msg, m_send, m_recv)
    zero_ref[...] = jnp.broadcast_to(total[2:3, :128], (8, 128))
    inv = lax.rsqrt(to_columns(total) / width + EPS)
    inv_ref[...] = inv
    cosine, sine = rope_factors(tab[...])
    heads = proj_ref.shape[2] // HEAD_DIM
    for i in range(2):
        inverse = inv_ref[:, i : i + 1]
        for h in range(heads):
            cols = slice(h * HEAD_DIM, (h + 1) * HEAD_DIM)
            v = proj_ref[i, :, cols] * inverse * gain_ref[i : i + 1, cols]
            v = (v * cosine + pltpu.roll(v, HALF, 1) * sine).astype(BF16)
            store(i, slice(None), h * HEAD_DIM, v)
    second.arrive()
    third.corner()
    third.arrive()
    for work in (first, second, third, gather):
        work.finish()
    for copy in keep:
        copy.wait()


def project(n, x, w, table, gain, seg, wo, gu):
    rows, width = x.shape
    span, cols = n * rows, w.shape[2]
    if spread_heads(cols):
        qkv = (shape((4, 3, span, cols // 4), BF16),)
    else:
        qkv = (shape((span, cols), BF16), shape((2, span, cols), BF16))
    return pl.pallas_call(
        functools.partial(proj_kernel, n),
        out_shape=(
            shape((span, width), BF16),
            shape((3, width, cols), BF16),
            shape((8,) + wo.shape, BF16),
            shape((8, gu.shape[1] // 2, gu.shape[2]), BF16),
            shape((2, span, cols), F32),
            qkv,
            shape((span, 128), F32),
            shape((8, 128), F32),
        ),
        in_specs=[VM, HB, HB, VM, VM, HB, HB],
        out_specs=(HB, HB, HB, HB, VM, (VM,) * len(qkv), VM, VM),
        scratch_shapes=[
            pltpu.VMEM((span, width), BF16),
            pltpu.VMEM((3, width, cols), BF16),
            pltpu.VMEM((span, 128), F32),
            pltpu.VMEM((n, 8, span), F32),
            pltpu.SemaphoreType.DMA((6,)),
            pltpu.SemaphoreType.DMA((3, 9)),
            pltpu.SemaphoreType.DMA((3, 9)),
            pltpu.SemaphoreType.DMA((n - 1,)),
            pltpu.SemaphoreType.DMA((n - 1,)),
        ]
        + line_sems(n),
        compiler_params=pltpu.CompilerParams(
            collective_id=1, has_side_effects=True, vmem_limit_bytes=VMEM_LIMIT
        ),
        name="project",
    )(x, w, table, gain, seg, wo, gu)


def score_mask(scores, key_first, query_first, starts, diagonal):
    key_pos = key_first + lax.broadcasted_iota(jnp.int32, scores.shape, 0)
    keep = key_pos >= starts
    if diagonal:
        query_pos = query_first + lax.broadcasted_iota(jnp.int32, scores.shape, 1)
        keep = keep & (key_pos <= query_pos)
    return jnp.where(keep, scores, FLOOR)


def segment_starts(first, size, bound):
    pos = first + lax.broadcasted_iota(jnp.int32, (1, size), 1)
    return jnp.where(pos >= bound, bound, 0)


def attend_kernel(
    q_ref,
    kv_ref,
    zero_ref,
    gu_ref,
    kvall_out,
    wgb_out,
    attn_ref,
    attn32_ref,
    lse_ref,
    bound_ref,
    kvall,
    peaks,
    sums,
    acct,
    zmsg,
    send,
    recv,
    z_send,
    z_recv,
    w_send,
    w_recv,
    keep_sem,
    w_local,
):
    s, c, u = where_am_i()
    span, cols = q_ref.shape
    heads = cols // HEAD_DIM
    xn, yn, dn = (s, c ^ 1, u), (s, c ^ 2, u), (s, c ^ 3, u)
    kvall[pl.ds(c, 1)] = kv_ref[...][None]
    zmsg[pl.ds(c, 1)] = zero_ref[...][None]
    greet(plane_peers() + [(None, dn), (None, (1 - s, c, u))])
    weight = upper_gate(gu_ref, wgb_out, w_send, w_recv, w_local)

    def sent(k, view, peer):
        return remote(view, view, send.at[k], recv.at[k], peer)

    bx, by, bd = c ^ 1, c ^ 2, c ^ 3
    zs = [
        remote(zmsg.at[c], zmsg.at[c], z_send.at[k], z_recv.at[k], peer)
        for k, peer in enumerate((xn, yn, dn))
    ]
    for copy in zs:
        copy.start()
    copies = [sent(0, kvall.at[c], xn), sent(1, kvall.at[c], yn)]
    for copy in copies:
        copy.start()
    for k, (b, peer) in enumerate(((bx, xn), (by, yn), (bd, dn))):
        remote(zmsg.at[b], zmsg.at[b], z_send.at[k], z_recv.at[k], peer).wait_recv()
    ahead = jnp.zeros((8, 128), F32)
    for j in range(4):
        ahead = ahead + jnp.where(j <= c, zmsg[j], 0.0)
    bounds = ahead.astype(jnp.int32)
    bound_ref[...] = bounds
    bound = bounds[:1, :1]

    peaks[...] = jnp.full_like(peaks, FLOOR)
    sums[...] = jnp.zeros_like(sums)
    acct[...] = jnp.zeros_like(acct)
    nq, tq = tiles(span, 512)
    nk, tk = tiles(span, 512)

    def update(number, diagonal):
        def over_queries(i, carry):
            first_q = c * span + i * tq
            starts = segment_starts(first_q, tq, bound)
            where_q = pl.ds(pl.multiple_of(i * tq, tq), tq)

            def over_keys(j, carry):
                first_k = number * span + j * tk
                where_k = pl.ds(pl.multiple_of(j * tk, tk), tk)
                for h in range(heads):
                    lanes = slice(h * HEAD_DIM, (h + 1) * HEAD_DIM)
                    scores = dot(kvall[number, 0, where_k, lanes], q_ref[where_q, lanes], NT)
                    scores = score_mask(scores * SCALE2, first_k, first_q, starts, diagonal)
                    old = peaks[h, :1, where_q]
                    new = jnp.maximum(old, jnp.max(scores, axis=0, keepdims=True))
                    factor = jnp.exp2(old - new)
                    weights = jnp.exp2(scores - new)
                    peaks[h, :1, where_q] = new
                    sums[h, :1, where_q] = sums[h, :1, where_q] * factor + jnp.sum(
                        weights, axis=0, keepdims=True
                    )
                    acct[h, :, where_q] = acct[h, :, where_q] * factor + dot(
                        kvall[number, 1, where_k, lanes], weights.astype(BF16), TN
                    )
                return carry

            return lax.fori_loop(0, nk, over_keys, carry)

        lax.fori_loop(0, nq, over_queries, 0)

    update(c, True)
    half = span // 2
    sent(0, kvall.at[bx], xn).wait_recv()
    more = [sent(2, kvall.at[bx, :, pl.ds(0, half)], yn)]
    more[0].start()
    copies += more
    sent(1, kvall.at[by], yn).wait_recv()
    more = [sent(3, kvall.at[by, :, pl.ds(half, half)], xn)]
    more[0].start()
    copies += more
    for b in (bx, by):

        @pl.when(b < c)
        def _():
            update(b, False)

    sent(2, kvall.at[bd, :, pl.ds(0, half)], yn).wait_recv()
    sent(3, kvall.at[bd, :, pl.ds(half, half)], xn).wait_recv()
    keep = pltpu.make_async_copy(kvall, kvall_out, keep_sem)
    keep.start()
    weight.start()

    @pl.when(bd < c)
    def _():
        update(bd, False)

    for h in range(heads):
        lanes = slice(h * HEAD_DIM, (h + 1) * HEAD_DIM)
        total = sums[h, :1, :]
        attention = jnp.transpose(acct[h] / total)
        attn32_ref[:, lanes] = attention
        attn_ref[:, lanes] = attention.astype(BF16)
        lse_ref[h, :1, :] = peaks[h, :1, :] + jnp.log2(total)
    for copy in copies + zs:
        copy.wait_send()
    weight.middle()
    weight.corner()
    weight.arrive()
    weight.finish()
    keep.wait()


def attend(q, kv, zero, gu):
    span, cols = q.shape
    heads = cols // HEAD_DIM
    return pl.pallas_call(
        attend_kernel,
        out_shape=(
            shape((4, 2, span, cols), BF16),
            shape((8, gu.shape[1] // 2, gu.shape[2]), BF16),
            shape((span, cols), BF16),
            shape((span, cols), F32),
            shape((heads, 8, span), F32),
            shape((8, 128), jnp.int32),
        ),
        in_specs=[VM] * 3 + [HB],
        out_specs=(HB, HB, VM, VM, VM, VM),
        scratch_shapes=[
            pltpu.VMEM((4, 2, span, cols), BF16),
            pltpu.VMEM((heads, 8, span), F32),
            pltpu.VMEM((heads, 8, span), F32),
            pltpu.VMEM((heads, HEAD_DIM, span), F32),
            pltpu.VMEM((4, 8, 128), F32),
            pltpu.SemaphoreType.DMA((4,)),
            pltpu.SemaphoreType.DMA((4,)),
            pltpu.SemaphoreType.DMA((3,)),
            pltpu.SemaphoreType.DMA((3,)),
            pltpu.SemaphoreType.DMA((9,)),
            pltpu.SemaphoreType.DMA((9,)),
            pltpu.SemaphoreType.DMA,
            pltpu.SemaphoreType.DMA,
        ],
        compiler_params=pltpu.CompilerParams(
            collective_id=2, has_side_effects=True, vmem_limit_bytes=VMEM_LIMIT
        ),
        name="attend",
    )(q, kv, zero, gu)


def upper_gate(gu_ref, out, send, recv, local):
    half = gu_ref.shape[1] // 2
    return PlaneGather(
        gu_ref.at[0, pl.ds(half, half)], lambda b: out.at[b], half // 2, send, recv, local
    )


def norms_back(source, keep, proj_ref, inv_ref, gain_ref, tab, dgain_ref):
    cosine, sine = rope_factors(tab[...])
    span, cols = proj_ref.shape[1:]
    dots = []
    for i in range(2):
        inverse = inv_ref[:, i : i + 1]
        row_dot = jnp.zeros((span, 1), F32)
        for h in range(cols // HEAD_DIM):
            lanes = slice(h * HEAD_DIM, (h + 1) * HEAD_DIM)
            v = source(i, h)
            v = v * cosine - pltpu.roll(v, HALF, 1) * sine
            values = proj_ref[i, :, lanes]
            dgain_ref[i : i + 1, lanes] = jnp.sum(v * values * inverse, axis=0, keepdims=True)
            v = v * gain_ref[i : i + 1, lanes]
            keep(i, h, v)
            row_dot = row_dot + jnp.sum(values * v, axis=-1, keepdims=True)
        dots.append(row_dot)
    return to_rows(*dots)


def attend_back_kernel(
    n,
    q_ref,
    kvall_ref,
    do_ref,
    attn32_ref,
    lse_ref,
    bound_ref,
    proj_ref,
    inv_ref,
    gain_ref,
    tab_ref,
    resid_hbm,
    resid_s_hbm,
    dgu_hbm,
    dgu_s_hbm,
    own_in,
    x_in,
    y_in,
    dproj_ref,
    dgain_ref,
    own_out,
    x_out,
    y_out,
    dq_ref,
    part,
    got,
    acc,
    delta,
    tab,
    msg,
    late_buffers,
    late_sems,
    send,
    recv,
    local_sem,
    m_send,
    m_recv,
):
    s, c, u = where_am_i()
    span, cols = q_ref.shape
    width = resid_hbm.shape[1]
    heads = cols // HEAD_DIM
    xn, yn = (s, c ^ 1, u), (s, c ^ 2, u)
    bx, by, bd = c ^ 1, c ^ 2, c ^ 3
    load = pltpu.make_async_copy(tab_ref.at[rows_of(c, span)], tab, local_sem)
    load.start()
    last = 2 * (dgu_hbm.shape[2] // late_buffers[2].shape[1])
    late = LatePiece(
        last - 2,
        (resid_hbm, resid_s_hbm, dgu_hbm, dgu_s_hbm),
        (own_out, x_out, y_out),
        late_buffers,
        late_sems,
    )
    late.load()
    pieces = Pieces([late.work()])
    greet(plane_peers() + all_uly_peers(n))
    bound = bound_ref[:1, :1]
    nq, tq = tiles(span, 512)
    nk, tk = tiles(span, 512)
    scale = HEAD_DIM ** (-0.5)
    dq_ref[...] = jnp.zeros_like(dq_ref)
    for h in range(heads):
        lanes = slice(h * HEAD_DIM, (h + 1) * HEAD_DIM)
        both = jnp.transpose(do_ref[:, lanes].astype(F32) * attn32_ref[:, lanes])
        delta[h, :1, :] = jnp.sum(both, axis=0, keepdims=True)

    def update(number, diagonal):
        acc[...] = jnp.zeros_like(acc)

        def over_queries(i, carry):
            first_q = c * span + i * tq
            starts = segment_starts(first_q, tq, bound)
            where_q = pl.ds(pl.multiple_of(i * tq, tq), tq)

            def over_keys(j, carry):
                first_k = number * span + j * tk
                where_k = pl.ds(pl.multiple_of(j * tk, tk), tk)
                for h in range(heads):
                    lanes = slice(h * HEAD_DIM, (h + 1) * HEAD_DIM)
                    keys = kvall_ref[number, 0, where_k, lanes]
                    values = kvall_ref[number, 1, where_k, lanes]
                    query, d_out = q_ref[where_q, lanes], do_ref[where_q, lanes]
                    scores = dot(keys, query, NT) * SCALE2
                    scores = score_mask(scores, first_k, first_q, starts, diagonal)
                    probs = jnp.exp2(scores - lse_ref[h, :1, where_q])
                    acc[1, where_k, lanes] += dot(probs.astype(BF16), d_out, NN)
                    d_probs = dot(values, d_out, NT)
                    d_scores = (probs * (d_probs - delta[h, :1, where_q])).astype(BF16)
                    acc[0, where_k, lanes] += dot(d_scores, query, NN) * scale
                    dq_ref[where_q, lanes] += dot(d_scores, keys, TN) * scale
                return carry

            return lax.fori_loop(0, nk, over_keys, carry)

        lax.fori_loop(0, nq, over_queries, 0)

    def work(number):
        @pl.when(number < c)
        def _():
            update(number, False)
            part[pl.ds(number, 1)] = acc[...].astype(BF16)[None]

        @pl.when(number > c)
        def _():
            part[pl.ds(number, 1)] = jnp.zeros_like(part[pl.ds(number, 1)])

    half = span // 2
    lo, hi = pl.ds(0, half), pl.ds(half, half)

    def sent(k, src, dst, peer):
        return remote(src, dst, send.at[k], recv.at[k], peer)

    pieces.step()
    work(bd)
    copies = [
        sent(0, part.at[bd, :, lo], got.at[0, :, lo], xn),
        sent(1, part.at[bd, :, hi], got.at[0, :, hi], yn),
    ]
    for copy in copies:
        copy.start()
    pieces.catch_up()
    work(bx)
    sent(1, part.at[bx, :, hi], got.at[0, :, hi], yn).wait_recv()
    part[bx, :, half:, :] = (
        part[bx, :, half:, :].astype(F32) + got[0, :, half:, :].astype(F32)
    ).astype(BF16)
    more = [sent(2, part.at[bx], got.at[1], xn)]
    more[0].start()
    copies += more
    work(by)
    sent(0, part.at[by, :, lo], got.at[0, :, lo], xn).wait_recv()
    part[by, :, :half, :] = (
        part[by, :, :half, :].astype(F32) + got[0, :, :half, :].astype(F32)
    ).astype(BF16)
    more = [sent(3, part.at[by], got.at[2], yn)]
    more[0].start()
    copies += more
    update(c, True)
    load.wait()

    cosine, sine = rope_factors(tab[...])

    def turn_back(i):
        inverse = inv_ref[:, i : i + 1]
        row_dot = jnp.zeros((span, 1), F32)
        for h in range(heads):
            lanes = slice(h * HEAD_DIM, (h + 1) * HEAD_DIM)
            source = dq_ref if i == 0 else acc.at[0]
            v = source[:, lanes]
            v = v * cosine - pltpu.roll(v, HALF, 1) * sine
            values = proj_ref[i, :, lanes]
            dgain_ref[i : i + 1, lanes] = jnp.sum(v * values * inverse, axis=0, keepdims=True)
            v = v * gain_ref[i : i + 1, lanes]
            source[:, lanes] = v
            row_dot = row_dot + jnp.sum(values * v, axis=-1, keepdims=True)
        return row_dot

    dots_q = turn_back(0)
    sent(2, part.at[bx], got.at[1], xn).wait_recv()
    sent(3, part.at[by], got.at[2], yn).wait_recv()
    acc[...] += got[1].astype(F32) + got[2].astype(F32)
    dproj_ref[2] = acc[1].astype(BF16)
    dots_k = turn_back(1)
    total = exchange_rows(n, to_rows(dots_q, dots_k), msg, m_send, m_recv)
    means = to_columns(total) / width
    for i in range(2):
        inverse = inv_ref[:, i : i + 1]
        factor = inverse**3 * means[:, i : i + 1]
        source = dq_ref if i == 0 else acc.at[0]
        dproj_ref[i] = (inverse * source[...] - proj_ref[i] * factor).astype(BF16)
    pieces.finish()
    late.plane.finish(1)
    for copy in copies:
        copy.wait_send()


def attend_back(
    n, q, kvall, d_out, attn32, lse, bound, proj, inv, gain, table, late, grads
):
    span, cols = q.shape
    heads = cols // HEAD_DIM
    width, ff = late[0].shape[1], late[2].shape[2]
    return pl.pallas_call(
        functools.partial(attend_back_kernel, n),
        out_shape=(shape((3, span, cols), BF16), shape((2, cols), F32))
        + tuple(shape(g.shape, BF16) for g in grads),
        in_specs=[VM] * 9 + [HB] * 8,
        out_specs=(VM, VM, HB, HB, HB),
        input_output_aliases={14: 2, 15: 3, 16: 4},
        scratch_shapes=[
            pltpu.VMEM((span, cols), F32),
            pltpu.VMEM((4, 2, span, cols), BF16),
            pltpu.VMEM((3, 2, span, cols), BF16),
            pltpu.VMEM((2, span, cols), F32),
            pltpu.VMEM((heads, 8, span), F32),
            pltpu.VMEM((span, 128), F32),
            pltpu.VMEM((n, 8, span), F32),
        ]
        + LatePiece.scratch(span, width, ff)
        + [
            pltpu.SemaphoreType.DMA((4,)),
            pltpu.SemaphoreType.DMA((4,)),
            pltpu.SemaphoreType.DMA,
            pltpu.SemaphoreType.DMA((n - 1,)),
            pltpu.SemaphoreType.DMA((n - 1,)),
        ],
        compiler_params=pltpu.CompilerParams(
            collective_id=3, has_side_effects=True, vmem_limit_bytes=VMEM_LIMIT
        ),
        name="attend_back",
    )(q, kvall, d_out, attn32, lse, bound, proj, inv, gain, table, *late, *grads)


class Keep:
    def __init__(self, sems):
        self.sems, self.copies = sems, []

    def __call__(self, src, dst):
        copy = pltpu.make_async_copy(src, dst, self.sems.at[len(self.copies)])
        copy.start()
        self.copies.append(copy)
        return copy

    def finish(self, but=()):
        for copy in self.copies:
            if not any(copy is done for done in but):
                copy.wait()


def forward_kernel(n, names, *refs):
    ref = SimpleNamespace(**dict(zip(names, refs)))
    x_ref, w_ref, tab_ref, gain_ref, seg_ref = ref.x, ref.w, ref.table, ref.gain, ref.seg
    wo_ref, gu_ref, down_ref, post_ref = ref.wo, ref.gu, ref.down, ref.post
    s, c, u = where_am_i()
    rows, width = x_ref.shape
    span, half = n * rows, rows // 2
    kb = w_ref.shape[1]
    xg, wq, proj, qkv = ref.v_xg, ref.v_wq, ref.v_proj, ref.v_qkv
    every, back, attn = ref.v_every, ref.v_back, ref.v_attn
    cols = proj.shape[2]
    quarter = cols // 4
    keep, load = Keep(ref.keep_sem), Keep(ref.load_sem)
    table = load(tab_ref.at[rows_of(c, span)], ref.v_tab)
    xg[rows_of(u, rows), :] = x_ref[...]
    peers = [(s, c ^ k, u) for k in (1, 2, 3)]
    greet(all_uly_peers(n) + [(None, peer) for peer in peers] + [(None, (1 - s, c, u))])

    def plane(k, src, block, half_rows):
        return PlaneGather(
            src, block, half_rows, ref.w_send.at[k], ref.w_recv.at[k], ref.w_local.at[k]
        )

    def plane_to(k, src, out):
        return plane(k, src, lambda b: out.at[b], src.shape[0] // 2)

    lower, upper = pl.ds(0, kb // 2), pl.ds(kb // 2, kb // 2)
    w_qkv = plane(0, w_ref, lambda b: wq.at[:, rows_of(b, kb)], kb // 2)
    w_out = plane_to(1, wo_ref, ref.o_wo)
    w_a = plane_to(2, gu_ref.at[0, lower], ref.o_wga)
    w_b = plane_to(3, gu_ref.at[0, upper], ref.o_wgb)
    w_c = plane_to(4, gu_ref.at[1], ref.o_wgc)
    w_d = plane_to(5, down_ref, ref.o_wd)

    gather = LineGather(n, rows, xg, ref.x_sems)
    gather.send(0)
    w_qkv.start()
    gather.wait(0)
    w_qkv.middle()
    w_out.start()
    if n > 2:
        gather.wait(1)
    w_qkv.corner()
    w_a.start()
    w_out.middle()
    for slot in range(2 if n > 2 else 1, n - 1):
        gather.wait(slot)
    w_qkv.arrive()
    keep(xg, ref.o_xg)
    keep(wq, ref.o_wq)
    count, size = tiles(span, 512)

    def project(i, carry):
        where = pl.ds(pl.multiple_of(i * size, size), size)
        xs = xg[where, :]
        proj[0, where, :] = dot(xs, wq[0], NN)
        proj[1, where, :] = dot(xs, wq[1], NN)
        value = dot(xs, wq[2], NN).astype(BF16)
        for q in range(4):
            qkv[q, 2, where, :] = value[:, q * quarter : (q + 1) * quarter]
        return carry

    lax.fori_loop(0, count, project, 0)
    keep(proj, ref.o_proj)
    squares = [jnp.sum(proj[i] * proj[i], axis=-1, keepdims=True) for i in range(2)]
    mine = to_rows(*squares)
    zeros = jnp.sum((1 - seg_ref[...]).astype(F32))
    row = lax.broadcasted_iota(jnp.int32, mine.shape, 0)
    mine = jnp.where(row == 2, zeros, mine)
    total = exchange_rows(n, mine, ref.v_msg, ref.m_send, ref.m_recv)
    zmsg = ref.v_zmsg
    zmsg[pl.ds(c, 1)] = jnp.broadcast_to(total[2:3, :128], (1, 8, 128))
    inv = ref.v_inv
    inv[...] = lax.rsqrt(to_columns(total) / width + EPS)
    table.wait()
    cosine, sine = rope_factors(ref.v_tab[...])
    for i in range(2):
        inverse = inv[:, i : i + 1]
        for h in range(cols // HEAD_DIM):
            lanes = slice(h * HEAD_DIM, (h + 1) * HEAD_DIM)
            v = proj[i, :, lanes] * inverse * gain_ref[i : i + 1, lanes]
            v = (v * cosine + pltpu.roll(v, HALF, 1) * sine).astype(BF16)
            group, inside = divmod(h * HEAD_DIM, quarter)
            qkv[group, i, :, inside : inside + HEAD_DIM] = v

    copies, arrivals = [], []
    a_send, a_recv, z_send, z_recv = ref.a_send, ref.a_recv, ref.z_send, ref.z_recv
    for k, peer in enumerate(peers):
        there = peer[1]
        copy = remote(qkv.at[there], every.at[c], a_send.at[k], a_recv.at[k], peer)
        copy.start()
        small = remote(zmsg.at[c], zmsg.at[c], z_send.at[k], z_recv.at[k], peer)
        small.start()
        copies += [copy, small]
        arrivals.append(remote(every.at[there], every.at[there], a_send.at[k], a_recv.at[k], peer))
        arrivals.append(remote(zmsg.at[there], zmsg.at[there], z_send.at[k], z_recv.at[k], peer))
    every[pl.ds(c, 1)] = qkv[pl.ds(c, 1)]
    keep(inv, ref.o_inv)
    w_a.middle()
    w_out.corner()
    w_out.arrive()
    load_o = load_blocks(ref.o_wo, ref.v_wo, ref.wo_sem, 1)
    for arrival in arrivals:
        arrival.wait_recv()
    w_b.start()
    keep(every, ref.o_every)
    bounds = (zmsg[0] + zmsg[1] + zmsg[2] + zmsg[3]).astype(jnp.int32)
    ref.v_bound[...] = bounds
    bound = bounds[:1, :1]
    peaks, sums, acct = ref.v_peaks, ref.v_sums, ref.v_acct
    att, lse = ref.v_att, ref.v_lse

    def attend(k, carry):
        i = c ^ (3 - k)
        first_q = i * span
        starts = segment_starts(first_q, span, bound)
        for h in range(quarter // HEAD_DIM):
            lanes = slice(h * HEAD_DIM, (h + 1) * HEAD_DIM)
            peaks[...] = jnp.full_like(peaks, FLOOR)
            sums[...] = jnp.zeros_like(sums)
            acct[...] = jnp.zeros_like(acct)

            def update(j, diagonal):
                scores = dot(every[j, 1, :, lanes], every[i, 0, :, lanes], NT) * SCALE2
                scores = score_mask(scores, j * span, first_q, starts, diagonal)
                old = peaks[:1, :]
                new = jnp.maximum(old, jnp.max(scores, axis=0, keepdims=True))
                factor = jnp.exp2(old - new)
                weights = jnp.exp2(scores - new)
                peaks[:1, :] = new
                sums[:1, :] = sums[:1, :] * factor + jnp.sum(weights, axis=0, keepdims=True)
                acct[...] = acct[...] * factor + dot(
                    every[j, 2, :, lanes], weights.astype(BF16), TN
                )

            def before(j, carry):
                update(j, False)
                return carry

            lax.fori_loop(0, i, before, 0)
            update(i, True)
            total = sums[:1, :]
            attention = acct[...] / total
            att[pl.ds(i, 1), lanes, :] = attention[None]
            back[pl.ds(k, 1), :, :, lanes] = (
                jnp.transpose(attention).astype(BF16).reshape(1, n, rows, HEAD_DIM)
            )
            lse[pl.ds(i, 1), h, :1, :] = (peaks[:1, :] + jnp.log2(total))[None]

        @pl.when(k < 3)
        def _():
            home(k, i, c).start()

        return carry

    def home(k, i, owner):
        return remote(
            back.at[k],
            attn.at[:, :, pl.ds(pl.multiple_of(owner * quarter, quarter), quarter)],
            ref.b_send.at[k],
            ref.b_recv.at[k],
            (s, i, u),
        )

    lax.fori_loop(0, 4, attend, 0)
    attn[:, :, pl.ds(pl.multiple_of(c * quarter, quarter), quarter)] = back[3]
    keep(att, ref.o_att)
    keep(lse, ref.o_lse)
    keep(ref.v_bound, ref.o_bound)
    w_a.corner()
    for k in range(3):
        i = c ^ (3 - k)
        home(k, i, i).wait_recv()
    keep(attn, ref.o_attn)
    wait_all(load_o)
    w_a.arrive()
    wg = ref.v_wg
    load(ref.o_wga, wg.at[0, :, lower])

    wo, part, group = ref.v_wo, ref.v_part, ref.v_group
    halves = Halves(n, rows)
    per_half, chunk_cols = part.shape[0] // 2, part.shape[2]

    def compute(chunk):
        h, q = divmod(chunk, per_half)
        lanes = slice(q * chunk_cols, (q + 1) * chunk_cols)

        def tile(index, start, size):
            part[chunk, start : start + size, :] = dot(
                halves.load(attn, index), wo[:, lanes], NN
            ).astype(BF16)

        halves.each(h, tile)

    reduce = LineReduce(n, half, part, ref.v_got, ref.r_sems)
    g_sems = ref.g_sems
    gathers = [LineGather(n, rows, group, g_sems, (h, half)) for h in range(2)]
    branch, resid = ref.v_branch, ref.v_resid
    gate, up, hidden = ref.v_gate, ref.v_up, ref.v_hidden

    def finish(h):
        where = slice(h * half, (h + 1) * half)
        reduce.last(branch.at[h], range(h * per_half, (h + 1) * per_half))
        values = branch[h]
        total = x_ref[where, :].astype(F32) + values * inverse_rms(values) * post_ref[0:1, :]
        resid[h] = total
        group[pl.ds(u, 1), where, :] = total.astype(BF16)[None]

    ff = gate.shape[2]
    ntile, tsize = tiles(ff, 512)

    def body(h, t):
        lanes = slice(t * tsize, (t + 1) * tsize)

        def tile(index, start, size):
            inputs = halves.load(group, index)
            gates = dot(inputs, wg[0, :, :, lanes].reshape(width, tsize), NN)
            ups = dot(inputs, wg[1, :, :, lanes].reshape(width, tsize), NN)
            halves.store(gate, index, lanes, gates.astype(BF16))
            halves.store(up, index, lanes, ups.astype(BF16))
            halves.store(
                hidden, index, lanes, (gates * jax.nn.sigmoid(gates) * ups).astype(BF16)
            )

        halves.each(h, tile)
        if h == 1:
            for out, src in ((ref.o_hidden, hidden), (ref.o_gate, gate), (ref.o_up, up)):
                keep(src.at[:, :, lanes], out.at[:, :, lanes])

    def hook(label):
        if label == "started":
            w_b.middle()
            w_c.start()
        if label == "sent":
            w_b.corner()
        if label == "b1":
            w_b.arrive()
            load(ref.o_wgb, wg.at[0, :, upper])
        if label == f"b{n - 2}":
            w_c.middle()
        if label == "first":
            keep(branch, ref.o_branch)
            keep(resid, ref.o_resid)
            w_c.corner()
            w_d.start()
            w_c.arrive()
            load(ref.o_wgc, wg.at[1])
            load.finish((table,))
        if label == f"g{n - 2}":
            keep(group, ref.o_group)

    reduce_norm_gather(n, reduce, gathers, compute, finish, Consume(ntile, body), hook)
    w_d.middle()
    w_d.corner()
    w_d.arrive()
    for k in range(3):
        home(k, c ^ (3 - k), c).wait_send()
    for copy in copies:
        copy.wait_send()
    for work in (w_qkv, w_out, w_a, w_b, w_c, w_d, gather):
        work.finish()
    keep.finish()


def forward(n, x, w, table, gain, seg, wo, gu, down, post):
    rows, width = x.shape
    span, cols, half = n * rows, w.shape[2], rows // 2
    quarter = cols // 4
    kb, ff = gu.shape[1:]
    ntile = tiles(ff, 512)[0]
    dma = pltpu.SemaphoreType.DMA
    ins = dict(
        x=(x, VM),
        w=(w, HB),
        table=(table, HB),
        gain=(gain, VM),
        seg=(seg, VM),
        wo=(wo, HB),
        gu=(gu, HB),
        down=(down, HB),
        post=(post, VM),
    )
    outs = dict(
        o_xg=((span, width), BF16),
        o_wq=((3, width, cols), BF16),
        o_wo=((8,) + wo.shape, BF16),
        o_wga=((8, kb // 2, ff), BF16),
        o_wgb=((8, kb // 2, ff), BF16),
        o_wgc=((8, kb, ff), BF16),
        o_wd=((8,) + down.shape, BF16),
        o_proj=((2, span, cols), F32),
        o_inv=((span, 128), F32),
        o_every=((4, 3, span, quarter), BF16),
        o_att=((4, quarter, span), F32),
        o_lse=((4, quarter // HEAD_DIM, 8, span), F32),
        o_bound=((8, 128), jnp.int32),
        o_attn=((n, rows, cols), BF16),
        o_branch=((2, half, width), F32),
        o_resid=((2, half, width), F32),
        o_group=((n, rows, width), BF16),
        o_gate=((n, rows, ff), BF16),
        o_up=((n, rows, ff), BF16),
        o_hidden=((n, rows, ff), BF16),
    )
    buffers = dict(
        v_xg=((span, width), BF16),
        v_wq=((3, width, cols), BF16),
        v_tab=((span, 128), F32),
        v_proj=((2, span, cols), F32),
        v_inv=((span, 128), F32),
        v_msg=((n, 8, span), F32),
        v_qkv=((4, 3, span, quarter), BF16),
        v_every=((4, 3, span, quarter), BF16),
        v_back=((4, n, rows, quarter), BF16),
        v_zmsg=((4, 8, 128), F32),
        v_bound=((8, 128), jnp.int32),
        v_peaks=((8, span), F32),
        v_sums=((8, span), F32),
        v_acct=((HEAD_DIM, span), F32),
        v_att=((4, quarter, span), F32),
        v_lse=((4, quarter // HEAD_DIM, 8, span), F32),
        v_attn=((n, rows, cols), BF16),
        v_wo=((cols, width), BF16),
        v_wg=((2, 8, kb, ff), BF16),
        v_group=((n, rows, width), BF16),
        v_branch=((2, half, width), F32),
        v_resid=((2, half, width), F32),
        v_gate=((n, rows, ff), BF16),
        v_up=((n, rows, ff), BF16),
        v_hidden=((n, rows, ff), BF16),
        v_part=((4, n * half, width // 2), BF16),
        v_got=((4, (n + 1) * half, width // 2), BF16),
    )
    sems = dict(
        keep_sem=(12 + 3 * ntile,),
        load_sem=(4,),
        wo_sem=(8,),
        w_send=(6, 9),
        w_recv=(6, 9),
        w_local=(6,),
        m_send=(n - 1,),
        m_recv=(n - 1,),
    )
    three, fours = (3,), dict(x_sems=(n - 1,), r_sems=(n - 1, 4), g_sems=(n - 1, 2))
    sems.update(a_send=three, a_recv=three, z_send=three, z_recv=three, b_send=three, b_recv=three)
    names = [*ins, *outs, *buffers, *sems, *fours]
    results = pl.pallas_call(
        functools.partial(forward_kernel, n, names),
        out_shape=[shape(*out) for out in outs.values()],
        in_specs=[spec for value, spec in ins.values()],
        out_specs=[HB] * len(outs),
        scratch_shapes=[pltpu.VMEM(*buffer) for buffer in buffers.values()]
        + [dma(dims) for dims in sems.values()]
        + [(dma(dims),) * 4 for dims in fours.values()],
        compiler_params=pltpu.CompilerParams(
            collective_id=10, has_side_effects=True, vmem_limit_bytes=VMEM_LIMIT
        ),
        name="forward",
    )(*[value for value, spec in ins.values()])
    return SimpleNamespace(**dict(zip(outs, results)))


def load_blocks(src, dst, sem, axis):
    blocks = src.shape[0]
    size = dst.shape[axis] // blocks
    copies = []
    for b in range(blocks):
        where = [slice(None)] * len(dst.shape)
        where[axis] = pl.ds(b * size, size)
        copies.append(pltpu.make_async_copy(src.at[b], dst.at[tuple(where)], sem.at[b]))
    for copy in copies:
        copy.start()
    return copies


def wait_all(copies):
    for copy in copies:
        copy.wait()


def mlp_in_kernel(
    n,
    attn_ref,
    wo_ref,
    x_ref,
    gain_ref,
    wga_ref,
    wgb_ref,
    gu_ref,
    down_ref,
    branch_out,
    resid_out,
    group_out,
    gate_out,
    up_out,
    hidden_out,
    wgc_out,
    wd_out,
    wo,
    wg,
    group,
    branch,
    resid,
    gate,
    up,
    hidden,
    part,
    got_rows,
    sem_o,
    local_sem,
    keep_sem,
    w_send,
    w_recv,
    *sems,
):
    s, c, u = where_am_i()
    rows, width = x_ref.shape
    load_o = load_blocks(wo_ref, wo, sem_o, 1)
    kb = wgc_out.shape[1]
    load_g = [
        pltpu.make_async_copy(wga_ref, wg.at[0, :, pl.ds(0, kb // 2)], local_sem.at[0]),
        pltpu.make_async_copy(wgb_ref, wg.at[0, :, pl.ds(kb // 2, kb // 2)], local_sem.at[1]),
        pltpu.make_async_copy(wgc_out, wg.at[1], local_sem.at[2]),
    ]
    greet(line_peers(n) + plane_peers() + [(None, (1 - s, c, u))])

    def plane(k, src, out, half_rows):
        return PlaneGather(
            src, lambda b: out.at[b], half_rows, w_send.at[k], w_recv.at[k], local_sem.at[3 + k]
        )

    first = plane(0, gu_ref.at[1], wgc_out, kb // 2)
    second = plane(1, down_ref, wd_out, down_ref.shape[0] // 2)
    first.start()
    load_g[0].start()
    load_g[1].start()
    wait_all(load_o)
    halves = Halves(n, rows)
    half = rows // 2
    per_half = part.shape[0] // 2
    chunk_cols = part.shape[2]

    def compute(chunk):
        h, q = divmod(chunk, per_half)
        cols = slice(q * chunk_cols, (q + 1) * chunk_cols)

        def tile(index, start, size):
            part[chunk, start : start + size, :] = dot(
                halves.load(attn_ref, index), wo[:, cols], NN
            ).astype(BF16)

        halves.each(h, tile)

    reduce = LineReduce(n, half, part, got_rows, sems[:4])
    gathers = [LineGather(n, rows, group, sems[4:], (h, half)) for h in range(2)]
    kept = []

    def keep(src, dst):
        copy = pltpu.make_async_copy(src, dst, keep_sem.at[len(kept)])
        copy.start()
        kept.append(copy)

    def finish(h):
        where = slice(h * half, (h + 1) * half)
        reduce.last(branch.at[h], range(h * per_half, (h + 1) * per_half))
        values = branch[h]
        total = x_ref[where, :].astype(F32) + values * inverse_rms(values) * gain_ref[0:1, :]
        resid[h] = total
        group[pl.ds(u, 1), where, :] = total.astype(BF16)[None]

    ff = gate.shape[2]
    ntile, tsize = tiles(ff, 512)

    def body(h, t):
        lanes = slice(t * tsize, (t + 1) * tsize)

        def tile(index, start, size):
            inputs = halves.load(group, index)
            gates = dot(inputs, wg[0, :, :, lanes].reshape(width, tsize), NN)
            ups = dot(inputs, wg[1, :, :, lanes].reshape(width, tsize), NN)
            halves.store(gate, index, lanes, gates.astype(BF16))
            halves.store(up, index, lanes, ups.astype(BF16))
            halves.store(
                hidden, index, lanes, (gates * jax.nn.sigmoid(gates) * ups).astype(BF16)
            )

        halves.each(h, tile)
        if h == 1:
            for src, dst in ((hidden, hidden_out), (gate, gate_out), (up, up_out)):
                keep(src.at[:, :, lanes], dst.at[:, :, lanes])

    def hook(label):
        if label == "b1":
            first.middle()
            second.start()
        if label == "first":
            keep(branch, branch_out)
            keep(resid, resid_out)
            first.corner()
            first.arrive()
            load_g[2].start()
            wait_all(load_g)
        if label == f"g{n - 2}":
            keep(group, group_out)
        if label == "t0":
            second.middle()

    reduce_norm_gather(n, reduce, gathers, compute, finish, Consume(ntile, body), hook)
    second.corner()
    second.arrive()
    for work in (first, second):
        work.finish()
    wait_all(kept)


def reduce_scratch(n, rows, width):
    cols = width // CHUNKS
    return [
        pltpu.VMEM((CHUNKS, n * rows, cols), BF16),
        pltpu.VMEM((CHUNKS, (n + 1) * rows, cols), BF16),
    ]


def half_scratch(n, rows, width):
    half, cols = rows // 2, width // 2
    return [
        pltpu.VMEM((4, n * half, cols), BF16),
        pltpu.VMEM((4, (n + 1) * half, cols), BF16),
    ]


def mlp_in(n, attn, wo, x, gain, wga, wgb, gu, down):
    rows, width = x.shape
    span, cols = attn.shape
    kb, ff = gu.shape[1:]
    ntile = tiles(ff, 512)[0]
    outs = pl.pallas_call(
        functools.partial(mlp_in_kernel, n),
        out_shape=(
            shape((2, rows // 2, width), F32),
            shape((2, rows // 2, width), F32),
            shape((n, rows, width), BF16),
            shape((n, rows, ff), BF16),
            shape((n, rows, ff), BF16),
            shape((n, rows, ff), BF16),
            shape((8, kb, ff), BF16),
            shape((8,) + down.shape, BF16),
        ),
        in_specs=[VM, HB, VM, VM, HB, HB, HB, HB],
        out_specs=(HB,) * 8,
        scratch_shapes=[
            pltpu.VMEM((cols, width), BF16),
            pltpu.VMEM((2, 8, kb, ff), BF16),
            pltpu.VMEM((n, rows, width), BF16),
            pltpu.VMEM((2, rows // 2, width), F32),
            pltpu.VMEM((2, rows // 2, width), F32),
            pltpu.VMEM((n, rows, ff), BF16),
            pltpu.VMEM((n, rows, ff), BF16),
            pltpu.VMEM((n, rows, ff), BF16),
        ]
        + half_scratch(n, rows, width)
        + [
            pltpu.SemaphoreType.DMA((8,)),
            pltpu.SemaphoreType.DMA((5,)),
            pltpu.SemaphoreType.DMA((3 + 3 * ntile,)),
            pltpu.SemaphoreType.DMA((2, 9)),
            pltpu.SemaphoreType.DMA((2, 9)),
        ]
        + line_sems(n, 4)
        + line_sems(n, 2),
        compiler_params=pltpu.CompilerParams(
            collective_id=4, has_side_effects=True, vmem_limit_bytes=VMEM_LIMIT
        ),
        name="mlp_in",
    )(attn.reshape(n, rows, cols), wo, x, gain, wga, wgb, gu, down)
    return outs


def mlp_out_kernel(
    n,
    hidden_ref,
    wd_ref,
    resid_ref,
    gain_ref,
    cot_ref,
    gate_hbm,
    up_hbm,
    gresid_ref,
    out_ref,
    group_out,
    dgu_out,
    dgain_ref,
    hidden_s,
    resid_s,
    dmlp_s,
    dgu_s,
    wd,
    mlp,
    group,
    gate_ref,
    up_ref,
    dgu,
    part,
    got_rows,
    sem_d,
    local_sem,
    keep_sem,
    s_send,
    s_recv,
    *sems,
):
    s, c, u = where_am_i()
    rows, width = cot_ref.shape
    load_d = load_blocks(wd_ref, wd, sem_d, 1)
    load_g = [
        pltpu.make_async_copy(gate_hbm, gate_ref, local_sem.at[0]),
        pltpu.make_async_copy(up_hbm, up_ref, local_sem.at[1]),
    ]
    greet(line_peers(n) + [(None, (1 - s, c, u))])
    sibling = Sibling(s_send, s_recv)
    halves = Halves(n, rows)
    half = rows // 2
    per_half = part.shape[0] // 2
    chunk_cols = part.shape[2]

    def compute(chunk):
        h, q = divmod(chunk, per_half)
        cols = slice(q * chunk_cols, (q + 1) * chunk_cols)
        if h == 0:
            wait_all(load_d[q * (8 // per_half) : (q + 1) * (8 // per_half)])

        def tile(index, start, size):
            part[chunk, start : start + size, :] = dot(
                halves.load(hidden_ref, index), wd[:, cols], NN
            ).astype(BF16)

        halves.each(h, tile)

    reduce = LineReduce(n, half, part, got_rows, sems[:4])
    gathers = [LineGather(n, rows, group, sems[4:], (h, half)) for h in range(2)]
    dgain_ref[...] = jnp.zeros_like(dgain_ref)

    def finish(h):
        where = slice(h * half, (h + 1) * half)
        reduce.last(mlp.at[h], range(h * per_half, (h + 1) * per_half))
        values = mlp[h]
        grad = cot_ref[where, :].astype(F32)
        d_mlp = norm_back(values, inverse_rms(values), grad * gain_ref[1:2, :], width)
        group[pl.ds(u, 1), where, :] = d_mlp.astype(BF16)[None]

    def rest(h):
        where = slice(h * half, (h + 1) * half)
        values = mlp[h]
        scaled = values * inverse_rms(values)
        out_ref[where, :] = (resid_ref[h] + scaled * gain_ref[1:2, :]).astype(BF16)
        dgain_ref[...] += jnp.sum(cot_ref[where, :].astype(F32) * scaled, axis=0, keepdims=True)

    ff = gate_ref.shape[2]
    ntile, tsize = tiles(ff, 512)
    kept = []

    def keep(src, dst):
        copy = pltpu.make_async_copy(src, dst, keep_sem.at[len(kept)])
        copy.start()
        kept.append(copy)

    def body(h, t):
        lanes = slice(t * tsize, (t + 1) * tsize)

        def tile(index, start, size):
            d_hidden = dot(halves.load(group, index), wd[lanes, :], NT)
            gate = halves.load(gate_ref, index, lanes).astype(F32)
            up = halves.load(up_ref, index, lanes).astype(F32)
            sig = jax.nn.sigmoid(gate)
            slope = sig * (1.0 + gate * (1.0 - sig))
            halves.store(dgu.at[0], index, lanes, (d_hidden * up * slope).astype(BF16))
            halves.store(dgu.at[1], index, lanes, (d_hidden * (gate * sig)).astype(BF16))

        halves.each(h, tile)
        where = pl.ds(h * half, half)
        view = dgu.at[:, :, where, lanes]
        sibling.start(view, dgu_s.at[:, :, where, lanes])
        keep(view, dgu_out.at[:, :, where, lanes])

    def hook(label):
        if label == "sent":
            sibling.start(hidden_ref, hidden_s)
            lanes = pl.ds(pl.multiple_of((1 - s) * (width // 2), width // 2), width // 2)
            sibling.start(gresid_ref.at[:, :, lanes], resid_s)
            for copy in load_g:
                copy.start()
        if label == "half":
            rest(0)
        if label == "first":
            rest(1)
            wait_all(load_g)
        if label == f"g{n - 2}":
            lanes = pl.ds(pl.multiple_of((1 - s) * (width // 2), width // 2), width // 2)
            sibling.start(group.at[:, :, lanes], dmlp_s)
            keep(group, group_out)

    reduce_norm_gather(n, reduce, gathers, compute, finish, Consume(ntile, body), hook)
    for i in range(3 + 2 * ntile):
        sibling.wait(i)
    sibling.finish()
    wait_all(kept)


def mlp_out(n, hidden, wd, resid, gain, cot, gate, up, gresid):
    rows, width = cot.shape
    ff = hidden.shape[2]
    ntile = tiles(ff, 512)[0]
    return pl.pallas_call(
        functools.partial(mlp_out_kernel, n),
        out_shape=(
            shape((rows, width), BF16),
            shape((n, rows, width), BF16),
            shape((2, n, rows, ff), BF16),
            shape((1, width), F32),
            shape((n, rows, ff), BF16),
            shape((n, rows, width // 2), BF16),
            shape((n, rows, width // 2), BF16),
            shape((2, n, rows, ff), BF16),
        ),
        in_specs=[VM, HB, VM, VM, VM, HB, HB, HB],
        out_specs=(VM, HB, HB, VM, HB, HB, HB, HB),
        scratch_shapes=[
            pltpu.VMEM((ff, width), BF16),
            pltpu.VMEM((2, rows // 2, width), F32),
            pltpu.VMEM((n, rows, width), BF16),
            pltpu.VMEM((n, rows, ff), BF16),
            pltpu.VMEM((n, rows, ff), BF16),
            pltpu.VMEM((2, n, rows, ff), BF16),
        ]
        + half_scratch(n, rows, width)
        + [
            pltpu.SemaphoreType.DMA((8,)),
            pltpu.SemaphoreType.DMA((2,)),
            pltpu.SemaphoreType.DMA((1 + 2 * ntile,)),
            pltpu.SemaphoreType.DMA((3 + 2 * ntile,)),
            pltpu.SemaphoreType.DMA((3 + 2 * ntile,)),
        ]
        + line_sems(n, 4)
        + line_sems(n, 2),
        compiler_params=pltpu.CompilerParams(
            collective_id=5, has_side_effects=True, vmem_limit_bytes=VMEM_LIMIT
        ),
        name="mlp_out",
    )(hidden, wd, resid, gain, cot, gate, up, gresid)


def mlp_back_kernel(
    n,
    dgu_hbm,
    wga_ref,
    wgb_ref,
    wgc_ref,
    cot_ref,
    branch_ref,
    gain_ref,
    wo_ref,
    hidden_hbm,
    dmlp_hbm,
    resid_hbm,
    hidden_s_hbm,
    dmlp_s_hbm,
    resid_s_hbm,
    dgu_s_hbm,
    dresid_ref,
    group_out,
    dattn_ref,
    dgain_ref,
    gown_out,
    gx_out,
    gy_out,
    down_own_out,
    down_x_out,
    down_y_out,
    wo,
    wg,
    group,
    part,
    got_rows,
    dgu_ref,
    hidden,
    hidden_s,
    dmlp,
    dmlp_s,
    gate_in,
    ring_d,
    ring_g,
    got_d,
    got_g,
    sem_o,
    sem_in,
    local_sem,
    d_send,
    d_recv,
    d_local,
    g_send,
    g_recv,
    g_local,
    *sems,
):
    s, c, u = where_am_i()
    rows, width = cot_ref.shape
    half = wga_ref.shape[1]
    chunk_cols = width // part.shape[0]
    per_chunk = chunk_cols // (2 * half)
    chunks = part.shape[0]

    def load_chunk(chunk):
        slot = chunk % 2
        where = pl.ds(chunk * per_chunk, per_chunk)
        return [
            pltpu.make_async_copy(
                wga_ref.at[where], wg.at[slot, 0, :, pl.ds(0, half)], local_sem.at[slot, 0]
            ),
            pltpu.make_async_copy(
                wgb_ref.at[where], wg.at[slot, 0, :, pl.ds(half, half)], local_sem.at[slot, 1]
            ),
            pltpu.make_async_copy(wgc_ref.at[where], wg.at[slot, 1], local_sem.at[slot, 2]),
        ]

    def start_chunk(chunk):
        for copy in load_chunk(chunk):
            copy.start()

    def fetch(k, src, dst):
        copy = pltpu.make_async_copy(src, dst, sem_in.at[k])
        copy.start()
        return copy

    load_dgu = fetch(0, dgu_hbm, dgu_ref)
    start_chunk(0)
    load_d = [
        fetch(1, hidden_hbm, hidden),
        fetch(2, half_columns(dmlp_hbm, s), dmlp),
        fetch(3, hidden_s_hbm, hidden_s),
        fetch(4, dmlp_s_hbm, dmlp_s),
    ]
    start_chunk(1)
    load_g = []
    if gate_in:
        resid, resid_s, dgu_s = gate_in
        load_g = [
            fetch(5, half_columns(resid_hbm, s), resid),
            fetch(6, resid_s_hbm, resid_s),
            fetch(7, dgu_s_hbm, dgu_s),
        ]
    load_o = load_blocks(wo_ref, wo, sem_o, 1)
    greet(line_peers(n) + plane_peers())
    load_dgu.wait()
    span = n * rows
    count, size = tiles(span, 512)

    def compute(chunk):
        wait_all(load_chunk(chunk))
        slot = chunk % 2

        def tile(i, carry):
            where = pl.ds(pl.multiple_of(i * size, size), size)
            part[chunk, where, :] = (
                dot(dgu_ref[0, where, :], wg[slot, 0].reshape(chunk_cols, -1), NT)
                + dot(dgu_ref[1, where, :], wg[slot, 1].reshape(chunk_cols, -1), NT)
            ).astype(BF16)
            return carry

        lax.fori_loop(0, count, tile, 0)
        if chunk + 2 < chunks:
            start_chunk(chunk + 2)

    rows_d, cols_g = ring_d.shape[2], ring_g.shape[3]
    tiles_g = dgu_hbm.shape[2] // cols_g

    def place_d(out, piece, part):
        size = rows_d if part is None else rows_d // 2
        return out.at[pl.ds(piece * rows_d + (part or 0) * size, size)]

    def place_g(out, piece, part):
        size = ring_g.shape[2] if part is None else ring_g.shape[2] // 2
        ci, tile = piece // tiles_g, piece % tiles_g
        return out.at[ci, pl.ds((part or 0) * size, size), pl.ds(tile * cols_g, cols_g)]

    down = PlaneReduce(
        ring_d, got_d, (down_own_out, down_x_out, down_y_out), place_d, d_send, d_recv, d_local
    )
    gate = PlaneReduce(ring_g, got_g, (gown_out, gx_out, gy_out), place_g, g_send, g_recv, g_local)
    down_piece = wide_piece(
        (hidden, dmlp), (hidden_s, dmlp_s), lambda p: slice(p * rows_d, (p + 1) * rows_d)
    )

    def gate_right(ref, piece):
        tile = piece % tiles_g
        return ref[piece // tiles_g, :, tile * cols_g : (tile + 1) * cols_g]

    n_d, n_g = got_d.shape[0], got_g.shape[0] if gate_in else 0
    work = [(down, p, down_piece) for p in range(n_d)]
    if gate_in:
        gate_piece = tall_piece((resid, dgu_ref), (resid_s, dgu_s), gate_right)
        work += [(gate, p, gate_piece) for p in range(n_g)]
    pieces = Pieces(work)

    def compute_and_piece(chunk):
        compute(chunk)
        if chunk == 0:
            wait_all(load_d)
        if chunk < 2:
            pieces.step()

    def reduce_hook(slot):
        if slot == 0:
            wait_all(load_g)
        pieces.step()

    LineReduce(n, rows, part, got_rows, sems[:4]).run(compute_and_piece, dresid_ref, reduce_hook)
    d_resid = dresid_ref[...] + cot_ref[...].astype(F32)
    dresid_ref[...] = d_resid
    branch = branch_ref[...]
    inverse = inverse_rms(branch)
    d_branch = norm_back(branch, inverse, d_resid * gain_ref[0:1, :], width)
    small = group.shape[0] == span
    if small:
        group[rows_of(u, rows), :] = d_branch.astype(BF16)
        gather = LineGather(n, rows, group, sems[4:])
    else:
        group[:rows, :] = d_branch.astype(BF16)
        own = pltpu.make_async_copy(
            group.at[pl.ds(0, rows)], group_out.at[rows_of(u, rows)], local_sem.at[2, 2]
        )
        own.start()
        own.wait()
        gather = LineGather(n, rows, group_out, sems[4:])
    gather.send(0)
    dgain_ref[...] = jnp.sum(d_resid * branch * inverse, axis=0, keepdims=True)
    wait_all(load_o)
    pieces.step()

    def gather_hook(slot):
        pieces.step()

    gather.run(gather_hook)
    if small:
        keep = pltpu.make_async_copy(group, group_out, local_sem.at[2, 2])
        keep.start()

    def tile(j, carry):
        where = pl.ds(pl.multiple_of(j * size, size), size)
        if small:
            rows_in = group[where, :]
        else:
            fetch = pltpu.make_async_copy(group_out.at[where], group, local_sem.at[2, 2])
            fetch.start()
            fetch.wait()
            rows_in = group[...]
        d_attn = dot(rows_in, wo[...], NT).astype(BF16)
        if len(dattn_ref.shape) == 3:
            cols = dattn_ref.shape[2]
            for q in range(4):
                dattn_ref[q, where, :] = d_attn[:, q * cols : (q + 1) * cols]
        else:
            dattn_ref[where, :] = d_attn
        return carry

    lax.fori_loop(0, count, tile, 0)
    pieces.finish()
    down.finish(n_d)
    gate.finish(n_g)
    if small:
        keep.wait()


def piece_scratch(slots, pieces, rows, cols):
    return (
        [pltpu.VMEM((slots, 4, rows, cols), BF16), pltpu.VMEM((pieces, rows, cols), BF16)],
        [
            pltpu.SemaphoreType.DMA((pieces, 6)),
            pltpu.SemaphoreType.DMA((pieces, 6)),
            pltpu.SemaphoreType.DMA((pieces,)),
        ],
    )


def mlp_back(
    n,
    dgu,
    wga,
    wgb,
    wgc,
    cot,
    branch,
    gain,
    wo,
    hidden,
    dmlp,
    resid,
    hidden_s,
    resid_s,
    dmlp_s,
    dgu_s,
):
    rows, width = branch.shape
    span, ff = dgu.shape[1:]
    cols = wo.shape[1]
    kb, kc = width // 8, wo.shape[2]
    count, size = tiles(ff, 512)
    ring_d, sems_d = piece_scratch(min(3, count), count, size, kc)
    here = 2 * count - LATER
    ring_g, sems_g = piece_scratch(min(3, max(here, 1)), max(here, 1), kb, size)
    chunk_blocks = width // CHUNKS // kb
    return pl.pallas_call(
        functools.partial(mlp_back_kernel, n),
        out_shape=(
            shape((rows, width), F32),
            shape((span, width), BF16),
            shape((4, span, cols // 4) if spread_heads(cols) else (span, cols), BF16),
            shape((1, width), F32),
        )
        + (shape((2, kb, ff), BF16),) * 3
        + (shape((ff, kc), BF16),) * 3,
        in_specs=[HB, HB, HB, HB, VM, VM, VM] + [HB] * 8,
        out_specs=(VM, HB, VM, VM) + (HB,) * 6,
        scratch_shapes=[
            pltpu.VMEM((cols, width), BF16),
            pltpu.VMEM((2, 2, chunk_blocks, kb, ff), BF16),
            pltpu.VMEM((min(span, 512), width), BF16),
        ]
        + reduce_scratch(n, rows, width)
        + [
            pltpu.VMEM((2, span, ff), BF16),
            pltpu.VMEM((span, ff), BF16),
            pltpu.VMEM((span, ff), BF16),
            pltpu.VMEM((span, width // 2), BF16),
            pltpu.VMEM((span, width // 2), BF16),
            (
                pltpu.VMEM((span, width // 2), BF16),
                pltpu.VMEM((span, width // 2), BF16),
                pltpu.VMEM((2, span, ff), BF16),
            )
            if here > 0
            else (),
            ring_d[0],
            ring_g[0],
            ring_d[1],
            ring_g[1],
            pltpu.SemaphoreType.DMA((8,)),
            pltpu.SemaphoreType.DMA((8,)),
            pltpu.SemaphoreType.DMA((3, 3)),
        ]
        + sems_d
        + sems_g
        + line_sems(n, CHUNKS)
        + line_sems(n),
        compiler_params=pltpu.CompilerParams(
            collective_id=6, has_side_effects=True, vmem_limit_bytes=VMEM_LIMIT
        ),
        name="mlp_back",
    )(
        dgu,
        wga,
        wgb,
        wgc,
        cot,
        branch,
        gain,
        wo,
        hidden,
        dmlp,
        resid,
        hidden_s,
        dmlp_s,
        resid_s,
        dgu_s,
    )


def proj_back_kernel(
    n,
    dproj_ref,
    wq_ref,
    dresid_ref,
    xg_ref,
    gcols_ref,
    gattn_ref,
    gmlp_ref,
    attn_ref,
    dbranch_ref,
    resid_hbm,
    resid_s_hbm,
    dgu_hbm,
    dgu_s_hbm,
    own_in,
    x_in,
    y_in,
    out_ref,
    gain_ref,
    own_out,
    x_out,
    y_out,
    oown_out,
    ox_out,
    oy_out,
    gown_out,
    gx_out,
    gy_out,
    wq,
    xs,
    xs_s,
    dproj_s,
    dbranch,
    dbranch_s,
    attn_s,
    total,
    part,
    got_rows,
    ring,
    got,
    sums,
    ring_o,
    got_o,
    late_buffers,
    late_sems,
    o_sems,
    local_sem,
    s_send,
    s_recv,
    q_send,
    q_recv,
    q_local,
    v_send,
    v_recv,
    m_send,
    m_recv,
    *sems,
):
    s, c, u = where_am_i()
    rows, width = dresid_ref.shape
    span = n * rows
    load = [
        pltpu.make_async_copy(wq_ref, wq, local_sem.at[0]),
        pltpu.make_async_copy(half_columns(xg_ref, s), xs, local_sem.at[1]),
        pltpu.make_async_copy(half_columns(dbranch_ref, s), dbranch, local_sem.at[2]),
    ]
    last = 2 * (dgu_hbm.shape[2] // late_buffers[2].shape[1])
    late = LatePiece(
        last - 1,
        (resid_hbm, resid_s_hbm, dgu_hbm, dgu_s_hbm),
        (gown_out, gx_out, gy_out),
        late_buffers,
        late_sems,
    )
    late.load()
    for copy in load:
        copy.start()
    corner = (s, c ^ 3, u)
    greet(all_uly_peers(n) + plane_peers() + [(None, corner), (None, (1 - s, c, u))])
    gains = GainSum(n, sums, (v_send, v_recv, m_send, m_recv))
    gains.start(gcols_ref, gattn_ref, gmlp_ref)
    sibling = Sibling(s_send, s_recv)
    sibling.start(attn_ref, attn_s)
    sibling.start(half_columns(dbranch_ref, 1 - s), dbranch_s)
    sibling.start(half_columns(xg_ref, 1 - s), xs_s)
    sibling.start(dproj_ref, dproj_s)
    load[0].wait()
    chunk_cols = width // part.shape[0]
    count, size = tiles(span, 512)

    def compute(chunk):
        cols = slice(chunk * chunk_cols, (chunk + 1) * chunk_cols)

        def tile(i, carry):
            where = pl.ds(pl.multiple_of(i * size, size), size)
            part[chunk, where, :] = (
                dot(dproj_ref[0, where, :], wq[0, cols, :], NT)
                + dot(dproj_ref[1, where, :], wq[1, cols, :], NT)
                + dot(dproj_ref[2, where, :], wq[2, cols, :], NT)
            ).astype(BF16)
            return carry

        lax.fori_loop(0, count, tile, 0)

    def place(out, piece, part):
        size = ring.shape[2] if part is None else ring.shape[2] // 2
        return out.at[piece, pl.ds((part or 0) * size, size)]

    weight = PlaneReduce(ring, got, (own_out, x_out, y_out), place, q_send, q_recv, q_local)
    compute_piece = tall_piece((xs, dproj_ref), (xs_s, dproj_s), lambda ref, piece: ref[piece])

    def place_o(out, piece, part):
        size = ring_o.shape[2] if part is None else ring_o.shape[2] // 2
        return out.at[pl.ds((part or 0) * size, size)]

    out_weight = PlaneReduce(ring_o, got_o, (oown_out, ox_out, oy_out), place_o, *o_sems)
    out_piece = wide_piece((attn_ref, dbranch), (attn_s, dbranch_s), lambda p: slice(None))
    pieces = Pieces(
        [late.work(), (out_weight, 0, out_piece)] + [(weight, p, compute_piece) for p in range(3)]
    )

    def compute_and_piece(chunk):
        compute(chunk)
        if chunk == 0:
            pieces.step()
        if chunk == 2:
            load[2].wait()
            sibling.wait(0)
            sibling.wait(1)
            pieces.step()

    def hook(slot):
        if slot == 0:
            load[1].wait()
            sibling.wait(2)
            sibling.wait(3)
            pieces.step()
            gains.over_ctx()
        if slot == 1:
            pieces.step()
            gains.over_uly()
        if slot == 2:
            pieces.step()

    LineReduce(n, rows, part, got_rows, sems[:4]).run(compute_and_piece, total, hook)
    out_ref[...] = (dresid_ref[...] + total[...]).astype(BF16)
    pieces.finish()
    gains.finish(gain_ref)
    weight.finish(3)
    out_weight.finish(1)
    late.plane.finish(1)
    sibling.finish()


class GainSum:
    def __init__(self, n, refs, sems):
        self.n = n
        self.all, self.core, self.plane, self.line = refs
        self.v_send, self.v_recv, self.m_send, self.m_recv = sems
        self.s, self.c, self.u = where_am_i()
        self.sent = []

    def copy(self, k, src, dst, peer):
        return remote(src, dst, self.v_send.at[k], self.v_recv.at[k], peer)

    def go(self, copy):
        copy.start()
        self.sent.append(copy)

    def start(self, cols, attn, mlp):
        half, local = self.all.shape[2], cols.shape[1]
        rows = jnp.zeros((8, half), F32)
        for h in range(2):
            self.all[h] = rows
        mine = self.u * local
        home = pl.ds(pl.multiple_of(lax.rem(mine, half), local), local)
        self.all[pl.ds(mine // half, 1), 0:2, home] = cols[...][None]
        for h in range(2):
            part = slice(h * half, (h + 1) * half)
            self.all[h, 2:3, :] = attn[:, part]
            self.all[h, 3:4, :] = mlp[:, part]
        self.go(self.copy(0, self.all.at[1 - self.s], self.core, (1 - self.s, self.c, self.u)))

    def over_ctx(self):
        s, c, u = self.s, self.c, self.u
        self.copy(0, self.all.at[s], self.core, (1 - s, c, u)).wait_recv()
        size = self.plane.shape[2]
        total = self.all[pl.ds(s, 1)][0] + self.core[...]
        for j in range(4):
            self.plane[j] = total[:, j * size : (j + 1) * size]
        for k in (1, 2, 3):
            self.go(self.copy(k, self.plane.at[c ^ k], self.line.at[k - 1], (s, c ^ k, u)))

    def over_uly(self):
        s, c, u = self.s, self.c, self.u
        total = self.plane[pl.ds(c, 1)][0]
        for k in (1, 2, 3):
            self.copy(k, self.plane.at[c ^ k], self.line.at[k - 1], (s, c ^ k, u)).wait_recv()
            total = total + self.line[k - 1]
        home = self.line.at[3 + u]
        self.line[pl.ds(3 + u, 1)] = total[None]
        for step in range(1, self.n):
            peer = (s, c, lax.rem(u + step, self.n))
            self.go(remote(home, home, self.m_send.at[step - 1], self.m_recv.at[step - 1], peer))

    def finish(self, out):
        s, c, u = self.s, self.c, self.u
        for step in range(1, self.n):
            source = lax.rem(u + self.n - step, self.n)
            place = self.line.at[3 + source]
            remote(
                place, place, self.m_send.at[step - 1], self.m_recv.at[step - 1], (s, c, source)
            ).wait_recv()
        total = self.line[3]
        for j in range(1, self.n):
            total = total + self.line[3 + j]
        out[...] = total[:4]
        for copy in self.sent:
            copy.wait_send()


def proj_back(
    n, dproj, wq, dresid, xg, gain_cols, gain_attn, gain_mlp, attn, dbranch, late, grads
):
    rows, width = dresid.shape
    span, cols = dproj.shape[1:]
    ring, sems = piece_scratch(3, 3, width // 8, cols)
    ring_o, sems_o = piece_scratch(1, 1, cols, width // 8)
    ff = late[2].shape[2]
    return pl.pallas_call(
        functools.partial(proj_back_kernel, n),
        out_shape=(shape((rows, width), BF16), shape((4, width // 8), F32))
        + (shape((3, width // 8, cols), BF16),) * 3
        + (shape((cols, width // 8), BF16),) * 3
        + tuple(shape(g.shape, BF16) for g in grads),
        in_specs=[VM, HB, VM, HB, VM, VM, VM, VM] + [HB] * 8,
        out_specs=(VM, VM) + (HB,) * 9,
        input_output_aliases={13: 8, 14: 9, 15: 10},
        scratch_shapes=[
            pltpu.VMEM((3, width, cols), BF16),
            pltpu.VMEM((span, width // 2), BF16),
            pltpu.VMEM((span, width // 2), BF16),
            pltpu.VMEM((3, span, cols), BF16),
            pltpu.VMEM((span, width // 2), BF16),
            pltpu.VMEM((span, width // 2), BF16),
            pltpu.VMEM((span, cols), BF16),
            pltpu.VMEM((rows, width), F32),
        ]
        + reduce_scratch(n, rows, width)
        + ring
        + [
            (
                pltpu.VMEM((2, 8, width // 2), F32),
                pltpu.VMEM((8, width // 2), F32),
                pltpu.VMEM((4, 8, width // 8), F32),
                pltpu.VMEM((3 + n, 8, width // 8), F32),
            ),
        ]
        + ring_o
        + LatePiece.scratch(span, width, ff)
        + [
            tuple(sems_o),
            pltpu.SemaphoreType.DMA((3,)),
            pltpu.SemaphoreType.DMA((4,)),
            pltpu.SemaphoreType.DMA((4,)),
        ]
        + sems
        + [
            pltpu.SemaphoreType.DMA((4,)),
            pltpu.SemaphoreType.DMA((4,)),
            pltpu.SemaphoreType.DMA((n - 1,)),
            pltpu.SemaphoreType.DMA((n - 1,)),
        ]
        + line_sems(n, CHUNKS),
        compiler_params=pltpu.CompilerParams(
            collective_id=7, has_side_effects=True, vmem_limit_bytes=VMEM_LIMIT
        ),
        name="proj_back",
    )(
        dproj,
        wq,
        dresid,
        xg,
        gain_cols,
        gain_attn,
        gain_mlp,
        attn,
        dbranch,
        *late,
        *grads,
    )


class PiecePlane(PlaneReduce):
    def __init__(self, ring, got, place, send, recv, local):
        super().__init__(ring, got, (0, 1, 2), place, send, recv, local)

    def halves(self):
        return 0, 1

    def own_copies(self, piece, blocks):
        return [
            pltpu.make_async_copy(
                blocks.at[self.c, h], self.place(0, piece, h), self.local.at[piece, h]
            )
            for h in range(2)
        ]

    def add(self, slot, block, half, piece):
        self.ring[slot, block, half] = (
            self.ring[slot, block, half].astype(F32) + self.got[piece, half].astype(F32)
        ).astype(BF16)


class Stream:
    def __init__(self, slots, sem, source, count):
        self.slots, self.sem, self.source, self.count = slots, sem, source, count
        for tile in range(slots.shape[0]):
            self.start(tile)

    def copy(self, tile):
        slot = tile % self.slots.shape[0]
        return pltpu.make_async_copy(self.source(tile), self.slots.at[slot], self.sem.at[slot])

    def start(self, tile):
        if tile < self.count:
            self.copy(tile).start()

    def wait(self, tile):
        self.copy(tile).wait()


def wide_blocks(own, other, out):
    rows = out.shape[2]

    def pair(i, carry):
        where = pl.ds(pl.multiple_of(i * 2 * rows, 2 * rows), 2 * rows)
        total = dot(own[0][...], own[1][:, where], TN) + dot(other[0][...], other[1][:, where], TN)
        total = total.astype(BF16)
        for j in range(2):
            part = total[:, j * rows : (j + 1) * rows]
            out[pl.ds(2 * i + j, 1)] = part.reshape(1, 2, rows, rows)
        return carry

    lax.fori_loop(0, 2, pair, 0)


def tall_blocks(own, other, out):
    rows = out.shape[2]

    def pair(i, carry):
        where = pl.ds(pl.multiple_of(i * 2 * rows, 2 * rows), 2 * rows)
        total = dot(own[0][:, where], own[1][...], TN) + dot(other[0][:, where], other[1][...], TN)
        total = total.astype(BF16)
        for j in range(2):
            for h in range(2):
                out[pl.ds(2 * i + j, 1), h] = total[
                    j * rows : (j + 1) * rows, h * rows : (h + 1) * rows
                ][None]
        return carry

    lax.fori_loop(0, 2, pair, 0)


def backward_kernel(n, names, *refs):
    ref = SimpleNamespace(**dict(zip(names, refs)))
    s, c, u = where_am_i()
    cot_ref, gain_ref, qk_gain_ref = ref.cot, ref.post, ref.gain
    rows, width = cot_ref.shape
    span = n * rows
    weights, dgu, dgu_s = ref.v_weights, ref.v_dgu, ref.v_dgu_s
    hidden, hidden_s, dmlp, dmlp_s = ref.v_hidden, ref.v_hidden_s, ref.v_dmlp, ref.v_dmlp_s
    resid, resid_s, branch, attn = ref.v_resid, ref.v_resid_s, ref.v_branch, ref.v_attn
    part, group, dresid = ref.v_part, ref.v_group, ref.v_dresid
    load = Keep(ref.load_sem)
    chunks, chunk_cols = part.shape[0], part.shape[2]
    kb = ref.wgc.shape[1]
    per_chunk = chunk_cols // kb
    lower, upper = kb // 2, kb // 2


    rows_g = ref.v_ring.shape[3]
    rows_d = cols_g = 2 * rows_g
    tiles_g = dgu.shape[2] // cols_g
    n_d, n_g = hidden.shape[1] // rows_d, 2 * tiles_g

    def hidden_tile(view, piece):
        return view.at[:, pl.ds(piece * rows_d, rows_d)]

    def gate_tile(view, piece):
        ci, tile = divmod(piece, tiles_g)
        return view.at[ci, :, pl.ds(tile * cols_g, cols_g)]

    def load_chunk(chunk):
        slot, copies = chunk % 2, []
        for b in range(per_chunk):
            block = chunk * per_chunk + b
            at = slot * 2 * chunk_cols + b * kb
            for k, (src, first, size) in enumerate(
                (
                    (ref.wga, at, lower),
                    (ref.wgb, at + lower, upper),
                    (ref.wgc, at + chunk_cols, kb),
                )
            ):
                copies.append(
                    pltpu.make_async_copy(
                        src.at[block],
                        weights.at[pl.ds(first, size)],
                        ref.chunk_sem.at[slot, 3 * b + k],
                    )
                )
        return copies

    def start_chunk(chunk):
        for copy in load_chunk(chunk):
            copy.start()

    load_dgu = load(ref.dgu, dgu)
    start_chunk(0)
    load_d = [
        load(ref.hidden, hidden),
        load(half_columns(ref.dmlp, s), dmlp),
        load(ref.dmlp_s, dmlp_s),
    ]
    stream_d = Stream(hidden_s, ref.hs_sem, lambda p: hidden_tile(ref.hidden_s, p), n_d)
    start_chunk(1)
    load_g = [
        load(half_columns(ref.resid, s), resid),
        load(ref.resid_s, resid_s),
        load(ref.branch, branch),
        load(ref.attn, attn),
    ]
    stream_g = Stream(dgu_s, ref.ds_sem, lambda p: gate_tile(ref.dgu_s, p), n_g)
    wo_row = 4 * chunk_cols
    wo_cols = ref.wo.shape[1]
    wo_view = weights.at[pl.ds(wo_row, wo_cols)]
    load_o = load_blocks(ref.wo, wo_view, ref.wo_sem, 1)
    peers = [(s, c ^ k, u) for k in (1, 2, 3)]
    greet(all_uly_peers(n) + [(None, peer) for peer in peers] + [(None, (1 - s, c, u))])
    sibling = Sibling(ref.s_send, ref.s_recv)
    sibling.start(half_columns(ref.xg, 1 - s), ref.v_xs_s)
    load_dgu.wait()
    count, size = tiles(span, 512)

    def compute(chunk):
        wait_all(load_chunk(chunk))
        at = (chunk % 2) * 2 * chunk_cols

        def tile(i, carry):
            where = pl.ds(pl.multiple_of(i * size, size), size)
            part[chunk, where, :] = (
                dot(dgu[0, where, :], weights[at : at + chunk_cols, :], NT)
                + dot(dgu[1, where, :], weights[at + chunk_cols : at + 2 * chunk_cols, :], NT)
            ).astype(BF16)
            return carry

        lax.fori_loop(0, count, tile, 0)
        if chunk + 2 < chunks:
            start_chunk(chunk + 2)

    def place(index, piece, half):
        if piece < n_d or piece == n_d + n_g:
            outs, first = (ref.o_down, piece * rows_d) if piece < n_d else (ref.o_out, 0)
            return outs[index].at[pl.ds(first + half * rows_g, rows_g)]
        if piece < n_d + n_g:
            ci, tile = divmod(piece - n_d, tiles_g)
            lanes = pl.ds(tile * cols_g + half * rows_g, rows_g)
            return ref.o_gate[index].at[ci, :, lanes]
        lanes = pl.ds(half * rows_g, rows_g)
        return ref.o_qkv[index].at[piece - n_d - n_g - 1, :, lanes]

    plane = PiecePlane(
        ref.v_ring, ref.v_got_p, place, ref.p_send, ref.p_recv, ref.p_local
    )
    def down_piece(out, piece):
        stream_d.wait(piece)
        own, other = hidden_tile(hidden, piece), hidden_s.at[piece % hidden_s.shape[0]]
        wide_blocks((own, dmlp), (other, dmlp_s), out)
        stream_d.start(piece + hidden_s.shape[0])

    def gate_piece(out, piece):
        number = piece - n_d
        stream_g.wait(number)
        own, other = gate_tile(dgu, number), dgu_s.at[number % dgu_s.shape[0]]
        tall_blocks((resid, own), (resid_s, other), out)
        stream_g.start(number + dgu_s.shape[0])

    def out_piece(out, piece):
        own = (attn, half_columns(group, s))
        wide_blocks(own, (ref.v_attn_s, ref.v_dbranch_s), out)

    cols = attn.shape[1]
    dproj = hidden.at[:, pl.ds(0, 3 * cols)]

    def qkv_piece(out, piece):
        lanes = pl.ds((piece - n_d - n_g - 1) * cols, cols)
        own = (dmlp, hidden.at[:, lanes])
        tall_blocks(own, (ref.v_xs_s, ref.v_dproj_s.at[:, lanes]), out)

    kinds = [down_piece] * n_d + [gate_piece] * n_g + [out_piece] + [qkv_piece] * 3
    pieces = Pieces([(plane, p, kind) for p, kind in enumerate(kinds)], AHEAD)

    def compute_and_piece(chunk):
        compute(chunk)
        if chunk == 0:
            wait_all(load_d)
        if chunk < 2:
            pieces.step()

    def reduce_hook(slot):
        if slot == 0:
            wait_all(load_g)
        pieces.step()

    sem_r = ref.r_sems
    sem_b = ref.b_sems
    LineReduce(n, rows, part, ref.v_got, sem_r).run(compute_and_piece, dresid, reduce_hook)
    d_resid = dresid[...] + cot_ref[...].astype(F32)
    dresid[...] = d_resid
    values = branch[...]
    inverse = inverse_rms(values)
    d_branch = norm_back(values, inverse, d_resid * gain_ref[0:1, :], width)
    group[rows_of(u, rows), :] = d_branch.astype(BF16)
    gather = LineGather(n, rows, group, ref.g_sems)
    gather.send(0)
    gain_attn = jnp.sum(d_resid * values * inverse, axis=0, keepdims=True)
    ref.v_gattn[...] = gain_attn
    quarter = cols // 4
    load_a = [
        load(ref.every.at[i, t], weights.at[pl.ds(0, span), pl.ds((3 * i + t) * quarter, quarter)])
        for i in range(4)
        for t in range(3)
    ]
    att, proj, tab = ref.v_att, ref.v_proj, ref.v_tab
    load_a.append(load(ref.att, att))
    load_p = [load(ref.proj, proj), load(ref.table.at[rows_of(c, span)], tab)]
    pieces.step()

    def gather_hook(slot):
        if slot == 0:
            pieces.step(2)
        if slot == 1:
            pieces.step()

    gather.run(gather_hook)
    wait_all(load_o)
    dattn, d_out = ref.v_dattn, ref.v_d_out

    def tile(j, carry):
        where = pl.ds(pl.multiple_of(j * size, size), size)
        d_attn = dot(group[where, :], weights[wo_row : wo_row + wo_cols, :], NT).astype(BF16)
        for q in range(4):
            dattn[q, where, :] = d_attn[:, q * quarter : (q + 1) * quarter]
        return carry

    lax.fori_loop(0, count, tile, 0)

    a_send, a_recv, h_send, h_recv = ref.a_send, ref.a_recv, ref.h_send, ref.h_recv
    copies = []
    for k, peer in enumerate(peers):
        copy = remote(dattn.at[peer[1]], d_out.at[c], a_send.at[k], a_recv.at[k], peer)
        copy.start()
        copies.append(copy)
    sibling.start(attn, ref.v_attn_s)
    sibling.start(half_columns(group, 1 - s), ref.v_dbranch_s)
    d_out[pl.ds(c, 1)] = dattn[pl.ds(c, 1)]
    dq, acc, delta, got = ref.v_dq, ref.v_acc, ref.v_delta, ref.v_home
    lse_ref = ref.lse
    dq[...] = jnp.zeros_like(dq)
    bound = ref.bound[:1, :1]
    scale = HEAD_DIM ** (-0.5)
    heads = quarter // HEAD_DIM
    wait_all(load_a)
    for k, peer in enumerate(peers):
        there = d_out.at[peer[1]]
        remote(there, there, a_send.at[k], a_recv.at[k], peer).wait_recv()
    pieces.step()
    for i in range(4):
        for h in range(heads):
            lanes = slice(h * HEAD_DIM, (h + 1) * HEAD_DIM)
            both = jnp.transpose(d_out[i, :, lanes].astype(F32)) * att[i, lanes, :]
            delta[i, h, :1, :] = jnp.sum(both, axis=0, keepdims=True)

    def seen(i, t, h):
        first = (3 * i + t) * quarter + h * HEAD_DIM
        return weights[:span, pl.ds(pl.multiple_of(first, HEAD_DIM), HEAD_DIM)]

    def going(j):
        first = pl.multiple_of(3 * j * quarter, 3 * quarter)
        return weights.at[pl.ds(wo_row, span), pl.ds(first, 3 * quarter)]

    def home(j):
        return remote(going(j), got.at[c], h_send.at[j], h_recv.at[c], (s, j, u))

    def step(j, carry):
        acc[...] = jnp.zeros_like(acc)
        for h in range(heads):
            lanes = slice(h * HEAD_DIM, (h + 1) * HEAD_DIM)

            def update(i, diagonal):
                starts = segment_starts(i * span, span, bound)
                keys, values = seen(j, 1, h), seen(j, 2, h)
                query, grad = seen(i, 0, h), d_out[i, :, lanes]
                scores = dot(keys, query, NT) * SCALE2
                scores = score_mask(scores, j * span, i * span, starts, diagonal)
                probs = jnp.exp2(scores - lse_ref[i, h, :1, :])
                acc[1, :, lanes] += dot(probs.astype(BF16), grad, NN)
                d_probs = dot(values, grad, NT)
                d_scores = (probs * (d_probs - delta[i, h, :1, :])).astype(BF16)
                acc[0, :, lanes] += dot(d_scores, query, NN) * scale
                dq[i, :, lanes] += dot(d_scores, keys, TN) * scale

            def after(i, carry):
                update(i, False)
                return carry

            update(j, True)
            lax.fori_loop(j + 1, 4, after, 0)
        first = pl.multiple_of(3 * j * quarter, 3 * quarter)
        weights[wo_row : wo_row + span, pl.ds(first, 3 * quarter)] = jnp.concatenate(
            [dq[j].astype(BF16), acc[0].astype(BF16), acc[1].astype(BF16)], axis=1
        )

        @pl.when(j != c)
        def _():
            home(j).start()

        return carry

    lax.fori_loop(0, 4, step, 0)
    load_q = [
        load(ref.wq.at[i], weights.at[pl.ds(0, width), pl.ds(i * cols, cols)]) for i in range(3)
    ]
    load_x = load(half_columns(ref.xg, s), dmlp)
    got[pl.ds(c, 1)] = going(c)[...][None]
    wait_all(load_p)
    for k in (1, 2, 3):
        j = c ^ k
        remote(got.at[j], got.at[j], h_send.at[c], h_recv.at[j], (s, j, u)).wait_recv()
    pieces.step()
    kept, inv_ref = (dq, ref.v_dk), ref.inv
    for j in range(4):
        hidden[:, 2 * cols + j * quarter : 2 * cols + (j + 1) * quarter] = got[
            j, :, 2 * quarter : 3 * quarter
        ]

    def source(i, h):
        group, inside = divmod(h, heads)
        first = i * quarter + inside * HEAD_DIM
        return got[group, :, first : first + HEAD_DIM].astype(F32)

    gcols = ref.v_gcols

    def store(i, h, values):
        group, inside = divmod(h, heads)
        kept[i][group, :, inside * HEAD_DIM : (inside + 1) * HEAD_DIM] = values

    dots = norms_back(source, store, proj, inv_ref, qk_gain_ref, tab, gcols)
    total = exchange_rows(n, dots, ref.v_msg, ref.m_send, ref.m_recv)
    means = to_columns(total) / width
    for i in range(2):
        inverse = inv_ref[:, i : i + 1]
        factor = inverse**3 * means[:, i : i + 1]
        for j in range(4):
            lanes = slice(j * quarter, (j + 1) * quarter)
            hidden[:, i * cols + j * quarter : i * cols + (j + 1) * quarter] = (
                inverse * kept[i][j] - proj[i, :, lanes] * factor
            ).astype(BF16)
    sibling.start(dproj, ref.v_dproj_s)
    gains = GainSum(
        n,
        ref.v_sums,
        (ref.v_send, ref.v_recv, ref.n_send, ref.n_recv),
    )
    gains.start(gcols, ref.v_gattn, ref.gmlp)
    wait_all(load_q)

    def compute_input(chunk):
        lanes = slice(chunk * chunk_cols, (chunk + 1) * chunk_cols)

        def tile(i, carry):
            where = pl.ds(pl.multiple_of(i * size, size), size)
            part[chunk, where, :] = dot(
                hidden[where, : 3 * cols], weights[lanes, : 3 * cols], NT
            ).astype(BF16)
            return carry

        lax.fori_loop(0, count, tile, 0)
        if chunk == 0:
            pieces.step()
        if chunk == 2:
            sibling.wait(1)
            sibling.wait(2)
            pieces.step()

    def input_hook(slot):
        if slot == 0:
            load_x.wait()
            sibling.wait(0)
            sibling.wait(3)
            gains.over_ctx()
        if slot == 1:
            gains.over_uly()
        pieces.step()

    LineReduce(n, rows, part, ref.v_got, sem_b).run(compute_input, branch, input_hook)
    ref.o_input[...] = (dresid[...] + branch[...]).astype(BF16)
    pieces.finish()
    gains.finish(ref.o_gain)
    plane.finish(len(kinds))
    sibling.finish()
    for j in range(4):

        @pl.when(j != c)
        def _():
            home(j).wait_send()

    for copy in copies:
        copy.wait_send()


def backward(n, ins):
    given = SimpleNamespace(**ins)
    rows, width = given.cot[0].shape
    span, ff = n * rows, given.hidden[0].shape[1]
    cols = given.attn[0].shape[1]
    quarter = cols // 4
    kb, kc = width // 8, given.wo[0].shape[2]
    n_d, size = tiles(ff, 512)
    dma = pltpu.SemaphoreType.DMA
    outs = dict(
        o_input=shape((rows, width), BF16),
        o_gain=shape((4, width // 8), F32),
        o_down=(shape((ff, kc), BF16),) * 3,
        o_gate=(shape((2, kb, ff), BF16),) * 3,
        o_out=(shape((cols, kc), BF16),) * 3,
        o_qkv=(shape((3, kb, cols), BF16),) * 3,
    )
    buffers = dict(
        v_weights=((width + cols, width), BF16),
        v_dgu=((2, span, ff), BF16),
        v_dgu_s=((3, span, size), BF16),
        v_hidden=((span, ff), BF16),
        v_hidden_s=((2, span, size), BF16),
        v_dmlp=((span, width // 2), BF16),
        v_dmlp_s=((span, width // 2), BF16),
        v_resid=((span, width // 2), BF16),
        v_resid_s=((span, width // 2), BF16),
        v_branch=((rows, width), F32),
        v_attn=((span, cols), BF16),
        v_dresid=((rows, width), F32),
        v_group=((span, width), BF16),
        v_part=((CHUNKS, span, width // CHUNKS), BF16),
        v_got=((CHUNKS, span + rows, width // CHUNKS), BF16),
        v_ring=((AHEAD + 1, 4, 2, kb, kb), BF16),
        v_got_p=((3 * n_d + 4, 2, kb, kb), BF16),
        v_gattn=((1, width), F32),
        v_att=((4, quarter, span), F32),
        v_proj=((2, span, cols), F32),
        v_tab=((span, 128), F32),
        v_dattn=((4, span, quarter), BF16),
        v_d_out=((4, span, quarter), BF16),
        v_dq=((4, span, quarter), F32),
        v_acc=((2, span, quarter), F32),
        v_delta=((4, quarter // HEAD_DIM, 8, span), F32),
        v_home=((4, span, 3 * quarter), BF16),
        v_dk=((4, span, quarter), F32),
        v_gcols=((2, cols), F32),
        v_msg=((n, 8, span), F32),
        v_xs_s=((span, width // 2), BF16),
        v_attn_s=((span, cols), BF16),
        v_dbranch_s=((span, width // 2), BF16),
        v_dproj_s=((span, 3 * cols), BF16),
    )
    sums = tuple(pltpu.VMEM(dims, F32) for dims in (((2, 8, width // 2), F32)[0], ((8, width // 2), F32)[0], ((4, 8, width // 8), F32)[0], ((3 + n, 8, width // 8), F32)[0]))
    sems = dict(
        load_sem=(32,),
        chunk_sem=(2, 3 * (width // CHUNKS // kb)),
        wo_sem=(8,),
        hs_sem=(2,),
        ds_sem=(3,),
        p_send=(3 * n_d + 4, 6),
        p_recv=(3 * n_d + 4, 6),
        p_local=(3 * n_d + 4, 2),
        a_send=(3,),
        a_recv=(3,),
    )
    four, line = (4,), (n - 1,)
    sems.update(s_send=four, s_recv=four, h_send=four, h_recv=four, v_send=four, v_recv=four)
    sems.update(m_send=line, m_recv=line, n_send=line, n_recv=line)
    fours = dict(r_sems=(n - 1, CHUNKS), b_sems=(n - 1, CHUNKS), g_sems=line)
    tuples = dict(v_sums=sums, **{name: (dma(dims),) * 4 for name, dims in fours.items()})
    names = [*ins, *outs, *buffers, *sems, *tuples]
    results = pl.pallas_call(
        functools.partial(backward_kernel, n, names),
        out_shape=list(outs.values()),
        in_specs=[spec for value, spec in ins.values()],
        out_specs=[VM, VM] + [(HB,) * 3] * 4,
        scratch_shapes=[pltpu.VMEM(*buffer) for buffer in buffers.values()]
        + [dma(dims) for dims in sems.values()]
        + list(tuples.values()),
        compiler_params=pltpu.CompilerParams(
            collective_id=11, has_side_effects=True, vmem_limit_bytes=63 * 1024 * 1024
        ),
        name="backward",
    )(*[value for value, spec in ins.values()])
    return SimpleNamespace(**dict(zip(outs, results)))


def rope_table(length):
    freqs = np.power(
        np.float32(ROPE_BASE), -(np.arange(HALF, dtype=np.float32) * 2.0 / HEAD_DIM)
    ).astype(np.float32)
    angles = (np.arange(length, dtype=np.float32)[:, None] * freqs[None, :]).astype(np.float64)
    return np.concatenate([np.cos(angles), np.sin(angles)], axis=1).astype(np.float32)


def on_device(
    n,
    table,
    tokens,
    segment_ids,
    qkv_weight,
    out_weight,
    gate_up,
    down_weight,
    qk_gain,
    post_gain,
    cotangent,
):
    x = tokens[0]
    width = x.shape[1]
    cot = cotangent[0]
    table = jnp.asarray(table)
    if spread_heads(qkv_weight.shape[2]):
        o = forward(
            n,
            x,
            qkv_weight,
            table,
            qk_gain,
            segment_ids,
            out_weight,
            gate_up,
            down_weight,
            post_gain,
        )
        group_x, wq, wo, proj, inv = o.o_xg, o.o_wq, o.o_wo, o.o_proj, o.o_inv
        wga, wgb, wgc, wd = o.o_wga, o.o_wgb, o.o_wgc, o.o_wd
        att, lse, bound, attn = o.o_att, o.o_lse, o.o_bound, o.o_attn
        branch, resid, group_resid = o.o_branch, o.o_resid, o.o_group
        gate, up, hidden = o.o_gate, o.o_up, o.o_hidden
        attn = attn.reshape(group_x.shape[0], -1)
        seen = (o.o_every,)
    else:
        group_x, wq, wo, wga, proj, qkv, inv, zero = project(
            n, x, qkv_weight, table, qk_gain, segment_ids, out_weight, gate_up
        )
        every, wgb, attn, att, lse, bound = attend(*qkv, zero, gate_up)
        seen, back = (qkv[0], every), attend_back
        branch, resid, group_resid, gate, up, hidden, wgc, wd = mlp_in(
            n, attn, wo, x, post_gain, wga, wgb, gate_up, down_weight
        )
    block_out, group_dmlp, dgu, gain_mlp, hidden_s, resid_s, dmlp_s, dgu_s = mlp_out(
        n, hidden, wd, resid, post_gain, cot, gate, up, group_resid
    )
    span, ff = n * x.shape[0], hidden.shape[2]
    branch = branch.reshape(x.shape)
    dgu, dgu_s = dgu.reshape(2, span, ff), dgu_s.reshape(2, span, ff)
    hidden, hidden_s = hidden.reshape(span, ff), hidden_s.reshape(span, ff)
    group_resid, group_dmlp = group_resid.reshape(span, width), group_dmlp.reshape(span, width)
    resid_s, dmlp_s = resid_s.reshape(span, width // 2), dmlp_s.reshape(span, width // 2)
    if spread_heads(qkv_weight.shape[2]):
        o = backward(
            n,
            dict(
                dgu=(dgu, HB),
                dgu_s=(dgu_s, HB),
                wga=(wga, HB),
                wgb=(wgb, HB),
                wgc=(wgc, HB),
                cot=(cot, VM),
                branch=(branch, HB),
                post=(post_gain, VM),
                gain=(qk_gain, VM),
                wo=(wo, HB),
                hidden=(hidden, HB),
                hidden_s=(hidden_s, HB),
                dmlp=(group_dmlp, HB),
                dmlp_s=(dmlp_s, HB),
                resid=(group_resid, HB),
                resid_s=(resid_s, HB),
                every=(seen[0], HB),
                att=(att, HB),
                lse=(lse, VM),
                bound=(bound, VM),
                attn=(attn, HB),
                proj=(proj, HB),
                inv=(inv, VM),
                table=(table, HB),
                wq=(wq, HB),
                xg=(group_x, HB),
                gmlp=(gain_mlp, VM),
            ),
        )
        input_grad, gain_part = o.o_input, o.o_gain
        qkv_grads, out_grads, gate_grads, down_grads = o.o_qkv, o.o_out, o.o_gate, o.o_down
    else:
        d_resid, group_dbranch, d_attn, gain_attn, *grads = mlp_back(
            n,
            dgu,
            wga,
            wgb,
            wgc,
            cot,
            branch,
            post_gain,
            wo,
            hidden,
            group_dmlp,
            group_resid,
            hidden_s,
            resid_s,
            dmlp_s,
            dgu_s,
        )
        gate_grads, down_grads = grads[:3], grads[3:]
        late = (group_resid, resid_s, dgu, dgu_s)
        d_proj, gain_cols, *gate_grads = back(
            n, *seen, d_attn, att, lse, bound, proj, inv, qk_gain, table, late, gate_grads
        )
        input_grad, gain_part, *grads = proj_back(
            n,
            d_proj,
            wq,
            d_resid,
            group_x,
            gain_cols,
            gain_attn,
            gain_mlp,
            attn,
            group_dbranch,
            late,
            gate_grads,
        )
        qkv_grads, out_grads, gate_grads = grads[:3], grads[3:6], grads[6:]

    def total(parts):
        return parts[0].astype(F32) + parts[1].astype(F32) + parts[2].astype(F32)

    return (
        block_out[None],
        input_grad[None],
        total(qkv_grads),
        total(out_grads),
        total(gate_grads),
        total(down_grads),
        gain_part,
    )


def solution(mesh):
    n = mesh.shape["uly"]
    in_specs = (
        P("slot", ("ctx", "uly"), None),
        P("slot", ("ctx", "uly")),
        P(None, ("slot", "ctx"), "uly"),
        P("uly", ("slot", "ctx")),
        P(None, ("slot", "ctx"), "uly"),
        P("uly", ("slot", "ctx")),
        P(None, "uly"),
        P(),
        P("slot", ("ctx", "uly"), None),
    )
    out_specs = (
        P("slot", ("ctx", "uly"), None),
        P("slot", ("ctx", "uly"), None),
        P(None, ("slot", "ctx"), "uly"),
        P("uly", ("slot", "ctx")),
        P(None, ("slot", "ctx"), "uly"),
        P("uly", ("slot", "ctx")),
        P(None, ("slot", "ctx")),
    )

    def whole(tokens, *rest):
        table = rope_table(tokens.shape[1])
        return jax.shard_map(
            functools.partial(on_device, n, table),
            mesh=mesh,
            in_specs=in_specs,
            out_specs=out_specs,
            check_vma=False,
        )(tokens, *rest)

    return whole
```

```python
import functools
from types import SimpleNamespace

import jax
import jax.numpy as jnp
import numpy as np
from jax import lax
from jax.experimental import pallas as pl
from jax.experimental.pallas import tpu as pltpu
from jax.sharding import PartitionSpec as P

HEAD_DIM = 128
HALF = HEAD_DIM // 2
EPS = 1e-06
ROPE_BASE = 500000.0
FLOOR = -1e30
LOG2E = 1.4426950408889634
SCALE2 = HEAD_DIM ** (-0.5) * LOG2E
MESH_ID = pl.DeviceIdType.MESH
BF16 = jnp.bfloat16
F32 = jnp.float32
VMEM_LIMIT = 62 * 1024 * 1024
CHUNKS = 4
AHEAD = 1
LATER = 2

VM = pl.BlockSpec(memory_space=pltpu.VMEM)
HB = pl.BlockSpec(memory_space=pl.ANY)


def shape(dims, dtype):
    return jax.ShapeDtypeStruct(dims, dtype)


def where_am_i():
    return lax.axis_index("slot"), lax.axis_index("ctx"), lax.axis_index("uly")


def rows_of(index, rows):
    return pl.ds(pl.multiple_of(index * rows, rows), rows)


def greet(peers):
    barrier = pltpu.get_barrier_semaphore()
    total = 0
    for condition, peer in peers:
        if condition is None:
            pl.semaphore_signal(barrier, inc=1, device_id=peer, device_id_type=MESH_ID)
            total = total + 1
        else:

            @pl.when(condition)
            def _():
                pl.semaphore_signal(barrier, inc=1, device_id=peer, device_id_type=MESH_ID)

            total = total + condition.astype(jnp.int32)
    pl.semaphore_wait(barrier, total)


def line_peers(n):
    s, c, u = where_am_i()
    return [(u > 0, (s, c, u - 1)), (u < n - 1, (s, c, u + 1))]


def plane_peers():
    s, c, u = where_am_i()
    return [(None, (s, c ^ 1, u)), (None, (s, c ^ 2, u))]


def remote(src, dst, send, recv, peer):
    return pltpu.make_async_remote_copy(
        src_ref=src,
        dst_ref=dst,
        send_sem=send,
        recv_sem=recv,
        device_id=peer,
        device_id_type=MESH_ID,
    )


def line_sems(n, chunks=None):
    dims = (n - 1,) if chunks is None else (n - 1, chunks)
    return [pltpu.SemaphoreType.DMA(dims)] * 4


class LineGather:
    def __init__(self, n, rows, buf, sems, part=None):
        self.n, self.rows, self.buf, self.sems, self.part = n, rows, buf, sems, part

    def copy(self, right, slot, shard):
        s, c, u = where_am_i()
        send_r, recv_r, send_l, recv_l = self.sems
        if self.part is None:
            view = self.buf.at[rows_of(shard, self.rows)]
        else:
            index, size = self.part
            view = self.buf.at[shard, pl.ds(index * size, size)]
            send_r, recv_r, send_l, recv_l = [sem.at[:, index] for sem in self.sems]
        if right:
            return remote(view, view, send_r.at[slot], recv_r.at[slot], (s, c, u + 1))
        return remote(view, view, send_l.at[slot], recv_l.at[slot], (s, c, u - 1))

    def send(self, slot):
        u, n = lax.axis_index("uly"), self.n

        @pl.when((u < n - 1) & (u - slot >= 0))
        def _():
            self.copy(True, slot, u - slot).start()

        @pl.when((u > 0) & (u + slot <= n - 1))
        def _():
            self.copy(False, slot, u + slot).start()

    def wait(self, slot):
        u, n = lax.axis_index("uly"), self.n

        @pl.when(u - 1 - slot >= 0)
        def _():
            self.copy(True, slot, u - 1 - slot).wait_recv()

        @pl.when(u + 1 + slot <= n - 1)
        def _():
            self.copy(False, slot, u + 1 + slot).wait_recv()

        if slot + 1 < n - 1:
            self.send(slot + 1)

    def finish(self):
        u, n = lax.axis_index("uly"), self.n
        for slot in range(n - 1):

            @pl.when((u < n - 1) & (u - slot >= 0))
            def _():
                self.copy(True, slot, u - slot).wait_send()

            @pl.when((u > 0) & (u + slot <= n - 1))
            def _():
                self.copy(False, slot, u + slot).wait_send()

    def run(self, hook=None):
        for slot in range(self.n - 1):
            self.wait(slot)
            if hook is not None:
                hook(slot)
        self.finish()


class LineReduce:
    def __init__(self, n, rows, part, got, sems):
        self.n, self.rows, self.sems = n, rows, sems
        self.part, self.got = part, got
        self.chunks = part.shape[0]

    def copy(self, right, slot, chunk, block):
        s, c, u = where_am_i()
        send_r, recv_r, send_l, recv_l = self.sems
        where = rows_of(block, self.rows)
        src = self.part.at[chunk, where]
        if right:
            return remote(
                src,
                self.got.at[chunk, rows_of(block + 1, self.rows)],
                send_r.at[slot, chunk],
                recv_r.at[slot, chunk],
                (s, c, u + 1),
            )
        return remote(
            src,
            self.got.at[chunk, where],
            send_l.at[slot, chunk],
            recv_l.at[slot, chunk],
            (s, c, u - 1),
        )

    def add(self, chunk, block, place):
        where = rows_of(block, self.rows)
        self.part[chunk, where, :] = (
            self.part[chunk, where, :].astype(F32)
            + self.got[chunk, rows_of(place, self.rows), :].astype(F32)
        ).astype(BF16)

    def step(self, slot, chunk):
        u, n = lax.axis_index("uly"), self.n
        block_r = n - 1 - slot + u
        block_l = slot - (n - 1) + u

        @pl.when(u <= slot)
        def _():
            if slot > 0:

                @pl.when(u > 0)
                def _():
                    self.copy(True, slot - 1, chunk, block_r).wait_recv()
                    self.add(chunk, block_r, block_r + 1)

            self.copy(True, slot, chunk, block_r).start()

        @pl.when(u >= n - 1 - slot)
        def _():
            if slot > 0:

                @pl.when(u < n - 1)
                def _():
                    self.copy(False, slot - 1, chunk, block_l).wait_recv()
                    self.add(chunk, block_l, block_l)

            self.copy(False, slot, chunk, block_l).start()

    def last(self, out, chunks=None):
        u, n = lax.axis_index("uly"), self.n
        where = rows_of(u, self.rows)
        width = self.part.shape[2]
        chunks = range(self.chunks) if chunks is None else chunks
        for number, chunk in enumerate(chunks):
            cols = slice(number * width, (number + 1) * width)
            out[:, cols] = self.part[chunk, where, :].astype(F32)

            @pl.when(u > 0)
            def _():
                self.copy(True, n - 2, chunk, u).wait_recv()
                out[:, cols] += self.got[chunk, rows_of(u + 1, self.rows), :].astype(F32)

            @pl.when(u < n - 1)
            def _():
                self.copy(False, n - 2, chunk, u).wait_recv()
                out[:, cols] += self.got[chunk, where, :].astype(F32)

    def finish(self):
        u, n = lax.axis_index("uly"), self.n
        for slot in range(n - 1):
            for chunk in range(self.chunks):

                @pl.when(u <= slot)
                def _():
                    self.copy(True, slot, chunk, n - 1 - slot + u).wait_send()

                @pl.when(u >= n - 1 - slot)
                def _():
                    self.copy(False, slot, chunk, slot - (n - 1) + u).wait_send()

    def run(self, compute, out, hook=None):
        for slot in range(self.n - 1):
            for chunk in range(self.chunks):
                if slot == 0:
                    compute(chunk)
                self.step(slot, chunk)
            if hook is not None:
                hook(slot)
        self.last(out)
        self.finish()


def reduce_norm_gather(n, reduce, gathers, compute, finish, consume, hook):
    per_half = reduce.chunks // 2
    slots = n - 1
    chunks = [range(h * per_half, (h + 1) * per_half) for h in range(2)]
    for chunk in chunks[0]:
        compute(chunk)
        reduce.step(0, chunk)
    for chunk in chunks[1]:
        compute(chunk)
    hook("started")
    for slot in range(1, slots):
        for chunk in chunks[0]:
            reduce.step(slot, chunk)
    for chunk in chunks[1]:
        reduce.step(0, chunk)
    hook("sent")
    finish(0)
    gathers[0].send(0)
    hook("half")
    for slot in range(1, slots):
        for chunk in chunks[1]:
            reduce.step(slot, chunk)
        gathers[0].wait(slot - 1)
        hook(f"b{slot}")
    finish(1)
    gathers[1].send(0)
    gathers[0].wait(slots - 1)
    hook("first")
    tiles = consume.tiles
    done = 0
    for slot in range(slots):
        while done < tiles * (slot + 1) // slots:
            consume(0, done)
            done += 1
        gathers[1].wait(slot)
        hook(f"g{slot}")
    for tile in range(tiles):
        consume(1, tile)
        hook(f"t{tile}")
    reduce.finish()
    for gather in gathers:
        gather.finish()


class Halves:
    def __init__(self, n, rows):
        self.n, self.half = n, rows // 2
        self.per_tile = min(n, max(512 // self.half, 1))
        self.count = n // self.per_tile

    def each(self, half, body):
        size = self.per_tile * self.half
        for t in range(self.count):
            index = (pl.ds(t * self.per_tile, self.per_tile), pl.ds(half * self.half, self.half))
            body(index, t * size, size)

    def load(self, ref, index, lanes=slice(None)):
        value = ref[index[0], index[1], lanes]
        return value.reshape(value.shape[0] * value.shape[1], value.shape[2])

    def store(self, ref, index, lanes, value):
        ref[index[0], index[1], lanes] = value.reshape(
            self.per_tile, self.half, value.shape[1]
        )


class Consume:
    def __init__(self, tiles, body):
        self.tiles, self.body = tiles, body

    def __call__(self, half, tile):
        self.body(half, tile)


class PlaneGather:
    SEMS = 9

    def __init__(self, src, block, half_rows, send, recv, local):
        self.s, self.c, self.u = where_am_i()
        self.src, self.block, self.half_rows = src, block, half_rows
        self.send_sem, self.recv_sem = send, recv
        s, c, u = self.s, self.c, self.u
        self.xn, self.yn, self.sib = (s, c ^ 1, u), (s, c ^ 2, u), (1 - s, c, u)
        self.started = []
        self.own = pltpu.make_async_copy(src, block(s * 4 + c), local)

    def half(self, b, part):
        rows = self.half_rows
        view = self.block(b)
        where = [slice(None)] * len(view.shape)
        where[-2] = pl.ds(part * rows, rows)
        return view.at[tuple(where)]

    def copy(self, k, view, peer, src=None):
        return remote(
            view if src is None else src, view, self.send_sem.at[k], self.recv_sem.at[k], peer
        )

    def go(self, *copies):
        for copy in copies:
            copy.start()
            self.started.append(copy)

    def start(self):
        own = self.block(self.s * 4 + self.c)
        self.go(
            self.copy(0, own, self.xn, self.src),
            self.copy(1, own, self.yn, self.src),
            self.copy(2, own, self.sib, self.src),
        )
        self.own.start()

    def middle(self):
        bx, by = self.s * 4 + (self.c ^ 1), self.s * 4 + (self.c ^ 2)
        self.copy(0, self.block(bx), self.xn).wait_recv()
        self.go(
            self.copy(3, self.half(bx, 0), self.yn), self.copy(4, self.block(bx), self.sib)
        )
        self.copy(1, self.block(by), self.yn).wait_recv()
        self.go(
            self.copy(5, self.half(by, 1), self.xn), self.copy(6, self.block(by), self.sib)
        )

    def corner(self):
        bd = self.s * 4 + (self.c ^ 3)
        self.copy(3, self.half(bd, 0), self.yn).wait_recv()
        self.go(self.copy(7, self.half(bd, 0), self.sib))
        self.copy(5, self.half(bd, 1), self.xn).wait_recv()
        self.go(self.copy(8, self.half(bd, 1), self.sib))

    def arrive(self):
        far, c = (1 - self.s) * 4, self.c
        self.copy(2, self.block(far + c), self.sib).wait_recv()
        self.copy(4, self.block(far + (c ^ 1)), self.sib).wait_recv()
        self.copy(6, self.block(far + (c ^ 2)), self.sib).wait_recv()
        self.copy(7, self.half(far + (c ^ 3), 0), self.sib).wait_recv()
        self.copy(8, self.half(far + (c ^ 3), 1), self.sib).wait_recv()
        self.own.wait()

    def finish(self):
        for copy in self.started:
            copy.wait_send()


class PlaneReduce:
    SEMS = 6

    def __init__(self, ring, got, outs, place, send, recv, local):
        self.s, self.c, self.u = where_am_i()
        s, c, u = self.s, self.c, self.u
        self.xn, self.yn = (s, c ^ 1, u), (s, c ^ 2, u)
        self.ring, self.got, self.outs, self.place = ring, got, outs, place
        self.send_sem, self.recv_sem, self.local = send, recv, local
        self.slots, self.rows = ring.shape[0], ring.shape[2]
        self.open = {}

    def halves(self):
        h = self.rows // 2
        return pl.ds(0, h), pl.ds(h, h)

    def copy(self, piece, k, src, dst, peer):
        return remote(src, dst, self.send_sem.at[piece, k], self.recv_sem.at[piece, k], peer)

    def slot(self, piece):
        if piece >= self.slots:
            self.close(piece - self.slots)
        return self.ring.at[piece % self.slots]

    def close(self, piece):
        if piece in self.open:
            remotes, own = self.open.pop(piece)
            for copy in remotes:
                copy.wait_send()
            wait_all(own)

    def first(self, piece):
        c = self.c
        lo, hi = self.halves()
        blocks = self.ring.at[piece % self.slots]
        own_out, out_x, out_y = self.outs
        bx, by, bd = c ^ 1, c ^ 2, c ^ 3
        copies = [
            self.copy(piece, 0, blocks.at[bd, lo], self.got.at[piece, lo], self.xn),
            self.copy(piece, 1, blocks.at[bd, hi], self.got.at[piece, hi], self.yn),
        ]
        for copy in copies:
            copy.start()
        own = self.own_copies(piece, blocks)
        for copy in own:
            copy.start()
        self.open[piece] = (copies, own)

    def own_copies(self, piece, blocks):
        place = self.place(self.outs[0], piece, None)
        return [pltpu.make_async_copy(blocks.at[self.c], place, self.local.at[piece])]

    def add(self, slot, block, half, piece):
        h = self.rows // 2
        where = slice(half * h, (half + 1) * h)
        self.ring[slot, block, where, :] = (
            self.ring[slot, block, where, :].astype(F32) + self.got[piece, where, :].astype(F32)
        ).astype(BF16)

    def second(self, piece):
        c = self.c
        lo, hi = self.halves()
        slot = piece % self.slots
        blocks = self.ring.at[slot]
        own_out, out_x, out_y = self.outs
        bx, by, bd = c ^ 1, c ^ 2, c ^ 3
        whole = [
            self.copy(piece, 2, blocks.at[bx, lo], self.place(out_x, piece, 0), self.xn),
            self.copy(piece, 3, blocks.at[by, hi], self.place(out_y, piece, 1), self.yn),
        ]
        for copy in whole:
            copy.start()
        self.open[piece][0].extend(whole)
        self.copy(piece, 0, blocks.at[bd, lo], self.got.at[piece, lo], self.xn).wait_recv()
        self.add(slot, by, 0, piece)
        first = self.copy(piece, 4, blocks.at[by, lo], self.place(out_y, piece, 0), self.yn)
        first.start()
        self.copy(piece, 1, blocks.at[bd, hi], self.got.at[piece, hi], self.yn).wait_recv()
        self.add(slot, bx, 1, piece)
        second = self.copy(piece, 5, blocks.at[bx, hi], self.place(out_x, piece, 1), self.xn)
        second.start()
        self.open[piece][0].extend([first, second])

    def finish(self, pieces):
        own_out, out_x, out_y = self.outs
        slot = self.ring.at[0]
        lo, hi = self.halves()
        for piece in range(pieces):
            self.close(piece)
            for k, out, half, peer in (
                (2, out_x, 0, self.xn),
                (3, out_y, 1, self.yn),
                (4, out_y, 0, self.yn),
                (5, out_x, 1, self.xn),
            ):
                where = self.place(out, piece, half)
                self.copy(piece, k, where, where, peer).wait_recv()


class Pieces:
    def __init__(self, work, ahead=2):
        self.work, self.done, self.behind, self.ahead = work, 0, [], ahead

    def step(self, count=1):
        for _ in range(count):
            if self.done < len(self.work):
                plane, piece, compute = self.work[self.done]
                compute(plane.slot(piece), piece)
                plane.first(piece)
                self.behind.append((plane, piece))
                self.done += 1
                if len(self.behind) > self.ahead:
                    self.catch_up()

    def catch_up(self):
        plane, piece = self.behind.pop(0)
        plane.second(piece)

    def finish(self):
        self.step(len(self.work))
        while self.behind:
            self.catch_up()


def wide_piece(own, other, lanes):
    def compute(out, piece):
        take = lanes(piece)
        cols = out.shape[2]

        def pair(i, carry):
            where = pl.ds(pl.multiple_of(i * 2 * cols, 2 * cols), 2 * cols)
            total = dot(own[0][:, take], own[1][:, where], TN) + dot(
                other[0][:, take], other[1][:, where], TN
            )
            total = total.astype(BF16)
            out[pl.ds(2 * i, 1)] = total[:, :cols][None]
            out[pl.ds(2 * i + 1, 1)] = total[:, cols:][None]
            return carry

        lax.fori_loop(0, 2, pair, 0)

    return compute


def tall_piece(own, other, right):
    def compute(out, piece):
        rows, cols = out.shape[1:]

        def pair(i, carry):
            where = pl.ds(pl.multiple_of(i * 2 * rows, 2 * rows), 2 * rows)
            total = dot(own[0][:, where], right(own[1], piece), TN) + dot(
                other[0][:, where], right(other[1], piece), TN
            )
            out[pl.ds(2 * i, 2)] = total.astype(BF16).reshape(2, rows, cols)
            return carry

        lax.fori_loop(0, 2, pair, 0)

    return compute


class LatePiece:
    def __init__(self, number, ins, outs, scratch, sems):
        s, c, u = where_am_i()
        resid_hbm, resid_s_hbm, dgu_hbm, dgu_s_hbm = ins
        resid, resid_s, right, right_s, ring, got = scratch
        send, recv, local, load_sem = sems
        cols = right.shape[1]
        ci, tile = divmod(number, dgu_hbm.shape[2] // cols)
        lanes = pl.ds(tile * cols, cols)
        pairs = (
            (half_columns(resid_hbm, s), resid),
            (resid_s_hbm, resid_s),
            (dgu_hbm.at[ci, :, lanes], right),
            (dgu_s_hbm.at[ci, :, lanes], right_s),
        )
        self.loads = [
            pltpu.make_async_copy(src, dst, load_sem.at[k]) for k, (src, dst) in enumerate(pairs)
        ]
        size = ring.shape[2]

        def place(out, piece, part):
            rows = size if part is None else size // 2
            return out.at[ci, pl.ds((part or 0) * rows, rows), lanes]

        self.plane = PlaneReduce(ring, got, outs, place, send, recv, local)
        self.compute = tall_piece(
            (resid, right), (resid_s, right_s), lambda ref, piece: ref[...]
        )

    def load(self):
        for copy in self.loads:
            copy.start()

    def work(self):
        def compute(out, piece):
            for copy in self.loads:
                copy.wait()
            self.compute(out, piece)

        return (self.plane, 0, compute)

    @staticmethod
    def scratch(span, width, ff):
        cols = min(ff, 512)
        ring, sems = piece_scratch(1, 1, width // 8, cols)
        buffers = (
            pltpu.VMEM((span, width // 2), BF16),
            pltpu.VMEM((span, width // 2), BF16),
            pltpu.VMEM((span, cols), BF16),
            pltpu.VMEM((span, cols), BF16),
            ring[0],
            ring[1],
        )
        return [buffers, tuple(sems) + (pltpu.SemaphoreType.DMA((4,)),)]


def half_columns(ref, s):
    half = ref.shape[1] // 2
    return ref.at[:, pl.ds(pl.multiple_of(s * half, half), half)]


class Sibling:
    def __init__(self, send, recv):
        s, c, u = where_am_i()
        self.peer, self.send, self.recv = (1 - s, c, u), send, recv
        self.copies = []

    def start(self, src, dst):
        k = len(self.copies)
        copy = remote(src, dst, self.send.at[k], self.recv.at[k], self.peer)
        copy.start()
        self.copies.append(copy)

    def wait(self, k):
        self.copies[k].wait_recv()

    def finish(self):
        for copy in self.copies:
            copy.wait_send()


def dot(a, b, dims):
    return lax.dot_general(a, b, ((dims[:1], dims[1:]), ((), ())), preferred_element_type=F32)


NN, NT, TN = (1, 0), (1, 1), (0, 0)


def tiles(total, size):
    size = min(total, size)
    return total // size, size


def inverse_rms(values):
    return lax.rsqrt(jnp.mean(values * values, axis=-1, keepdims=True) + EPS)


def norm_back(values, inverse, grad_scaled, width):
    return inverse * grad_scaled - values * inverse**3 * (
        jnp.sum(values * grad_scaled, axis=-1, keepdims=True) / width
    )


def rope_factors(table):
    lane = lax.broadcasted_iota(jnp.int32, table.shape, 1)
    turned = pltpu.roll(table, HALF, 1)
    cosine = jnp.where(lane < HALF, table, turned)
    sine = jnp.where(lane < HALF, -turned, table)
    return cosine, sine


def exchange_rows(n, mine, msg, send, recv):
    s, c, u = where_am_i()
    msg[pl.ds(u, 1)] = mine[None]
    copies = []
    for step in range(1, n):
        peer = lax.rem(u + step, n)
        copy = remote(msg.at[u], msg.at[u], send.at[step - 1], recv.at[step - 1], (s, c, peer))
        copy.start()
        copies.append(copy)
    for step in range(1, n):
        source = lax.rem(u + n - step, n)
        remote(
            msg.at[source], msg.at[source], send.at[step - 1], recv.at[step - 1], (s, c, source)
        ).wait_recv()
    total = msg[0]
    for j in range(1, n):
        total = total + msg[j]
    for copy in copies:
        copy.wait_send()
    return total


def to_rows(col0, col1):
    span = col0.shape[0]
    lane = lax.broadcasted_iota(jnp.int32, (span, 128), 1)
    both = jnp.where(lane == 0, col0, jnp.where(lane == 1, col1, 0.0))
    return jnp.transpose(both)[:8]


def to_columns(rows8):
    return jnp.transpose(jnp.concatenate([rows8] * 16, axis=0))


def all_uly_peers(n):
    s, c, u = where_am_i()
    return [(None, (s, c, lax.rem(u + k, n))) for k in range(1, n)]


def spread_heads(cols):
    return cols % (4 * HEAD_DIM) == 0


def proj_kernel(
    n,
    x_ref,
    w_ref,
    tab_ref,
    gain_ref,
    seg_ref,
    wo_ref,
    gu_ref,
    xg_out,
    wq_out,
    wo_out,
    wga_out,
    proj_ref,
    qkv_refs,
    inv_ref,
    zero_ref,
    xg,
    wq,
    tab,
    msg,
    local_sem,
    w_send,
    w_recv,
    m_send,
    m_recv,
    *line,
):
    s, c, u = where_am_i()
    rows, width = x_ref.shape
    span = n * rows
    kb = w_ref.shape[1]
    sib = (1 - s, c, u)
    tab_copy = pltpu.make_async_copy(tab_ref.at[rows_of(c, span)], tab, local_sem.at[0])
    tab_copy.start()
    xg[rows_of(u, rows), :] = x_ref[...]
    greet(all_uly_peers(n) + plane_peers() + [(None, sib)])

    def plane(k, src, block, half_rows):
        return PlaneGather(
            src, block, half_rows, w_send.at[k], w_recv.at[k], local_sem.at[3 + k]
        )

    half = kb // 2
    gather = LineGather(n, rows, xg, line)
    first = plane(0, w_ref, lambda b: wq.at[:, rows_of(b, kb)], half)
    second = plane(1, wo_ref, lambda b: wo_out.at[b], wo_ref.shape[0] // 2)
    third = plane(2, gu_ref.at[0, pl.ds(0, half)], lambda b: wga_out.at[b], half // 2)
    gather.send(0)
    first.start()
    gather.wait(0)
    first.middle()
    second.start()
    if n > 2:
        gather.wait(1)
    first.corner()
    second.middle()
    third.start()
    for slot in range(2 if n > 2 else 1, n - 1):
        gather.wait(slot)
    first.arrive()
    tab_copy.wait()
    keep = [
        pltpu.make_async_copy(xg, xg_out, local_sem.at[1]),
        pltpu.make_async_copy(wq, wq_out, local_sem.at[2]),
    ]
    for copy in keep:
        copy.start()

    count, size = tiles(span, 512)

    def store(i, where, first, values):
        if len(qkv_refs) == 1:
            (ref,) = qkv_refs
            size = ref.shape[3]
            for at in range(0, values.shape[1], min(size, values.shape[1])):
                group, inside = divmod(first + at, size)
                part = values[:, at : at + size]
                ref[group, i, where, inside : inside + part.shape[1]] = part
        else:
            ref = qkv_refs[0] if i == 0 else qkv_refs[1].at[i - 1]
            ref[where, first : first + values.shape[1]] = values

    def project(i, carry):
        where = pl.ds(pl.multiple_of(i * size, size), size)
        xs = xg[where, :]
        proj_ref[0, where, :] = dot(xs, wq[0], NN)
        proj_ref[1, where, :] = dot(xs, wq[1], NN)
        store(2, where, 0, dot(xs, wq[2], NN).astype(BF16))
        return carry

    lax.fori_loop(0, count, project, 0)
    squares = [jnp.sum(proj_ref[i] * proj_ref[i], axis=-1, keepdims=True) for i in range(2)]
    mine = to_rows(*squares)
    zeros = jnp.sum((1 - seg_ref[...]).astype(F32))
    row = lax.broadcasted_iota(jnp.int32, mine.shape, 0)
    mine = jnp.where(row == 2, zeros, mine)
    second.corner()
    third.middle()
    total = exchange_rows(n, mine, msg, m_send, m_recv)
    zero_ref[...] = jnp.broadcast_to(total[2:3, :128], (8, 128))
    inv = lax.rsqrt(to_columns(total) / width + EPS)
    inv_ref[...] = inv
    cosine, sine = rope_factors(tab[...])
    heads = proj_ref.shape[2] // HEAD_DIM
    for i in range(2):
        inverse = inv_ref[:, i : i + 1]
        for h in range(heads):
            cols = slice(h * HEAD_DIM, (h + 1) * HEAD_DIM)
            v = proj_ref[i, :, cols] * inverse * gain_ref[i : i + 1, cols]
            v = (v * cosine + pltpu.roll(v, HALF, 1) * sine).astype(BF16)
            store(i, slice(None), h * HEAD_DIM, v)
    second.arrive()
    third.corner()
    third.arrive()
    for work in (first, second, third, gather):
        work.finish()
    for copy in keep:
        copy.wait()


def project(n, x, w, table, gain, seg, wo, gu):
    rows, width = x.shape
    span, cols = n * rows, w.shape[2]
    if spread_heads(cols):
        qkv = (shape((4, 3, span, cols // 4), BF16),)
    else:
        qkv = (shape((span, cols), BF16), shape((2, span, cols), BF16))
    return pl.pallas_call(
        functools.partial(proj_kernel, n),
        out_shape=(
            shape((span, width), BF16),
            shape((3, width, cols), BF16),
            shape((8,) + wo.shape, BF16),
            shape((8, gu.shape[1] // 2, gu.shape[2]), BF16),
            shape((2, span, cols), F32),
            qkv,
            shape((span, 128), F32),
            shape((8, 128), F32),
        ),
        in_specs=[VM, HB, HB, VM, VM, HB, HB],
        out_specs=(HB, HB, HB, HB, VM, (VM,) * len(qkv), VM, VM),
        scratch_shapes=[
            pltpu.VMEM((span, width), BF16),
            pltpu.VMEM((3, width, cols), BF16),
            pltpu.VMEM((span, 128), F32),
            pltpu.VMEM((n, 8, span), F32),
            pltpu.SemaphoreType.DMA((6,)),
            pltpu.SemaphoreType.DMA((3, 9)),
            pltpu.SemaphoreType.DMA((3, 9)),
            pltpu.SemaphoreType.DMA((n - 1,)),
            pltpu.SemaphoreType.DMA((n - 1,)),
        ]
        + line_sems(n),
        compiler_params=pltpu.CompilerParams(
            collective_id=1, has_side_effects=True, vmem_limit_bytes=VMEM_LIMIT
        ),
        name="project",
    )(x, w, table, gain, seg, wo, gu)


def score_mask(scores, key_first, query_first, starts, diagonal):
    key_pos = key_first + lax.broadcasted_iota(jnp.int32, scores.shape, 0)
    keep = key_pos >= starts
    if diagonal:
        query_pos = query_first + lax.broadcasted_iota(jnp.int32, scores.shape, 1)
        keep = keep & (key_pos <= query_pos)
    return jnp.where(keep, scores, FLOOR)


def segment_starts(first, size, bound):
    pos = first + lax.broadcasted_iota(jnp.int32, (1, size), 1)
    return jnp.where(pos >= bound, bound, 0)


def attend_kernel(
    q_ref,
    kv_ref,
    zero_ref,
    gu_ref,
    kvall_out,
    wgb_out,
    attn_ref,
    attn32_ref,
    lse_ref,
    bound_ref,
    kvall,
    peaks,
    sums,
    acct,
    zmsg,
    send,
    recv,
    z_send,
    z_recv,
    w_send,
    w_recv,
    keep_sem,
    w_local,
):
    s, c, u = where_am_i()
    span, cols = q_ref.shape
    heads = cols // HEAD_DIM
    xn, yn, dn = (s, c ^ 1, u), (s, c ^ 2, u), (s, c ^ 3, u)
    kvall[pl.ds(c, 1)] = kv_ref[...][None]
    zmsg[pl.ds(c, 1)] = zero_ref[...][None]
    greet(plane_peers() + [(None, dn), (None, (1 - s, c, u))])
    weight = upper_gate(gu_ref, wgb_out, w_send, w_recv, w_local)

    def sent(k, view, peer):
        return remote(view, view, send.at[k], recv.at[k], peer)

    bx, by, bd = c ^ 1, c ^ 2, c ^ 3
    zs = [
        remote(zmsg.at[c], zmsg.at[c], z_send.at[k], z_recv.at[k], peer)
        for k, peer in enumerate((xn, yn, dn))
    ]
    for copy in zs:
        copy.start()
    copies = [sent(0, kvall.at[c], xn), sent(1, kvall.at[c], yn)]
    for copy in copies:
        copy.start()
    for k, (b, peer) in enumerate(((bx, xn), (by, yn), (bd, dn))):
        remote(zmsg.at[b], zmsg.at[b], z_send.at[k], z_recv.at[k], peer).wait_recv()
    ahead = jnp.zeros((8, 128), F32)
    for j in range(4):
        ahead = ahead + jnp.where(j <= c, zmsg[j], 0.0)
    bounds = ahead.astype(jnp.int32)
    bound_ref[...] = bounds
    bound = bounds[:1, :1]

    peaks[...] = jnp.full_like(peaks, FLOOR)
    sums[...] = jnp.zeros_like(sums)
    acct[...] = jnp.zeros_like(acct)
    nq, tq = tiles(span, 512)
    nk, tk = tiles(span, 512)

    def update(number, diagonal):
        def over_queries(i, carry):
            first_q = c * span + i * tq
            starts = segment_starts(first_q, tq, bound)
            where_q = pl.ds(pl.multiple_of(i * tq, tq), tq)

            def over_keys(j, carry):
                first_k = number * span + j * tk
                where_k = pl.ds(pl.multiple_of(j * tk, tk), tk)
                for h in range(heads):
                    lanes = slice(h * HEAD_DIM, (h + 1) * HEAD_DIM)
                    scores = dot(kvall[number, 0, where_k, lanes], q_ref[where_q, lanes], NT)
                    scores = score_mask(scores * SCALE2, first_k, first_q, starts, diagonal)
                    old = peaks[h, :1, where_q]
                    new = jnp.maximum(old, jnp.max(scores, axis=0, keepdims=True))
                    factor = jnp.exp2(old - new)
                    weights = jnp.exp2(scores - new)
                    peaks[h, :1, where_q] = new
                    sums[h, :1, where_q] = sums[h, :1, where_q] * factor + jnp.sum(
                        weights, axis=0, keepdims=True
                    )
                    acct[h, :, where_q] = acct[h, :, where_q] * factor + dot(
                        kvall[number, 1, where_k, lanes], weights.astype(BF16), TN
                    )
                return carry

            return lax.fori_loop(0, nk, over_keys, carry)

        lax.fori_loop(0, nq, over_queries, 0)

    update(c, True)
    half = span // 2
    sent(0, kvall.at[bx], xn).wait_recv()
    more = [sent(2, kvall.at[bx, :, pl.ds(0, half)], yn)]
    more[0].start()
    copies += more
    sent(1, kvall.at[by], yn).wait_recv()
    more = [sent(3, kvall.at[by, :, pl.ds(half, half)], xn)]
    more[0].start()
    copies += more
    for b in (bx, by):

        @pl.when(b < c)
        def _():
            update(b, False)

    sent(2, kvall.at[bd, :, pl.ds(0, half)], yn).wait_recv()
    sent(3, kvall.at[bd, :, pl.ds(half, half)], xn).wait_recv()
    keep = pltpu.make_async_copy(kvall, kvall_out, keep_sem)
    keep.start()
    weight.start()

    @pl.when(bd < c)
    def _():
        update(bd, False)

    for h in range(heads):
        lanes = slice(h * HEAD_DIM, (h + 1) * HEAD_DIM)
        total = sums[h, :1, :]
        attention = jnp.transpose(acct[h] / total)
        attn32_ref[:, lanes] = attention
        attn_ref[:, lanes] = attention.astype(BF16)
        lse_ref[h, :1, :] = peaks[h, :1, :] + jnp.log2(total)
    for copy in copies + zs:
        copy.wait_send()
    weight.middle()
    weight.corner()
    weight.arrive()
    weight.finish()
    keep.wait()


def attend(q, kv, zero, gu):
    span, cols = q.shape
    heads = cols // HEAD_DIM
    return pl.pallas_call(
        attend_kernel,
        out_shape=(
            shape((4, 2, span, cols), BF16),
            shape((8, gu.shape[1] // 2, gu.shape[2]), BF16),
            shape((span, cols), BF16),
            shape((span, cols), F32),
            shape((heads, 8, span), F32),
            shape((8, 128), jnp.int32),
        ),
        in_specs=[VM] * 3 + [HB],
        out_specs=(HB, HB, VM, VM, VM, VM),
        scratch_shapes=[
            pltpu.VMEM((4, 2, span, cols), BF16),
            pltpu.VMEM((heads, 8, span), F32),
            pltpu.VMEM((heads, 8, span), F32),
            pltpu.VMEM((heads, HEAD_DIM, span), F32),
            pltpu.VMEM((4, 8, 128), F32),
            pltpu.SemaphoreType.DMA((4,)),
            pltpu.SemaphoreType.DMA((4,)),
            pltpu.SemaphoreType.DMA((3,)),
            pltpu.SemaphoreType.DMA((3,)),
            pltpu.SemaphoreType.DMA((9,)),
            pltpu.SemaphoreType.DMA((9,)),
            pltpu.SemaphoreType.DMA,
            pltpu.SemaphoreType.DMA,
        ],
        compiler_params=pltpu.CompilerParams(
            collective_id=2, has_side_effects=True, vmem_limit_bytes=VMEM_LIMIT
        ),
        name="attend",
    )(q, kv, zero, gu)


def upper_gate(gu_ref, out, send, recv, local):
    half = gu_ref.shape[1] // 2
    return PlaneGather(
        gu_ref.at[0, pl.ds(half, half)], lambda b: out.at[b], half // 2, send, recv, local
    )


def norms_back(source, keep, proj_ref, inv_ref, gain_ref, tab, dgain_ref):
    cosine, sine = rope_factors(tab[...])
    span, cols = proj_ref.shape[1:]
    dots = []
    for i in range(2):
        inverse = inv_ref[:, i : i + 1]
        row_dot = jnp.zeros((span, 1), F32)
        for h in range(cols // HEAD_DIM):
            lanes = slice(h * HEAD_DIM, (h + 1) * HEAD_DIM)
            v = source(i, h)
            v = v * cosine - pltpu.roll(v, HALF, 1) * sine
            values = proj_ref[i, :, lanes]
            dgain_ref[i : i + 1, lanes] = jnp.sum(v * values * inverse, axis=0, keepdims=True)
            v = v * gain_ref[i : i + 1, lanes]
            keep(i, h, v)
            row_dot = row_dot + jnp.sum(values * v, axis=-1, keepdims=True)
        dots.append(row_dot)
    return to_rows(*dots)


def attend_back_kernel(
    n,
    q_ref,
    kvall_ref,
    do_ref,
    attn32_ref,
    lse_ref,
    bound_ref,
    proj_ref,
    inv_ref,
    gain_ref,
    tab_ref,
    resid_hbm,
    resid_s_hbm,
    dgu_hbm,
    dgu_s_hbm,
    own_in,
    x_in,
    y_in,
    dproj_ref,
    dgain_ref,
    own_out,
    x_out,
    y_out,
    dq_ref,
    part,
    got,
    acc,
    delta,
    tab,
    msg,
    late_buffers,
    late_sems,
    send,
    recv,
    local_sem,
    m_send,
    m_recv,
):
    s, c, u = where_am_i()
    span, cols = q_ref.shape
    width = resid_hbm.shape[1]
    heads = cols // HEAD_DIM
    xn, yn = (s, c ^ 1, u), (s, c ^ 2, u)
    bx, by, bd = c ^ 1, c ^ 2, c ^ 3
    load = pltpu.make_async_copy(tab_ref.at[rows_of(c, span)], tab, local_sem)
    load.start()
    last = 2 * (dgu_hbm.shape[2] // late_buffers[2].shape[1])
    late = LatePiece(
        last - 2,
        (resid_hbm, resid_s_hbm, dgu_hbm, dgu_s_hbm),
        (own_out, x_out, y_out),
        late_buffers,
        late_sems,
    )
    late.load()
    pieces = Pieces([late.work()])
    greet(plane_peers() + all_uly_peers(n))
    bound = bound_ref[:1, :1]
    nq, tq = tiles(span, 512)
    nk, tk = tiles(span, 512)
    scale = HEAD_DIM ** (-0.5)
    dq_ref[...] = jnp.zeros_like(dq_ref)
    for h in range(heads):
        lanes = slice(h * HEAD_DIM, (h + 1) * HEAD_DIM)
        both = jnp.transpose(do_ref[:, lanes].astype(F32) * attn32_ref[:, lanes])
        delta[h, :1, :] = jnp.sum(both, axis=0, keepdims=True)

    def update(number, diagonal):
        acc[...] = jnp.zeros_like(acc)

        def over_queries(i, carry):
            first_q = c * span + i * tq
            starts = segment_starts(first_q, tq, bound)
            where_q = pl.ds(pl.multiple_of(i * tq, tq), tq)

            def over_keys(j, carry):
                first_k = number * span + j * tk
                where_k = pl.ds(pl.multiple_of(j * tk, tk), tk)
                for h in range(heads):
                    lanes = slice(h * HEAD_DIM, (h + 1) * HEAD_DIM)
                    keys = kvall_ref[number, 0, where_k, lanes]
                    values = kvall_ref[number, 1, where_k, lanes]
                    query, d_out = q_ref[where_q, lanes], do_ref[where_q, lanes]
                    scores = dot(keys, query, NT) * SCALE2
                    scores = score_mask(scores, first_k, first_q, starts, diagonal)
                    probs = jnp.exp2(scores - lse_ref[h, :1, where_q])
                    acc[1, where_k, lanes] += dot(probs.astype(BF16), d_out, NN)
                    d_probs = dot(values, d_out, NT)
                    d_scores = (probs * (d_probs - delta[h, :1, where_q])).astype(BF16)
                    acc[0, where_k, lanes] += dot(d_scores, query, NN) * scale
                    dq_ref[where_q, lanes] += dot(d_scores, keys, TN) * scale
                return carry

            return lax.fori_loop(0, nk, over_keys, carry)

        lax.fori_loop(0, nq, over_queries, 0)

    def work(number):
        @pl.when(number < c)
        def _():
            update(number, False)
            part[pl.ds(number, 1)] = acc[...].astype(BF16)[None]

        @pl.when(number > c)
        def _():
            part[pl.ds(number, 1)] = jnp.zeros_like(part[pl.ds(number, 1)])

    half = span // 2
    lo, hi = pl.ds(0, half), pl.ds(half, half)

    def sent(k, src, dst, peer):
        return remote(src, dst, send.at[k], recv.at[k], peer)

    pieces.step()
    work(bd)
    copies = [
        sent(0, part.at[bd, :, lo], got.at[0, :, lo], xn),
        sent(1, part.at[bd, :, hi], got.at[0, :, hi], yn),
    ]
    for copy in copies:
        copy.start()
    pieces.catch_up()
    work(bx)
    sent(1, part.at[bx, :, hi], got.at[0, :, hi], yn).wait_recv()
    part[bx, :, half:, :] = (
        part[bx, :, half:, :].astype(F32) + got[0, :, half:, :].astype(F32)
    ).astype(BF16)
    more = [sent(2, part.at[bx], got.at[1], xn)]
    more[0].start()
    copies += more
    work(by)
    sent(0, part.at[by, :, lo], got.at[0, :, lo], xn).wait_recv()
    part[by, :, :half, :] = (
        part[by, :, :half, :].astype(F32) + got[0, :, :half, :].astype(F32)
    ).astype(BF16)
    more = [sent(3, part.at[by], got.at[2], yn)]
    more[0].start()
    copies += more
    update(c, True)
    load.wait()

    cosine, sine = rope_factors(tab[...])

    def turn_back(i):
        inverse = inv_ref[:, i : i + 1]
        row_dot = jnp.zeros((span, 1), F32)
        for h in range(heads):
            lanes = slice(h * HEAD_DIM, (h + 1) * HEAD_DIM)
            source = dq_ref if i == 0 else acc.at[0]
            v = source[:, lanes]
            v = v * cosine - pltpu.roll(v, HALF, 1) * sine
            values = proj_ref[i, :, lanes]
            dgain_ref[i : i + 1, lanes] = jnp.sum(v * values * inverse, axis=0, keepdims=True)
            v = v * gain_ref[i : i + 1, lanes]
            source[:, lanes] = v
            row_dot = row_dot + jnp.sum(values * v, axis=-1, keepdims=True)
        return row_dot

    dots_q = turn_back(0)
    sent(2, part.at[bx], got.at[1], xn).wait_recv()
    sent(3, part.at[by], got.at[2], yn).wait_recv()
    acc[...] += got[1].astype(F32) + got[2].astype(F32)
    dproj_ref[2] = acc[1].astype(BF16)
    dots_k = turn_back(1)
    total = exchange_rows(n, to_rows(dots_q, dots_k), msg, m_send, m_recv)
    means = to_columns(total) / width
    for i in range(2):
        inverse = inv_ref[:, i : i + 1]
        factor = inverse**3 * means[:, i : i + 1]
        source = dq_ref if i == 0 else acc.at[0]
        dproj_ref[i] = (inverse * source[...] - proj_ref[i] * factor).astype(BF16)
    pieces.finish()
    late.plane.finish(1)
    for copy in copies:
        copy.wait_send()


def attend_back(
    n, q, kvall, d_out, attn32, lse, bound, proj, inv, gain, table, late, grads
):
    span, cols = q.shape
    heads = cols // HEAD_DIM
    width, ff = late[0].shape[1], late[2].shape[2]
    return pl.pallas_call(
        functools.partial(attend_back_kernel, n),
        out_shape=(shape((3, span, cols), BF16), shape((2, cols), F32))
        + tuple(shape(g.shape, BF16) for g in grads),
        in_specs=[VM] * 9 + [HB] * 8,
        out_specs=(VM, VM, HB, HB, HB),
        input_output_aliases={14: 2, 15: 3, 16: 4},
        scratch_shapes=[
            pltpu.VMEM((span, cols), F32),
            pltpu.VMEM((4, 2, span, cols), BF16),
            pltpu.VMEM((3, 2, span, cols), BF16),
            pltpu.VMEM((2, span, cols), F32),
            pltpu.VMEM((heads, 8, span), F32),
            pltpu.VMEM((span, 128), F32),
            pltpu.VMEM((n, 8, span), F32),
        ]
        + LatePiece.scratch(span, width, ff)
        + [
            pltpu.SemaphoreType.DMA((4,)),
            pltpu.SemaphoreType.DMA((4,)),
            pltpu.SemaphoreType.DMA,
            pltpu.SemaphoreType.DMA((n - 1,)),
            pltpu.SemaphoreType.DMA((n - 1,)),
        ],
        compiler_params=pltpu.CompilerParams(
            collective_id=3, has_side_effects=True, vmem_limit_bytes=VMEM_LIMIT
        ),
        name="attend_back",
    )(q, kvall, d_out, attn32, lse, bound, proj, inv, gain, table, *late, *grads)


class Keep:
    def __init__(self, sems):
        self.sems, self.copies = sems, []

    def __call__(self, src, dst):
        copy = pltpu.make_async_copy(src, dst, self.sems.at[len(self.copies)])
        copy.start()
        self.copies.append(copy)
        return copy

    def finish(self, but=()):
        for copy in self.copies:
            if not any(copy is done for done in but):
                copy.wait()


def forward_kernel(n, names, *refs):
    ref = SimpleNamespace(**dict(zip(names, refs)))
    x_ref, w_ref, tab_ref, gain_ref, seg_ref = ref.x, ref.w, ref.table, ref.gain, ref.seg
    wo_ref, gu_ref, down_ref, post_ref = ref.wo, ref.gu, ref.down, ref.post
    s, c, u = where_am_i()
    rows, width = x_ref.shape
    span, half = n * rows, rows // 2
    kb = w_ref.shape[1]
    xg, wq, proj, qkv = ref.v_xg, ref.v_wq, ref.v_proj, ref.v_qkv
    every, back, attn = ref.v_every, ref.v_back, ref.v_attn
    cols = proj.shape[2]
    quarter = cols // 4
    keep, load = Keep(ref.keep_sem), Keep(ref.load_sem)
    table = load(tab_ref.at[rows_of(c, span)], ref.v_tab)
    xg[rows_of(u, rows), :] = x_ref[...]
    peers = [(s, c ^ k, u) for k in (1, 2, 3)]
    greet(all_uly_peers(n) + [(None, peer) for peer in peers] + [(None, (1 - s, c, u))])

    def plane(k, src, block, half_rows):
        return PlaneGather(
            src, block, half_rows, ref.w_send.at[k], ref.w_recv.at[k], ref.w_local.at[k]
        )

    def plane_to(k, src, out):
        return plane(k, src, lambda b: out.at[b], src.shape[0] // 2)

    lower, upper = pl.ds(0, kb // 2), pl.ds(kb // 2, kb // 2)
    w_qkv = plane(0, w_ref, lambda b: wq.at[:, rows_of(b, kb)], kb // 2)
    w_out = plane_to(1, wo_ref, ref.o_wo)
    w_a = plane_to(2, gu_ref.at[0, lower], ref.o_wga)
    w_b = plane_to(3, gu_ref.at[0, upper], ref.o_wgb)
    w_c = plane_to(4, gu_ref.at[1], ref.o_wgc)
    w_d = plane_to(5, down_ref, ref.o_wd)

    gather = LineGather(n, rows, xg, ref.x_sems)
    gather.send(0)
    w_qkv.start()
    gather.wait(0)
    w_qkv.middle()
    w_out.start()
    if n > 2:
        gather.wait(1)
    w_qkv.corner()
    w_a.start()
    w_out.middle()
    for slot in range(2 if n > 2 else 1, n - 1):
        gather.wait(slot)
    w_qkv.arrive()
    keep(xg, ref.o_xg)
    keep(wq, ref.o_wq)
    count, size = tiles(span, 512)

    def project(i, carry):
        where = pl.ds(pl.multiple_of(i * size, size), size)
        xs = xg[where, :]
        proj[0, where, :] = dot(xs, wq[0], NN)
        proj[1, where, :] = dot(xs, wq[1], NN)
        value = dot(xs, wq[2], NN).astype(BF16)
        for q in range(4):
            qkv[q, 2, where, :] = value[:, q * quarter : (q + 1) * quarter]
        return carry

    lax.fori_loop(0, count, project, 0)
    keep(proj, ref.o_proj)
    squares = [jnp.sum(proj[i] * proj[i], axis=-1, keepdims=True) for i in range(2)]
    mine = to_rows(*squares)
    zeros = jnp.sum((1 - seg_ref[...]).astype(F32))
    row = lax.broadcasted_iota(jnp.int32, mine.shape, 0)
    mine = jnp.where(row == 2, zeros, mine)
    total = exchange_rows(n, mine, ref.v_msg, ref.m_send, ref.m_recv)
    zmsg = ref.v_zmsg
    zmsg[pl.ds(c, 1)] = jnp.broadcast_to(total[2:3, :128], (1, 8, 128))
    inv = ref.v_inv
    inv[...] = lax.rsqrt(to_columns(total) / width + EPS)
    table.wait()
    cosine, sine = rope_factors(ref.v_tab[...])
    for i in range(2):
        inverse = inv[:, i : i + 1]
        for h in range(cols // HEAD_DIM):
            lanes = slice(h * HEAD_DIM, (h + 1) * HEAD_DIM)
            v = proj[i, :, lanes] * inverse * gain_ref[i : i + 1, lanes]
            v = (v * cosine + pltpu.roll(v, HALF, 1) * sine).astype(BF16)
            group, inside = divmod(h * HEAD_DIM, quarter)
            qkv[group, i, :, inside : inside + HEAD_DIM] = v

    copies, arrivals = [], []
    a_send, a_recv, z_send, z_recv = ref.a_send, ref.a_recv, ref.z_send, ref.z_recv
    for k, peer in enumerate(peers):
        there = peer[1]
        copy = remote(qkv.at[there], every.at[c], a_send.at[k], a_recv.at[k], peer)
        copy.start()
        small = remote(zmsg.at[c], zmsg.at[c], z_send.at[k], z_recv.at[k], peer)
        small.start()
        copies += [copy, small]
        arrivals.append(remote(every.at[there], every.at[there], a_send.at[k], a_recv.at[k], peer))
        arrivals.append(remote(zmsg.at[there], zmsg.at[there], z_send.at[k], z_recv.at[k], peer))
    every[pl.ds(c, 1)] = qkv[pl.ds(c, 1)]
    keep(inv, ref.o_inv)
    w_a.middle()
    w_out.corner()
    w_out.arrive()
    load_o = load_blocks(ref.o_wo, ref.v_wo, ref.wo_sem, 1)
    for arrival in arrivals:
        arrival.wait_recv()
    w_b.start()
    keep(every, ref.o_every)
    bounds = (zmsg[0] + zmsg[1] + zmsg[2] + zmsg[3]).astype(jnp.int32)
    ref.v_bound[...] = bounds
    bound = bounds[:1, :1]
    peaks, sums, acct = ref.v_peaks, ref.v_sums, ref.v_acct
    att, lse = ref.v_att, ref.v_lse

    def attend(k, carry):
        i = c ^ (3 - k)
        first_q = i * span
        starts = segment_starts(first_q, span, bound)
        for h in range(quarter // HEAD_DIM):
            lanes = slice(h * HEAD_DIM, (h + 1) * HEAD_DIM)
            peaks[...] = jnp.full_like(peaks, FLOOR)
            sums[...] = jnp.zeros_like(sums)
            acct[...] = jnp.zeros_like(acct)

            def update(j, diagonal):
                scores = dot(every[j, 1, :, lanes], every[i, 0, :, lanes], NT) * SCALE2
                scores = score_mask(scores, j * span, first_q, starts, diagonal)
                old = peaks[:1, :]
                new = jnp.maximum(old, jnp.max(scores, axis=0, keepdims=True))
                factor = jnp.exp2(old - new)
                weights = jnp.exp2(scores - new)
                peaks[:1, :] = new
                sums[:1, :] = sums[:1, :] * factor + jnp.sum(weights, axis=0, keepdims=True)
                acct[...] = acct[...] * factor + dot(
                    every[j, 2, :, lanes], weights.astype(BF16), TN
                )

            def before(j, carry):
                update(j, False)
                return carry

            lax.fori_loop(0, i, before, 0)
            update(i, True)
            total = sums[:1, :]
            attention = acct[...] / total
            att[pl.ds(i, 1), lanes, :] = attention[None]
            back[pl.ds(k, 1), :, :, lanes] = (
                jnp.transpose(attention).astype(BF16).reshape(1, n, rows, HEAD_DIM)
            )
            lse[pl.ds(i, 1), h, :1, :] = (peaks[:1, :] + jnp.log2(total))[None]

        @pl.when(k < 3)
        def _():
            home(k, i, c).start()

        return carry

    def home(k, i, owner):
        return remote(
            back.at[k],
            attn.at[:, :, pl.ds(pl.multiple_of(owner * quarter, quarter), quarter)],
            ref.b_send.at[k],
            ref.b_recv.at[k],
            (s, i, u),
        )

    lax.fori_loop(0, 4, attend, 0)
    attn[:, :, pl.ds(pl.multiple_of(c * quarter, quarter), quarter)] = back[3]
    keep(att, ref.o_att)
    keep(lse, ref.o_lse)
    keep(ref.v_bound, ref.o_bound)
    w_a.corner()
    for k in range(3):
        i = c ^ (3 - k)
        home(k, i, i).wait_recv()
    keep(attn, ref.o_attn)
    wait_all(load_o)
    w_a.arrive()
    wg = ref.v_wg
    load(ref.o_wga, wg.at[0, :, lower])

    wo, part, group = ref.v_wo, ref.v_part, ref.v_group
    halves = Halves(n, rows)
    per_half, chunk_cols = part.shape[0] // 2, part.shape[2]

    def compute(chunk):
        h, q = divmod(chunk, per_half)
        lanes = slice(q * chunk_cols, (q + 1) * chunk_cols)

        def tile(index, start, size):
            part[chunk, start : start + size, :] = dot(
                halves.load(attn, index), wo[:, lanes], NN
            ).astype(BF16)

        halves.each(h, tile)

    reduce = LineReduce(n, half, part, ref.v_got, ref.r_sems)
    g_sems = ref.g_sems
    gathers = [LineGather(n, rows, group, g_sems, (h, half)) for h in range(2)]
    branch, resid = ref.v_branch, ref.v_resid
    gate, up, hidden = ref.v_gate, ref.v_up, ref.v_hidden

    def finish(h):
        where = slice(h * half, (h + 1) * half)
        reduce.last(branch.at[h], range(h * per_half, (h + 1) * per_half))
        values = branch[h]
        total = x_ref[where, :].astype(F32) + values * inverse_rms(values) * post_ref[0:1, :]
        resid[h] = total
        group[pl.ds(u, 1), where, :] = total.astype(BF16)[None]

    ff = gate.shape[2]
    ntile, tsize = tiles(ff, 512)

    def body(h, t):
        lanes = slice(t * tsize, (t + 1) * tsize)

        def tile(index, start, size):
            inputs = halves.load(group, index)
            gates = dot(inputs, wg[0, :, :, lanes].reshape(width, tsize), NN)
            ups = dot(inputs, wg[1, :, :, lanes].reshape(width, tsize), NN)
            halves.store(gate, index, lanes, gates.astype(BF16))
            halves.store(up, index, lanes, ups.astype(BF16))
            halves.store(
                hidden, index, lanes, (gates * jax.nn.sigmoid(gates) * ups).astype(BF16)
            )

        halves.each(h, tile)
        if h == 1:
            for out, src in ((ref.o_hidden, hidden), (ref.o_gate, gate), (ref.o_up, up)):
                keep(src.at[:, :, lanes], out.at[:, :, lanes])

    def hook(label):
        if label == "started":
            w_b.middle()
            w_c.start()
        if label == "sent":
            w_b.corner()
        if label == "b1":
            w_b.arrive()
            load(ref.o_wgb, wg.at[0, :, upper])
        if label == f"b{n - 2}":
            w_c.middle()
        if label == "first":
            keep(branch, ref.o_branch)
            keep(resid, ref.o_resid)
            w_c.corner()
            w_d.start()
            w_c.arrive()
            load(ref.o_wgc, wg.at[1])
            load.finish((table,))
        if label == f"g{n - 2}":
            keep(group, ref.o_group)

    reduce_norm_gather(n, reduce, gathers, compute, finish, Consume(ntile, body), hook)
    w_d.middle()
    w_d.corner()
    w_d.arrive()
    for k in range(3):
        home(k, c ^ (3 - k), c).wait_send()
    for copy in copies:
        copy.wait_send()
    for work in (w_qkv, w_out, w_a, w_b, w_c, w_d, gather):
        work.finish()
    keep.finish()


def forward(n, x, w, table, gain, seg, wo, gu, down, post):
    rows, width = x.shape
    span, cols, half = n * rows, w.shape[2], rows // 2
    quarter = cols // 4
    kb, ff = gu.shape[1:]
    ntile = tiles(ff, 512)[0]
    dma = pltpu.SemaphoreType.DMA
    ins = dict(
        x=(x, VM),
        w=(w, HB),
        table=(table, HB),
        gain=(gain, VM),
        seg=(seg, VM),
        wo=(wo, HB),
        gu=(gu, HB),
        down=(down, HB),
        post=(post, VM),
    )
    outs = dict(
        o_xg=((span, width), BF16),
        o_wq=((3, width, cols), BF16),
        o_wo=((8,) + wo.shape, BF16),
        o_wga=((8, kb // 2, ff), BF16),
        o_wgb=((8, kb // 2, ff), BF16),
        o_wgc=((8, kb, ff), BF16),
        o_wd=((8,) + down.shape, BF16),
        o_proj=((2, span, cols), F32),
        o_inv=((span, 128), F32),
        o_every=((4, 3, span, quarter), BF16),
        o_att=((4, quarter, span), F32),
        o_lse=((4, quarter // HEAD_DIM, 8, span), F32),
        o_bound=((8, 128), jnp.int32),
        o_attn=((n, rows, cols), BF16),
        o_branch=((2, half, width), F32),
        o_resid=((2, half, width), F32),
        o_group=((n, rows, width), BF16),
        o_gate=((n, rows, ff), BF16),
        o_up=((n, rows, ff), BF16),
        o_hidden=((n, rows, ff), BF16),
    )
    buffers = dict(
        v_xg=((span, width), BF16),
        v_wq=((3, width, cols), BF16),
        v_tab=((span, 128), F32),
        v_proj=((2, span, cols), F32),
        v_inv=((span, 128), F32),
        v_msg=((n, 8, span), F32),
        v_qkv=((4, 3, span, quarter), BF16),
        v_every=((4, 3, span, quarter), BF16),
        v_back=((4, n, rows, quarter), BF16),
        v_zmsg=((4, 8, 128), F32),
        v_bound=((8, 128), jnp.int32),
        v_peaks=((8, span), F32),
        v_sums=((8, span), F32),
        v_acct=((HEAD_DIM, span), F32),
        v_att=((4, quarter, span), F32),
        v_lse=((4, quarter // HEAD_DIM, 8, span), F32),
        v_attn=((n, rows, cols), BF16),
        v_wo=((cols, width), BF16),
        v_wg=((2, 8, kb, ff), BF16),
        v_group=((n, rows, width), BF16),
        v_branch=((2, half, width), F32),
        v_resid=((2, half, width), F32),
        v_gate=((n, rows, ff), BF16),
        v_up=((n, rows, ff), BF16),
        v_hidden=((n, rows, ff), BF16),
        v_part=((4, n * half, width // 2), BF16),
        v_got=((4, (n + 1) * half, width // 2), BF16),
    )
    sems = dict(
        keep_sem=(12 + 3 * ntile,),
        load_sem=(4,),
        wo_sem=(8,),
        w_send=(6, 9),
        w_recv=(6, 9),
        w_local=(6,),
        m_send=(n - 1,),
        m_recv=(n - 1,),
    )
    three, fours = (3,), dict(x_sems=(n - 1,), r_sems=(n - 1, 4), g_sems=(n - 1, 2))
    sems.update(a_send=three, a_recv=three, z_send=three, z_recv=three, b_send=three, b_recv=three)
    names = [*ins, *outs, *buffers, *sems, *fours]
    results = pl.pallas_call(
        functools.partial(forward_kernel, n, names),
        out_shape=[shape(*out) for out in outs.values()],
        in_specs=[spec for value, spec in ins.values()],
        out_specs=[HB] * len(outs),
        scratch_shapes=[pltpu.VMEM(*buffer) for buffer in buffers.values()]
        + [dma(dims) for dims in sems.values()]
        + [(dma(dims),) * 4 for dims in fours.values()],
        compiler_params=pltpu.CompilerParams(
            collective_id=10, has_side_effects=True, vmem_limit_bytes=VMEM_LIMIT
        ),
        name="forward",
    )(*[value for value, spec in ins.values()])
    return SimpleNamespace(**dict(zip(outs, results)))


def load_blocks(src, dst, sem, axis):
    blocks = src.shape[0]
    size = dst.shape[axis] // blocks
    copies = []
    for b in range(blocks):
        where = [slice(None)] * len(dst.shape)
        where[axis] = pl.ds(b * size, size)
        copies.append(pltpu.make_async_copy(src.at[b], dst.at[tuple(where)], sem.at[b]))
    for copy in copies:
        copy.start()
    return copies


def wait_all(copies):
    for copy in copies:
        copy.wait()


def mlp_in_kernel(
    n,
    attn_ref,
    wo_ref,
    x_ref,
    gain_ref,
    wga_ref,
    wgb_ref,
    gu_ref,
    down_ref,
    branch_out,
    resid_out,
    group_out,
    gate_out,
    up_out,
    hidden_out,
    wgc_out,
    wd_out,
    wo,
    wg,
    group,
    branch,
    resid,
    gate,
    up,
    hidden,
    part,
    got_rows,
    sem_o,
    local_sem,
    keep_sem,
    w_send,
    w_recv,
    *sems,
):
    s, c, u = where_am_i()
    rows, width = x_ref.shape
    load_o = load_blocks(wo_ref, wo, sem_o, 1)
    kb = wgc_out.shape[1]
    load_g = [
        pltpu.make_async_copy(wga_ref, wg.at[0, :, pl.ds(0, kb // 2)], local_sem.at[0]),
        pltpu.make_async_copy(wgb_ref, wg.at[0, :, pl.ds(kb // 2, kb // 2)], local_sem.at[1]),
        pltpu.make_async_copy(wgc_out, wg.at[1], local_sem.at[2]),
    ]
    greet(line_peers(n) + plane_peers() + [(None, (1 - s, c, u))])

    def plane(k, src, out, half_rows):
        return PlaneGather(
            src, lambda b: out.at[b], half_rows, w_send.at[k], w_recv.at[k], local_sem.at[3 + k]
        )

    first = plane(0, gu_ref.at[1], wgc_out, kb // 2)
    second = plane(1, down_ref, wd_out, down_ref.shape[0] // 2)
    first.start()
    load_g[0].start()
    load_g[1].start()
    wait_all(load_o)
    halves = Halves(n, rows)
    half = rows // 2
    per_half = part.shape[0] // 2
    chunk_cols = part.shape[2]

    def compute(chunk):
        h, q = divmod(chunk, per_half)
        cols = slice(q * chunk_cols, (q + 1) * chunk_cols)

        def tile(index, start, size):
            part[chunk, start : start + size, :] = dot(
                halves.load(attn_ref, index), wo[:, cols], NN
            ).astype(BF16)

        halves.each(h, tile)

    reduce = LineReduce(n, half, part, got_rows, sems[:4])
    gathers = [LineGather(n, rows, group, sems[4:], (h, half)) for h in range(2)]
    kept = []

    def keep(src, dst):
        copy = pltpu.make_async_copy(src, dst, keep_sem.at[len(kept)])
        copy.start()
        kept.append(copy)

    def finish(h):
        where = slice(h * half, (h + 1) * half)
        reduce.last(branch.at[h], range(h * per_half, (h + 1) * per_half))
        values = branch[h]
        total = x_ref[where, :].astype(F32) + values * inverse_rms(values) * gain_ref[0:1, :]
        resid[h] = total
        group[pl.ds(u, 1), where, :] = total.astype(BF16)[None]

    ff = gate.shape[2]
    ntile, tsize = tiles(ff, 512)

    def body(h, t):
        lanes = slice(t * tsize, (t + 1) * tsize)

        def tile(index, start, size):
            inputs = halves.load(group, index)
            gates = dot(inputs, wg[0, :, :, lanes].reshape(width, tsize), NN)
            ups = dot(inputs, wg[1, :, :, lanes].reshape(width, tsize), NN)
            halves.store(gate, index, lanes, gates.astype(BF16))
            halves.store(up, index, lanes, ups.astype(BF16))
            halves.store(
                hidden, index, lanes, (gates * jax.nn.sigmoid(gates) * ups).astype(BF16)
            )

        halves.each(h, tile)
        if h == 1:
            for src, dst in ((hidden, hidden_out), (gate, gate_out), (up, up_out)):
                keep(src.at[:, :, lanes], dst.at[:, :, lanes])

    def hook(label):
        if label == "b1":
            first.middle()
            second.start()
        if label == "first":
            keep(branch, branch_out)
            keep(resid, resid_out)
            first.corner()
            first.arrive()
            load_g[2].start()
            wait_all(load_g)
        if label == f"g{n - 2}":
            keep(group, group_out)
        if label == "t0":
            second.middle()

    reduce_norm_gather(n, reduce, gathers, compute, finish, Consume(ntile, body), hook)
    second.corner()
    second.arrive()
    for work in (first, second):
        work.finish()
    wait_all(kept)


def reduce_scratch(n, rows, width):
    cols = width // CHUNKS
    return [
        pltpu.VMEM((CHUNKS, n * rows, cols), BF16),
        pltpu.VMEM((CHUNKS, (n + 1) * rows, cols), BF16),
    ]


def half_scratch(n, rows, width):
    half, cols = rows // 2, width // 2
    return [
        pltpu.VMEM((4, n * half, cols), BF16),
        pltpu.VMEM((4, (n + 1) * half, cols), BF16),
    ]


def mlp_in(n, attn, wo, x, gain, wga, wgb, gu, down):
    rows, width = x.shape
    span, cols = attn.shape
    kb, ff = gu.shape[1:]
    ntile = tiles(ff, 512)[0]
    outs = pl.pallas_call(
        functools.partial(mlp_in_kernel, n),
        out_shape=(
            shape((2, rows // 2, width), F32),
            shape((2, rows // 2, width), F32),
            shape((n, rows, width), BF16),
            shape((n, rows, ff), BF16),
            shape((n, rows, ff), BF16),
            shape((n, rows, ff), BF16),
            shape((8, kb, ff), BF16),
            shape((8,) + down.shape, BF16),
        ),
        in_specs=[VM, HB, VM, VM, HB, HB, HB, HB],
        out_specs=(HB,) * 8,
        scratch_shapes=[
            pltpu.VMEM((cols, width), BF16),
            pltpu.VMEM((2, 8, kb, ff), BF16),
            pltpu.VMEM((n, rows, width), BF16),
            pltpu.VMEM((2, rows // 2, width), F32),
            pltpu.VMEM((2, rows // 2, width), F32),
            pltpu.VMEM((n, rows, ff), BF16),
            pltpu.VMEM((n, rows, ff), BF16),
            pltpu.VMEM((n, rows, ff), BF16),
        ]
        + half_scratch(n, rows, width)
        + [
            pltpu.SemaphoreType.DMA((8,)),
            pltpu.SemaphoreType.DMA((5,)),
            pltpu.SemaphoreType.DMA((3 + 3 * ntile,)),
            pltpu.SemaphoreType.DMA((2, 9)),
            pltpu.SemaphoreType.DMA((2, 9)),
        ]
        + line_sems(n, 4)
        + line_sems(n, 2),
        compiler_params=pltpu.CompilerParams(
            collective_id=4, has_side_effects=True, vmem_limit_bytes=VMEM_LIMIT
        ),
        name="mlp_in",
    )(attn.reshape(n, rows, cols), wo, x, gain, wga, wgb, gu, down)
    return outs


def mlp_out_kernel(
    n,
    hidden_ref,
    wd_ref,
    resid_ref,
    gain_ref,
    cot_ref,
    gate_hbm,
    up_hbm,
    gresid_ref,
    out_ref,
    group_out,
    dgu_out,
    dgain_ref,
    hidden_s,
    resid_s,
    dmlp_s,
    dgu_s,
    wd,
    mlp,
    group,
    gate_ref,
    up_ref,
    dgu,
    part,
    got_rows,
    sem_d,
    local_sem,
    keep_sem,
    s_send,
    s_recv,
    *sems,
):
    s, c, u = where_am_i()
    rows, width = cot_ref.shape
    load_d = load_blocks(wd_ref, wd, sem_d, 1)
    load_g = [
        pltpu.make_async_copy(gate_hbm, gate_ref, local_sem.at[0]),
        pltpu.make_async_copy(up_hbm, up_ref, local_sem.at[1]),
    ]
    greet(line_peers(n) + [(None, (1 - s, c, u))])
    sibling = Sibling(s_send, s_recv)
    halves = Halves(n, rows)
    half = rows // 2
    per_half = part.shape[0] // 2
    chunk_cols = part.shape[2]

    def compute(chunk):
        h, q = divmod(chunk, per_half)
        cols = slice(q * chunk_cols, (q + 1) * chunk_cols)
        if h == 0:
            wait_all(load_d[q * (8 // per_half) : (q + 1) * (8 // per_half)])

        def tile(index, start, size):
            part[chunk, start : start + size, :] = dot(
                halves.load(hidden_ref, index), wd[:, cols], NN
            ).astype(BF16)

        halves.each(h, tile)

    reduce = LineReduce(n, half, part, got_rows, sems[:4])
    gathers = [LineGather(n, rows, group, sems[4:], (h, half)) for h in range(2)]
    dgain_ref[...] = jnp.zeros_like(dgain_ref)

    def finish(h):
        where = slice(h * half, (h + 1) * half)
        reduce.last(mlp.at[h], range(h * per_half, (h + 1) * per_half))
        values = mlp[h]
        grad = cot_ref[where, :].astype(F32)
        d_mlp = norm_back(values, inverse_rms(values), grad * gain_ref[1:2, :], width)
        group[pl.ds(u, 1), where, :] = d_mlp.astype(BF16)[None]

    def rest(h):
        where = slice(h * half, (h + 1) * half)
        values = mlp[h]
        scaled = values * inverse_rms(values)
        out_ref[where, :] = (resid_ref[h] + scaled * gain_ref[1:2, :]).astype(BF16)
        dgain_ref[...] += jnp.sum(cot_ref[where, :].astype(F32) * scaled, axis=0, keepdims=True)

    ff = gate_ref.shape[2]
    ntile, tsize = tiles(ff, 512)
    kept = []

    def keep(src, dst):
        copy = pltpu.make_async_copy(src, dst, keep_sem.at[len(kept)])
        copy.start()
        kept.append(copy)

    def body(h, t):
        lanes = slice(t * tsize, (t + 1) * tsize)

        def tile(index, start, size):
            d_hidden = dot(halves.load(group, index), wd[lanes, :], NT)
            gate = halves.load(gate_ref, index, lanes).astype(F32)
            up = halves.load(up_ref, index, lanes).astype(F32)
            sig = jax.nn.sigmoid(gate)
            slope = sig * (1.0 + gate * (1.0 - sig))
            halves.store(dgu.at[0], index, lanes, (d_hidden * up * slope).astype(BF16))
            halves.store(dgu.at[1], index, lanes, (d_hidden * (gate * sig)).astype(BF16))

        halves.each(h, tile)
        where = pl.ds(h * half, half)
        view = dgu.at[:, :, where, lanes]
        sibling.start(view, dgu_s.at[:, :, where, lanes])
        keep(view, dgu_out.at[:, :, where, lanes])

    def hook(label):
        if label == "sent":
            sibling.start(hidden_ref, hidden_s)
            lanes = pl.ds(pl.multiple_of((1 - s) * (width // 2), width // 2), width // 2)
            sibling.start(gresid_ref.at[:, :, lanes], resid_s)
            for copy in load_g:
                copy.start()
        if label == "half":
            rest(0)
        if label == "first":
            rest(1)
            wait_all(load_g)
        if label == f"g{n - 2}":
            lanes = pl.ds(pl.multiple_of((1 - s) * (width // 2), width // 2), width // 2)
            sibling.start(group.at[:, :, lanes], dmlp_s)
            keep(group, group_out)

    reduce_norm_gather(n, reduce, gathers, compute, finish, Consume(ntile, body), hook)
    for i in range(3 + 2 * ntile):
        sibling.wait(i)
    sibling.finish()
    wait_all(kept)


def mlp_out(n, hidden, wd, resid, gain, cot, gate, up, gresid):
    rows, width = cot.shape
    ff = hidden.shape[2]
    ntile = tiles(ff, 512)[0]
    return pl.pallas_call(
        functools.partial(mlp_out_kernel, n),
        out_shape=(
            shape((rows, width), BF16),
            shape((n, rows, width), BF16),
            shape((2, n, rows, ff), BF16),
            shape((1, width), F32),
            shape((n, rows, ff), BF16),
            shape((n, rows, width // 2), BF16),
            shape((n, rows, width // 2), BF16),
            shape((2, n, rows, ff), BF16),
        ),
        in_specs=[VM, HB, VM, VM, VM, HB, HB, HB],
        out_specs=(VM, HB, HB, VM, HB, HB, HB, HB),
        scratch_shapes=[
            pltpu.VMEM((ff, width), BF16),
            pltpu.VMEM((2, rows // 2, width), F32),
            pltpu.VMEM((n, rows, width), BF16),
            pltpu.VMEM((n, rows, ff), BF16),
            pltpu.VMEM((n, rows, ff), BF16),
            pltpu.VMEM((2, n, rows, ff), BF16),
        ]
        + half_scratch(n, rows, width)
        + [
            pltpu.SemaphoreType.DMA((8,)),
            pltpu.SemaphoreType.DMA((2,)),
            pltpu.SemaphoreType.DMA((1 + 2 * ntile,)),
            pltpu.SemaphoreType.DMA((3 + 2 * ntile,)),
            pltpu.SemaphoreType.DMA((3 + 2 * ntile,)),
        ]
        + line_sems(n, 4)
        + line_sems(n, 2),
        compiler_params=pltpu.CompilerParams(
            collective_id=5, has_side_effects=True, vmem_limit_bytes=VMEM_LIMIT
        ),
        name="mlp_out",
    )(hidden, wd, resid, gain, cot, gate, up, gresid)


def mlp_back_kernel(
    n,
    dgu_hbm,
    wga_ref,
    wgb_ref,
    wgc_ref,
    cot_ref,
    branch_ref,
    gain_ref,
    wo_ref,
    hidden_hbm,
    dmlp_hbm,
    resid_hbm,
    hidden_s_hbm,
    dmlp_s_hbm,
    resid_s_hbm,
    dgu_s_hbm,
    dresid_ref,
    group_out,
    dattn_ref,
    dgain_ref,
    gown_out,
    gx_out,
    gy_out,
    down_own_out,
    down_x_out,
    down_y_out,
    wo,
    wg,
    group,
    part,
    got_rows,
    dgu_ref,
    hidden,
    hidden_s,
    dmlp,
    dmlp_s,
    gate_in,
    ring_d,
    ring_g,
    got_d,
    got_g,
    sem_o,
    sem_in,
    local_sem,
    d_send,
    d_recv,
    d_local,
    g_send,
    g_recv,
    g_local,
    *sems,
):
    s, c, u = where_am_i()
    rows, width = cot_ref.shape
    half = wga_ref.shape[1]
    chunk_cols = width // part.shape[0]
    per_chunk = chunk_cols // (2 * half)
    chunks = part.shape[0]

    def load_chunk(chunk):
        slot = chunk % 2
        where = pl.ds(chunk * per_chunk, per_chunk)
        return [
            pltpu.make_async_copy(
                wga_ref.at[where], wg.at[slot, 0, :, pl.ds(0, half)], local_sem.at[slot, 0]
            ),
            pltpu.make_async_copy(
                wgb_ref.at[where], wg.at[slot, 0, :, pl.ds(half, half)], local_sem.at[slot, 1]
            ),
            pltpu.make_async_copy(wgc_ref.at[where], wg.at[slot, 1], local_sem.at[slot, 2]),
        ]

    def start_chunk(chunk):
        for copy in load_chunk(chunk):
            copy.start()

    def fetch(k, src, dst):
        copy = pltpu.make_async_copy(src, dst, sem_in.at[k])
        copy.start()
        return copy

    load_dgu = fetch(0, dgu_hbm, dgu_ref)
    start_chunk(0)
    load_d = [
        fetch(1, hidden_hbm, hidden),
        fetch(2, half_columns(dmlp_hbm, s), dmlp),
        fetch(3, hidden_s_hbm, hidden_s),
        fetch(4, dmlp_s_hbm, dmlp_s),
    ]
    start_chunk(1)
    load_g = []
    if gate_in:
        resid, resid_s, dgu_s = gate_in
        load_g = [
            fetch(5, half_columns(resid_hbm, s), resid),
            fetch(6, resid_s_hbm, resid_s),
            fetch(7, dgu_s_hbm, dgu_s),
        ]
    load_o = load_blocks(wo_ref, wo, sem_o, 1)
    greet(line_peers(n) + plane_peers())
    load_dgu.wait()
    span = n * rows
    count, size = tiles(span, 512)

    def compute(chunk):
        wait_all(load_chunk(chunk))
        slot = chunk % 2

        def tile(i, carry):
            where = pl.ds(pl.multiple_of(i * size, size), size)
            part[chunk, where, :] = (
                dot(dgu_ref[0, where, :], wg[slot, 0].reshape(chunk_cols, -1), NT)
                + dot(dgu_ref[1, where, :], wg[slot, 1].reshape(chunk_cols, -1), NT)
            ).astype(BF16)
            return carry

        lax.fori_loop(0, count, tile, 0)
        if chunk + 2 < chunks:
            start_chunk(chunk + 2)

    rows_d, cols_g = ring_d.shape[2], ring_g.shape[3]
    tiles_g = dgu_hbm.shape[2] // cols_g

    def place_d(out, piece, part):
        size = rows_d if part is None else rows_d // 2
        return out.at[pl.ds(piece * rows_d + (part or 0) * size, size)]

    def place_g(out, piece, part):
        size = ring_g.shape[2] if part is None else ring_g.shape[2] // 2
        ci, tile = piece // tiles_g, piece % tiles_g
        return out.at[ci, pl.ds((part or 0) * size, size), pl.ds(tile * cols_g, cols_g)]

    down = PlaneReduce(
        ring_d, got_d, (down_own_out, down_x_out, down_y_out), place_d, d_send, d_recv, d_local
    )
    gate = PlaneReduce(ring_g, got_g, (gown_out, gx_out, gy_out), place_g, g_send, g_recv, g_local)
    down_piece = wide_piece(
        (hidden, dmlp), (hidden_s, dmlp_s), lambda p: slice(p * rows_d, (p + 1) * rows_d)
    )

    def gate_right(ref, piece):
        tile = piece % tiles_g
        return ref[piece // tiles_g, :, tile * cols_g : (tile + 1) * cols_g]

    n_d, n_g = got_d.shape[0], got_g.shape[0] if gate_in else 0
    work = [(down, p, down_piece) for p in range(n_d)]
    if gate_in:
        gate_piece = tall_piece((resid, dgu_ref), (resid_s, dgu_s), gate_right)
        work += [(gate, p, gate_piece) for p in range(n_g)]
    pieces = Pieces(work)

    def compute_and_piece(chunk):
        compute(chunk)
        if chunk == 0:
            wait_all(load_d)
        if chunk < 2:
            pieces.step()

    def reduce_hook(slot):
        if slot == 0:
            wait_all(load_g)
        pieces.step()

    LineReduce(n, rows, part, got_rows, sems[:4]).run(compute_and_piece, dresid_ref, reduce_hook)
    d_resid = dresid_ref[...] + cot_ref[...].astype(F32)
    dresid_ref[...] = d_resid
    branch = branch_ref[...]
    inverse = inverse_rms(branch)
    d_branch = norm_back(branch, inverse, d_resid * gain_ref[0:1, :], width)
    small = group.shape[0] == span
    if small:
        group[rows_of(u, rows), :] = d_branch.astype(BF16)
        gather = LineGather(n, rows, group, sems[4:])
    else:
        group[:rows, :] = d_branch.astype(BF16)
        own = pltpu.make_async_copy(
            group.at[pl.ds(0, rows)], group_out.at[rows_of(u, rows)], local_sem.at[2, 2]
        )
        own.start()
        own.wait()
        gather = LineGather(n, rows, group_out, sems[4:])
    gather.send(0)
    dgain_ref[...] = jnp.sum(d_resid * branch * inverse, axis=0, keepdims=True)
    wait_all(load_o)
    pieces.step()

    def gather_hook(slot):
        pieces.step()

    gather.run(gather_hook)
    if small:
        keep = pltpu.make_async_copy(group, group_out, local_sem.at[2, 2])
        keep.start()

    def tile(j, carry):
        where = pl.ds(pl.multiple_of(j * size, size), size)
        if small:
            rows_in = group[where, :]
        else:
            fetch = pltpu.make_async_copy(group_out.at[where], group, local_sem.at[2, 2])
            fetch.start()
            fetch.wait()
            rows_in = group[...]
        d_attn = dot(rows_in, wo[...], NT).astype(BF16)
        if len(dattn_ref.shape) == 3:
            cols = dattn_ref.shape[2]
            for q in range(4):
                dattn_ref[q, where, :] = d_attn[:, q * cols : (q + 1) * cols]
        else:
            dattn_ref[where, :] = d_attn
        return carry

    lax.fori_loop(0, count, tile, 0)
    pieces.finish()
    down.finish(n_d)
    gate.finish(n_g)
    if small:
        keep.wait()


def piece_scratch(slots, pieces, rows, cols):
    return (
        [pltpu.VMEM((slots, 4, rows, cols), BF16), pltpu.VMEM((pieces, rows, cols), BF16)],
        [
            pltpu.SemaphoreType.DMA((pieces, 6)),
            pltpu.SemaphoreType.DMA((pieces, 6)),
            pltpu.SemaphoreType.DMA((pieces,)),
        ],
    )


def mlp_back(
    n,
    dgu,
    wga,
    wgb,
    wgc,
    cot,
    branch,
    gain,
    wo,
    hidden,
    dmlp,
    resid,
    hidden_s,
    resid_s,
    dmlp_s,
    dgu_s,
):
    rows, width = branch.shape
    span, ff = dgu.shape[1:]
    cols = wo.shape[1]
    kb, kc = width // 8, wo.shape[2]
    count, size = tiles(ff, 512)
    ring_d, sems_d = piece_scratch(min(3, count), count, size, kc)
    here = 2 * count - LATER
    ring_g, sems_g = piece_scratch(min(3, max(here, 1)), max(here, 1), kb, size)
    chunk_blocks = width // CHUNKS // kb
    return pl.pallas_call(
        functools.partial(mlp_back_kernel, n),
        out_shape=(
            shape((rows, width), F32),
            shape((span, width), BF16),
            shape((4, span, cols // 4) if spread_heads(cols) else (span, cols), BF16),
            shape((1, width), F32),
        )
        + (shape((2, kb, ff), BF16),) * 3
        + (shape((ff, kc), BF16),) * 3,
        in_specs=[HB, HB, HB, HB, VM, VM, VM] + [HB] * 8,
        out_specs=(VM, HB, VM, VM) + (HB,) * 6,
        scratch_shapes=[
            pltpu.VMEM((cols, width), BF16),
            pltpu.VMEM((2, 2, chunk_blocks, kb, ff), BF16),
            pltpu.VMEM((min(span, 512), width), BF16),
        ]
        + reduce_scratch(n, rows, width)
        + [
            pltpu.VMEM((2, span, ff), BF16),
            pltpu.VMEM((span, ff), BF16),
            pltpu.VMEM((span, ff), BF16),
            pltpu.VMEM((span, width // 2), BF16),
            pltpu.VMEM((span, width // 2), BF16),
            (
                pltpu.VMEM((span, width // 2), BF16),
                pltpu.VMEM((span, width // 2), BF16),
                pltpu.VMEM((2, span, ff), BF16),
            )
            if here > 0
            else (),
            ring_d[0],
            ring_g[0],
            ring_d[1],
            ring_g[1],
            pltpu.SemaphoreType.DMA((8,)),
            pltpu.SemaphoreType.DMA((8,)),
            pltpu.SemaphoreType.DMA((3, 3)),
        ]
        + sems_d
        + sems_g
        + line_sems(n, CHUNKS)
        + line_sems(n),
        compiler_params=pltpu.CompilerParams(
            collective_id=6, has_side_effects=True, vmem_limit_bytes=VMEM_LIMIT
        ),
        name="mlp_back",
    )(
        dgu,
        wga,
        wgb,
        wgc,
        cot,
        branch,
        gain,
        wo,
        hidden,
        dmlp,
        resid,
        hidden_s,
        dmlp_s,
        resid_s,
        dgu_s,
    )


def proj_back_kernel(
    n,
    dproj_ref,
    wq_ref,
    dresid_ref,
    xg_ref,
    gcols_ref,
    gattn_ref,
    gmlp_ref,
    attn_ref,
    dbranch_ref,
    resid_hbm,
    resid_s_hbm,
    dgu_hbm,
    dgu_s_hbm,
    own_in,
    x_in,
    y_in,
    out_ref,
    gain_ref,
    own_out,
    x_out,
    y_out,
    oown_out,
    ox_out,
    oy_out,
    gown_out,
    gx_out,
    gy_out,
    wq,
    xs,
    xs_s,
    dproj_s,
    dbranch,
    dbranch_s,
    attn_s,
    total,
    part,
    got_rows,
    ring,
    got,
    sums,
    ring_o,
    got_o,
    late_buffers,
    late_sems,
    o_sems,
    local_sem,
    s_send,
    s_recv,
    q_send,
    q_recv,
    q_local,
    v_send,
    v_recv,
    m_send,
    m_recv,
    *sems,
):
    s, c, u = where_am_i()
    rows, width = dresid_ref.shape
    span = n * rows
    load = [
        pltpu.make_async_copy(wq_ref, wq, local_sem.at[0]),
        pltpu.make_async_copy(half_columns(xg_ref, s), xs, local_sem.at[1]),
        pltpu.make_async_copy(half_columns(dbranch_ref, s), dbranch, local_sem.at[2]),
    ]
    last = 2 * (dgu_hbm.shape[2] // late_buffers[2].shape[1])
    late = LatePiece(
        last - 1,
        (resid_hbm, resid_s_hbm, dgu_hbm, dgu_s_hbm),
        (gown_out, gx_out, gy_out),
        late_buffers,
        late_sems,
    )
    late.load()
    for copy in load:
        copy.start()
    corner = (s, c ^ 3, u)
    greet(all_uly_peers(n) + plane_peers() + [(None, corner), (None, (1 - s, c, u))])
    gains = GainSum(n, sums, (v_send, v_recv, m_send, m_recv))
    gains.start(gcols_ref, gattn_ref, gmlp_ref)
    sibling = Sibling(s_send, s_recv)
    sibling.start(attn_ref, attn_s)
    sibling.start(half_columns(dbranch_ref, 1 - s), dbranch_s)
    sibling.start(half_columns(xg_ref, 1 - s), xs_s)
    sibling.start(dproj_ref, dproj_s)
    load[0].wait()
    chunk_cols = width // part.shape[0]
    count, size = tiles(span, 512)

    def compute(chunk):
        cols = slice(chunk * chunk_cols, (chunk + 1) * chunk_cols)

        def tile(i, carry):
            where = pl.ds(pl.multiple_of(i * size, size), size)
            part[chunk, where, :] = (
                dot(dproj_ref[0, where, :], wq[0, cols, :], NT)
                + dot(dproj_ref[1, where, :], wq[1, cols, :], NT)
                + dot(dproj_ref[2, where, :], wq[2, cols, :], NT)
            ).astype(BF16)
            return carry

        lax.fori_loop(0, count, tile, 0)

    def place(out, piece, part):
        size = ring.shape[2] if part is None else ring.shape[2] // 2
        return out.at[piece, pl.ds((part or 0) * size, size)]

    weight = PlaneReduce(ring, got, (own_out, x_out, y_out), place, q_send, q_recv, q_local)
    compute_piece = tall_piece((xs, dproj_ref), (xs_s, dproj_s), lambda ref, piece: ref[piece])

    def place_o(out, piece, part):
        size = ring_o.shape[2] if part is None else ring_o.shape[2] // 2
        return out.at[pl.ds((part or 0) * size, size)]

    out_weight = PlaneReduce(ring_o, got_o, (oown_out, ox_out, oy_out), place_o, *o_sems)
    out_piece = wide_piece((attn_ref, dbranch), (attn_s, dbranch_s), lambda p: slice(None))
    pieces = Pieces(
        [late.work(), (out_weight, 0, out_piece)] + [(weight, p, compute_piece) for p in range(3)]
    )

    def compute_and_piece(chunk):
        compute(chunk)
        if chunk == 0:
            pieces.step()
        if chunk == 2:
            load[2].wait()
            sibling.wait(0)
            sibling.wait(1)
            pieces.step()

    def hook(slot):
        if slot == 0:
            load[1].wait()
            sibling.wait(2)
            sibling.wait(3)
            pieces.step()
            gains.over_ctx()
        if slot == 1:
            pieces.step()
            gains.over_uly()
        if slot == 2:
            pieces.step()

    LineReduce(n, rows, part, got_rows, sems[:4]).run(compute_and_piece, total, hook)
    out_ref[...] = (dresid_ref[...] + total[...]).astype(BF16)
    pieces.finish()
    gains.finish(gain_ref)
    weight.finish(3)
    out_weight.finish(1)
    late.plane.finish(1)
    sibling.finish()


class GainSum:
    def __init__(self, n, refs, sems):
        self.n = n
        self.all, self.core, self.plane, self.line = refs
        self.v_send, self.v_recv, self.m_send, self.m_recv = sems
        self.s, self.c, self.u = where_am_i()
        self.sent = []

    def copy(self, k, src, dst, peer):
        return remote(src, dst, self.v_send.at[k], self.v_recv.at[k], peer)

    def go(self, copy):
        copy.start()
        self.sent.append(copy)

    def start(self, cols, attn, mlp):
        half, local = self.all.shape[2], cols.shape[1]
        rows = jnp.zeros((8, half), F32)
        for h in range(2):
            self.all[h] = rows
        mine = self.u * local
        home = pl.ds(pl.multiple_of(lax.rem(mine, half), local), local)
        self.all[pl.ds(mine // half, 1), 0:2, home] = cols[...][None]
        for h in range(2):
            part = slice(h * half, (h + 1) * half)
            self.all[h, 2:3, :] = attn[:, part]
            self.all[h, 3:4, :] = mlp[:, part]
        self.go(self.copy(0, self.all.at[1 - self.s], self.core, (1 - self.s, self.c, self.u)))

    def over_ctx(self):
        s, c, u = self.s, self.c, self.u
        self.copy(0, self.all.at[s], self.core, (1 - s, c, u)).wait_recv()
        size = self.plane.shape[2]
        total = self.all[pl.ds(s, 1)][0] + self.core[...]
        for j in range(4):
            self.plane[j] = total[:, j * size : (j + 1) * size]
        for k in (1, 2, 3):
            self.go(self.copy(k, self.plane.at[c ^ k], self.line.at[k - 1], (s, c ^ k, u)))

    def over_uly(self):
        s, c, u = self.s, self.c, self.u
        total = self.plane[pl.ds(c, 1)][0]
        for k in (1, 2, 3):
            self.copy(k, self.plane.at[c ^ k], self.line.at[k - 1], (s, c ^ k, u)).wait_recv()
            total = total + self.line[k - 1]
        home = self.line.at[3 + u]
        self.line[pl.ds(3 + u, 1)] = total[None]
        for step in range(1, self.n):
            peer = (s, c, lax.rem(u + step, self.n))
            self.go(remote(home, home, self.m_send.at[step - 1], self.m_recv.at[step - 1], peer))

    def finish(self, out):
        s, c, u = self.s, self.c, self.u
        for step in range(1, self.n):
            source = lax.rem(u + self.n - step, self.n)
            place = self.line.at[3 + source]
            remote(
                place, place, self.m_send.at[step - 1], self.m_recv.at[step - 1], (s, c, source)
            ).wait_recv()
        total = self.line[3]
        for j in range(1, self.n):
            total = total + self.line[3 + j]
        out[...] = total[:4]
        for copy in self.sent:
            copy.wait_send()


def proj_back(
    n, dproj, wq, dresid, xg, gain_cols, gain_attn, gain_mlp, attn, dbranch, late, grads
):
    rows, width = dresid.shape
    span, cols = dproj.shape[1:]
    ring, sems = piece_scratch(3, 3, width // 8, cols)
    ring_o, sems_o = piece_scratch(1, 1, cols, width // 8)
    ff = late[2].shape[2]
    return pl.pallas_call(
        functools.partial(proj_back_kernel, n),
        out_shape=(shape((rows, width), BF16), shape((4, width // 8), F32))
        + (shape((3, width // 8, cols), BF16),) * 3
        + (shape((cols, width // 8), BF16),) * 3
        + tuple(shape(g.shape, BF16) for g in grads),
        in_specs=[VM, HB, VM, HB, VM, VM, VM, VM] + [HB] * 8,
        out_specs=(VM, VM) + (HB,) * 9,
        input_output_aliases={13: 8, 14: 9, 15: 10},
        scratch_shapes=[
            pltpu.VMEM((3, width, cols), BF16),
            pltpu.VMEM((span, width // 2), BF16),
            pltpu.VMEM((span, width // 2), BF16),
            pltpu.VMEM((3, span, cols), BF16),
            pltpu.VMEM((span, width // 2), BF16),
            pltpu.VMEM((span, width // 2), BF16),
            pltpu.VMEM((span, cols), BF16),
            pltpu.VMEM((rows, width), F32),
        ]
        + reduce_scratch(n, rows, width)
        + ring
        + [
            (
                pltpu.VMEM((2, 8, width // 2), F32),
                pltpu.VMEM((8, width // 2), F32),
                pltpu.VMEM((4, 8, width // 8), F32),
                pltpu.VMEM((3 + n, 8, width // 8), F32),
            ),
        ]
        + ring_o
        + LatePiece.scratch(span, width, ff)
        + [
            tuple(sems_o),
            pltpu.SemaphoreType.DMA((3,)),
            pltpu.SemaphoreType.DMA((4,)),
            pltpu.SemaphoreType.DMA((4,)),
        ]
        + sems
        + [
            pltpu.SemaphoreType.DMA((4,)),
            pltpu.SemaphoreType.DMA((4,)),
            pltpu.SemaphoreType.DMA((n - 1,)),
            pltpu.SemaphoreType.DMA((n - 1,)),
        ]
        + line_sems(n, CHUNKS),
        compiler_params=pltpu.CompilerParams(
            collective_id=7, has_side_effects=True, vmem_limit_bytes=VMEM_LIMIT
        ),
        name="proj_back",
    )(
        dproj,
        wq,
        dresid,
        xg,
        gain_cols,
        gain_attn,
        gain_mlp,
        attn,
        dbranch,
        *late,
        *grads,
    )


class PiecePlane(PlaneReduce):
    def __init__(self, ring, got, place, send, recv, local):
        super().__init__(ring, got, (0, 1, 2), place, send, recv, local)

    def halves(self):
        return 0, 1

    def own_copies(self, piece, blocks):
        return [
            pltpu.make_async_copy(
                blocks.at[self.c, h], self.place(0, piece, h), self.local.at[piece, h]
            )
            for h in range(2)
        ]

    def add(self, slot, block, half, piece):
        self.ring[slot, block, half] = (
            self.ring[slot, block, half].astype(F32) + self.got[piece, half].astype(F32)
        ).astype(BF16)


class Stream:
    def __init__(self, slots, sem, source, count):
        self.slots, self.sem, self.source, self.count = slots, sem, source, count
        for tile in range(slots.shape[0]):
            self.start(tile)

    def copy(self, tile):
        slot = tile % self.slots.shape[0]
        return pltpu.make_async_copy(self.source(tile), self.slots.at[slot], self.sem.at[slot])

    def start(self, tile):
        if tile < self.count:
            self.copy(tile).start()

    def wait(self, tile):
        self.copy(tile).wait()


def wide_blocks(own, other, out):
    rows = out.shape[2]

    def pair(i, carry):
        where = pl.ds(pl.multiple_of(i * 2 * rows, 2 * rows), 2 * rows)
        total = dot(own[0][...], own[1][:, where], TN) + dot(other[0][...], other[1][:, where], TN)
        total = total.astype(BF16)
        for j in range(2):
            part = total[:, j * rows : (j + 1) * rows]
            out[pl.ds(2 * i + j, 1)] = part.reshape(1, 2, rows, rows)
        return carry

    lax.fori_loop(0, 2, pair, 0)


def tall_blocks(own, other, out):
    rows = out.shape[2]

    def pair(i, carry):
        where = pl.ds(pl.multiple_of(i * 2 * rows, 2 * rows), 2 * rows)
        total = dot(own[0][:, where], own[1][...], TN) + dot(other[0][:, where], other[1][...], TN)
        total = total.astype(BF16)
        for j in range(2):
            for h in range(2):
                out[pl.ds(2 * i + j, 1), h] = total[
                    j * rows : (j + 1) * rows, h * rows : (h + 1) * rows
                ][None]
        return carry

    lax.fori_loop(0, 2, pair, 0)


def backward_kernel(n, names, *refs):
    ref = SimpleNamespace(**dict(zip(names, refs)))
    s, c, u = where_am_i()
    cot_ref, gain_ref, qk_gain_ref = ref.cot, ref.post, ref.gain
    rows, width = cot_ref.shape
    span = n * rows
    weights, dgu, dgu_s = ref.v_weights, ref.v_dgu, ref.v_dgu_s
    hidden, hidden_s, dmlp, dmlp_s = ref.v_hidden, ref.v_hidden_s, ref.v_dmlp, ref.v_dmlp_s
    resid, resid_s, branch, attn = ref.v_resid, ref.v_resid_s, ref.v_branch, ref.v_attn
    part, group, dresid = ref.v_part, ref.v_group, ref.v_dresid
    load = Keep(ref.load_sem)
    chunks, chunk_cols = part.shape[0], part.shape[2]
    kb = ref.wgc.shape[1]
    per_chunk = chunk_cols // kb
    lower, upper = kb // 2, kb // 2


    rows_g = ref.v_ring.shape[3]
    rows_d = cols_g = 2 * rows_g
    tiles_g = dgu.shape[2] // cols_g
    n_d, n_g = hidden.shape[1] // rows_d, 2 * tiles_g

    def hidden_tile(view, piece):
        return view.at[:, pl.ds(piece * rows_d, rows_d)]

    def gate_tile(view, piece):
        ci, tile = divmod(piece, tiles_g)
        return view.at[ci, :, pl.ds(tile * cols_g, cols_g)]

    def load_chunk(chunk):
        slot, copies = chunk % 2, []
        for b in range(per_chunk):
            block = chunk * per_chunk + b
            at = slot * 2 * chunk_cols + b * kb
            for k, (src, first, size) in enumerate(
                (
                    (ref.wga, at, lower),
                    (ref.wgb, at + lower, upper),
                    (ref.wgc, at + chunk_cols, kb),
                )
            ):
                copies.append(
                    pltpu.make_async_copy(
                        src.at[block],
                        weights.at[pl.ds(first, size)],
                        ref.chunk_sem.at[slot, 3 * b + k],
                    )
                )
        return copies

    def start_chunk(chunk):
        for copy in load_chunk(chunk):
            copy.start()

    load_dgu = load(ref.dgu, dgu)
    start_chunk(0)
    load_d = [
        load(ref.hidden, hidden),
        load(half_columns(ref.dmlp, s), dmlp),
        load(ref.dmlp_s, dmlp_s),
    ]
    stream_d = Stream(hidden_s, ref.hs_sem, lambda p: hidden_tile(ref.hidden_s, p), n_d)
    start_chunk(1)
    load_g = [
        load(half_columns(ref.resid, s), resid),
        load(ref.resid_s, resid_s),
        load(ref.branch, branch),
        load(ref.attn, attn),
    ]
    stream_g = Stream(dgu_s, ref.ds_sem, lambda p: gate_tile(ref.dgu_s, p), n_g)
    wo_row = 4 * chunk_cols
    wo_cols = ref.wo.shape[1]
    wo_view = weights.at[pl.ds(wo_row, wo_cols)]
    load_o = load_blocks(ref.wo, wo_view, ref.wo_sem, 1)
    peers = [(s, c ^ k, u) for k in (1, 2, 3)]
    greet(all_uly_peers(n) + [(None, peer) for peer in peers] + [(None, (1 - s, c, u))])
    sibling = Sibling(ref.s_send, ref.s_recv)
    sibling.start(half_columns(ref.xg, 1 - s), ref.v_xs_s)
    load_dgu.wait()
    count, size = tiles(span, 512)

    def compute(chunk):
        wait_all(load_chunk(chunk))
        at = (chunk % 2) * 2 * chunk_cols

        def tile(i, carry):
            where = pl.ds(pl.multiple_of(i * size, size), size)
            part[chunk, where, :] = (
                dot(dgu[0, where, :], weights[at : at + chunk_cols, :], NT)
                + dot(dgu[1, where, :], weights[at + chunk_cols : at + 2 * chunk_cols, :], NT)
            ).astype(BF16)
            return carry

        lax.fori_loop(0, count, tile, 0)
        if chunk + 2 < chunks:
            start_chunk(chunk + 2)

    def place(index, piece, half):
        if piece < n_d or piece == n_d + n_g:
            outs, first = (ref.o_down, piece * rows_d) if piece < n_d else (ref.o_out, 0)
            return outs[index].at[pl.ds(first + half * rows_g, rows_g)]
        if piece < n_d + n_g:
            ci, tile = divmod(piece - n_d, tiles_g)
            lanes = pl.ds(tile * cols_g + half * rows_g, rows_g)
            return ref.o_gate[index].at[ci, :, lanes]
        lanes = pl.ds(half * rows_g, rows_g)
        return ref.o_qkv[index].at[piece - n_d - n_g - 1, :, lanes]

    plane = PiecePlane(
        ref.v_ring, ref.v_got_p, place, ref.p_send, ref.p_recv, ref.p_local
    )
    def down_piece(out, piece):
        stream_d.wait(piece)
        own, other = hidden_tile(hidden, piece), hidden_s.at[piece % hidden_s.shape[0]]
        wide_blocks((own, dmlp), (other, dmlp_s), out)
        stream_d.start(piece + hidden_s.shape[0])

    def gate_piece(out, piece):
        number = piece - n_d
        stream_g.wait(number)
        own, other = gate_tile(dgu, number), dgu_s.at[number % dgu_s.shape[0]]
        tall_blocks((resid, own), (resid_s, other), out)
        stream_g.start(number + dgu_s.shape[0])

    def out_piece(out, piece):
        own = (attn, half_columns(group, s))
        wide_blocks(own, (ref.v_attn_s, ref.v_dbranch_s), out)

    cols = attn.shape[1]
    dproj = hidden.at[:, pl.ds(0, 3 * cols)]

    def qkv_piece(out, piece):
        lanes = pl.ds((piece - n_d - n_g - 1) * cols, cols)
        own = (dmlp, hidden.at[:, lanes])
        tall_blocks(own, (ref.v_xs_s, ref.v_dproj_s.at[:, lanes]), out)

    kinds = [down_piece] * n_d + [gate_piece] * n_g + [out_piece] + [qkv_piece] * 3
    pieces = Pieces([(plane, p, kind) for p, kind in enumerate(kinds)], AHEAD)

    def compute_and_piece(chunk):
        compute(chunk)
        if chunk == 0:
            wait_all(load_d)
        if chunk < 2:
            pieces.step()

    def reduce_hook(slot):
        if slot == 0:
            wait_all(load_g)
        pieces.step()

    sem_r = ref.r_sems
    sem_b = ref.b_sems
    LineReduce(n, rows, part, ref.v_got, sem_r).run(compute_and_piece, dresid, reduce_hook)
    d_resid = dresid[...] + cot_ref[...].astype(F32)
    dresid[...] = d_resid
    values = branch[...]
    inverse = inverse_rms(values)
    d_branch = norm_back(values, inverse, d_resid * gain_ref[0:1, :], width)
    group[rows_of(u, rows), :] = d_branch.astype(BF16)
    gather = LineGather(n, rows, group, ref.g_sems)
    gather.send(0)
    gain_attn = jnp.sum(d_resid * values * inverse, axis=0, keepdims=True)
    ref.v_gattn[...] = gain_attn
    quarter = cols // 4
    load_a = [
        load(ref.every.at[i, t], weights.at[pl.ds(0, span), pl.ds((3 * i + t) * quarter, quarter)])
        for i in range(4)
        for t in range(3)
    ]
    att, proj, tab = ref.v_att, ref.v_proj, ref.v_tab
    load_a.append(load(ref.att, att))
    load_p = [load(ref.proj, proj), load(ref.table.at[rows_of(c, span)], tab)]
    pieces.step()

    def gather_hook(slot):
        if slot == 0:
            pieces.step(2)
        if slot == 1:
            pieces.step()

    gather.run(gather_hook)
    wait_all(load_o)
    dattn, d_out = ref.v_dattn, ref.v_d_out

    def tile(j, carry):
        where = pl.ds(pl.multiple_of(j * size, size), size)
        d_attn = dot(group[where, :], weights[wo_row : wo_row + wo_cols, :], NT).astype(BF16)
        for q in range(4):
            dattn[q, where, :] = d_attn[:, q * quarter : (q + 1) * quarter]
        return carry

    lax.fori_loop(0, count, tile, 0)

    a_send, a_recv, h_send, h_recv = ref.a_send, ref.a_recv, ref.h_send, ref.h_recv
    copies = []
    for k, peer in enumerate(peers):
        copy = remote(dattn.at[peer[1]], d_out.at[c], a_send.at[k], a_recv.at[k], peer)
        copy.start()
        copies.append(copy)
    sibling.start(attn, ref.v_attn_s)
    sibling.start(half_columns(group, 1 - s), ref.v_dbranch_s)
    d_out[pl.ds(c, 1)] = dattn[pl.ds(c, 1)]
    dq, acc, delta, got = ref.v_dq, ref.v_acc, ref.v_delta, ref.v_home
    lse_ref = ref.lse
    dq[...] = jnp.zeros_like(dq)
    bound = ref.bound[:1, :1]
    scale = HEAD_DIM ** (-0.5)
    heads = quarter // HEAD_DIM
    wait_all(load_a)
    for k, peer in enumerate(peers):
        there = d_out.at[peer[1]]
        remote(there, there, a_send.at[k], a_recv.at[k], peer).wait_recv()
    pieces.step()
    for i in range(4):
        for h in range(heads):
            lanes = slice(h * HEAD_DIM, (h + 1) * HEAD_DIM)
            both = jnp.transpose(d_out[i, :, lanes].astype(F32)) * att[i, lanes, :]
            delta[i, h, :1, :] = jnp.sum(both, axis=0, keepdims=True)

    def seen(i, t, h):
        first = (3 * i + t) * quarter + h * HEAD_DIM
        return weights[:span, pl.ds(pl.multiple_of(first, HEAD_DIM), HEAD_DIM)]

    def going(j):
        first = pl.multiple_of(3 * j * quarter, 3 * quarter)
        return weights.at[pl.ds(wo_row, span), pl.ds(first, 3 * quarter)]

    def home(j):
        return remote(going(j), got.at[c], h_send.at[j], h_recv.at[c], (s, j, u))

    def step(j, carry):
        acc[...] = jnp.zeros_like(acc)
        for h in range(heads):
            lanes = slice(h * HEAD_DIM, (h + 1) * HEAD_DIM)

            def update(i, diagonal):
                starts = segment_starts(i * span, span, bound)
                keys, values = seen(j, 1, h), seen(j, 2, h)
                query, grad = seen(i, 0, h), d_out[i, :, lanes]
                scores = dot(keys, query, NT) * SCALE2
                scores = score_mask(scores, j * span, i * span, starts, diagonal)
                probs = jnp.exp2(scores - lse_ref[i, h, :1, :])
                acc[1, :, lanes] += dot(probs.astype(BF16), grad, NN)
                d_probs = dot(values, grad, NT)
                d_scores = (probs * (d_probs - delta[i, h, :1, :])).astype(BF16)
                acc[0, :, lanes] += dot(d_scores, query, NN) * scale
                dq[i, :, lanes] += dot(d_scores, keys, TN) * scale

            def after(i, carry):
                update(i, False)
                return carry

            update(j, True)
            lax.fori_loop(j + 1, 4, after, 0)
        first = pl.multiple_of(3 * j * quarter, 3 * quarter)
        weights[wo_row : wo_row + span, pl.ds(first, 3 * quarter)] = jnp.concatenate(
            [dq[j].astype(BF16), acc[0].astype(BF16), acc[1].astype(BF16)], axis=1
        )

        @pl.when(j != c)
        def _():
            home(j).start()

        return carry

    lax.fori_loop(0, 4, step, 0)
    load_q = [
        load(ref.wq.at[i], weights.at[pl.ds(0, width), pl.ds(i * cols, cols)]) for i in range(3)
    ]
    load_x = load(half_columns(ref.xg, s), dmlp)
    got[pl.ds(c, 1)] = going(c)[...][None]
    wait_all(load_p)
    for k in (1, 2, 3):
        j = c ^ k
        remote(got.at[j], got.at[j], h_send.at[c], h_recv.at[j], (s, j, u)).wait_recv()
    pieces.step()
    kept, inv_ref = (dq, ref.v_dk), ref.inv
    for j in range(4):
        hidden[:, 2 * cols + j * quarter : 2 * cols + (j + 1) * quarter] = got[
            j, :, 2 * quarter : 3 * quarter
        ]

    def source(i, h):
        group, inside = divmod(h, heads)
        first = i * quarter + inside * HEAD_DIM
        return got[group, :, first : first + HEAD_DIM].astype(F32)

    gcols = ref.v_gcols

    def store(i, h, values):
        group, inside = divmod(h, heads)
        kept[i][group, :, inside * HEAD_DIM : (inside + 1) * HEAD_DIM] = values

    dots = norms_back(source, store, proj, inv_ref, qk_gain_ref, tab, gcols)
    total = exchange_rows(n, dots, ref.v_msg, ref.m_send, ref.m_recv)
    means = to_columns(total) / width
    for i in range(2):
        inverse = inv_ref[:, i : i + 1]
        factor = inverse**3 * means[:, i : i + 1]
        for j in range(4):
            lanes = slice(j * quarter, (j + 1) * quarter)
            hidden[:, i * cols + j * quarter : i * cols + (j + 1) * quarter] = (
                inverse * kept[i][j] - proj[i, :, lanes] * factor
            ).astype(BF16)
    sibling.start(dproj, ref.v_dproj_s)
    gains = GainSum(
        n,
        ref.v_sums,
        (ref.v_send, ref.v_recv, ref.n_send, ref.n_recv),
    )
    gains.start(gcols, ref.v_gattn, ref.gmlp)
    wait_all(load_q)

    def compute_input(chunk):
        lanes = slice(chunk * chunk_cols, (chunk + 1) * chunk_cols)

        def tile(i, carry):
            where = pl.ds(pl.multiple_of(i * size, size), size)
            part[chunk, where, :] = dot(
                hidden[where, : 3 * cols], weights[lanes, : 3 * cols], NT
            ).astype(BF16)
            return carry

        lax.fori_loop(0, count, tile, 0)
        if chunk == 0:
            pieces.step()
        if chunk == 2:
            sibling.wait(1)
            sibling.wait(2)
            pieces.step()

    def input_hook(slot):
        if slot == 0:
            load_x.wait()
            sibling.wait(0)
            sibling.wait(3)
            gains.over_ctx()
        if slot == 1:
            gains.over_uly()
        pieces.step()

    LineReduce(n, rows, part, ref.v_got, sem_b).run(compute_input, branch, input_hook)
    ref.o_input[...] = (dresid[...] + branch[...]).astype(BF16)
    pieces.finish()
    gains.finish(ref.o_gain)
    plane.finish(len(kinds))
    sibling.finish()
    for j in range(4):

        @pl.when(j != c)
        def _():
            home(j).wait_send()

    for copy in copies:
        copy.wait_send()


def backward(n, ins):
    given = SimpleNamespace(**ins)
    rows, width = given.cot[0].shape
    span, ff = n * rows, given.hidden[0].shape[1]
    cols = given.attn[0].shape[1]
    quarter = cols // 4
    kb, kc = width // 8, given.wo[0].shape[2]
    n_d, size = tiles(ff, 512)
    dma = pltpu.SemaphoreType.DMA
    outs = dict(
        o_input=shape((rows, width), BF16),
        o_gain=shape((4, width // 8), F32),
        o_down=(shape((ff, kc), BF16),) * 3,
        o_gate=(shape((2, kb, ff), BF16),) * 3,
        o_out=(shape((cols, kc), BF16),) * 3,
        o_qkv=(shape((3, kb, cols), BF16),) * 3,
    )
    buffers = dict(
        v_weights=((width + cols, width), BF16),
        v_dgu=((2, span, ff), BF16),
        v_dgu_s=((3, span, size), BF16),
        v_hidden=((span, ff), BF16),
        v_hidden_s=((2, span, size), BF16),
        v_dmlp=((span, width // 2), BF16),
        v_dmlp_s=((span, width // 2), BF16),
        v_resid=((span, width // 2), BF16),
        v_resid_s=((span, width // 2), BF16),
        v_branch=((rows, width), F32),
        v_attn=((span, cols), BF16),
        v_dresid=((rows, width), F32),
        v_group=((span, width), BF16),
        v_part=((CHUNKS, span, width // CHUNKS), BF16),
        v_got=((CHUNKS, span + rows, width // CHUNKS), BF16),
        v_ring=((AHEAD + 1, 4, 2, kb, kb), BF16),
        v_got_p=((3 * n_d + 4, 2, kb, kb), BF16),
        v_gattn=((1, width), F32),
        v_att=((4, quarter, span), F32),
        v_proj=((2, span, cols), F32),
        v_tab=((span, 128), F32),
        v_dattn=((4, span, quarter), BF16),
        v_d_out=((4, span, quarter), BF16),
        v_dq=((4, span, quarter), F32),
        v_acc=((2, span, quarter), F32),
        v_delta=((4, quarter // HEAD_DIM, 8, span), F32),
        v_home=((4, span, 3 * quarter), BF16),
        v_dk=((4, span, quarter), F32),
        v_gcols=((2, cols), F32),
        v_msg=((n, 8, span), F32),
        v_xs_s=((span, width // 2), BF16),
        v_attn_s=((span, cols), BF16),
        v_dbranch_s=((span, width // 2), BF16),
        v_dproj_s=((span, 3 * cols), BF16),
    )
    sums = tuple(pltpu.VMEM(dims, F32) for dims in (((2, 8, width // 2), F32)[0], ((8, width // 2), F32)[0], ((4, 8, width // 8), F32)[0], ((3 + n, 8, width // 8), F32)[0]))
    sems = dict(
        load_sem=(32,),
        chunk_sem=(2, 3 * (width // CHUNKS // kb)),
        wo_sem=(8,),
        hs_sem=(2,),
        ds_sem=(3,),
        p_send=(3 * n_d + 4, 6),
        p_recv=(3 * n_d + 4, 6),
        p_local=(3 * n_d + 4, 2),
        a_send=(3,),
        a_recv=(3,),
    )
    four, line = (4,), (n - 1,)
    sems.update(s_send=four, s_recv=four, h_send=four, h_recv=four, v_send=four, v_recv=four)
    sems.update(m_send=line, m_recv=line, n_send=line, n_recv=line)
    fours = dict(r_sems=(n - 1, CHUNKS), b_sems=(n - 1, CHUNKS), g_sems=line)
    tuples = dict(v_sums=sums, **{name: (dma(dims),) * 4 for name, dims in fours.items()})
    names = [*ins, *outs, *buffers, *sems, *tuples]
    results = pl.pallas_call(
        functools.partial(backward_kernel, n, names),
        out_shape=list(outs.values()),
        in_specs=[spec for value, spec in ins.values()],
        out_specs=[VM, VM] + [(HB,) * 3] * 4,
        scratch_shapes=[pltpu.VMEM(*buffer) for buffer in buffers.values()]
        + [dma(dims) for dims in sems.values()]
        + list(tuples.values()),
        compiler_params=pltpu.CompilerParams(
            collective_id=11, has_side_effects=True, vmem_limit_bytes=63 * 1024 * 1024
        ),
        name="backward",
    )(*[value for value, spec in ins.values()])
    return SimpleNamespace(**dict(zip(outs, results)))


def rope_table(length):
    freqs = np.power(
        np.float32(ROPE_BASE), -(np.arange(HALF, dtype=np.float32) * 2.0 / HEAD_DIM)
    ).astype(np.float32)
    angles = (np.arange(length, dtype=np.float32)[:, None] * freqs[None, :]).astype(np.float64)
    return np.concatenate([np.cos(angles), np.sin(angles)], axis=1).astype(np.float32)


def on_device(
    n,
    table,
    tokens,
    segment_ids,
    qkv_weight,
    out_weight,
    gate_up,
    down_weight,
    qk_gain,
    post_gain,
    cotangent,
):
    x = tokens[0]
    width = x.shape[1]
    cot = cotangent[0]
    table = jnp.asarray(table)
    if spread_heads(qkv_weight.shape[2]):
        o = forward(
            n,
            x,
            qkv_weight,
            table,
            qk_gain,
            segment_ids,
            out_weight,
            gate_up,
            down_weight,
            post_gain,
        )
        group_x, wq, wo, proj, inv = o.o_xg, o.o_wq, o.o_wo, o.o_proj, o.o_inv
        wga, wgb, wgc, wd = o.o_wga, o.o_wgb, o.o_wgc, o.o_wd
        att, lse, bound, attn = o.o_att, o.o_lse, o.o_bound, o.o_attn
        branch, resid, group_resid = o.o_branch, o.o_resid, o.o_group
        gate, up, hidden = o.o_gate, o.o_up, o.o_hidden
        attn = attn.reshape(group_x.shape[0], -1)
        seen = (o.o_every,)
    else:
        group_x, wq, wo, wga, proj, qkv, inv, zero = project(
            n, x, qkv_weight, table, qk_gain, segment_ids, out_weight, gate_up
        )
        every, wgb, attn, att, lse, bound = attend(*qkv, zero, gate_up)
        seen, back = (qkv[0], every), attend_back
        branch, resid, group_resid, gate, up, hidden, wgc, wd = mlp_in(
            n, attn, wo, x, post_gain, wga, wgb, gate_up, down_weight
        )
    block_out, group_dmlp, dgu, gain_mlp, hidden_s, resid_s, dmlp_s, dgu_s = mlp_out(
        n, hidden, wd, resid, post_gain, cot, gate, up, group_resid
    )
    span, ff = n * x.shape[0], hidden.shape[2]
    branch = branch.reshape(x.shape)
    dgu, dgu_s = dgu.reshape(2, span, ff), dgu_s.reshape(2, span, ff)
    hidden, hidden_s = hidden.reshape(span, ff), hidden_s.reshape(span, ff)
    group_resid, group_dmlp = group_resid.reshape(span, width), group_dmlp.reshape(span, width)
    resid_s, dmlp_s = resid_s.reshape(span, width // 2), dmlp_s.reshape(span, width // 2)
    if spread_heads(qkv_weight.shape[2]):
        o = backward(
            n,
            dict(
                dgu=(dgu, HB),
                dgu_s=(dgu_s, HB),
                wga=(wga, HB),
                wgb=(wgb, HB),
                wgc=(wgc, HB),
                cot=(cot, VM),
                branch=(branch, HB),
                post=(post_gain, VM),
                gain=(qk_gain, VM),
                wo=(wo, HB),
                hidden=(hidden, HB),
                hidden_s=(hidden_s, HB),
                dmlp=(group_dmlp, HB),
                dmlp_s=(dmlp_s, HB),
                resid=(group_resid, HB),
                resid_s=(resid_s, HB),
                every=(seen[0], HB),
                att=(att, HB),
                lse=(lse, VM),
                bound=(bound, VM),
                attn=(attn, HB),
                proj=(proj, HB),
                inv=(inv, VM),
                table=(table, HB),
                wq=(wq, HB),
                xg=(group_x, HB),
                gmlp=(gain_mlp, VM),
            ),
        )
        input_grad, gain_part = o.o_input, o.o_gain
        qkv_grads, out_grads, gate_grads, down_grads = o.o_qkv, o.o_out, o.o_gate, o.o_down
    else:
        d_resid, group_dbranch, d_attn, gain_attn, *grads = mlp_back(
            n,
            dgu,
            wga,
            wgb,
            wgc,
            cot,
            branch,
            post_gain,
            wo,
            hidden,
            group_dmlp,
            group_resid,
            hidden_s,
            resid_s,
            dmlp_s,
            dgu_s,
        )
        gate_grads, down_grads = grads[:3], grads[3:]
        late = (group_resid, resid_s, dgu, dgu_s)
        d_proj, gain_cols, *gate_grads = back(
            n, *seen, d_attn, att, lse, bound, proj, inv, qk_gain, table, late, gate_grads
        )
        input_grad, gain_part, *grads = proj_back(
            n,
            d_proj,
            wq,
            d_resid,
            group_x,
            gain_cols,
            gain_attn,
            gain_mlp,
            attn,
            group_dbranch,
            late,
            gate_grads,
        )
        qkv_grads, out_grads, gate_grads = grads[:3], grads[3:6], grads[6:]

    def total(parts):
        return parts[0].astype(F32) + parts[1].astype(F32) + parts[2].astype(F32)

    return (
        block_out[None],
        input_grad[None],
        total(qkv_grads),
        total(out_grads),
        total(gate_grads),
        total(down_grads),
        gain_part,
    )


def solution(mesh):
    n = mesh.shape["uly"]
    in_specs = (
        P("slot", ("ctx", "uly"), None),
        P("slot", ("ctx", "uly")),
        P(None, ("slot", "ctx"), "uly"),
        P("uly", ("slot", "ctx")),
        P(None, ("slot", "ctx"), "uly"),
        P("uly", ("slot", "ctx")),
        P(None, "uly"),
        P(),
        P("slot", ("ctx", "uly"), None),
    )
    out_specs = (
        P("slot", ("ctx", "uly"), None),
        P("slot", ("ctx", "uly"), None),
        P(None, ("slot", "ctx"), "uly"),
        P("uly", ("slot", "ctx")),
        P(None, ("slot", "ctx"), "uly"),
        P("uly", ("slot", "ctx")),
        P(None, ("slot", "ctx")),
    )

    def whole(tokens, *rest):
        table = rope_table(tokens.shape[1])
        return jax.shard_map(
            functools.partial(on_device, n, table),
            mesh=mesh,
            in_specs=in_specs,
            out_specs=out_specs,
            check_vma=False,
        )(tokens, *rest)

    return whole
```
